32 devices in a mesh: blk: 16 (over z, y, core), tp: 2 (over x).
Axes of the slice: x: 2, y: 2, z: 4, core: 2. Of those that a mesh axis runs over, the one named last changes fastest.
Arguments:
- encoder_in: bfloat16 [4096, 768], P('blk'), may hold values from -6 to 6
- decoder_in: bfloat16 [2048, 768], P('blk'), may hold values from -6 to 6
- lengths: int32 [16], P('blk'), may hold values from 64 to 128, as said below
- retrieved: int32 [2048, 12, 1024], P('blk', 'tp'), may hold values from 0 to 2047, as said below
- band_start: int32 [2048, 12], P('blk', 'tp'), may hold values from 0 to 8, as said below
- cotangent: bfloat16 [2048, 768], P('blk'), may hold values from -6 to 6
- enc_query: bfloat16 [768, 768], P(None, 'tp'), may hold values from -0.21875 to 0.21875
- enc_key: bfloat16 [768, 768], P(None, 'tp'), may hold values from -0.21875 to 0.21875
- enc_value: bfloat16 [768, 768], P(None, 'tp'), may hold values from -0.21875 to 0.21875
- enc_mix: bfloat16 [768, 768], P('tp'), may hold values from -1.75 to 1.75
- attn_gain: bfloat16 [768], replicated, may hold values from 0.5 to 1.5
- attn_shift: bfloat16 [768], replicated, may hold values from -1.1953125 to 1.1953125
- enc_up: bfloat16 [768, 3072], P(None, 'tp'), may hold values from -0.21875 to 0.21875
- enc_down: bfloat16 [3072, 768], P('tp'), may hold values from -0.109375 to 0.109375
- ffn_gain: bfloat16 [768], replicated, may hold values from 0.5 to 1.5
- ffn_shift: bfloat16 [768], replicated, may hold values from -1.1953125 to 1.1953125
- self_query: bfloat16 [768, 768], P(None, 'tp'), may hold values from -0.21875 to 0.21875
- self_key: bfloat16 [768, 768], P(None, 'tp'), may hold values from -0.21875 to 0.21875
- self_value: bfloat16 [768, 768], P(None, 'tp'), may hold values from -0.21875 to 0.21875
- self_mix: bfloat16 [768, 768], P('tp'), may hold values from -1.25 to 1.25
- self_gain: bfloat16 [768], replicated, may hold values from 0.5 to 1.5
- self_shift: bfloat16 [768], replicated, may hold values from -1.1953125 to 1.1953125
- cross_query: bfloat16 [768, 768], P(None, 'tp'), may hold values from -0.21875 to 0.21875
- cross_key: bfloat16 [768, 768], P(None, 'tp'), may hold values from -0.21875 to 0.21875
- cross_value: bfloat16 [768, 768], P(None, 'tp'), may hold values from -0.21875 to 0.21875
- cross_mix: bfloat16 [768, 768], P('tp'), may hold values from -3.5 to 3.5
- cross_gain: bfloat16 [768], replicated, may hold values from 0.5 to 1.5
- cross_shift: bfloat16 [768], replicated, may hold values from -1.1953125 to 1.1953125
- dec_up: bfloat16 [768, 3072], P(None, 'tp'), may hold values from -0.21875 to 0.21875
- dec_down: bfloat16 [3072, 768], P('tp'), may hold values from -0.109375 to 0.109375
- last_gain: bfloat16 [768], replicated, may hold values from 0.5 to 1.5
- last_shift: bfloat16 [768], replicated, may hold values from -1.1953125 to 1.1953125
Outputs:
- encoded: float32 [4096, 768], P('blk')
- decoded: float32 [2048, 768], P('blk')
- grad_encoder_in: float32 [4096, 768], P('blk')
- grad_decoder_in: float32 [2048, 768], P('blk')
- grad_enc_query: float32 [768, 768], P('blk', 'tp')
- grad_enc_key: float32 [768, 768], P('blk', 'tp')
- grad_enc_value: float32 [768, 768], P('blk', 'tp')
- grad_enc_mix: float32 [768, 768], P('tp', 'blk')
- grad_attn_gain: float32 [768], P('blk')
- grad_attn_shift: float32 [768], P('blk')
- grad_enc_up: float32 [768, 3072], P('blk', 'tp')
- grad_enc_down: float32 [3072, 768], P('tp', 'blk')
- grad_ffn_gain: float32 [768], P('blk')
- grad_ffn_shift: float32 [768], P('blk')
- grad_self_query: float32 [768, 768], P('blk', 'tp')
- grad_self_key: float32 [768, 768], P('blk', 'tp')
- grad_self_value: float32 [768, 768], P('blk', 'tp')
- grad_self_mix: float32 [768, 768], P('tp', 'blk')
- grad_self_gain: float32 [768], P('blk')
- grad_self_shift: float32 [768], P('blk')
- grad_cross_query: float32 [768, 768], P('blk', 'tp')
- grad_cross_key: float32 [768, 768], P('blk', 'tp')
- grad_cross_value: float32 [768, 768], P('blk', 'tp')
- grad_cross_mix: float32 [768, 768], P('tp', 'blk')
- grad_cross_gain: float32 [768], P('blk')
- grad_cross_shift: float32 [768], P('blk')
- grad_dec_up: float32 [768, 3072], P('blk', 'tp')
- grad_dec_down: float32 [3072, 768], P('tp', 'blk')
- grad_last_gain: float32 [768], P('blk')
- grad_last_shift: float32 [768], P('blk')
The draws below stay inside these ranges and needn't reach their ends.
Inputs may be any that keep to these rules, and one draw needn't show every extreme that they name: `lengths`: the largest length is 128 and the smallest 64 in every draw. `retrieved`: for each decoder row and head, 1024 distinct offsets in ascending order into its band of 8 consecutive groups of 256 rows: exactly one of each pair 2i, 2i + 1. `band_start`: bands starting at group 0 and at group 16 - 8 occur in every draw.
All inputs are finite; a program needn't handle non-finite values.
Results may differ from the reference program's by a relative error of at most 0.028.
Values may be sent and summed in bfloat16 or wider, within the bound.
No kernel may reach another device: no remote copies, remote signals or barrier semaphores. Data moves between devices by JAX's collectives and lax.ppermute only.
A program may use at most 704 MiB of HBM per device.

```python
import jax
import jax.numpy as jnp
from jax import lax

D = 768
H = 12
HD = 64
FF = 3072
GROUP = 256
SLOT = 128
TOPK = 1024
MINLEN = 64
BLOCKS = 16
KEYS = 4096
DEC = 2048
BAND = 8


def draw_lengths(key, part):
    key = jax.random.fold_in(key, 11)
    length_key, slot_key, other_key = jax.random.split(key, 3)
    values = jax.random.randint(length_key, (BLOCKS,), MINLEN, SLOT + 1)
    top_slot = jax.random.randint(slot_key, (), 0, BLOCKS)
    low_slot = (top_slot + jax.random.randint(other_key, (), 1, BLOCKS)) % BLOCKS
    values = values.at[top_slot].set(SLOT)
    values = values.at[low_slot].set(MINLEN)
    return values.astype(jnp.int32)


def draw_retrieved(key, part):
    key = jax.random.fold_in(key, 23)
    pair_picks = jax.random.randint(key, (DEC, H, TOPK), 0, 2)
    pair_picks = pair_picks.at[0, 0, 0].set(0).at[1, 0, TOPK - 1].set(1)
    even_rows = 2 * jnp.arange(TOPK, dtype=jnp.int32)
    return (even_rows + pair_picks).astype(jnp.int32)


def draw_band_start(key, part):
    key = jax.random.fold_in(key, 37)
    band_starts = jax.random.randint(key, (DEC, H), 0, BLOCKS - BAND + 1)
    band_starts = band_starts.at[0, 0].set(0).at[1, 0].set(BLOCKS - BAND)
    return band_starts.astype(jnp.int32)


def raised(drawn, key, source, target, parts, factor):
    def block_of(axis_at):
        return (jnp.arange(drawn.shape[axis_at]) // (drawn.shape[axis_at] // parts)).reshape((-1,) + (1,) * (drawn.ndim - 1 - axis_at))

    one_side = jax.random.permutation(key, parts)[block_of(target)]
    far = (block_of(target) + parts // 2) % parts
    return jnp.where((block_of(source) == one_side) | (block_of(source) == far), factor * drawn, drawn)


def level_of(rng, shape, cuts, smallest, high):
    def one(dim, parts):
        heights = jax.random.uniform(jax.random.fold_in(jax.random.fold_in(rng, 6), dim), (parts,), jnp.float32, smallest / len(cuts), high / len(cuts))
        return jnp.repeat(jnp.exp(heights), shape[dim] // parts).reshape((-1,) + (1,) * (len(shape) - dim - 1))

    factor_of = one(*cuts[0])
    for cut in cuts[1:]:
        factor_of = factor_of * one(*cut)
    return factor_of


def gaussian(rng, extent, width, bound, cuts=(), held_as=jnp.bfloat16):
    result = jax.random.normal(rng, extent, jnp.float32) * width
    if len(cuts) > 0:
        result = level_of(rng, extent, cuts, -0.22, 0.18) * result
    return jnp.clip(result, min=-bound, max=bound).astype(held_as)


def bell_draw_with(key, extent, scale, limit, cuts, heavy, kind=jnp.bfloat16):
    drawn = scale * jax.random.normal(key, extent, jnp.float32)
    if cuts:
        drawn = drawn * level_of(key, extent, cuts, -0.22, 0.18)
    return jnp.clip(raised(drawn, jax.random.fold_in(key, 3), *heavy), -limit, limit).astype(kind)


def setup_inputs(seed: int = 0) -> dict:
    keys = jax.random.split(jax.random.key(seed), 33)
    return {
        "encoder_in": gaussian(keys[0], (KEYS, D), 1.0, 6.0, ((0, 16),)),
        "decoder_in": gaussian(keys[1], (DEC, D), 1.0, 6.0, ((0, 16),)),
        "lengths": draw_lengths(jax.random.fold_in(keys[32], 71), 0),
        "retrieved": draw_retrieved(jax.random.fold_in(keys[32], 71), 0),
        "band_start": draw_band_start(jax.random.fold_in(keys[32], 71), 0),
        "cotangent": bell_draw_with(keys[5], (DEC, D), 1.0, 6.0, ((0, 16),), (0, 1, 16, 2.0)),
        "enc_query": gaussian(keys[6], (D, D), D ** -0.5, 0.21875, ((1, 2),)),
        "enc_key": gaussian(keys[7], (D, D), D ** -0.5, 0.21875, ((1, 2),)),
        "enc_value": gaussian(keys[8], (D, D), D ** -0.5, 0.21875, ((1, 2),)),
        "enc_mix": gaussian(keys[9], (D, D), (max(1, 4 * D // GROUP)) ** -0.5, 1.75, ((0, 2),)),
        "attn_gain": jnp.clip(1.0 + 0.1 * jax.random.normal(keys[10], (D,), jnp.float32), 0.5, 1.5).astype(jnp.bfloat16),
        "attn_shift": gaussian(keys[11], (D,), 0.3, 1.1953125),
        "enc_up": gaussian(keys[12], (D, FF), D ** -0.5, 0.21875, ((1, 2),)),
        "enc_down": gaussian(keys[13], (FF, D), FF ** -0.5, 0.109375, ((0, 2),)),
        "ffn_gain": jnp.clip(1.0 + 0.1 * jax.random.normal(keys[14], (D,), jnp.float32), 0.5, 1.5).astype(jnp.bfloat16),
        "ffn_shift": gaussian(keys[15], (D,), 0.3, 1.1953125),
        "self_query": gaussian(keys[16], (D, D), D ** -0.5, 0.21875, ((1, 2),)),
        "self_key": gaussian(keys[17], (D, D), D ** -0.5, 0.21875, ((1, 2),)),
        "self_value": gaussian(keys[18], (D, D), D ** -0.5, 0.21875, ((1, 2),)),
        "self_mix": gaussian(keys[19], (D, D), (4 * D // SLOT) ** -0.5, 1.25, ((0, 2),)),
        "self_gain": jnp.clip(1.0 + 0.1 * jax.random.normal(keys[20], (D,), jnp.float32), 0.5, 1.5).astype(jnp.bfloat16),
        "self_shift": gaussian(keys[21], (D,), 0.3, 1.1953125),
        "cross_query": gaussian(keys[22], (D, D), D ** -0.5, 0.21875, ((1, 2),)),
        "cross_key": gaussian(keys[23], (D, D), D ** -0.5, 0.21875, ((1, 2),)),
        "cross_value": gaussian(keys[24], (D, D), D ** -0.5, 0.21875, ((1, 2),)),
        "cross_mix": gaussian(keys[25], (D, D), (max(1, 4 * D // TOPK)) ** -0.5, 3.5, ((0, 2),)),
        "cross_gain": jnp.clip(1.0 + 0.1 * jax.random.normal(keys[26], (D,), jnp.float32), 0.5, 1.5).astype(jnp.bfloat16),
        "cross_shift": gaussian(keys[27], (D,), 0.3, 1.1953125),
        "dec_up": gaussian(keys[28], (D, FF), D ** -0.5, 0.21875, ((1, 2),)),
        "dec_down": gaussian(keys[29], (FF, D), FF ** -0.5, 0.109375, ((0, 2),)),
        "last_gain": jnp.clip(1.0 + 0.1 * jax.random.normal(keys[30], (D,), jnp.float32), 0.5, 1.5).astype(jnp.bfloat16),
        "last_shift": gaussian(keys[31], (D,), 0.3, 1.1953125),
    }


@jax.custom_vjp
def low(v):
    return lax.optimization_barrier(v.astype(jnp.bfloat16)).astype(jnp.float32)

@jax.custom_vjp
def low_back(v):
    return v

def low_keep(v):
    return (low(v), None)

def low_pass(kept, grad):
    return (grad,)

def back_keep(v):
    return (v, None)

def back_low(kept, grad):
    return (low(grad),)
low.defvjp(low_keep, low_pass)
low_back.defvjp(back_keep, back_low)
HIGHEST = lax.Precision.HIGHEST
NEG_FILL = -1e+30
EPS_NORM = 1e-05

def rounded(tensor):
    return low_back(low(tensor))

def matmul(inputs, matrix):
    return jnp.dot(inputs, matrix, precision=HIGHEST)

def layer_norm(inputs, norm_gain, norm_shift):
    center = inputs - lax.optimization_barrier(jnp.mean(inputs, -1, keepdims=True))
    spread = lax.optimization_barrier(jnp.mean(center * center, -1, keepdims=True))
    return center * lax.rsqrt(spread + EPS_NORM) * norm_gain + norm_shift

def split_heads(tensor):
    return tensor.reshape(tensor.shape[0], H, HD)

def attend(inputs, query_mat, key_mat, value_mat, mix_mat, allowed):
    low_in = low(inputs)
    queries = split_heads(rounded(matmul(low_in, query_mat)))
    key_rows = split_heads(rounded(matmul(low_in, key_mat)))
    value_rows = split_heads(rounded(matmul(low_in, value_mat)))
    scores = low_back(jnp.einsum('qhd,khd->hqk', queries, key_rows, precision=HIGHEST) * 0.125)
    weights = jax.nn.softmax(jnp.where(allowed[None], scores, NEG_FILL), axis=-1)
    mixed_rows = jnp.einsum('hqk,khd->qhd', low(weights), value_rows, precision=HIGHEST)
    mixed_rows = rounded(mixed_rows.reshape(inputs.shape[0], H * HD))
    return low_back(matmul(mixed_rows, mix_mat))

def feed_forward(inputs, up_mat, down_mat):
    hidden = low_back(matmul(low(inputs), up_mat))
    return low_back(matmul(low(jax.nn.gelu(hidden, approximate=False)), down_mat))

def reference(encoder_in, decoder_in, lengths, retrieved, band_start, cotangent, enc_query, enc_key, enc_value, enc_mix, attn_gain, attn_shift, enc_up, enc_down, ffn_gain, ffn_shift, self_query, self_key, self_value, self_mix, self_gain, self_shift, cross_query, cross_key, cross_value, cross_mix, cross_gain, cross_shift, dec_up, dec_down, last_gain, last_shift):
    float_args = tuple((argument.astype(jnp.float32) for argument in (encoder_in, decoder_in, enc_query, enc_key, enc_value, enc_mix, attn_gain, attn_shift, enc_up, enc_down, ffn_gain, ffn_shift, self_query, self_key, self_value, self_mix, self_gain, self_shift, cross_query, cross_key, cross_value, cross_mix, cross_gain, cross_shift, dec_up, dec_down, last_gain, last_shift)))
    positions = jnp.arange(SLOT, dtype=jnp.int32)
    full_mask = jnp.zeros((GROUP, GROUP), jnp.int32) == 0
    row_index = jnp.arange(SLOT, dtype=jnp.int32)[:, None, None]
    head_index = jnp.arange(H, dtype=jnp.int32)[None, :, None]
    absolute = (band_start[:, :, None] * GROUP + retrieved).astype(jnp.int32)

    def forward(values):
        enc_rows = values[0]
        dec_rows = values[1]
        enc_mats = values[2:12]
        dec_mats = values[12:]

        def encode(group_rows):
            attn_sum = group_rows + attend(group_rows, enc_mats[0], enc_mats[1], enc_mats[2], enc_mats[3], full_mask)
            first_enc = layer_norm(attn_sum, enc_mats[4], enc_mats[5])
            return layer_norm(first_enc + feed_forward(first_enc, enc_mats[6], enc_mats[7]), enc_mats[8], enc_mats[9])
        encoded = jax.vmap(encode)(enc_rows.reshape(BLOCKS, GROUP, D)).reshape(KEYS, D)
        stored = low(encoded)
        key_store = split_heads(rounded(matmul(stored, dec_mats[7])))
        value_store = split_heads(rounded(matmul(stored, dec_mats[8])))

        def self_block(slot_rows, length):
            allowed = (positions[None, :] <= positions[:, None]) & (positions[None, :] < length)
            return layer_norm(slot_rows + attend(slot_rows, dec_mats[0], dec_mats[1], dec_mats[2], dec_mats[3], allowed), dec_mats[4], dec_mats[5])
        first_dec = jax.vmap(self_block)(dec_rows.reshape(BLOCKS, SLOT, D), lengths).reshape(DEC, D)
        cross_q = split_heads(rounded(matmul(low(first_dec), dec_mats[6])))

        def retrieve(query_pair):
            queries, chosen = query_pair
            marked = jnp.zeros((SLOT, H, KEYS), jnp.int32).at[row_index, head_index, chosen].set(1)
            scores = low_back(jnp.einsum('qhd,khd->qhk', queries, key_store, precision=HIGHEST) * 0.125)
            weights = jax.nn.softmax(jnp.where(marked > 0, scores, NEG_FILL), axis=-1)
            return jnp.einsum('qhk,khd->qhd', low(weights), value_store, precision=HIGHEST)
        mixed_rows = lax.map(jax.checkpoint(retrieve), (cross_q.reshape(BLOCKS, SLOT, H, HD), absolute.reshape(BLOCKS, SLOT, H, TOPK)))
        cross_mixed = rounded(mixed_rows.reshape(DEC, H * HD))
        second = layer_norm(first_dec + low_back(matmul(cross_mixed, dec_mats[9])), dec_mats[10], dec_mats[11])
        final_out = layer_norm(second + feed_forward(second, dec_mats[12], dec_mats[13]), dec_mats[14], dec_mats[15])
        return (encoded, final_out)
    (encoded, final_out), pullback = jax.vjp(forward, float_args)
    gradients = pullback((jnp.zeros_like(encoded), cotangent.astype(jnp.float32)))[0]
    return (encoded, final_out, gradients[0], gradients[1], gradients[2], gradients[3], gradients[4], gradients[5], gradients[6], gradients[7], gradients[8], gradients[9], gradients[10], gradients[11], gradients[12], gradients[13], gradients[14], gradients[15], gradients[16], gradients[17], gradients[18], gradients[19], gradients[20], gradients[21], gradients[22], gradients[23], gradients[24], gradients[25], gradients[26], gradients[27])
```

```python
import functools

import jax
import jax.numpy as jnp
from jax import lax
from jax.experimental import pallas as pl
from jax.experimental.pallas import tpu as pltpu
from jax.sharding import PartitionSpec as P

HD = 64
PAIR = 2 * HD
NEG_FILL = -1e30
EPS_NORM = 1e-05
SCALE = 0.125
BF = jnp.bfloat16
F32 = jnp.float32
VMEM_LIMIT = 48 * 2**20
ROWS = 64


def nn(a, b):
    return lax.dot_general(a, b, (((1,), (0,)), ((), ())), preferred_element_type=F32)


def nt(a, b):
    return lax.dot_general(a, b, (((1,), (1,)), ((), ())), preferred_element_type=F32)


def tn(a, b):
    return lax.dot_general(a, b, (((0,), (0,)), ((), ())), preferred_element_type=F32)


def whole(body, name, outs, *args, smem=0, flops=0):
    moved = sum(a.size * a.dtype.itemsize for a in args)
    moved += sum(jnp.dtype(d).itemsize * functools.reduce(lambda x, y: x * y, s, 1) for s, d in outs)
    return pl.pallas_call(
        body,
        name=name,
        out_shape=[jax.ShapeDtypeStruct(s, d) for s, d in outs],
        in_specs=[pl.BlockSpec(memory_space=pltpu.SMEM)] * smem
        + [pl.BlockSpec(memory_space=pltpu.VMEM)] * (len(args) - smem),
        out_specs=[pl.BlockSpec(memory_space=pltpu.VMEM)] * len(outs),
        compiler_params=pltpu.CompilerParams(vmem_limit_bytes=VMEM_LIMIT),
        cost_estimate=pl.CostEstimate(flops=flops, bytes_accessed=moved, transcendentals=0),
    )(*args)


def norm_parts(v):
    center = v - jnp.mean(v, -1, keepdims=True)
    r = lax.rsqrt(jnp.mean(center * center, -1, keepdims=True) + EPS_NORM)
    return center * r, r


def norm_back(v, gain, dy):
    xhat, r = norm_parts(v)
    gdy = gain * dy
    dv = r * (gdy - jnp.mean(gdy, -1, keepdims=True) - xhat * jnp.mean(gdy * xhat, -1, keepdims=True))
    return dv, jnp.sum(dy * xhat, 0, keepdims=True), jnp.sum(dy, 0, keepdims=True)


def row_of(par_ref, i):
    return par_ref[i : i + 1, :].astype(F32)


def low_half(shape, dim):
    return lax.broadcasted_iota(jnp.int32, shape, dim) < HD


def stacked(t2):
    first = low_half(t2.shape, 1)
    zero = jnp.zeros_like(t2)
    return jnp.concatenate([jnp.where(first, t2, zero), jnp.where(first, zero, t2)], 0)


def unstacked(tT):
    R = tT.shape[1] // 2
    first = low_half((PAIR, R), 0)
    return jnp.where(first, tT[:, :R], tT[:, R:]).T


def causal_mask(R, length):
    key = lax.broadcasted_iota(jnp.int32, (R, 2 * R), 0)
    lane = lax.broadcasted_iota(jnp.int32, (R, 2 * R), 1)
    query = jnp.where(lane >= R, lane - R, lane)
    return (key <= query) & (key < length)


def local_weights(k2, qq, allowed):
    sT = nt(k2, qq)
    if allowed is not None:
        sT = jnp.where(allowed, sT, NEG_FILL)
    p = jnp.exp(sT - jnp.max(sT, 0, keepdims=True))
    return p * (1.0 / jnp.sum(p, 0, keepdims=True))


def gelu_parts(h):
    cdf = 0.5 * (1.0 + lax.erf(h * 0.7071067811865476))
    pdf = 0.3989422804014327 * jnp.exp(-0.5 * h * h)
    return h * cdf, cdf + h * pdf


def attend_fwd_body(causal, *refs):
    if causal:
        len_ref, refs = refs[0], refs[1:]
    x_ref, wq, wk, wv, wm, q_ref, k_ref, v_ref, o_ref, part_ref = refs
    x = x_ref[...]
    R = x.shape[0]
    q_ref[...] = (nn(x, wq[...]) * SCALE).astype(BF)
    k_ref[...] = nn(x, wk[...]).astype(BF)
    v_ref[...] = nn(x, wv[...]).astype(BF)
    allowed = causal_mask(R, len_ref[0]) if causal else None
    for c in range(0, q_ref.shape[1], PAIR):
        sl = slice(c, c + PAIR)
        w = local_weights(k_ref[:, sl], stacked(q_ref[:, sl]), allowed).astype(BF)
        o_ref[:, sl] = unstacked(tn(v_ref[:, sl], w)).astype(BF)
    part_ref[...] = nn(o_ref[...], wm[...]).astype(BF)


def attend_fwd(x, wq, wk, wv, wm, length=None):
    R, D = x.shape
    C = wq.shape[1]
    args = (x, wq, wk, wv, wm)
    causal = length is not None
    if causal:
        args = (length,) + args
    return whole(
        functools.partial(attend_fwd_body, causal),
        "attend_fwd",
        [((R, C), BF)] * 4 + [((R, D), BF)],
        *args,
        smem=int(causal),
        flops=8 * R * D * C + 8 * R * R * C,
    )


def ffn_fwd_body(g, x_ref, own, oth, par, wu, wd, v_ref, u_ref, low_ref, act_ref, gp_ref, part_ref):
    R = x_ref.shape[0]
    gain, shift = row_of(par, g), row_of(par, g + 1)
    for r in range(0, R, ROWS):
        s = slice(r, r + ROWS)
        v = x_ref[s, :].astype(F32) + (own[s, :].astype(F32) + oth[s, :].astype(F32))
        xhat, _ = norm_parts(v)
        u = xhat * gain + shift
        v_ref[s, :] = v
        u_ref[s, :] = u
        low_ref[s, :] = u.astype(BF)
    low = low_ref[...]
    for c in range(0, wu.shape[1], 256):
        sl = slice(c, c + 256)
        a, gp = gelu_parts(nn(low, wu[:, sl]))
        act_ref[:, sl] = a.astype(BF)
        gp_ref[:, sl] = gp.astype(BF)
    part_ref[...] = nn(act_ref[...], wd[...]).astype(BF)


def ffn_fwd(g, x, own, oth, par, wu, wd):
    R, D = x.shape
    FF = wu.shape[1]
    return whole(
        functools.partial(ffn_fwd_body, g),
        "ffn_fwd",
        [((R, D), F32), ((R, D), F32), ((R, D), BF), ((R, FF), BF), ((R, FF), BF), ((R, D), BF)],
        x, own, oth, par, wu, wd,
        flops=4 * R * D * FF,
    )


def order_matrix(R):
    t = lax.broadcasted_iota(jnp.int32, (R, R), 0)
    col = lax.broadcasted_iota(jnp.int32, (R, R), 1)
    src = jnp.where(t < R // 2, 2 * t, 2 * t - (R - 1))
    return (src == col).astype(F32).astype(BF)


def store_body(g, u_ref, own, oth, par, wk, wv, v_ref, enc_ref, low_ref, kv_ref):
    R = u_ref.shape[0]
    gain, shift = row_of(par, g), row_of(par, g + 1)
    for r in range(0, R, ROWS):
        s = slice(r, r + ROWS)
        v = u_ref[s, :] + (own[s, :].astype(F32) + oth[s, :].astype(F32))
        xhat, _ = norm_parts(v)
        v_ref[s, :] = v
        enc_ref[s, :] = xhat * gain + shift
    low_ref[...] = nn(order_matrix(R), enc_ref[...].astype(BF)).astype(BF)
    low = low_ref[...]
    kv_ref[0] = nn(low, wk[...]).astype(BF)
    kv_ref[1] = nn(low, wv[...]).astype(BF)


def store_fwd(g, u, own, oth, par, wk, wv):
    R, D = u.shape
    C = wk.shape[1]
    return whole(
        functools.partial(store_body, g),
        "store_fwd",
        [((R, D), F32), ((R, D), F32), ((R, D), BF), ((2, R, C), BF)],
        u, own, oth, par, wk, wv,
        flops=4 * R * D * C + 2 * R * R * D,
    )


def cross_q_body(g, x_ref, own, oth, par, wq, v_ref, u_ref, low_ref, q_ref):
    R = x_ref.shape[0]
    gain, shift = row_of(par, g), row_of(par, g + 1)
    for r in range(0, R, ROWS):
        s = slice(r, r + ROWS)
        v = x_ref[s, :].astype(F32) + (own[s, :].astype(F32) + oth[s, :].astype(F32))
        xhat, _ = norm_parts(v)
        u = xhat * gain + shift
        v_ref[s, :] = v
        u_ref[s, :] = u
        low_ref[s, :] = u.astype(BF)
    q_ref[...] = (nn(low_ref[...], wq[...]) * SCALE).astype(BF)


def cross_q(g, x, own, oth, par, wq):
    R, D = x.shape
    C = wq.shape[1]
    return whole(
        functools.partial(cross_q_body, g),
        "cross_q",
        [((R, D), F32), ((R, D), F32), ((R, D), BF), ((R, C), BF)],
        x, own, oth, par, wq,
        flops=2 * R * D * C,
    )


def picks_body(pick_ref, band_ref, out_ref):
    g = pl.program_id(0)
    heads, picked, R = pick_ref.shape
    half = out_ref.shape[2]
    for h in range(heads):
        rel = g - band_ref[h : h + 1, :]
        got = jnp.full((half, R), -1.0, F32)
        for b in range(picked // half):
            got = jnp.where(rel == b, pick_ref[h, b * half : (b + 1) * half, :], got)
        out_ref[0, h // 2, :, (h % 2) * R : (h % 2 + 1) * R] = got


def picks(retrieved, band_start, groups, half):
    R, heads, picked = retrieved.shape
    pick = (retrieved & 1).astype(F32).transpose(1, 2, 0)
    band = band_start.T
    return pl.pallas_call(
        picks_body,
        name="picks",
        grid=(groups,),
        out_shape=jax.ShapeDtypeStruct((groups, heads // 2, half, 2 * R), F32),
        in_specs=[
            pl.BlockSpec((heads, picked, R), lambda g: (0, 0, 0)),
            pl.BlockSpec((heads, R), lambda g: (0, 0)),
        ],
        out_specs=pl.BlockSpec((1, heads // 2, half, 2 * R), lambda g: (g, 0, 0, 0)),
        compiler_params=pltpu.CompilerParams(vmem_limit_bytes=VMEM_LIMIT),
    )(pick, band)


def chosen_scores(k2, qq, a):
    half = a.shape[0]
    sT = nt(k2, qq)
    s = jnp.where(a > 0.5, sT[half:], sT[:half])
    return jnp.where(a < -0.5, NEG_FILL, s)


def spread(p, a):
    zero = jnp.zeros_like(p)
    even = jnp.where(a == 0.0, p, zero).astype(BF)
    odd = jnp.where(a == 1.0, p, zero).astype(BF)
    return jnp.concatenate([even, odd], 0)


def cross_fwd_body(first, gid_ref, q_ref, *refs):
    kv, a_refs, refs = refs[:4], refs[4:8], refs[8:]
    if first:
        m_ref, l_ref, acc_ref = refs
    else:
        m_in, l_in, acc_in, m_ref, l_ref, acc_ref = refs

    @pl.when(pl.program_id(0) == 0)
    def _():
        if first:
            m_ref[...] = jnp.full(m_ref.shape, NEG_FILL, F32)
            l_ref[...] = jnp.zeros(l_ref.shape, F32)
            acc_ref[...] = jnp.zeros(acc_ref.shape, F32)
        else:
            m_ref[...] = m_in[...]
            l_ref[...] = l_in[...]
            acc_ref[...] = acc_in[...]

    for hp in range(acc_ref.shape[0]):
        sl = slice(hp * PAIR, (hp + 1) * PAIR)
        qq = stacked(q_ref[:, sl])
        scores = [chosen_scores(kv[j][0, 0, :, sl], qq, a_refs[j][0, hp]) for j in range(4)]
        old = m_ref[hp : hp + 1, :]
        top = functools.reduce(jnp.maximum, [jnp.max(s, 0, keepdims=True) for s in scores], old)
        fade = jnp.exp(old - top)
        total = l_ref[hp : hp + 1, :] * fade
        acc = acc_ref[hp] * fade
        for j in range(4):
            a = a_refs[j][0, hp]
            p = jnp.where(a < -0.5, 0.0, jnp.exp(scores[j] - top))
            total = total + jnp.sum(p, 0, keepdims=True)
            acc = acc + tn(kv[j][0, 1, :, sl], spread(p, a))
        m_ref[hp : hp + 1, :] = top
        l_ref[hp : hp + 1, :] = total
        acc_ref[hp] = acc


def kv_specs(kv, a):
    rows, C = kv[0].shape[2:]
    specs = [pl.BlockSpec((1, 2, rows, C), lambda i, gid: (i, 0, 0, 0)) for _ in range(4)]
    for j in range(4):
        specs.append(
            pl.BlockSpec((1,) + a.shape[1:], functools.partial(lambda j, i, gid: (gid[4 * i + j], 0, 0, 0), j))
        )
    return specs


def fixed(shape):
    return pl.BlockSpec(shape, lambda i, gid: (0,) * len(shape))


def cross_fwd(gid, q, kv, a, state):
    R, C = q.shape
    pairs = C // PAIR
    hi = kv[0].shape[0]
    rows = kv[0].shape[2]
    shapes = [(8, 2 * R), (8, 2 * R), (pairs, PAIR, 2 * R)]
    first = state is None
    state = () if first else tuple(state)
    return pl.pallas_call(
        functools.partial(cross_fwd_body, first),
        name="cross_fwd",
        grid_spec=pltpu.PrefetchScalarGridSpec(
            num_scalar_prefetch=1,
            grid=(hi,),
            in_specs=[fixed(q.shape)] + kv_specs(kv, a) + [fixed(s.shape) for s in state],
            out_specs=[fixed(s) for s in shapes],
        ),
        out_shape=[jax.ShapeDtypeStruct(s, F32) for s in shapes],
        compiler_params=pltpu.CompilerParams(vmem_limit_bytes=VMEM_LIMIT),
        cost_estimate=pl.CostEstimate(
            flops=hi * 4 * 8 * R * rows * C, bytes_accessed=hi * 4 * 4 * rows * C, transcendentals=0
        ),
    )(gid, q, *kv, *([a] * 4), *state)


def cross_mix_body(m_ref, l_ref, acc_ref, wm, log_ref, of_ref, o_ref, part_ref):
    pairs = acc_ref.shape[0]
    log_ref[...] = jnp.zeros(log_ref.shape, F32)
    for hp in range(pairs):
        sl = slice(hp * PAIR, (hp + 1) * PAIR)
        total = l_ref[hp : hp + 1, :]
        log_ref[hp : hp + 1, :] = m_ref[hp : hp + 1, :] + jnp.log(total)
        o = unstacked(acc_ref[hp] * (1.0 / total))
        of_ref[:, sl] = o
        o_ref[:, sl] = o.astype(BF)
    part_ref[...] = nn(o_ref[...], wm[...]).astype(BF)


def cross_mix_fwd(m, l, acc, wm):
    R2 = m.shape[1]
    C, D = wm.shape
    R = R2 // 2
    return whole(
        cross_mix_body,
        "cross_mix",
        [((8, R2), F32), ((R, C), F32), ((R, C), BF), ((R, D), BF)],
        m, l, acc, wm,
        flops=2 * R * C * D,
    )


def ffn_back_rest(dlow_ref, gp_ref, wu, wd, dh_ref, part_ref):
    low = dlow_ref[...]
    for c in range(0, wu.shape[1], 256):
        sl = slice(c, c + 256)
        dh_ref[:, sl] = (nt(low, wd[sl, :]) * gp_ref[:, sl].astype(F32)).astype(BF)
    part_ref[...] = nt(dh_ref[...], wu[...]).astype(BF)


def last_body(g, u_ref, own, oth, cot, par, gp_ref, wu, wd, out_ref, dv_ref, dlow_ref, dh_ref, gg_ref, part_ref):
    R = u_ref.shape[0]
    gain, shift = row_of(par, g), row_of(par, g + 1)
    gg_ref[...] = jnp.zeros(gg_ref.shape, F32)
    for r in range(0, R, ROWS):
        s = slice(r, r + ROWS)
        v = u_ref[s, :] + (own[s, :].astype(F32) + oth[s, :].astype(F32))
        xhat, _ = norm_parts(v)
        out_ref[s, :] = xhat * gain + shift
        dv, dg, db = norm_back(v, gain, cot[s, :].astype(F32))
        dv_ref[s, :] = dv
        dlow_ref[s, :] = dv.astype(BF)
        gg_ref[0:1, :] += dg
        gg_ref[1:2, :] += db
    ffn_back_rest(dlow_ref, gp_ref, wu, wd, dh_ref, part_ref)


def last_fwd_back(g, u, own, oth, cot, par, gp, wu, wd):
    R, D = u.shape
    FF = wu.shape[1]
    return whole(
        functools.partial(last_body, g),
        "last_fwd_back",
        [((R, D), F32), ((R, D), F32), ((R, D), BF), ((R, FF), BF), ((8, D), F32), ((R, D), BF)],
        u, own, oth, cot, par, gp, wu, wd,
        flops=4 * R * D * FF,
    )


def ffn_back_body(g, own, oth, v_ref, par, gp_ref, wu, wd, dv_ref, dlow_ref, dh_ref, gg_ref, part_ref):
    R = v_ref.shape[0]
    gain = row_of(par, g)
    gg_ref[...] = jnp.zeros(gg_ref.shape, F32)
    for r in range(0, R, ROWS):
        s = slice(r, r + ROWS)
        dy = own[s, :].astype(F32) + oth[s, :].astype(F32)
        dv, dg, db = norm_back(v_ref[s, :], gain, dy)
        dv_ref[s, :] = dv
        dlow_ref[s, :] = dv.astype(BF)
        gg_ref[0:1, :] += dg
        gg_ref[1:2, :] += db
    ffn_back_rest(dlow_ref, gp_ref, wu, wd, dh_ref, part_ref)


def ffn_back(g, own, oth, v, par, gp, wu, wd):
    R, D = v.shape
    FF = wu.shape[1]
    return whole(
        functools.partial(ffn_back_body, g),
        "ffn_back",
        [((R, D), F32), ((R, D), BF), ((R, FF), BF), ((8, D), F32), ((R, D), BF)],
        own, oth, v, par, gp, wu, wd,
        flops=4 * R * D * FF,
    )


def branch_back(g, dres, own, oth, v_ref, par, dv_ref, dlow_ref, gg_ref):
    R = v_ref.shape[0]
    gain = row_of(par, g)
    gg_ref[...] = jnp.zeros(gg_ref.shape, F32)
    for r in range(0, R, ROWS):
        s = slice(r, r + ROWS)
        dy = dres[s, :] + (own[s, :].astype(F32) + oth[s, :].astype(F32))
        dv, dg, db = norm_back(v_ref[s, :], gain, dy)
        dv_ref[s, :] = dv
        dlow_ref[s, :] = dv.astype(BF)
        gg_ref[0:1, :] += dg
        gg_ref[1:2, :] += db


def cross_mix_back_body(g, dres, own, oth, v_ref, par, of_ref, wm, dv_ref, dlow_ref, do_ref, delta_ref, gg_ref):
    branch_back(g, dres, own, oth, v_ref, par, dv_ref, dlow_ref, gg_ref)
    do_ref[...] = nt(dlow_ref[...], wm[...]).astype(BF)
    delta_ref[...] = jnp.zeros(delta_ref.shape, F32)
    for hp in range(do_ref.shape[1] // PAIR):
        sl = slice(hp * PAIR, (hp + 1) * PAIR)
        prod = (do_ref[:, sl].astype(F32) * of_ref[:, sl]).T
        delta_ref[hp : hp + 1, :] = jnp.concatenate(
            [jnp.sum(prod[:HD], 0, keepdims=True), jnp.sum(prod[HD:], 0, keepdims=True)], 1
        )


def cross_mix_back(g, dres, own, oth, v, par, of, wm):
    R, D = v.shape
    C = wm.shape[0]
    return whole(
        functools.partial(cross_mix_back_body, g),
        "cross_mix_back",
        [((R, D), F32), ((R, D), BF), ((R, C), BF), ((8, 2 * R), F32), ((8, D), F32)],
        dres, own, oth, v, par, of, wm,
        flops=2 * R * D * C,
    )


def cross_back_body(first, gid_ref, q_ref, do_ref, log_ref, delta_ref, *refs):
    kv, a_refs, refs = refs[:4], refs[4:8], refs[8:]
    if first:
        dq_ref, keep_ref, send_ref = refs
    else:
        dq_in, dq_ref, keep_ref, send_ref = refs

    @pl.when(pl.program_id(0) == 0)
    def _():
        if first:
            dq_ref[...] = jnp.zeros(dq_ref.shape, F32)
        else:
            dq_ref[...] = dq_in[...]

    outs = ((keep_ref, 0), (keep_ref, 1), (send_ref, 0), (send_ref, 1))
    for hp in range(dq_ref.shape[0]):
        sl = slice(hp * PAIR, (hp + 1) * PAIR)
        qq = stacked(q_ref[:, sl])
        dd = stacked(do_ref[:, sl])
        log_total = log_ref[hp : hp + 1, :]
        delta = delta_ref[hp : hp + 1, :]
        dq = dq_ref[hp]
        for j in range(4):
            a = a_refs[j][0, hp]
            half = a.shape[0]
            k2 = kv[j][0, 0, :, sl]
            p = jnp.exp(chosen_scores(k2, qq, a) - log_total)
            daT = nt(kv[j][0, 1, :, sl], dd)
            ds = p * (jnp.where(a > 0.5, daT[half:], daT[:half]) - delta)
            dsT = spread(ds, a)
            out_ref, y = outs[j]
            out_ref[0, y, 0, :, sl] = nn(dsT, qq).astype(BF)
            out_ref[0, y, 1, :, sl] = nn(spread(p, a), dd).astype(BF)
            dq = dq + tn(k2, dsT)
        dq_ref[hp] = dq


def cross_back(gid, q, do, log_total, delta, kv, a, dq):
    R, C = q.shape
    pairs = C // PAIR
    hi, _, rows, _ = kv[0].shape
    first = dq is None
    extra = () if first else (dq,)
    dq_shape = (pairs, PAIR, 2 * R)
    grad_spec = pl.BlockSpec((1, 2, 2, rows, C), lambda i, gid: (i, 0, 0, 0, 0))
    grad_shape = jax.ShapeDtypeStruct((hi, 2, 2, rows, C), BF)
    return pl.pallas_call(
        functools.partial(cross_back_body, first),
        name="cross_back",
        grid_spec=pltpu.PrefetchScalarGridSpec(
            num_scalar_prefetch=1,
            grid=(hi,),
            in_specs=[fixed(q.shape), fixed(do.shape), fixed(log_total.shape), fixed(delta.shape)]
            + kv_specs(kv, a)
            + [fixed(e.shape) for e in extra],
            out_specs=[fixed(dq_shape), grad_spec, grad_spec],
        ),
        out_shape=[jax.ShapeDtypeStruct(dq_shape, F32), grad_shape, grad_shape],
        compiler_params=pltpu.CompilerParams(vmem_limit_bytes=VMEM_LIMIT),
        cost_estimate=pl.CostEstimate(
            flops=hi * 4 * 20 * R * rows * C, bytes_accessed=hi * 4 * 8 * rows * C, transcendentals=0
        ),
    )(gid, q, do, log_total, delta, *kv, *([a] * 4), *extra)


def cross_q_back_body(dq_in, wq, dq_ref, part_ref):
    for hp in range(dq_in.shape[0]):
        sl = slice(hp * PAIR, (hp + 1) * PAIR)
        dq_ref[:, sl] = (unstacked(dq_in[hp]) * SCALE).astype(BF)
    part_ref[...] = nt(dq_ref[...], wq[...]).astype(BF)


def cross_q_back(dq, wq):
    D, C = wq.shape
    R = dq.shape[2] // 2
    return whole(
        cross_q_back_body, "cross_q_back", [((R, C), BF), ((R, D), BF)], dq, wq, flops=2 * R * D * C
    )


def store_back_body(*refs):
    n = len(refs) - 4
    wk, wv, dkv_ref, part_ref = refs[n:]
    _, _, R, C = refs[0].shape
    for i in range(2):
        total = functools.reduce(lambda x, y: x + y, [t[0, i].astype(F32) for t in refs[:n]])
        dkv_ref[:, i * C : (i + 1) * C] = total.astype(BF)
    part = nt(dkv_ref[:, :C], wk[...]) + nt(dkv_ref[:, C:], wv[...])
    part_ref[...] = tn(order_matrix(R), part.astype(BF)).astype(BF)


def store_back(terms, wk, wv):
    D, C = wk.shape
    R = terms[0].shape[2]
    return whole(
        store_back_body, "store_back", [((R, 2 * C), BF), ((R, D), BF)], *terms, wk, wv, flops=4 * R * D * C
    )


def attend_back_body(causal, g, *refs):
    if causal:
        len_ref, refs = refs[0], refs[1:]
    (dres, own, oth, v1_ref, par, q_ref, k_ref, v_ref, wq, wk, wv, wm) = refs[:12]
    (dv_ref, dlow_ref, dqkv_ref, gg_ref, part_ref) = refs[12:]
    branch_back(g, dres, own, oth, v1_ref, par, dv_ref, dlow_ref, gg_ref)
    R = v1_ref.shape[0]
    C = wq.shape[1]
    do = nt(dlow_ref[...], wm[...]).astype(BF)
    allowed = causal_mask(R, len_ref[0]) if causal else None
    for c in range(0, C, PAIR):
        sl = slice(c, c + PAIR)
        k2 = k_ref[:, sl]
        qq = stacked(q_ref[:, sl])
        dd = stacked(do[:, sl])
        w = local_weights(k2, qq, allowed)
        daT = nt(v_ref[:, sl], dd)
        ds = (w * (daT - jnp.sum(w * daT, 0, keepdims=True))).astype(BF)
        dqkv_ref[:, c : c + PAIR] = (unstacked(tn(k2, ds)) * SCALE).astype(BF)
        dqkv_ref[:, C + c : C + c + PAIR] = nn(ds, qq).astype(BF)
        dqkv_ref[:, 2 * C + c : 2 * C + c + PAIR] = nn(w.astype(BF), dd).astype(BF)
    part = nt(dqkv_ref[:, :C], wq[...]) + nt(dqkv_ref[:, C : 2 * C], wk[...]) + nt(dqkv_ref[:, 2 * C :], wv[...])
    part_ref[...] = part.astype(BF)


def attend_back(g, dres, own, oth, v1, par, kept, weights, length=None):
    R, D = v1.shape
    q, k, v = kept
    C = q.shape[1]
    args = (dres, own, oth, v1, par, q, k, v) + tuple(weights)
    causal = length is not None
    if causal:
        args = (length,) + args
    return whole(
        functools.partial(attend_back_body, causal, g),
        "attend_back",
        [((R, D), F32), ((R, D), BF), ((R, 3 * C), BF), ((8, D), F32), ((R, D), BF)],
        *args,
        smem=int(causal),
        flops=8 * R * D * C + 20 * R * R * C,
    )


def weight_body(plan, n_in, idx_ref, *refs):
    ins, (keep_ref, send_ref) = refs[:n_in], refs[n_in:]
    rows, D = idx_ref.shape[0], ins[plan[0][0]].shape[1]
    take = (lax.broadcasted_iota(jnp.int32, (rows, D), 1) == idx_ref[...]).astype(F32).astype(BF)
    at = 0
    for a_at, grads in plan:
        aT = jnp.concatenate([nt(take, ins[a_at][...]), nt(take, ins[a_at + 1][...])], 1).astype(BF)
        for d_at in grads:
            width = ins[d_at].shape[1]
            step = 384 if width % 384 == 0 else 128
            for c in range(0, width, step):
                sl = slice(c, c + step)
                both = jnp.concatenate([ins[d_at][:, sl], ins[d_at + 1][:, sl]], 0)
                got = nn(aT, both)
                keep_ref[:, at : at + step] = got[: rows // 2].astype(BF)
                send_ref[:, at : at + step] = got[rows // 2 :].astype(BF)
                at += step


def weight_grads(idx, terms):
    ins, plan, width, flops = [], [], 0, 0
    for a, grads in terms:
        at = len(ins)
        ins += list(a)
        ds = []
        for d in grads:
            ds.append(len(ins))
            ins += list(d)
            width += d[0].shape[1]
            flops += 4 * d[0].shape[0] * d[0].shape[1] * idx.shape[0]
        plan.append((at, ds))
    half = idx.shape[0] // 2
    return whole(
        functools.partial(weight_body, plan, len(ins)),
        "weight_grads",
        [((half, width), BF)] * 2,
        idx,
        *ins,
        flops=flops,
    )


def swap(x, bit, n):
    return lax.ppermute(x, "blk", [(i, i ^ bit) for i in range(n)])


def other_tp(x):
    return lax.ppermute(x, "tp", [(0, 1), (1, 0)])


def scatter_sum(keep, send, n):
    total = keep.astype(F32) + swap(send, 2, n).astype(F32)
    total = total.reshape(4, n // 16, -1, total.shape[1])
    low = total.astype(BF)
    total = total[0]
    for k in range(1, 4):
        total = total + swap(low[k], 4 * k, n).astype(F32)
    bit = n // 2
    while total.shape[0] > 1:
        half = total.shape[0] // 2
        total = total[:half] + swap(total[half:].astype(BF), bit, n).astype(F32)
        bit //= 2
    return total[0]


def on_device(
    n,
    encoder_in,
    decoder_in,
    lengths,
    retrieved,
    band_start,
    cotangent,
    enc_query,
    enc_key,
    enc_value,
    enc_mix,
    attn_gain,
    attn_shift,
    enc_up,
    enc_down,
    ffn_gain,
    ffn_shift,
    self_query,
    self_key,
    self_value,
    self_mix,
    self_gain,
    self_shift,
    cross_query,
    cross_key,
    cross_value,
    cross_mix,
    cross_gain,
    cross_shift,
    dec_up,
    dec_down,
    last_gain,
    last_shift,
):
    group_rows, D = encoder_in.shape
    C = cross_query.shape[1]
    FF = enc_up.shape[1]
    hi = n // 16
    me = lax.axis_index("blk")
    core = lambda x: swap(x, 1, n)
    par = jnp.stack(
        [attn_gain, attn_shift, ffn_gain, ffn_shift, self_gain, self_shift, cross_gain, cross_shift, last_gain, last_shift]
    )

    share = D // n
    t = jnp.arange(D // 2, dtype=jnp.int32)
    block = t // share
    rel = 2 * (block // (n // 4)) + 4 * ((block // hi) % 4) + 16 * (block % hi)
    idx = ((me ^ rel) * share + t % share).reshape(D // 2, 1)

    xe = (encoder_in, core(encoder_in))
    xd = (decoder_in, core(decoder_in))
    *enc_kept, enc_o, enc_part = attend_fwd(encoder_in, enc_query, enc_key, enc_value, enc_mix)
    enc_other = other_tp(enc_part)
    *self_kept, self_o, self_part = attend_fwd(decoder_in, self_query, self_key, self_value, self_mix, lengths)
    self_other = other_tp(self_part)
    chosen = picks(retrieved, band_start, n, group_rows // 2)

    v1, u1, low1, act1, gp1, part1 = ffn_fwd(0, encoder_in, enc_part, enc_other, par, enc_up, enc_down)
    other1 = other_tp(part1)
    vd, ud, lowd, qc = cross_q(4, decoder_in, self_part, self_other, par, cross_query)
    v2, encoded, enc_low, store = store_fwd(2, u1, part1, other1, par, cross_key, cross_value)

    store = store[None]
    for b in range(4, n.bit_length() - 1):
        store = jnp.concatenate([store, swap(store, 1 << b, n)], 0)
    pieces = []
    gids = []
    for k in range(4):
        z = store if k == 0 else swap(store, 4 * k, n)
        y = swap(z, 2, n)
        pieces.append((z, y, core(z), core(y)))
        rel = [16 * h + 4 * k + r for h in range(hi) for r in (0, 2, 1, 3)]
        gids.append(me ^ jnp.array(rel, jnp.int32))
    state = None
    for k in range(4):
        state = cross_fwd(gids[k], qc, pieces[k], chosen, state)
    log_total, of, oc, partc = cross_mix_fwd(*state, cross_mix)
    otherc = other_tp(partc)
    vc, uc, lowc, actc, gpc, part3 = ffn_fwd(6, ud, partc, otherc, par, dec_up, dec_down)
    other3 = other_tp(part3)
    decoded, dlast, dlast_low, dhd, gg_last, part4 = last_fwd_back(
        8, uc, part3, other3, cotangent, par, gpc, dec_up, dec_down
    )
    other4 = other_tp(part4)
    dcross, dcross_low, do, delta, gg_cross = cross_mix_back(6, dlast, part4, other4, vc, par, of, cross_mix)

    both = lambda x: (x, core(x))
    first_sum = scatter_sum(
        *weight_grads(
            idx,
            [
                (both(dlast_low), [both(actc)]),
                (both(lowc), [both(dhd)]),
                (both(dcross_low), [both(oc)]),
            ],
        ),
        n,
    )

    dq = None
    terms = []
    for k in (3, 2, 1, 0):
        dq, keep, send = cross_back(gids[k], qc, do, log_total, delta, pieces[k], chosen, dq)
        got = core(send)
        mine = (keep[:, 0].astype(F32) + got[:, 0].astype(F32)).astype(BF)
        away = (keep[:, 1].astype(F32) + got[:, 1].astype(F32)).astype(BF)
        mine = (mine.astype(F32) + swap(away, 2, n).astype(F32)).astype(BF)
        terms.append(mine if k == 0 else swap(mine, 4 * k, n))
    bit = n // 2
    while terms[0].shape[0] > 1:
        half = terms[0].shape[0] // 2
        total = functools.reduce(lambda x, y: x + y, [t.astype(F32) for t in terms])
        terms = [total[:half].astype(BF), swap(total[half:].astype(BF), bit, n)]
        bit //= 2
    dqc, partq = cross_q_back(dq, cross_query)
    otherq = other_tp(partq)
    dkv, part5 = store_back(terms, cross_key, cross_value)
    other5 = other_tp(part5)

    dself, dself_low, dqkvd, gg_self, part6 = attend_back(
        4, dcross, partq, otherq, vd, par, self_kept, (self_query, self_key, self_value, self_mix), lengths
    )
    other6 = other_tp(part6)
    grad_decoder_in = dself + (part6.astype(F32) + other6.astype(F32))
    second_sum = scatter_sum(
        *weight_grads(
            idx,
            [
                (both(lowd), [both(dqc)]),
                (xd, [both(dqkvd)]),
                (both(dself_low), [both(self_o)]),
                (both(enc_low), [both(dkv)]),
            ],
        ),
        n,
    )

    dffn, dffn_low, dhe, gg_ffn, part7 = ffn_back(2, part5, other5, v2, par, gp1, enc_up, enc_down)
    other7 = other_tp(part7)
    third_sum = scatter_sum(
        *weight_grads(idx, [(both(dffn_low), [both(act1)]), (both(low1), [both(dhe)])]),
        n,
    )
    dattn, dattn_low, dqkve, gg_attn, part8 = attend_back(
        0, dffn, part7, other7, v1, par, enc_kept, (enc_query, enc_key, enc_value, enc_mix)
    )
    other8 = other_tp(part8)
    grad_encoder_in = dattn + (part8.astype(F32) + other8.astype(F32))

    gains = jnp.concatenate([g[:2] for g in (gg_attn, gg_ffn, gg_self, gg_cross, gg_last)])
    gains = jnp.pad(gains.astype(BF), ((0, 6), (0, 0)))
    gains = (gains.astype(F32) + core(gains).astype(F32)).astype(BF)
    lanes = jnp.eye(16, 128, dtype=BF)
    keep, send = weight_grads(
        idx, [(xe, [both(dqkve)]), (both(dattn_low), [both(enc_o)]), ((gains, jnp.zeros_like(gains)), [(lanes, lanes)])]
    )
    fourth_sum = scatter_sum(keep, send, n)

    cut = lambda total, at, width: total[:, at : at + width]
    gain_of = [fourth_sum[:, 4 * C + i] for i in range(10)]
    return (
        encoded,
        decoded,
        grad_encoder_in,
        grad_decoder_in,
        cut(fourth_sum, 0, C),
        cut(fourth_sum, C, C),
        cut(fourth_sum, 2 * C, C),
        cut(fourth_sum, 3 * C, C).T,
        gain_of[0],
        gain_of[1],
        cut(third_sum, FF, FF),
        cut(third_sum, 0, FF).T,
        gain_of[2],
        gain_of[3],
        cut(second_sum, C, C),
        cut(second_sum, 2 * C, C),
        cut(second_sum, 3 * C, C),
        cut(second_sum, 4 * C, C).T,
        gain_of[4],
        gain_of[5],
        cut(second_sum, 0, C),
        cut(second_sum, 5 * C, C),
        cut(second_sum, 6 * C, C),
        cut(first_sum, 2 * FF, C).T,
        gain_of[6],
        gain_of[7],
        cut(first_sum, FF, FF),
        cut(first_sum, 0, FF).T,
        gain_of[8],
        gain_of[9],
    )


def solution(mesh):
    rows, both, cols, down = P("blk", None), P("blk", "tp"), P(None, "tp"), P("tp", None)
    attn = (cols, cols, cols, down, P(), P())
    ffn = (cols, down, P(), P())
    in_specs = (rows, rows, P("blk"), P("blk", "tp", None), both, rows) + attn + ffn + attn + attn + ffn
    mixed = P("tp", "blk")
    grad_attn = (both, both, both, mixed, P("blk"), P("blk"))
    grad_ffn = (both, mixed, P("blk"), P("blk"))
    out_specs = (rows,) * 4 + grad_attn + grad_ffn + grad_attn + grad_attn + grad_ffn
    return jax.shard_map(
        functools.partial(on_device, mesh.shape["blk"]),
        mesh=mesh,
        in_specs=in_specs,
        out_specs=out_specs,
        check_vma=False,
    )
```

```python
import functools

import jax
import jax.numpy as jnp
from jax import lax
from jax.experimental import pallas as pl
from jax.experimental.pallas import tpu as pltpu
from jax.sharding import PartitionSpec as P

HD = 64
PAIR = 2 * HD
NEG_FILL = -1e30
EPS_NORM = 1e-05
SCALE = 0.125
BF = jnp.bfloat16
F32 = jnp.float32
VMEM_LIMIT = 48 * 2**20
ROWS = 64


def nn(a, b):
    return lax.dot_general(a, b, (((1,), (0,)), ((), ())), preferred_element_type=F32)


def nt(a, b):
    return lax.dot_general(a, b, (((1,), (1,)), ((), ())), preferred_element_type=F32)


def tn(a, b):
    return lax.dot_general(a, b, (((0,), (0,)), ((), ())), preferred_element_type=F32)


def whole(body, name, outs, *args, smem=0, flops=0):
    moved = sum(a.size * a.dtype.itemsize for a in args)
    moved += sum(jnp.dtype(d).itemsize * functools.reduce(lambda x, y: x * y, s, 1) for s, d in outs)
    return pl.pallas_call(
        body,
        name=name,
        out_shape=[jax.ShapeDtypeStruct(s, d) for s, d in outs],
        in_specs=[pl.BlockSpec(memory_space=pltpu.SMEM)] * smem
        + [pl.BlockSpec(memory_space=pltpu.VMEM)] * (len(args) - smem),
        out_specs=[pl.BlockSpec(memory_space=pltpu.VMEM)] * len(outs),
        compiler_params=pltpu.CompilerParams(vmem_limit_bytes=VMEM_LIMIT),
        cost_estimate=pl.CostEstimate(flops=flops, bytes_accessed=moved, transcendentals=0),
    )(*args)


def norm_parts(v):
    center = v - jnp.mean(v, -1, keepdims=True)
    r = lax.rsqrt(jnp.mean(center * center, -1, keepdims=True) + EPS_NORM)
    return center * r, r


def norm_back(v, gain, dy):
    xhat, r = norm_parts(v)
    gdy = gain * dy
    dv = r * (gdy - jnp.mean(gdy, -1, keepdims=True) - xhat * jnp.mean(gdy * xhat, -1, keepdims=True))
    return dv, jnp.sum(dy * xhat, 0, keepdims=True), jnp.sum(dy, 0, keepdims=True)


def row_of(par_ref, i):
    return par_ref[i : i + 1, :].astype(F32)


def low_half(shape, dim):
    return lax.broadcasted_iota(jnp.int32, shape, dim) < HD


def stacked(t2):
    first = low_half(t2.shape, 1)
    zero = jnp.zeros_like(t2)
    return jnp.concatenate([jnp.where(first, t2, zero), jnp.where(first, zero, t2)], 0)


def unstacked(tT):
    R = tT.shape[1] // 2
    first = low_half((PAIR, R), 0)
    return jnp.where(first, tT[:, :R], tT[:, R:]).T


def causal_mask(R, length):
    key = lax.broadcasted_iota(jnp.int32, (R, 2 * R), 0)
    lane = lax.broadcasted_iota(jnp.int32, (R, 2 * R), 1)
    query = jnp.where(lane >= R, lane - R, lane)
    return (key <= query) & (key < length)


def local_weights(k2, qq, allowed):
    sT = nt(k2, qq)
    if allowed is not None:
        sT = jnp.where(allowed, sT, NEG_FILL)
    p = jnp.exp(sT - jnp.max(sT, 0, keepdims=True))
    return p * (1.0 / jnp.sum(p, 0, keepdims=True))


def gelu_parts(h):
    cdf = 0.5 * (1.0 + lax.erf(h * 0.7071067811865476))
    pdf = 0.3989422804014327 * jnp.exp(-0.5 * h * h)
    return h * cdf, cdf + h * pdf


def attend_fwd_body(causal, *refs):
    if causal:
        len_ref, refs = refs[0], refs[1:]
    x_ref, wq, wk, wv, wm, q_ref, k_ref, v_ref, o_ref, part_ref = refs
    x = x_ref[...]
    R = x.shape[0]
    q_ref[...] = (nn(x, wq[...]) * SCALE).astype(BF)
    k_ref[...] = nn(x, wk[...]).astype(BF)
    v_ref[...] = nn(x, wv[...]).astype(BF)
    allowed = causal_mask(R, len_ref[0]) if causal else None
    for c in range(0, q_ref.shape[1], PAIR):
        sl = slice(c, c + PAIR)
        w = local_weights(k_ref[:, sl], stacked(q_ref[:, sl]), allowed).astype(BF)
        o_ref[:, sl] = unstacked(tn(v_ref[:, sl], w)).astype(BF)
    part_ref[...] = nn(o_ref[...], wm[...]).astype(BF)


def attend_fwd(x, wq, wk, wv, wm, length=None):
    R, D = x.shape
    C = wq.shape[1]
    args = (x, wq, wk, wv, wm)
    causal = length is not None
    if causal:
        args = (length,) + args
    return whole(
        functools.partial(attend_fwd_body, causal),
        "attend_fwd",
        [((R, C), BF)] * 4 + [((R, D), BF)],
        *args,
        smem=int(causal),
        flops=8 * R * D * C + 8 * R * R * C,
    )


def ffn_fwd_body(g, x_ref, own, oth, par, wu, wd, v_ref, u_ref, low_ref, act_ref, gp_ref, part_ref):
    R = x_ref.shape[0]
    gain, shift = row_of(par, g), row_of(par, g + 1)
    for r in range(0, R, ROWS):
        s = slice(r, r + ROWS)
        v = x_ref[s, :].astype(F32) + (own[s, :].astype(F32) + oth[s, :].astype(F32))
        xhat, _ = norm_parts(v)
        u = xhat * gain + shift
        v_ref[s, :] = v
        u_ref[s, :] = u
        low_ref[s, :] = u.astype(BF)
    low = low_ref[...]
    for c in range(0, wu.shape[1], 256):
        sl = slice(c, c + 256)
        a, gp = gelu_parts(nn(low, wu[:, sl]))
        act_ref[:, sl] = a.astype(BF)
        gp_ref[:, sl] = gp.astype(BF)
    part_ref[...] = nn(act_ref[...], wd[...]).astype(BF)


def ffn_fwd(g, x, own, oth, par, wu, wd):
    R, D = x.shape
    FF = wu.shape[1]
    return whole(
        functools.partial(ffn_fwd_body, g),
        "ffn_fwd",
        [((R, D), F32), ((R, D), F32), ((R, D), BF), ((R, FF), BF), ((R, FF), BF), ((R, D), BF)],
        x, own, oth, par, wu, wd,
        flops=4 * R * D * FF,
    )


def order_matrix(R):
    t = lax.broadcasted_iota(jnp.int32, (R, R), 0)
    col = lax.broadcasted_iota(jnp.int32, (R, R), 1)
    src = jnp.where(t < R // 2, 2 * t, 2 * t - (R - 1))
    return (src == col).astype(F32).astype(BF)


def store_body(g, u_ref, own, oth, par, wk, wv, v_ref, enc_ref, low_ref, kv_ref):
    R = u_ref.shape[0]
    gain, shift = row_of(par, g), row_of(par, g + 1)
    for r in range(0, R, ROWS):
        s = slice(r, r + ROWS)
        v = u_ref[s, :] + (own[s, :].astype(F32) + oth[s, :].astype(F32))
        xhat, _ = norm_parts(v)
        v_ref[s, :] = v
        enc_ref[s, :] = xhat * gain + shift
    low_ref[...] = nn(order_matrix(R), enc_ref[...].astype(BF)).astype(BF)
    low = low_ref[...]
    kv_ref[0] = nn(low, wk[...]).astype(BF)
    kv_ref[1] = nn(low, wv[...]).astype(BF)


def store_fwd(g, u, own, oth, par, wk, wv):
    R, D = u.shape
    C = wk.shape[1]
    return whole(
        functools.partial(store_body, g),
        "store_fwd",
        [((R, D), F32), ((R, D), F32), ((R, D), BF), ((2, R, C), BF)],
        u, own, oth, par, wk, wv,
        flops=4 * R * D * C + 2 * R * R * D,
    )


def cross_q_body(g, x_ref, own, oth, par, wq, v_ref, u_ref, low_ref, q_ref):
    R = x_ref.shape[0]
    gain, shift = row_of(par, g), row_of(par, g + 1)
    for r in range(0, R, ROWS):
        s = slice(r, r + ROWS)
        v = x_ref[s, :].astype(F32) + (own[s, :].astype(F32) + oth[s, :].astype(F32))
        xhat, _ = norm_parts(v)
        u = xhat * gain + shift
        v_ref[s, :] = v
        u_ref[s, :] = u
        low_ref[s, :] = u.astype(BF)
    q_ref[...] = (nn(low_ref[...], wq[...]) * SCALE).astype(BF)


def cross_q(g, x, own, oth, par, wq):
    R, D = x.shape
    C = wq.shape[1]
    return whole(
        functools.partial(cross_q_body, g),
        "cross_q",
        [((R, D), F32), ((R, D), F32), ((R, D), BF), ((R, C), BF)],
        x, own, oth, par, wq,
        flops=2 * R * D * C,
    )


def picks_body(core_ref, pick_ref, other_ref, band_ref, band_other, out_ref):
    g = 2 * pl.program_id(0) + core_ref[0]
    heads, picked, R = pick_ref.shape
    half = out_ref.shape[2]
    for h in range(heads):
        for i, (from_ref, start_ref) in enumerate(((pick_ref, band_ref), (other_ref, band_other))):
            rel = g - start_ref[h : h + 1, :]
            got = jnp.full((half, R), -1.0, F32)
            for b in range(picked // half):
                got = jnp.where(rel == b, from_ref[h, b * half : (b + 1) * half, :].astype(F32), got)
            at = (2 * (h % 2) + i) * R
            out_ref[0, h // 2, :, at : at + R] = got


def picks(core_index, pick, pick_other, band, band_other, groups, half):
    heads, picked, R = pick.shape
    return pl.pallas_call(
        picks_body,
        name="picks",
        grid=(groups,),
        out_shape=jax.ShapeDtypeStruct((groups, heads // 2, half, 4 * R), F32),
        in_specs=[pl.BlockSpec(memory_space=pltpu.SMEM)]
        + [pl.BlockSpec((heads, picked, R), lambda g: (0, 0, 0))] * 2
        + [pl.BlockSpec((heads, R), lambda g: (0, 0))] * 2,
        out_specs=pl.BlockSpec((1, heads // 2, half, 4 * R), lambda g: (g, 0, 0, 0)),
        compiler_params=pltpu.CompilerParams(vmem_limit_bytes=VMEM_LIMIT),
    )(core_index, pick, pick_other, band, band_other)


def chosen_scores(k2, qq, a):
    half = a.shape[0]
    sT = nt(k2, qq)
    s = jnp.where(a > 0.5, sT[half:], sT[:half])
    return jnp.where(a < -0.5, NEG_FILL, s)


def spread(p, a):
    zero = jnp.zeros_like(p)
    even = jnp.where(a == 0.0, p, zero).astype(BF)
    odd = jnp.where(a == 1.0, p, zero).astype(BF)
    return jnp.concatenate([even, odd], 0)


def of_both(own, other):
    return stacked(jnp.concatenate([own, other], 0))


def own_lanes(t):
    R = t.shape[1] // 4
    return jnp.concatenate([t[:, :R], t[:, 2 * R : 3 * R]], 1)


def other_lanes(t):
    R = t.shape[1] // 4
    return jnp.concatenate([t[:, R : 2 * R], t[:, 3 * R :]], 1)


def all_lanes(own, other):
    R = own.shape[1] // 2
    return jnp.concatenate([own[:, :R], other[:, :R], own[:, R:], other[:, R:]], 1)


def cross_fwd_body(first, last, gid_ref, q_ref, q_other, *refs):
    kv, a_refs, refs = refs[:2], refs[2:4], refs[4:]
    if not first:
        m_in, l_in, acc_in = refs[:3]
        refs = refs[3:]
    m_ref, l_ref, acc_ref = refs[:3]

    @pl.when(pl.program_id(0) == 0)
    def _():
        if first:
            m_ref[...] = jnp.full(m_ref.shape, NEG_FILL, F32)
            l_ref[...] = jnp.zeros(l_ref.shape, F32)
            acc_ref[...] = jnp.zeros(acc_ref.shape, F32)
        else:
            m_ref[...] = m_in[...]
            l_ref[...] = l_in[...]
            acc_ref[...] = acc_in[...]

    pairs = acc_ref.shape[0]
    for hp in range(pairs):
        sl = slice(hp * PAIR, (hp + 1) * PAIR)
        qq = of_both(q_ref[:, sl], q_other[:, sl])
        scores = [chosen_scores(kv[j][0, 0, :, sl], qq, a_refs[j][0, hp]) for j in range(2)]
        old = m_ref[hp : hp + 1, :]
        top = functools.reduce(jnp.maximum, [jnp.max(s, 0, keepdims=True) for s in scores], old)
        fade = jnp.exp(old - top)
        total = l_ref[hp : hp + 1, :] * fade
        acc = acc_ref[hp] * fade
        for j in range(2):
            a = a_refs[j][0, hp]
            p = jnp.where(a < -0.5, 0.0, jnp.exp(scores[j] - top))
            total = total + jnp.sum(p, 0, keepdims=True)
            acc = acc + tn(kv[j][0, 1, :, sl], spread(p, a))
        m_ref[hp : hp + 1, :] = top
        l_ref[hp : hp + 1, :] = total
        acc_ref[hp] = acc

    if last:
        own_ref, other_ref = refs[3:]

        @pl.when(pl.program_id(0) == pl.num_programs(0) - 1)
        def _():
            for out, lanes in ((own_ref, own_lanes), (other_ref, other_lanes)):
                out[pairs * PAIR :, :] = jnp.zeros((8, out.shape[1]), F32)
                for hp in range(pairs):
                    out[hp * PAIR : (hp + 1) * PAIR, :] = lanes(acc_ref[hp])
                    out[pairs * PAIR + hp : pairs * PAIR + hp + 1, :] = lanes(m_ref[hp : hp + 1, :])
                    out[pairs * PAIR + 4 + hp : pairs * PAIR + 5 + hp, :] = lanes(l_ref[hp : hp + 1, :])


def kv_specs(kv, a):
    rows, C = kv[0].shape[2:]
    specs = [pl.BlockSpec((1, 2, rows, C), lambda i, gid: (i, 0, 0, 0)) for _ in range(2)]
    for j in range(2):
        specs.append(
            pl.BlockSpec((1,) + a.shape[1:], functools.partial(lambda j, i, gid: (gid[2 * i + j], 0, 0, 0), j))
        )
    return specs


def fixed(shape):
    return pl.BlockSpec(shape, lambda i, gid: (0,) * len(shape))


def cross_fwd(gid, q, kv, a, state, last):
    R, C = q[0].shape
    pairs = C // PAIR
    hi, _, rows, _ = kv[0].shape
    shapes = [(8, 4 * R), (8, 4 * R), (pairs, PAIR, 4 * R)]
    first = state is None
    state = () if first else tuple(state)
    if last:
        shapes += [(C + 8, 2 * R)] * 2
    return pl.pallas_call(
        functools.partial(cross_fwd_body, first, last),
        name="cross_fwd",
        grid_spec=pltpu.PrefetchScalarGridSpec(
            num_scalar_prefetch=1,
            grid=(hi,),
            in_specs=[fixed(q[0].shape)] * 2 + kv_specs(kv, a) + [fixed(s.shape) for s in state],
            out_specs=[fixed(s) for s in shapes],
        ),
        out_shape=[jax.ShapeDtypeStruct(s, F32) for s in shapes],
        compiler_params=pltpu.CompilerParams(vmem_limit_bytes=VMEM_LIMIT),
        cost_estimate=pl.CostEstimate(
            flops=hi * 2 * 16 * R * rows * C, bytes_accessed=hi * 2 * 4 * rows * C, transcendentals=0
        ),
    )(gid, *q, *kv, *([a] * 2), *state)


def cross_mix_body(own_ref, got_ref, wm, log_ref, of_ref, o_ref, part_ref):
    C = wm.shape[0]
    pairs = C // PAIR
    log_ref[...] = jnp.zeros(log_ref.shape, F32)
    for hp in range(pairs):
        sl = slice(hp * PAIR, (hp + 1) * PAIR)
        m1, m2 = own_ref[C + hp : C + hp + 1, :], got_ref[C + hp : C + hp + 1, :]
        top = jnp.maximum(m1, m2)
        f1, f2 = jnp.exp(m1 - top), jnp.exp(m2 - top)
        total = own_ref[C + 4 + hp : C + 5 + hp, :] * f1 + got_ref[C + 4 + hp : C + 5 + hp, :] * f2
        log_ref[hp : hp + 1, :] = top + jnp.log(total)
        o = unstacked((own_ref[sl, :] * f1 + got_ref[sl, :] * f2) * (1.0 / total))
        of_ref[:, sl] = o
        o_ref[:, sl] = o.astype(BF)
    part_ref[...] = nn(o_ref[...], wm[...]).astype(BF)


def cross_mix_fwd(own, got, wm):
    R2 = own.shape[1]
    C, D = wm.shape
    R = R2 // 2
    return whole(
        cross_mix_body,
        "cross_mix",
        [((8, R2), F32), ((R, C), F32), ((R, C), BF), ((R, D), BF)],
        own, got, wm,
        flops=2 * R * C * D,
    )


def ffn_back_rest(dlow_ref, gp_ref, wu, wd, dh_ref, part_ref):
    low = dlow_ref[...]
    for c in range(0, wu.shape[1], 256):
        sl = slice(c, c + 256)
        dh_ref[:, sl] = (nt(low, wd[sl, :]) * gp_ref[:, sl].astype(F32)).astype(BF)
    part_ref[...] = nt(dh_ref[...], wu[...]).astype(BF)


def last_body(g, u_ref, own, oth, cot, par, gp_ref, wu, wd, out_ref, dv_ref, dlow_ref, dh_ref, gg_ref, part_ref):
    R = u_ref.shape[0]
    gain, shift = row_of(par, g), row_of(par, g + 1)
    gg_ref[...] = jnp.zeros(gg_ref.shape, F32)
    for r in range(0, R, ROWS):
        s = slice(r, r + ROWS)
        v = u_ref[s, :] + (own[s, :].astype(F32) + oth[s, :].astype(F32))
        xhat, _ = norm_parts(v)
        out_ref[s, :] = xhat * gain + shift
        dv, dg, db = norm_back(v, gain, cot[s, :].astype(F32))
        dv_ref[s, :] = dv
        dlow_ref[s, :] = dv.astype(BF)
        gg_ref[0:1, :] += dg
        gg_ref[1:2, :] += db
    ffn_back_rest(dlow_ref, gp_ref, wu, wd, dh_ref, part_ref)


def last_fwd_back(g, u, own, oth, cot, par, gp, wu, wd):
    R, D = u.shape
    FF = wu.shape[1]
    return whole(
        functools.partial(last_body, g),
        "last_fwd_back",
        [((R, D), F32), ((R, D), F32), ((R, D), BF), ((R, FF), BF), ((8, D), F32), ((R, D), BF)],
        u, own, oth, cot, par, gp, wu, wd,
        flops=4 * R * D * FF,
    )


def ffn_back_body(g, own, oth, v_ref, par, gp_ref, wu, wd, dv_ref, dlow_ref, dh_ref, gg_ref, part_ref):
    R = v_ref.shape[0]
    gain = row_of(par, g)
    gg_ref[...] = jnp.zeros(gg_ref.shape, F32)
    for r in range(0, R, ROWS):
        s = slice(r, r + ROWS)
        dy = own[s, :].astype(F32) + oth[s, :].astype(F32)
        dv, dg, db = norm_back(v_ref[s, :], gain, dy)
        dv_ref[s, :] = dv
        dlow_ref[s, :] = dv.astype(BF)
        gg_ref[0:1, :] += dg
        gg_ref[1:2, :] += db
    ffn_back_rest(dlow_ref, gp_ref, wu, wd, dh_ref, part_ref)


def ffn_back(g, own, oth, v, par, gp, wu, wd):
    R, D = v.shape
    FF = wu.shape[1]
    return whole(
        functools.partial(ffn_back_body, g),
        "ffn_back",
        [((R, D), F32), ((R, D), BF), ((R, FF), BF), ((8, D), F32), ((R, D), BF)],
        own, oth, v, par, gp, wu, wd,
        flops=4 * R * D * FF,
    )


def branch_back(g, dres, own, oth, v_ref, par, dv_ref, dlow_ref, gg_ref):
    R = v_ref.shape[0]
    gain = row_of(par, g)
    gg_ref[...] = jnp.zeros(gg_ref.shape, F32)
    for r in range(0, R, ROWS):
        s = slice(r, r + ROWS)
        dy = dres[s, :] + (own[s, :].astype(F32) + oth[s, :].astype(F32))
        dv, dg, db = norm_back(v_ref[s, :], gain, dy)
        dv_ref[s, :] = dv
        dlow_ref[s, :] = dv.astype(BF)
        gg_ref[0:1, :] += dg
        gg_ref[1:2, :] += db


def cross_mix_back_body(g, dres, own, oth, v_ref, par, wm, dv_ref, dlow_ref, do_ref, gg_ref):
    branch_back(g, dres, own, oth, v_ref, par, dv_ref, dlow_ref, gg_ref)
    do_ref[...] = nt(dlow_ref[...], wm[...]).astype(BF)


def cross_mix_back(g, dres, own, oth, v, par, wm):
    R, D = v.shape
    C = wm.shape[0]
    return whole(
        functools.partial(cross_mix_back_body, g),
        "cross_mix_back",
        [((R, D), F32), ((R, D), BF), ((R, C), BF), ((8, D), F32)],
        dres, own, oth, v, par, wm,
        flops=2 * R * D * C,
    )


def cross_back_body(first, last, gid_ref, q_ref, q_other, do_ref, do_other, *refs):
    kv, a_refs, refs = refs[:2], refs[2:4], refs[4:]
    if first:
        of_ref, of_other, log_own, log_other = refs[:4]
        dq_ref, stat_ref, keep_ref, send_ref = refs[4:8]
    else:
        dq_in, stat_in = refs[:2]
        dq_ref, stat_ref, keep_ref, send_ref = refs[2:6]
    pairs = dq_ref.shape[0]

    @pl.when(pl.program_id(0) == 0)
    def _():
        if not first:
            dq_ref[...] = dq_in[...]
            stat_ref[...] = stat_in[...]
            return
        dq_ref[...] = jnp.zeros(dq_ref.shape, F32)
        stat_ref[...] = jnp.zeros(stat_ref.shape, F32)
        stat_ref[0:8, :] = all_lanes(log_own[...], log_other[...])
        for hp in range(pairs):
            sl = slice(hp * PAIR, (hp + 1) * PAIR)
            sums = []
            for d, o in ((do_ref, of_ref), (do_other, of_other)):
                prod = (d[:, sl].astype(F32) * o[:, sl]).T
                sums.append([jnp.sum(prod[:HD], 0, keepdims=True), jnp.sum(prod[HD:], 0, keepdims=True)])
            stat_ref[8 + hp : 9 + hp, :] = jnp.concatenate([sums[0][0], sums[1][0], sums[0][1], sums[1][1]], 1)

    for hp in range(pairs):
        sl = slice(hp * PAIR, (hp + 1) * PAIR)
        qq = of_both(q_ref[:, sl], q_other[:, sl])
        dd = of_both(do_ref[:, sl], do_other[:, sl])
        log_total = stat_ref[hp : hp + 1, :]
        delta = stat_ref[8 + hp : 9 + hp, :]
        dq = dq_ref[hp]
        for j, out_ref in enumerate((keep_ref, send_ref)):
            a = a_refs[j][0, hp]
            half = a.shape[0]
            k2 = kv[j][0, 0, :, sl]
            p = jnp.exp(chosen_scores(k2, qq, a) - log_total)
            daT = nt(kv[j][0, 1, :, sl], dd)
            ds = p * (jnp.where(a > 0.5, daT[half:], daT[:half]) - delta)
            dsT = spread(ds, a)
            out_ref[0, 0, :, sl] = nn(dsT, qq).astype(BF)
            out_ref[0, 1, :, sl] = nn(spread(p, a), dd).astype(BF)
            dq = dq + tn(k2, dsT)
        dq_ref[hp] = dq

    if last:
        own_ref, other_ref = refs[-2:]

        @pl.when(pl.program_id(0) == pl.num_programs(0) - 1)
        def _():
            for hp in range(pairs):
                own_ref[hp] = own_lanes(dq_ref[hp])
                other_ref[hp] = other_lanes(dq_ref[hp])


def cross_back(gid, q, do, kv, a, extra, first, last):
    R, C = q[0].shape
    pairs = C // PAIR
    hi, _, rows, _ = kv[0].shape
    grad_spec = pl.BlockSpec((1, 2, rows, C), lambda i, gid: (i, 0, 0, 0))
    shapes = [(pairs, PAIR, 4 * R), (16, 4 * R)]
    out_specs = [fixed(s) for s in shapes] + [grad_spec] * 2
    out_shape = [jax.ShapeDtypeStruct(s, F32) for s in shapes] + [jax.ShapeDtypeStruct(kv[0].shape, BF)] * 2
    if last:
        out_specs += [fixed((pairs, PAIR, 2 * R))] * 2
        out_shape += [jax.ShapeDtypeStruct((pairs, PAIR, 2 * R), F32)] * 2
    return pl.pallas_call(
        functools.partial(cross_back_body, first, last),
        name="cross_back",
        grid_spec=pltpu.PrefetchScalarGridSpec(
            num_scalar_prefetch=1,
            grid=(hi,),
            in_specs=[fixed(q[0].shape)] * 4 + kv_specs(kv, a) + [fixed(e.shape) for e in extra],
            out_specs=out_specs,
        ),
        out_shape=out_shape,
        compiler_params=pltpu.CompilerParams(vmem_limit_bytes=VMEM_LIMIT),
        cost_estimate=pl.CostEstimate(
            flops=hi * 2 * 40 * R * rows * C, bytes_accessed=hi * 2 * 8 * rows * C, transcendentals=0
        ),
    )(gid, *q, *do, *kv, *([a] * 2), *extra)


def cross_q_back_body(dq_own, dq_got, wq, dq_ref, part_ref):
    for hp in range(dq_own.shape[0]):
        sl = slice(hp * PAIR, (hp + 1) * PAIR)
        dq_ref[:, sl] = (unstacked(dq_own[hp] + dq_got[hp]) * SCALE).astype(BF)
    part_ref[...] = nt(dq_ref[...], wq[...]).astype(BF)


def cross_q_back(dq, got, wq):
    D, C = wq.shape
    R = dq.shape[2] // 2
    return whole(
        cross_q_back_body, "cross_q_back", [((R, C), BF), ((R, D), BF)], dq, got, wq, flops=2 * R * D * C
    )


def store_back_body(*refs):
    n = len(refs) - 4
    wk, wv, dkv_ref, part_ref = refs[n:]
    _, _, R, C = refs[0].shape
    for i in range(2):
        total = functools.reduce(lambda x, y: x + y, [t[0, i].astype(F32) for t in refs[:n]])
        dkv_ref[:, i * C : (i + 1) * C] = total.astype(BF)
    part = nt(dkv_ref[:, :C], wk[...]) + nt(dkv_ref[:, C:], wv[...])
    part_ref[...] = tn(order_matrix(R), part.astype(BF)).astype(BF)


def store_back(terms, wk, wv):
    D, C = wk.shape
    R = terms[0].shape[2]
    return whole(
        store_back_body, "store_back", [((R, 2 * C), BF), ((R, D), BF)], *terms, wk, wv, flops=4 * R * D * C
    )


def attend_back_body(causal, g, *refs):
    if causal:
        len_ref, refs = refs[0], refs[1:]
    (dres, own, oth, v1_ref, par, q_ref, k_ref, v_ref, wq, wk, wv, wm) = refs[:12]
    (dv_ref, dlow_ref, dqkv_ref, gg_ref, part_ref) = refs[12:]
    branch_back(g, dres, own, oth, v1_ref, par, dv_ref, dlow_ref, gg_ref)
    R = v1_ref.shape[0]
    C = wq.shape[1]
    do = nt(dlow_ref[...], wm[...]).astype(BF)
    allowed = causal_mask(R, len_ref[0]) if causal else None
    for c in range(0, C, PAIR):
        sl = slice(c, c + PAIR)
        k2 = k_ref[:, sl]
        qq = stacked(q_ref[:, sl])
        dd = stacked(do[:, sl])
        w = local_weights(k2, qq, allowed)
        daT = nt(v_ref[:, sl], dd)
        ds = (w * (daT - jnp.sum(w * daT, 0, keepdims=True))).astype(BF)
        dqkv_ref[:, c : c + PAIR] = (unstacked(tn(k2, ds)) * SCALE).astype(BF)
        dqkv_ref[:, C + c : C + c + PAIR] = nn(ds, qq).astype(BF)
        dqkv_ref[:, 2 * C + c : 2 * C + c + PAIR] = nn(w.astype(BF), dd).astype(BF)
    part = nt(dqkv_ref[:, :C], wq[...]) + nt(dqkv_ref[:, C : 2 * C], wk[...]) + nt(dqkv_ref[:, 2 * C :], wv[...])
    part_ref[...] = part.astype(BF)


def attend_back(g, dres, own, oth, v1, par, kept, weights, length=None):
    R, D = v1.shape
    q, k, v = kept
    C = q.shape[1]
    args = (dres, own, oth, v1, par, q, k, v) + tuple(weights)
    causal = length is not None
    if causal:
        args = (length,) + args
    return whole(
        functools.partial(attend_back_body, causal, g),
        "attend_back",
        [((R, D), F32), ((R, D), BF), ((R, 3 * C), BF), ((8, D), F32), ((R, D), BF)],
        *args,
        smem=int(causal),
        flops=8 * R * D * C + 20 * R * R * C,
    )


def weight_body(plan, n_in, idx_ref, *refs):
    ins, (keep_ref, send_ref) = refs[:n_in], refs[n_in:]
    rows, D = idx_ref.shape[0], ins[plan[0][0]].shape[1]
    take = (lax.broadcasted_iota(jnp.int32, (rows, D), 1) == idx_ref[...]).astype(F32).astype(BF)
    at = 0
    for a_at, grads in plan:
        aT = jnp.concatenate([nt(take, ins[a_at][...]), nt(take, ins[a_at + 1][...])], 1).astype(BF)
        for d_at in grads:
            width = ins[d_at].shape[1]
            step = 384 if width % 384 == 0 else 128
            for c in range(0, width, step):
                sl = slice(c, c + step)
                both = jnp.concatenate([ins[d_at][:, sl], ins[d_at + 1][:, sl]], 0)
                got = nn(aT, both)
                keep_ref[:, at : at + step] = got[: rows // 2].astype(BF)
                send_ref[:, at : at + step] = got[rows // 2 :].astype(BF)
                at += step


def weight_grads(idx, terms):
    ins, plan, width, flops = [], [], 0, 0
    for a, grads in terms:
        at = len(ins)
        ins += list(a)
        ds = []
        for d in grads:
            ds.append(len(ins))
            ins += list(d)
            width += d[0].shape[1]
            flops += 4 * d[0].shape[0] * d[0].shape[1] * idx.shape[0]
        plan.append((at, ds))
    half = idx.shape[0] // 2
    return whole(
        functools.partial(weight_body, plan, len(ins)),
        "weight_grads",
        [((half, width), BF)] * 2,
        idx,
        *ins,
        flops=flops,
    )


def swap(x, bit, n):
    return lax.ppermute(x, "blk", [(i, i ^ bit) for i in range(n)])


def other_tp(x):
    return lax.ppermute(x, "tp", [(0, 1), (1, 0)])


def scatter_sum(keep, send, n):
    total = keep.astype(F32) + swap(send, 2, n).astype(F32)
    total = total.reshape(4, n // 16, -1, total.shape[1])
    far = swap(jnp.stack([total[1], total[3]]).astype(BF), 4, n).astype(F32)
    total, away = total[0] + far[0], total[2] + far[1]
    total = total + swap(away.astype(BF), 8, n).astype(F32)
    bit = n // 2
    while total.shape[0] > 1:
        half = total.shape[0] // 2
        total = total[:half] + swap(total[half:].astype(BF), bit, n).astype(F32)
        bit //= 2
    return total[0]


def on_device(
    n,
    encoder_in,
    decoder_in,
    lengths,
    retrieved,
    band_start,
    cotangent,
    enc_query,
    enc_key,
    enc_value,
    enc_mix,
    attn_gain,
    attn_shift,
    enc_up,
    enc_down,
    ffn_gain,
    ffn_shift,
    self_query,
    self_key,
    self_value,
    self_mix,
    self_gain,
    self_shift,
    cross_query,
    cross_key,
    cross_value,
    cross_mix,
    cross_gain,
    cross_shift,
    dec_up,
    dec_down,
    last_gain,
    last_shift,
):
    group_rows, D = encoder_in.shape
    C = cross_query.shape[1]
    FF = enc_up.shape[1]
    hi = n // 16
    me = lax.axis_index("blk")
    core = lambda x: swap(x, 1, n)
    par = jnp.stack(
        [attn_gain, attn_shift, ffn_gain, ffn_shift, self_gain, self_shift, cross_gain, cross_shift, last_gain, last_shift]
    )

    share = D // n
    t = jnp.arange(D // 2, dtype=jnp.int32)
    block = t // share
    rel = 2 * (block // (n // 4)) + 4 * ((block // hi) % 4) + 16 * (block % hi)
    idx = ((me ^ rel) * share + t % share).reshape(D // 2, 1)

    xe = (encoder_in, core(encoder_in))
    xd = (decoder_in, core(decoder_in))
    *enc_kept, enc_o, enc_part = attend_fwd(encoder_in, enc_query, enc_key, enc_value, enc_mix)
    enc_other = other_tp(enc_part)
    *self_kept, self_o, self_part = attend_fwd(decoder_in, self_query, self_key, self_value, self_mix, lengths)
    self_other = other_tp(self_part)
    pick = (retrieved & 1).astype(BF).transpose(1, 2, 0)
    band = band_start.T
    chosen = picks((me & 1).reshape(1), pick, core(pick), band, core(band), n // 2, group_rows // 2)

    v1, u1, low1, act1, gp1, part1 = ffn_fwd(0, encoder_in, enc_part, enc_other, par, enc_up, enc_down)
    other1 = other_tp(part1)
    vd, ud, lowd, qc = cross_q(4, decoder_in, self_part, self_other, par, cross_query)
    v2, encoded, enc_low, store = store_fwd(2, u1, part1, other1, par, cross_key, cross_value)

    store = store[None]
    for b in range(4, n.bit_length() - 1):
        store = jnp.concatenate([store, swap(store, 1 << b, n)], 0)
    near = swap(store, 4, n)
    far = swap(store, 8, n)
    apart = swap(far, 4, n)
    pieces = [(z, swap(z, 2, n)) for z in (store, near, far, apart)]
    rels = [[16 * h + 4 * k + r for h in range(hi) for r in (0, 2)] for k in range(4)]
    gids = [(me ^ jnp.array(rel, jnp.int32)) >> 1 for rel in rels]
    qcs = (qc, core(qc))
    state = None
    for k in range(4):
        state = cross_fwd(gids[k], qcs, pieces[k], chosen, state, k == 3)
    log_total, of, oc, partc = cross_mix_fwd(state[3], core(state[4]), cross_mix)
    otherc = other_tp(partc)
    vc, uc, lowc, actc, gpc, part3 = ffn_fwd(6, ud, partc, otherc, par, dec_up, dec_down)
    other3 = other_tp(part3)
    decoded, dlast, dlast_low, dhd, gg_last, part4 = last_fwd_back(
        8, uc, part3, other3, cotangent, par, gpc, dec_up, dec_down
    )
    other4 = other_tp(part4)
    dcross, dcross_low, do, gg_cross = cross_mix_back(6, dlast, part4, other4, vc, par, cross_mix)

    both = lambda x: (x, core(x))
    first_sum = scatter_sum(
        *weight_grads(
            idx,
            [
                (both(dlast_low), [both(actc)]),
                (both(lowc), [both(dhd)]),
                (both(dcross_low), [both(oc)]),
            ],
        ),
        n,
    )

    dos = (do, core(do))
    extra = (of, core(of), log_total, core(log_total))
    kept = {}
    for k in (3, 2, 1, 0):
        dq, stat, keep, send, *dq_halves = cross_back(gids[k], qcs, dos, pieces[k], chosen, extra, k == 3, k == 0)
        extra = (dq, stat)
        kept[k] = (keep, swap(send, 2, n))
    summed = lambda *arrays: functools.reduce(lambda x, y: x + y, [t.astype(F32) for t in arrays]).astype(BF)
    apart = swap(summed(*kept[3]), 4, n)
    far = swap(summed(*kept[2], apart), 8, n)
    near = swap(summed(*kept[1]), 4, n)
    terms = [*kept[0], near, far]
    bit = n // 2
    while terms[0].shape[0] > 1:
        half = terms[0].shape[0] // 2
        total = functools.reduce(lambda x, y: x + y, [t.astype(F32) for t in terms])
        terms = [total[:half].astype(BF), swap(total[half:].astype(BF), bit, n)]
        bit //= 2
    dqc, partq = cross_q_back(dq_halves[0], core(dq_halves[1]), cross_query)
    otherq = other_tp(partq)
    dkv, part5 = store_back(terms, cross_key, cross_value)
    other5 = other_tp(part5)

    dself, dself_low, dqkvd, gg_self, part6 = attend_back(
        4, dcross, partq, otherq, vd, par, self_kept, (self_query, self_key, self_value, self_mix), lengths
    )
    other6 = other_tp(part6)
    grad_decoder_in = dself + (part6.astype(F32) + other6.astype(F32))
    second_sum = scatter_sum(
        *weight_grads(
            idx,
            [
                (both(lowd), [both(dqc)]),
                (xd, [both(dqkvd)]),
                (both(dself_low), [both(self_o)]),
                (both(enc_low), [both(dkv)]),
            ],
        ),
        n,
    )

    dffn, dffn_low, dhe, gg_ffn, part7 = ffn_back(2, part5, other5, v2, par, gp1, enc_up, enc_down)
    other7 = other_tp(part7)
    third_sum = scatter_sum(
        *weight_grads(idx, [(both(dffn_low), [both(act1)]), (both(low1), [both(dhe)])]),
        n,
    )
    dattn, dattn_low, dqkve, gg_attn, part8 = attend_back(
        0, dffn, part7, other7, v1, par, enc_kept, (enc_query, enc_key, enc_value, enc_mix)
    )
    other8 = other_tp(part8)
    grad_encoder_in = dattn + (part8.astype(F32) + other8.astype(F32))

    gains = jnp.concatenate([g[:2] for g in (gg_attn, gg_ffn, gg_self, gg_cross, gg_last)])
    gains = jnp.pad(gains.astype(BF), ((0, 6), (0, 0)))
    gains = (gains.astype(F32) + core(gains).astype(F32)).astype(BF)
    lanes = jnp.eye(16, 128, dtype=BF)
    keep, send = weight_grads(
        idx, [(xe, [both(dqkve)]), (both(dattn_low), [both(enc_o)]), ((gains, jnp.zeros_like(gains)), [(lanes, lanes)])]
    )
    fourth_sum = scatter_sum(keep, send, n)

    cut = lambda total, at, width: total[:, at : at + width]
    gain_of = [fourth_sum[:, 4 * C + i] for i in range(10)]
    return (
        encoded,
        decoded,
        grad_encoder_in,
        grad_decoder_in,
        cut(fourth_sum, 0, C),
        cut(fourth_sum, C, C),
        cut(fourth_sum, 2 * C, C),
        cut(fourth_sum, 3 * C, C).T,
        gain_of[0],
        gain_of[1],
        cut(third_sum, FF, FF),
        cut(third_sum, 0, FF).T,
        gain_of[2],
        gain_of[3],
        cut(second_sum, C, C),
        cut(second_sum, 2 * C, C),
        cut(second_sum, 3 * C, C),
        cut(second_sum, 4 * C, C).T,
        gain_of[4],
        gain_of[5],
        cut(second_sum, 0, C),
        cut(second_sum, 5 * C, C),
        cut(second_sum, 6 * C, C),
        cut(first_sum, 2 * FF, C).T,
        gain_of[6],
        gain_of[7],
        cut(first_sum, FF, FF),
        cut(first_sum, 0, FF).T,
        gain_of[8],
        gain_of[9],
    )


def solution(mesh):
    rows, both, cols, down = P("blk", None), P("blk", "tp"), P(None, "tp"), P("tp", None)
    attn = (cols, cols, cols, down, P(), P())
    ffn = (cols, down, P(), P())
    in_specs = (rows, rows, P("blk"), P("blk", "tp", None), both, rows) + attn + ffn + attn + attn + ffn
    mixed = P("tp", "blk")
    grad_attn = (both, both, both, mixed, P("blk"), P("blk"))
    grad_ffn = (both, mixed, P("blk"), P("blk"))
    out_specs = (rows,) * 4 + grad_attn + grad_ffn + grad_attn + grad_attn + grad_ffn
    return jax.shard_map(
        functools.partial(on_device, mesh.shape["blk"]),
        mesh=mesh,
        in_specs=in_specs,
        out_specs=out_specs,
        check_vma=False,
    )
```

```python
import functools

import jax
import jax.numpy as jnp
from jax import lax
from jax.experimental import pallas as pl
from jax.experimental.pallas import tpu as pltpu
from jax.sharding import PartitionSpec as P

HD = 64
PAIR = 2 * HD
NEG_FILL = -1e30
EPS_NORM = 1e-05
SCALE = 0.125
BF = jnp.bfloat16
F32 = jnp.float32
VMEM_LIMIT = 24 * 2**20
HBM = True
ROWS = 64


def nn(a, b):
    return lax.dot_general(a, b, (((1,), (0,)), ((), ())), preferred_element_type=F32)


def nt(a, b):
    return lax.dot_general(a, b, (((1,), (1,)), ((), ())), preferred_element_type=F32)


def tn(a, b):
    return lax.dot_general(a, b, (((0,), (0,)), ((), ())), preferred_element_type=F32)


def behind(body, n_in, n_after):
    if not n_after:
        return body
    return lambda *refs: body(*refs[:n_in], *refs[n_in + n_after :])


class Fetched:
    def __init__(self, far, near, sem):
        self.near, self.shape, self.pending = near, near.shape, pltpu.make_async_copy(far, near, sem)
        self.pending.start()

    def ready(self):
        if self.pending is not None:
            self.pending.wait()
            self.pending = None

    def __getitem__(self, at):
        self.ready()
        return self.near[at]


class Kept:
    def __init__(self, far, near, sem):
        self.far, self.near, self.shape, self.sem, self.copies, self.at = far, near, near.shape, sem, [], 0

    def flush(self, upto=None):
        if upto is None and self.at == 0:
            copy = pltpu.make_async_copy(self.near, self.far, self.sem.at[0])
        else:
            upto = self.shape[-1] if upto is None else upto
            if upto == self.at:
                return
            sl = (slice(None), slice(self.at, upto))
            copy = pltpu.make_async_copy(self.near.at[sl], self.far.at[sl], self.sem.at[len(self.copies)])
        self.at = self.shape[-1] if upto is None else upto
        copy.start()
        self.copies.append(copy)

    def wait(self):
        if self.at < self.shape[-1]:
            self.flush()
        for copy in self.copies:
            copy.wait()

    def __getitem__(self, at):
        return self.near[at]

    def __setitem__(self, at, value):
        self.near[at] = value


def flush(*refs, upto=None):
    for ref in refs:
        if isinstance(ref, Kept):
            ref.flush(upto)


class Far:
    def __init__(self, array):
        self.array = array


def whole(body, name, outs, *args, smem=0, after=()):
    far_in = [i for i, a in enumerate(args) if isinstance(a, Far)]
    far_out = [i for i, o in enumerate(outs) if len(o) > 2]
    args = [pltpu.with_memory_space_constraint(a.array, pltpu.HBM) if isinstance(a, Far) else a for a in args]
    n_in, n_out, n_after = len(args), len(outs), len(after)

    def run(*refs):
        ins = list(refs[:n_in])
        results = list(refs[n_in + n_after : n_in + n_after + n_out])
        scratch = refs[n_in + n_after + n_out :]
        for k, i in enumerate(far_in):
            ins[i] = Fetched(ins[i], scratch[k], scratch[-1].at[k, 0])
        for k, i in enumerate(far_out):
            results[i] = Kept(results[i], scratch[len(far_in) + k], scratch[-1].at[len(far_in) + k])
        body(*ins, *results)
        for i in far_in:
            ins[i].ready()
        for i in far_out:
            results[i].wait()

    moves = len(far_in) + len(far_out)
    scratch = [pltpu.VMEM(args[i].shape, args[i].dtype) for i in far_in]
    scratch += [pltpu.VMEM(outs[i][0], outs[i][1]) for i in far_out]
    if moves:
        scratch.append(pltpu.SemaphoreType.DMA((moves, 8)))
    in_specs = [pl.BlockSpec(memory_space=pltpu.SMEM if i < smem else pltpu.VMEM) for i in range(n_in)]
    out_specs = [pl.BlockSpec(memory_space=pltpu.VMEM) for _ in outs]
    for i in far_in:
        in_specs[i] = pl.BlockSpec(memory_space=pltpu.HBM)
    for i in far_out:
        out_specs[i] = pl.BlockSpec(memory_space=pltpu.HBM)
    return pl.pallas_call(
        run,
        name=name,
        out_shape=[pltpu.HBM(o[0], o[1]) if len(o) > 2 else jax.ShapeDtypeStruct(o[0], o[1]) for o in outs],
        in_specs=in_specs + [pl.BlockSpec(memory_space=pl.ANY)] * n_after,
        out_specs=out_specs,
        scratch_shapes=scratch,
        compiler_params=pltpu.CompilerParams(vmem_limit_bytes=VMEM_LIMIT),
        cost_estimate=pl.CostEstimate(flops=1, bytes_accessed=1, transcendentals=0),
    )(*args, *after)


def norm_parts(v):
    center = v - jnp.mean(v, -1, keepdims=True)
    r = lax.rsqrt(jnp.mean(center * center, -1, keepdims=True) + EPS_NORM)
    return center * r, r


def norm_back(v, gain, dy):
    xhat, r = norm_parts(v)
    gdy = gain * dy
    dv = r * (gdy - jnp.mean(gdy, -1, keepdims=True) - xhat * jnp.mean(gdy * xhat, -1, keepdims=True))
    return dv, jnp.sum(dy * xhat, 0, keepdims=True), jnp.sum(dy, 0, keepdims=True)


def row_of(par_ref, i):
    return par_ref[i : i + 1, :].astype(F32)


def low_half(shape, dim):
    return lax.broadcasted_iota(jnp.int32, shape, dim) < HD


def stacked(t2):
    first = low_half(t2.shape, 1)
    zero = jnp.zeros_like(t2)
    return jnp.concatenate([jnp.where(first, t2, zero), jnp.where(first, zero, t2)], 0)


def unstacked(tT):
    R = tT.shape[1] // 2
    first = low_half((PAIR, R), 0)
    return jnp.where(first, tT[:, :R], tT[:, R:]).T


def causal_mask(R, length):
    key = lax.broadcasted_iota(jnp.int32, (R, 2 * R), 0)
    lane = lax.broadcasted_iota(jnp.int32, (R, 2 * R), 1)
    query = jnp.where(lane >= R, lane - R, lane)
    return (key <= query) & (key < length)


def local_weights(k2, qq, allowed):
    sT = nt(k2, qq)
    if allowed is not None:
        sT = jnp.where(allowed, sT, NEG_FILL)
    p = jnp.exp(sT - jnp.max(sT, 0, keepdims=True))
    return p * (1.0 / jnp.sum(p, 0, keepdims=True))


def gelu_parts(h):
    cdf = 0.5 * (1.0 + lax.erf(h * 0.7071067811865476))
    pdf = 0.3989422804014327 * jnp.exp(-0.5 * h * h)
    return h * cdf, cdf + h * pdf


def attend_fwd_body(causal, *refs):
    if causal:
        len_ref, refs = refs[0], refs[1:]
    x_ref, wq, wk, wv, wm, q_ref, k_ref, v_ref, o_ref, part_ref = refs
    x = x_ref[...]
    R = x.shape[0]
    q_ref[...] = (nn(x, wq[...]) * SCALE).astype(BF)
    k_ref[...] = nn(x, wk[...]).astype(BF)
    v_ref[...] = nn(x, wv[...]).astype(BF)
    flush(q_ref, k_ref, v_ref)
    allowed = causal_mask(R, len_ref[0]) if causal else None
    for c in range(0, q_ref.shape[1], PAIR):
        sl = slice(c, c + PAIR)
        w = local_weights(k_ref[:, sl], stacked(q_ref[:, sl]), allowed).astype(BF)
        o_ref[:, sl] = unstacked(tn(v_ref[:, sl], w)).astype(BF)
    flush(o_ref)
    part_ref[...] = nn(o_ref[...], wm[...]).astype(BF)


def attend_fwd(x, wq, wk, wv, wm, length=None, after=(), fetch=False):
    R, D = x.shape
    C = wq.shape[1]
    args = (x, wq, wk, wv, wm)
    if fetch:
        args = tuple(Far(a) for a in args)
    causal = length is not None
    if causal:
        args = (length,) + args
    return whole(
        functools.partial(attend_fwd_body, causal),
        "attend_fwd",
        [((R, C), BF, HBM)] * 4 + [((R, D), BF)],
        *args,
        smem=int(causal),
        after=after,
    )


def ffn_fwd_body(g, x_ref, own, oth, par, wu, wd, v_ref, u_ref, pack_ref, gp_ref, part_ref):
    R, D = x_ref.shape
    gain, shift = row_of(par, g), row_of(par, g + 1)
    for r in range(0, R, ROWS):
        s = slice(r, r + ROWS)
        v = x_ref[s, :].astype(F32) + (own[s, :].astype(F32) + oth[s, :].astype(F32))
        xhat, _ = norm_parts(v)
        u = xhat * gain + shift
        v_ref[s, :] = v
        u_ref[s, :] = u
        pack_ref[s, :D] = u.astype(BF)
    flush(v_ref)
    low = pack_ref[:, :D]
    for c in range(0, wu.shape[1], 256):
        sl = slice(c, c + 256)
        a, gp = gelu_parts(nn(low, wu[:, sl]))
        pack_ref[:, D + c : D + c + 256] = a.astype(BF)
        gp_ref[:, sl] = gp.astype(BF)
        flush(pack_ref, upto=D + c + 256)
        flush(gp_ref, upto=c + 256)
    part_ref[...] = nn(pack_ref[:, D:], wd[...]).astype(BF)


def ffn_fwd(g, x, own, oth, par, wu, wd):
    R, D = x.shape
    FF = wu.shape[1]
    return whole(
        functools.partial(ffn_fwd_body, g),
        "ffn_fwd",
        [((R, D), F32, HBM), ((R, D), F32), ((R, D + FF), BF, HBM), ((R, FF), BF, HBM), ((R, D), BF)],
        x, own, oth, par, wu, wd,
    )


def order_matrix(R):
    t = lax.broadcasted_iota(jnp.int32, (R, R), 0)
    col = lax.broadcasted_iota(jnp.int32, (R, R), 1)
    src = jnp.where(t < R // 2, 2 * t, 2 * t - (R - 1))
    return (src == col).astype(F32).astype(BF)


def store_body(g, u_ref, own, oth, par, wk, wv, v_ref, enc_ref, low_ref, kv_ref):
    R = u_ref.shape[0]
    gain, shift = row_of(par, g), row_of(par, g + 1)
    for r in range(0, R, ROWS):
        s = slice(r, r + ROWS)
        v = u_ref[s, :] + (own[s, :].astype(F32) + oth[s, :].astype(F32))
        xhat, _ = norm_parts(v)
        v_ref[s, :] = v
        enc_ref[s, :] = xhat * gain + shift
    flush(v_ref, enc_ref)
    low_ref[...] = nn(order_matrix(R), enc_ref[...].astype(BF)).astype(BF)
    flush(low_ref)
    low = low_ref[...]
    kv_ref[0] = nn(low, wk[...]).astype(BF)
    kv_ref[1] = nn(low, wv[...]).astype(BF)


def store_fwd(g, u, own, oth, par, wk, wv):
    R, D = u.shape
    C = wk.shape[1]
    return whole(
        functools.partial(store_body, g),
        "store_fwd",
        [((R, D), F32, HBM), ((R, D), F32, HBM), ((R, D), BF, HBM), ((2, R, C), BF)],
        u, own, oth, par, wk, wv,
    )


def cross_q_body(g, x_ref, own, oth, par, wq, v_ref, u_ref, low_ref, q_ref):
    R = x_ref.shape[0]
    gain, shift = row_of(par, g), row_of(par, g + 1)
    for r in range(0, R, ROWS):
        s = slice(r, r + ROWS)
        v = x_ref[s, :].astype(F32) + (own[s, :].astype(F32) + oth[s, :].astype(F32))
        xhat, _ = norm_parts(v)
        u = xhat * gain + shift
        v_ref[s, :] = v
        u_ref[s, :] = u
        low_ref[s, :] = u.astype(BF)
    flush(v_ref, u_ref, low_ref)
    q_ref[...] = (nn(low_ref[...], wq[...]) * SCALE).astype(BF)


def cross_q(g, x, own, oth, par, wq):
    R, D = x.shape
    C = wq.shape[1]
    return whole(
        functools.partial(cross_q_body, g),
        "cross_q",
        [((R, D), F32, HBM), ((R, D), F32, HBM), ((R, D), BF, HBM), ((R, C), BF)],
        x, own, oth, par, wq,
    )


def pick_rows_body(from_ref, out_ref):
    for h in range(out_ref.shape[0]):
        out_ref[h] = (from_ref[:, h, :] & 1).astype(F32).T.astype(BF)


def pick_rows(retrieved, after):
    R, heads, picked = retrieved.shape
    return whole(pick_rows_body, "pick_rows", [((heads, picked, R), BF)], retrieved, after=after)[0]


def picks_body(core_ref, pick_ref, other_ref, band_ref, band_other, out_ref):
    g = 2 * pl.program_id(0) + core_ref[0]
    heads, picked, R = pick_ref.shape
    half = out_ref.shape[2]
    for h in range(heads):
        for i, (from_ref, start_ref) in enumerate(((pick_ref, band_ref), (other_ref, band_other))):
            rel = g - start_ref[h : h + 1, :]
            got = jnp.full((half, R), -1.0, F32)
            for b in range(picked // half):
                got = jnp.where(rel == b, from_ref[h, b * half : (b + 1) * half, :].astype(F32), got)
            at = (2 * (h % 2) + i) * R
            out_ref[0, h // 2, :, at : at + R] = got


def picks(core_index, pick, pick_other, band, band_other, groups, half):
    heads, picked, R = pick.shape
    return pl.pallas_call(
        picks_body,
        name="picks",
        grid=(groups,),
        out_shape=pltpu.HBM((groups, heads // 2, half, 4 * R), F32),
        in_specs=[pl.BlockSpec(memory_space=pltpu.SMEM)]
        + [pl.BlockSpec((heads, picked, R), lambda g: (0, 0, 0))] * 2
        + [pl.BlockSpec((heads, R), lambda g: (0, 0))] * 2,
        out_specs=pl.BlockSpec((1, heads // 2, half, 4 * R), lambda g: (g, 0, 0, 0)),
        compiler_params=pltpu.CompilerParams(vmem_limit_bytes=VMEM_LIMIT),
    )(core_index, pick, pick_other, band, band_other)


def chosen_scores(k2, qq, a):
    half = a.shape[0]
    sT = nt(k2, qq)
    s = jnp.where(a > 0.5, sT[half:], sT[:half])
    return jnp.where(a < -0.5, NEG_FILL, s)


def spread(p, a):
    zero = jnp.zeros_like(p)
    even = jnp.where(a == 0.0, p, zero).astype(BF)
    odd = jnp.where(a == 1.0, p, zero).astype(BF)
    return jnp.concatenate([even, odd], 0)


def of_both(own, other):
    return stacked(jnp.concatenate([own, other], 0))


def own_lanes(t):
    R = t.shape[1] // 4
    return jnp.concatenate([t[:, :R], t[:, 2 * R : 3 * R]], 1)


def other_lanes(t):
    R = t.shape[1] // 4
    return jnp.concatenate([t[:, R : 2 * R], t[:, 3 * R :]], 1)


def all_lanes(own, other):
    R = own.shape[1] // 2
    return jnp.concatenate([own[:, :R], other[:, :R], own[:, R:], other[:, R:]], 1)


def cross_fwd_body(first, last, gid_ref, q_ref, q_other, *refs):
    kv, a_refs, refs = refs[:2], refs[2:4], refs[4:]
    if not first:
        m_in, l_in, acc_in = refs[:3]
        refs = refs[3:]
    m_ref, l_ref, acc_ref = refs[:3]

    @pl.when(pl.program_id(0) == 0)
    def _():
        if first:
            m_ref[...] = jnp.full(m_ref.shape, NEG_FILL, F32)
            l_ref[...] = jnp.zeros(l_ref.shape, F32)
            acc_ref[...] = jnp.zeros(acc_ref.shape, F32)
        else:
            m_ref[...] = m_in[...]
            l_ref[...] = l_in[...]
            acc_ref[...] = acc_in[...]

    pairs = acc_ref.shape[0]
    for hp in range(pairs):
        sl = slice(hp * PAIR, (hp + 1) * PAIR)
        qq = of_both(q_ref[:, sl], q_other[:, sl])
        scores = [chosen_scores(kv[j][0, 0, :, sl], qq, a_refs[j][0, hp]) for j in range(2)]
        old = m_ref[hp : hp + 1, :]
        top = functools.reduce(jnp.maximum, [jnp.max(s, 0, keepdims=True) for s in scores], old)
        fade = jnp.exp(old - top)
        total = l_ref[hp : hp + 1, :] * fade
        acc = acc_ref[hp] * fade
        for j in range(2):
            a = a_refs[j][0, hp]
            p = jnp.where(a < -0.5, 0.0, jnp.exp(scores[j] - top))
            total = total + jnp.sum(p, 0, keepdims=True)
            acc = acc + tn(kv[j][0, 1, :, sl], spread(p, a))
        m_ref[hp : hp + 1, :] = top
        l_ref[hp : hp + 1, :] = total
        acc_ref[hp] = acc

    if last:
        own_ref, other_ref = refs[3:]

        @pl.when(pl.program_id(0) == pl.num_programs(0) - 1)
        def _():
            for out, lanes in ((own_ref, own_lanes), (other_ref, other_lanes)):
                out[pairs * PAIR :, :] = jnp.zeros((8, out.shape[1]), F32)
                for hp in range(pairs):
                    out[hp * PAIR : (hp + 1) * PAIR, :] = lanes(acc_ref[hp])
                    out[pairs * PAIR + hp : pairs * PAIR + hp + 1, :] = lanes(m_ref[hp : hp + 1, :])
                    out[pairs * PAIR + 4 + hp : pairs * PAIR + 5 + hp, :] = lanes(l_ref[hp : hp + 1, :])


def kv_specs(kv, a):
    rows, C = kv[0].shape[2:]
    specs = [pl.BlockSpec((1, 2, rows, C), lambda i, gid: (i, 0, 0, 0)) for _ in range(2)]
    for j in range(2):
        specs.append(
            pl.BlockSpec((1,) + a.shape[1:], functools.partial(lambda j, i, gid: (gid[2 * i + j], 0, 0, 0), j))
        )
    return specs


def fixed(shape):
    return pl.BlockSpec(shape, lambda i, gid: (0,) * len(shape))


def cross_fwd(gid, q, kv, a, state, last):
    R, C = q[0].shape
    pairs = C // PAIR
    hi, _, rows, _ = kv[0].shape
    shapes = [(8, 4 * R), (8, 4 * R), (pairs, PAIR, 4 * R)]
    first = state is None
    state = () if first else tuple(state)
    if last:
        shapes += [(C + 8, 2 * R)] * 2
    return pl.pallas_call(
        functools.partial(cross_fwd_body, first, last),
        name="cross_fwd",
        grid_spec=pltpu.PrefetchScalarGridSpec(
            num_scalar_prefetch=1,
            grid=(hi,),
            in_specs=[fixed(q[0].shape)] * 2 + kv_specs(kv, a) + [fixed(s.shape) for s in state],
            out_specs=[fixed(s) for s in shapes],
        ),
        out_shape=[jax.ShapeDtypeStruct(s, F32) for s in shapes],
        compiler_params=pltpu.CompilerParams(vmem_limit_bytes=VMEM_LIMIT),
        cost_estimate=pl.CostEstimate(flops=1, bytes_accessed=1, transcendentals=0),
    )(gid, *q, *kv, *([pltpu.with_memory_space_constraint(a, pltpu.HBM)] * 2), *state)


def merged(own_ref, got_ref, hp, C):
    sl = slice(hp * PAIR, (hp + 1) * PAIR)
    m, l = slice(C + hp, C + hp + 1), slice(C + 4 + hp, C + 5 + hp)
    m1, m2 = own_ref[m, :], got_ref[m, :]
    top = jnp.maximum(m1, m2)
    f1, f2 = jnp.exp(m1 - top), jnp.exp(m2 - top)
    total = own_ref[l, :] * f1 + got_ref[l, :] * f2
    return top + jnp.log(total), unstacked((own_ref[sl, :] * f1 + got_ref[sl, :] * f2) * (1.0 / total))


def cross_mix_body(own_ref, got_ref, wm, log_ref, of_ref, o_ref, part_ref):
    C = wm.shape[0]
    log_ref[...] = jnp.zeros(log_ref.shape, F32)
    for hp in range(C // PAIR):
        sl = slice(hp * PAIR, (hp + 1) * PAIR)
        log_ref[hp : hp + 1, :], o = merged(own_ref, got_ref, hp, C)
        of_ref[:, sl] = o
        o_ref[:, sl] = o.astype(BF)
    part_ref[...] = nn(o_ref[...], wm[...]).astype(BF)


def cross_mix_fwd(own, got, wm):
    R2 = own.shape[1]
    C, D = wm.shape
    R = R2 // 2
    return whole(
        cross_mix_body,
        "cross_mix",
        [((8, R2), F32), ((R, C), F32), ((R, C), BF), ((R, D), BF)],
        own, got, wm,
    )


def cross_merge_body(own_ref, got_ref, log_ref, of_ref):
    C = of_ref.shape[1]
    log_ref[...] = jnp.zeros(log_ref.shape, F32)
    for hp in range(C // PAIR):
        log_ref[hp : hp + 1, :], of_ref[:, hp * PAIR : (hp + 1) * PAIR] = merged(own_ref, got_ref, hp, C)


def cross_merge(own, got):
    rows, R2 = own.shape
    return whole(cross_merge_body, "cross_merge", [((8, R2), F32), ((R2 // 2, rows - 8), F32)], own, got)


def ffn_back_rest(pack_ref, gp_ref, wu, wd, part_ref):
    D = wu.shape[0]
    low = pack_ref[:, :D]
    for c in range(0, wu.shape[1], 256):
        sl = slice(c, c + 256)
        pack_ref[:, D + c : D + c + 256] = (nt(low, wd[sl, :]) * gp_ref[:, sl].astype(F32)).astype(BF)
    part_ref[...] = nt(pack_ref[:, D:], wu[...]).astype(BF)


def last_body(g, u_ref, own, oth, cot, par, gp_ref, wu, wd, out_ref, dv_ref, pack_ref, gg_ref, part_ref):
    R, D = u_ref.shape
    gain, shift = row_of(par, g), row_of(par, g + 1)
    gg_ref[...] = jnp.zeros(gg_ref.shape, F32)
    for r in range(0, R, ROWS):
        s = slice(r, r + ROWS)
        v = u_ref[s, :] + (own[s, :].astype(F32) + oth[s, :].astype(F32))
        xhat, _ = norm_parts(v)
        out_ref[s, :] = xhat * gain + shift
        dv, dg, db = norm_back(v, gain, cot[s, :].astype(F32))
        dv_ref[s, :] = dv
        pack_ref[s, :D] = dv.astype(BF)
        gg_ref[0:1, :] += dg
        gg_ref[1:2, :] += db
    flush(gg_ref, out_ref)
    ffn_back_rest(pack_ref, gp_ref, wu, wd, part_ref)


def last_fwd_back(g, u, own, oth, cot, par, gp, wu, wd):
    R, D = u.shape
    FF = wu.shape[1]
    return whole(
        functools.partial(last_body, g),
        "last_fwd_back",
        [((R, D), F32, HBM), ((R, D), F32), ((R, D + FF), BF), ((8, D), F32, HBM), ((R, D), BF)],
        u, own, oth, cot, par, gp, wu, wd,
    )


def ffn_back_body(g, own, oth, v_ref, par, gp_ref, wu, wd, dv_ref, pack_ref, gg_ref, part_ref):
    R, D = v_ref.shape
    gain = row_of(par, g)
    gg_ref[...] = jnp.zeros(gg_ref.shape, F32)
    for r in range(0, R, ROWS):
        s = slice(r, r + ROWS)
        dy = own[s, :].astype(F32) + oth[s, :].astype(F32)
        dv, dg, db = norm_back(v_ref[s, :], gain, dy)
        dv_ref[s, :] = dv
        pack_ref[s, :D] = dv.astype(BF)
        gg_ref[0:1, :] += dg
        gg_ref[1:2, :] += db
    flush(gg_ref)
    ffn_back_rest(pack_ref, gp_ref, wu, wd, part_ref)


def ffn_back(g, own, oth, v, par, gp, wu, wd, after):
    R, D = v.shape
    FF = wu.shape[1]
    return whole(
        functools.partial(ffn_back_body, g),
        "ffn_back",
        [((R, D), F32), ((R, D + FF), BF), ((8, D), F32, HBM), ((R, D), BF)],
        own, oth, v, par, gp, wu, wd,
        after=after,
    )


def branch_back(g, dres, own, oth, v_ref, par, dv_ref, dlow_ref, gg_ref):
    R, D = v_ref.shape
    gain = row_of(par, g)
    gg_ref[...] = jnp.zeros(gg_ref.shape, F32)
    for r in range(0, R, ROWS):
        s = slice(r, r + ROWS)
        dy = dres[s, :] + (own[s, :].astype(F32) + oth[s, :].astype(F32))
        dv, dg, db = norm_back(v_ref[s, :], gain, dy)
        dv_ref[s, :] = dv
        dlow_ref[s, :D] = dv.astype(BF)
        gg_ref[0:1, :] += dg
        gg_ref[1:2, :] += db


def cross_mix_back_body(g, dres, own, oth, v_ref, par, wm, dv_ref, pack_ref, gg_ref):
    branch_back(g, dres, own, oth, v_ref, par, dv_ref, pack_ref, gg_ref)
    flush(dv_ref, gg_ref)
    D = v_ref.shape[1]
    pack_ref[:, D:] = nt(pack_ref[:, :D], wm[...]).astype(BF)


def cross_mix_back(g, dres, own, oth, v, par, wm):
    R, D = v.shape
    C = wm.shape[0]
    return whole(
        functools.partial(cross_mix_back_body, g),
        "cross_mix_back",
        [((R, D), F32, HBM), ((R, D + C), BF), ((8, D), F32, HBM)],
        dres, own, oth, v, par, wm,
    )


def cross_back_body(first, last, gid_ref, q_ref, q_other, do_pack, do_pack_other, *refs):
    C = q_ref.shape[1]
    skip = do_pack.shape[1] - C
    do_ref, do_other = do_pack.at[:, skip:], do_pack_other.at[:, skip:]
    kv, a_refs, refs = refs[:2], refs[2:4], refs[4:]
    if first:
        of_ref, of_other, log_own, log_other = refs[:4]
        dq_ref, stat_ref, keep_ref, send_ref = refs[4:8]
    else:
        dq_in, stat_in = refs[:2]
        dq_ref, stat_ref, keep_ref, send_ref = refs[2:6]
    pairs = dq_ref.shape[0]

    @pl.when(pl.program_id(0) == 0)
    def _():
        if not first:
            dq_ref[...] = dq_in[...]
            stat_ref[...] = stat_in[...]
            return
        dq_ref[...] = jnp.zeros(dq_ref.shape, F32)
        stat_ref[...] = jnp.zeros(stat_ref.shape, F32)
        stat_ref[0:8, :] = all_lanes(log_own[...], log_other[...])
        for hp in range(pairs):
            sl = slice(hp * PAIR, (hp + 1) * PAIR)
            sums = []
            for d, o in ((do_ref, of_ref), (do_other, of_other)):
                prod = (d[:, sl].astype(F32) * o[:, sl]).T
                sums.append([jnp.sum(prod[:HD], 0, keepdims=True), jnp.sum(prod[HD:], 0, keepdims=True)])
            stat_ref[8 + hp : 9 + hp, :] = jnp.concatenate([sums[0][0], sums[1][0], sums[0][1], sums[1][1]], 1)

    for hp in range(pairs):
        sl = slice(hp * PAIR, (hp + 1) * PAIR)
        qq = of_both(q_ref[:, sl], q_other[:, sl])
        dd = of_both(do_ref[:, sl], do_other[:, sl])
        log_total = stat_ref[hp : hp + 1, :]
        delta = stat_ref[8 + hp : 9 + hp, :]
        dq = dq_ref[hp]
        for j, out_ref in enumerate((keep_ref, send_ref)):
            a = a_refs[j][0, hp]
            half = a.shape[0]
            k2 = kv[j][0, 0, :, sl]
            p = jnp.exp(chosen_scores(k2, qq, a) - log_total)
            daT = nt(kv[j][0, 1, :, sl], dd)
            ds = p * (jnp.where(a > 0.5, daT[half:], daT[:half]) - delta)
            dsT = spread(ds, a)
            out_ref[0, 0, :, sl] = nn(dsT, qq).astype(BF)
            out_ref[0, 1, :, sl] = nn(spread(p, a), dd).astype(BF)
            dq = dq + tn(k2, dsT)
        dq_ref[hp] = dq

    if last:
        own_ref, other_ref = refs[-2:]

        @pl.when(pl.program_id(0) == pl.num_programs(0) - 1)
        def _():
            for hp in range(pairs):
                own_ref[hp] = own_lanes(dq_ref[hp])
                other_ref[hp] = other_lanes(dq_ref[hp])


def cross_back(gid, q, do, kv, a, extra, first, last, after=()):
    R, C = q[0].shape
    pairs = C // PAIR
    hi, _, rows, _ = kv[0].shape
    grad_spec = pl.BlockSpec((1, 2, rows, C), lambda i, gid: (i, 0, 0, 0))
    shapes = [(pairs, PAIR, 4 * R), (16, 4 * R)]
    out_specs = [fixed(s) for s in shapes] + [grad_spec] * 2
    out_shape = [jax.ShapeDtypeStruct(s, F32) for s in shapes] + [jax.ShapeDtypeStruct(kv[0].shape, BF)] * 2
    if last:
        out_specs += [fixed((pairs, PAIR, 2 * R))] * 2
        out_shape += [jax.ShapeDtypeStruct((pairs, PAIR, 2 * R), F32)] * 2
    return pl.pallas_call(
        behind(functools.partial(cross_back_body, first, last), 9 + len(extra), len(after)),
        name="cross_back",
        grid_spec=pltpu.PrefetchScalarGridSpec(
            num_scalar_prefetch=1,
            grid=(hi,),
            in_specs=[fixed(q[0].shape)] * 2
            + [fixed(do[0].shape)] * 2
            + kv_specs(kv, a)
            + [fixed(e.shape) for e in extra]
            + [pl.BlockSpec(memory_space=pl.ANY)] * len(after),
            out_specs=out_specs,
        ),
        out_shape=out_shape,
        compiler_params=pltpu.CompilerParams(vmem_limit_bytes=VMEM_LIMIT),
        cost_estimate=pl.CostEstimate(flops=1, bytes_accessed=1, transcendentals=0),
    )(gid, *q, *do, *kv, *([pltpu.with_memory_space_constraint(a, pltpu.HBM)] * 2), *extra, *after)


def cross_q_back_body(dq_own, dq_got, wq, dq_ref, part_ref):
    for hp in range(dq_own.shape[0]):
        sl = slice(hp * PAIR, (hp + 1) * PAIR)
        dq_ref[:, sl] = (unstacked(dq_own[hp] + dq_got[hp]) * SCALE).astype(BF)
    flush(dq_ref)
    part_ref[...] = nt(dq_ref[...], wq[...]).astype(BF)


def cross_q_back(dq, got, wq, after):
    D, C = wq.shape
    R = dq.shape[2] // 2
    return whole(cross_q_back_body, "cross_q_back", [((R, C), BF), ((R, D), BF)], dq, got, wq, after=after)


def store_back_body(spread_at, *refs):
    n = len(refs) - 4
    wk, wv, dkv_ref, part_ref = refs[n:]
    R, C = dkv_ref.shape[0], dkv_ref.shape[1] // 2
    for i in range(2):
        parts = [t[0, i] for t in refs[:spread_at]]
        if spread_at < n:
            parts.append(refs[spread_at + i][0, 0])
        total = functools.reduce(lambda x, y: x + y, [t.astype(F32) for t in parts])
        dkv_ref[:, i * C : (i + 1) * C] = total.astype(BF)
    part = nt(dkv_ref[:, :C], wk[...]) + nt(dkv_ref[:, C:], wv[...])
    part_ref[...] = tn(order_matrix(R), part.astype(BF)).astype(BF)


def store_back(terms, wk, wv, after):
    D, C = wk.shape
    R = terms[0].shape[2]
    full = [t for t in terms if not isinstance(t, list)]
    halves = [h for t in terms if isinstance(t, list) for h in t]
    return whole(
        functools.partial(store_back_body, len(full)),
        "store_back",
        [((R, 2 * C), BF), ((R, D), BF)],
        *full, *halves, wk, wv,
        after=after,
    )


def attend_back_body(causal, g, n_more, *refs):
    if causal:
        len_ref, refs = refs[0], refs[1:]
    (dres, own, oth, v1_ref, par, q_ref, k_ref, v_ref, wq, wk, wv, wm) = refs[:12]
    R, D = v1_ref.shape
    dv_ref, pack_ref, gg_ref, part_ref = refs[12 + n_more : 16 + n_more]
    branch_back(g, dres, own, oth, v1_ref, par, dv_ref, pack_ref, gg_ref)
    flush(dv_ref, gg_ref)
    if n_more:
        gains_ref = refs[-1]
        rows = [gg_ref[0:2, :]] + [other[0:2, :] for other in refs[12 : 12 + n_more]]
        rows.append(jnp.zeros((gains_ref.shape[0] - 2 - 2 * n_more, D), F32))
        gains_ref[...] = jnp.concatenate(rows, 0).astype(BF)
        flush(gains_ref)
    C = wq.shape[1]
    do = nt(pack_ref[:, :D], wm[...]).astype(BF)
    allowed = causal_mask(R, len_ref[0]) if causal else None
    for c in range(0, C, PAIR):
        sl = slice(c, c + PAIR)
        k2 = k_ref[:, sl]
        qq = stacked(q_ref[:, sl])
        dd = stacked(do[:, sl])
        w = local_weights(k2, qq, allowed)
        daT = nt(v_ref[:, sl], dd)
        ds = (w * (daT - jnp.sum(w * daT, 0, keepdims=True))).astype(BF)
        at = D + c
        pack_ref[:, at : at + PAIR] = (unstacked(tn(k2, ds)) * SCALE).astype(BF)
        pack_ref[:, at + C : at + C + PAIR] = nn(ds, qq).astype(BF)
        pack_ref[:, at + 2 * C : at + 2 * C + PAIR] = nn(w.astype(BF), dd).astype(BF)
    flush(pack_ref)
    part = nt(pack_ref[:, D : D + C], wq[...]) + nt(pack_ref[:, D + C : D + 2 * C], wk[...])
    part_ref[...] = (part + nt(pack_ref[:, D + 2 * C :], wv[...])).astype(BF)


def attend_back(g, dres, own, oth, v1, par, kept, weights, length=None, more=(), after=()):
    R, D = v1.shape
    C = kept[0].shape[1]
    args = (dres, own, oth, v1, par, *kept, *weights, *more)
    causal = length is not None
    if causal:
        args = (length,) + args
    return whole(
        functools.partial(attend_back_body, causal, g, len(more)),
        "attend_back",
        [((R, D), F32, HBM), ((R, D + 3 * C), BF), ((8, D), F32, HBM), ((R, D), BF)]
        + [((16, D), BF)] * bool(more),
        *args,
        smem=int(causal),
        after=after,
    )


def weight_body(plan, sources, n_in, idx_ref, *refs):
    ins, outs = refs[:n_in], refs[n_in:]
    rows, D = idx_ref.shape[0], plan[0][2]
    take = (lax.broadcasted_iota(jnp.int32, (rows, D), 1) == idx_ref[...]).astype(F32).astype(BF)
    half = rows // 2
    at = 0
    for a_at, off, D, grads in plan:
        parts = [nt(take, ins[a_at + i][:, off : off + D]) for i in range(sources)]
        aT = jnp.concatenate(parts, 1).astype(BF)
        for d_at, d_off, width in grads:
            step = 384 if width % 384 == 0 else 128
            for c in range(d_off, d_off + width, step):
                dy = jnp.concatenate([ins[d_at + i][:, c : c + step] for i in range(sources)], 0)
                got = nn(aT, dy)
                outs[0][:, at : at + step] = got[:half].astype(BF)
                outs[1][:, at : at + step] = got[half:].astype(BF)
                at += step


def weight_grads(idx, D, terms, after=()):
    ins, plan, width = [], [], 0
    for a, off, grads in terms:
        at = len(ins)
        ins += list(a)
        ds = []
        for d, d_off, w in grads:
            ds.append((len(ins), d_off, w))
            ins += list(d)
            width += w
        plan.append((at, off, D, ds))
    half = idx.shape[0] // 2
    return whole(
        functools.partial(weight_body, plan, len(terms[0][0]), len(ins)),
        "weight_grads",
        [((half, width), BF)] * 2,
        idx,
        *ins,
        after=after,
    )


def swap(x, bit, n):
    return lax.ppermute(x, "blk", [(i, i ^ bit) for i in range(n)])


def tied(x, *before):
    return lax.optimization_barrier((x, *before))[0]


def other_tp(x):
    return lax.ppermute(x, "tp", [(0, 1), (1, 0)])


class Halving:
    def __init__(self, keep, send, n, bits):
        self.keep, self.n, self.bits = keep, n, bits
        self.got = swap(send, bits[0], n)

    def step(self, *before):
        got = tied(self.got, *before) if before else self.got
        total = self.keep.astype(F32) + got.astype(F32)
        self.bits = self.bits[1:]
        if not self.bits:
            return total
        half = total.shape[0] // 2
        send = total[half:].astype(BF)
        self.keep = total[:half]
        self.got = swap(send, self.bits[0], self.n)
        return send

    def end(self, *before):
        while len(self.bits) > 1:
            self.step(*before)
        return self.step(*before)


def on_device(
    n,
    encoder_in,
    decoder_in,
    lengths,
    retrieved,
    band_start,
    cotangent,
    enc_query,
    enc_key,
    enc_value,
    enc_mix,
    attn_gain,
    attn_shift,
    enc_up,
    enc_down,
    ffn_gain,
    ffn_shift,
    self_query,
    self_key,
    self_value,
    self_mix,
    self_gain,
    self_shift,
    cross_query,
    cross_key,
    cross_value,
    cross_mix,
    cross_gain,
    cross_shift,
    dec_up,
    dec_down,
    last_gain,
    last_shift,
):
    group_rows, D = encoder_in.shape
    C = cross_query.shape[1]
    FF = enc_up.shape[1]
    hi = n // 16
    me = lax.axis_index("blk")
    core = lambda x: swap(x, 1, n)
    par = jnp.stack(
        [attn_gain, attn_shift, ffn_gain, ffn_shift, self_gain, self_shift, cross_gain, cross_shift, last_gain, last_shift]
    )

    share = D // n
    t = jnp.arange(D // 2, dtype=jnp.int32)
    block = t // share
    bits = [1 << i for i in range(n.bit_length() - 1)]

    def rows_by(order):
        rel = sum(((block >> (len(order) - 1 - i)) & 1) * bit for i, bit in enumerate(order))
        return ((me ^ rel) * share + t % share).reshape(D // 2, 1)

    idx = rows_by(bits[1:])

    both = lambda x: (x, core(x))
    summed = lambda *arrays: functools.reduce(lambda x, y: x + y, [t.astype(F32) for t in arrays]).astype(BF)

    *enc_kept, enc_o, enc_part = attend_fwd(encoder_in, enc_query, enc_key, enc_value, enc_mix, fetch=True)
    enc_other = other_tp(enc_part)
    pick = pick_rows(retrieved, (enc_part,))
    band = band_start.T
    pick_other, band_other = core(pick), core(band)
    *self_kept, self_o, self_part = attend_fwd(
        decoder_in, self_query, self_key, self_value, self_mix, lengths, (pick,)
    )
    enc_other = tied(enc_other, self_part)
    v1, u1, pack1, gp1, part1 = ffn_fwd(0, encoder_in, enc_part, enc_other, par, enc_up, enc_down)
    other1 = other_tp(part1)
    enc_os = both(tied(enc_o, part1))
    xes, xds, self_os, packs1 = (both(tied(a, enc_os[1])) for a in (encoder_in, decoder_in, self_o, pack1))
    other1 = tied(other1, *(pair[1] for pair in (xes, xds, self_os, packs1)))
    v2, encoded, enc_low, store = store_fwd(2, u1, part1, other1, par, cross_key, cross_value)

    store = store[None]
    for b in range(4, n.bit_length() - 1):
        store = jnp.concatenate([store, swap(store, 1 << b, n)], 0)
    rels = [[16 * h + 4 * k + r for h in range(hi) for r in (0, 2)] for k in range(4)]
    gids = [(me ^ jnp.array(rel, jnp.int32)) >> 1 for rel in rels]
    far = swap(store, 8, n)
    near = swap(store, 4, n)
    y_own = swap(store, 2, n)
    self_part = tied(self_part, store)
    self_other = other_tp(self_part)
    vd, ud, lowd, qc = cross_q(4, decoder_in, self_part, self_other, par, cross_query)
    qcs, lowds, enc_lows = both(qc), both(lowd), both(enc_low)
    near = tied(near, qcs[1])
    y_near = swap(near, 2, n)
    far = tied(far, near, y_own)
    apart = swap(far, 4, n)
    y_far = swap(far, 2, n)
    chosen = picks((me & 1).reshape(1), tied(pick, far), pick_other, band, band_other, n // 2, group_rows // 2)
    pieces = [(tied(store, y_near, apart), y_own), (near, y_near), (far, y_far)]
    state = cross_fwd(gids[0], qcs, pieces[0], chosen, None, False)
    y_apart = swap(apart, 2, n)
    pieces.append((apart, y_apart))
    state = cross_fwd(gids[1], qcs, pieces[1], chosen, state, False)
    state = cross_fwd(gids[2], qcs, pieces[2], chosen, state, False)
    state_own, state_other = cross_fwd(gids[3], qcs, pieces[3], chosen, state, True)[3:]
    log_own, of_own, oc, partc = cross_mix_fwd(state_own, core(state_other), cross_mix)
    otherc = other_tp(partc)
    log_other, of_other = cross_merge(state_other, core(tied(state_own, partc)))
    ocs = both(oc)
    otherc = tied(otherc, of_other, ocs[1])

    vc, uc, packc, gpc, part3 = ffn_fwd(6, ud, partc, otherc, par, dec_up, dec_down)
    other3 = other_tp(part3)
    packc_y = swap(packc, 2, n)
    decoded, dlast, dpackc, gg_last, part4 = last_fwd_back(8, uc, part3, other3, cotangent, par, gpc, dec_up, dec_down)
    other4 = tied(other_tp(part4), packc_y)
    dpackc_y = swap(dpackc, 2, n)
    dcross, dpacko, gg_cross = cross_mix_back(6, dlast, part4, other4, vc, par, cross_mix)

    dpackos = both(dpacko)
    dpackc_y = tied(dpackc_y, dpackos[1])
    back = lambda k, extra, after: cross_back(
        gids[k], qcs, dpackos, pieces[k], chosen, extra, k == 3, k == 0, after
    )
    *extra, keep3, send3 = back(3, (of_own, of_other, log_own, log_other), (dpackc_y,))
    got3 = swap(send3, 2, n)
    *extra, keep2, send2 = back(2, extra, ())
    got2 = swap(send2, 2, n)
    sum3 = summed(keep3, tied(got3, send2))
    apart = swap(sum3, 4, n)
    *extra, keep1, send1 = back(1, extra, (sum3,))
    got1 = swap(send1, 2, n)
    got2 = tied(got2, send1)
    sum2 = [summed(keep2[:, i : i + 1], got2[:, i : i + 1], apart[:, i : i + 1]) for i in range(2)]
    far = [swap(half, 8, n) for half in sum2]
    _, _, keep0, send0, dq_own, dq_other = back(0, extra, sum2)
    got0 = swap(send0, 2, n)
    sum1 = summed(keep1, tied(got1, send0, far[0]))
    near = swap(sum1, 4, n)
    terms = [keep0, got0, near, jnp.concatenate(far, 1) if hi > 1 else far]
    bit = n // 2
    while hi > 1 and terms[0].shape[0] > 1:
        half = terms[0].shape[0] // 2
        total = functools.reduce(lambda x, y: x + y, [t.astype(F32) for t in terms])
        terms = [total[:half].astype(BF), swap(total[half:].astype(BF), bit, n)]
        bit //= 2

    pairs, dpairs = (packc, packc_y), (dpackc, dpackc_y)
    first = weight_grads(
        rows_by(bits[:1] + bits[2:]), D, [(dpairs, 0, [(pairs, D, FF)]), (pairs, 0, [(dpairs, D, FF)])], (sum1,)
    )
    first = Halving(*first, n, bits[:1] + bits[2:])
    dqc, partq = cross_q_back(dq_own, core(tied(dq_other, sum1)), cross_query, (first.keep,))
    otherq = other_tp(partq)
    first_z = first.step(partq)
    dself, dpackd, gg_self, part6 = attend_back(
        4, dcross, partq, tied(otherq, got0, near, far[1], first_z), vd, par, self_kept,
        (self_query, self_key, self_value, self_mix), lengths,
    )
    dqcs, dpackds = both(dqc), both(dpackd)
    second = Halving(*weight_grads(idx, D, [(xds, 0, [(dpackds, D, 3 * C)])]), n, bits[1:])
    third = weight_grads(
        idx,
        D,
        [(lowds, 0, [(dqcs, 0, C)]), (dpackds, 0, [(self_os, 0, C)]), (dpackos, 0, [(ocs, 0, C)])],
        (second.keep,),
    )
    third = Halving(*third, n, bits[1:])

    dkv, part5 = store_back(terms, cross_key, cross_value, (third.keep,))
    other5 = other_tp(part5)
    dkvs = both(dkv)
    first_z = first.step(part5)
    second_z = second.step(part5)
    dffn, dpack1, gg_ffn, part7 = ffn_back(
        2, part5, tied(other5, first_z, second_z), v2, par, gp1, enc_up, enc_down, ()
    )
    other7 = other_tp(part7)
    dpacks1 = both(dpack1)
    third_z = third.step(part7)
    fifth = weight_grads(
        idx, D, [(enc_lows, 0, [(dkvs, 0, 2 * C)]), (dpacks1, 0, [(packs1, D, FF)])], (third_z,)
    )
    fifth = Halving(*fifth, n, bits[1:])
    sixth = Halving(*weight_grads(idx, D, [(packs1, 0, [(dpacks1, D, FF)])], (fifth.keep,)), n, bits[1:])
    first_sum = first.end(sixth.keep)
    second_z = second.step(sixth.keep)
    dattn, dpacke, _, part8, gains = attend_back(
        0, dffn, part7, tied(other7, first_sum, second_z), v1, par, enc_kept, (enc_query, enc_key, enc_value, enc_mix), None,
        (gg_ffn, gg_self, gg_cross, gg_last),
    )
    lanes = jnp.eye(16, 128, dtype=BF)
    dpackes = both(dpacke)
    gains = both(gains)
    z_first = bits[2:] + bits[1:2]
    fourth = weight_grads(
        rows_by(z_first),
        D,
        [
            (xes, 0, [(dpackes, D, 3 * C)]),
            (dpackes, 0, [(enc_os, 0, C)]),
            (gains, 0, [((lanes, lanes), 0, 128)]),
        ],
    )
    fourth = Halving(*fourth, n, z_first)
    other6, other8 = other_tp(tied(part6, fourth.keep)), other_tp(tied(part8, fourth.keep))
    second_sum = second.end(fourth.keep)
    third_z = third.step(fourth.keep)
    fifth_z = fifth.step(second_sum, third_z)
    fourth_z = fourth.step(fifth_z, other6, other8)
    third_sum = third.end(fourth_z)
    sixth_z = sixth.step(third_sum)
    fifth_z = fifth.step(sixth_z)
    fourth_z = fourth.step(fifth_z)
    sixth_z = sixth.step(fourth_z)
    fifth_sum, fourth_sum, sixth_sum = fifth.end(), fourth.end(), sixth.end()
    grad_encoder_in = dattn + (part8.astype(F32) + other8.astype(F32))
    grad_decoder_in = dself + (part6.astype(F32) + other6.astype(F32))

    cut = lambda total, at, width: total[:, at : at + width]
    gain_of = [fourth_sum[:, 4 * C + i] for i in range(10)]
    return (
        encoded,
        decoded,
        grad_encoder_in,
        grad_decoder_in,
        cut(fourth_sum, 0, C),
        cut(fourth_sum, C, C),
        cut(fourth_sum, 2 * C, C),
        cut(fourth_sum, 3 * C, C).T,
        gain_of[0],
        gain_of[1],
        sixth_sum,
        cut(fifth_sum, 2 * C, FF).T,
        gain_of[2],
        gain_of[3],
        cut(second_sum, 0, C),
        cut(second_sum, C, C),
        cut(second_sum, 2 * C, C),
        cut(third_sum, C, C).T,
        gain_of[4],
        gain_of[5],
        cut(third_sum, 0, C),
        cut(fifth_sum, 0, C),
        cut(fifth_sum, C, C),
        cut(third_sum, 2 * C, C).T,
        gain_of[6],
        gain_of[7],
        cut(first_sum, FF, FF),
        cut(first_sum, 0, FF).T,
        gain_of[8],
        gain_of[9],
    )


def solution(mesh):
    rows, both, cols, down = P("blk", None), P("blk", "tp"), P(None, "tp"), P("tp", None)
    attn = (cols, cols, cols, down, P(), P())
    ffn = (cols, down, P(), P())
    in_specs = (rows, rows, P("blk"), P("blk", "tp", None), both, rows) + attn + ffn + attn + attn + ffn
    mixed = P("tp", "blk")
    grad_attn = (both, both, both, mixed, P("blk"), P("blk"))
    grad_ffn = (both, mixed, P("blk"), P("blk"))
    out_specs = (rows,) * 4 + grad_attn + grad_ffn + grad_attn + grad_attn + grad_ffn
    return jax.shard_map(
        functools.partial(on_device, mesh.shape["blk"]),
        mesh=mesh,
        in_specs=in_specs,
        out_specs=out_specs,
        check_vma=False,
    )
```

```python
import functools

import jax
import jax.numpy as jnp
from jax import lax
from jax.experimental import pallas as pl
from jax.experimental.pallas import tpu as pltpu
from jax.sharding import PartitionSpec as P

HD = 64
PAIR = 2 * HD
NEG_FILL = -1e30
EPS_NORM = 1e-05
SCALE = 0.125
BF = jnp.bfloat16
F32 = jnp.float32
VMEM_LIMIT = 24 * 2**20
HBM = True
ROWS = 64


def nn(a, b):
    return lax.dot_general(a, b, (((1,), (0,)), ((), ())), preferred_element_type=F32)


def nt(a, b):
    return lax.dot_general(a, b, (((1,), (1,)), ((), ())), preferred_element_type=F32)


def tn(a, b):
    return lax.dot_general(a, b, (((0,), (0,)), ((), ())), preferred_element_type=F32)


def behind(body, n_in, n_after):
    if not n_after:
        return body
    return lambda *refs: body(*refs[:n_in], *refs[n_in + n_after :])


class Fetched:
    def __init__(self, far, near, sem):
        self.near, self.shape, self.pending = near, near.shape, pltpu.make_async_copy(far, near, sem)
        self.pending.start()

    def ready(self):
        if self.pending is not None:
            self.pending.wait()
            self.pending = None

    def __getitem__(self, at):
        self.ready()
        return self.near[at]


class Kept:
    def __init__(self, far, near, sem):
        self.far, self.near, self.shape, self.sem, self.copies, self.at = far, near, near.shape, sem, [], 0

    def flush(self, upto=None):
        if upto is None and self.at == 0:
            copy = pltpu.make_async_copy(self.near, self.far, self.sem.at[0])
        else:
            upto = self.shape[-1] if upto is None else upto
            if upto == self.at:
                return
            sl = (slice(None), slice(self.at, upto))
            copy = pltpu.make_async_copy(self.near.at[sl], self.far.at[sl], self.sem.at[len(self.copies)])
        self.at = self.shape[-1] if upto is None else upto
        copy.start()
        self.copies.append(copy)

    def wait(self):
        if self.at < self.shape[-1]:
            self.flush()
        for copy in self.copies:
            copy.wait()

    def __getitem__(self, at):
        return self.near[at]

    def __setitem__(self, at, value):
        self.near[at] = value


def flush(*refs, upto=None):
    for ref in refs:
        if isinstance(ref, Kept):
            ref.flush(upto)


class Far:
    def __init__(self, array):
        self.array = array


def whole(body, name, outs, *args, smem=0, after=()):
    far_in = [i for i, a in enumerate(args) if isinstance(a, Far)]
    far_out = [i for i, o in enumerate(outs) if len(o) > 2]
    args = [pltpu.with_memory_space_constraint(a.array, pltpu.HBM) if isinstance(a, Far) else a for a in args]
    n_in, n_out, n_after = len(args), len(outs), len(after)

    def run(*refs):
        ins = list(refs[:n_in])
        results = list(refs[n_in + n_after : n_in + n_after + n_out])
        scratch = refs[n_in + n_after + n_out :]
        for k, i in enumerate(far_in):
            ins[i] = Fetched(ins[i], scratch[k], scratch[-1].at[k, 0])
        for k, i in enumerate(far_out):
            results[i] = Kept(results[i], scratch[len(far_in) + k], scratch[-1].at[len(far_in) + k])
        body(*ins, *results)
        for i in far_in:
            ins[i].ready()
        for i in far_out:
            results[i].wait()

    moves = len(far_in) + len(far_out)
    scratch = [pltpu.VMEM(args[i].shape, args[i].dtype) for i in far_in]
    scratch += [pltpu.VMEM(outs[i][0], outs[i][1]) for i in far_out]
    if moves:
        scratch.append(pltpu.SemaphoreType.DMA((moves, 8)))
    in_specs = [pl.BlockSpec(memory_space=pltpu.SMEM if i < smem else pltpu.VMEM) for i in range(n_in)]
    out_specs = [pl.BlockSpec(memory_space=pltpu.VMEM) for _ in outs]
    for i in far_in:
        in_specs[i] = pl.BlockSpec(memory_space=pltpu.HBM)
    for i in far_out:
        out_specs[i] = pl.BlockSpec(memory_space=pltpu.HBM)
    return pl.pallas_call(
        run,
        name=name,
        out_shape=[pltpu.HBM(o[0], o[1]) if len(o) > 2 else jax.ShapeDtypeStruct(o[0], o[1]) for o in outs],
        in_specs=in_specs + [pl.BlockSpec(memory_space=pl.ANY)] * n_after,
        out_specs=out_specs,
        scratch_shapes=scratch,
        compiler_params=pltpu.CompilerParams(vmem_limit_bytes=VMEM_LIMIT),
        cost_estimate=pl.CostEstimate(flops=1, bytes_accessed=1, transcendentals=0),
    )(*args, *after)


def norm_parts(v):
    center = v - jnp.mean(v, -1, keepdims=True)
    r = lax.rsqrt(jnp.mean(center * center, -1, keepdims=True) + EPS_NORM)
    return center * r, r


def norm_back(v, gain, dy):
    xhat, r = norm_parts(v)
    gdy = gain * dy
    dv = r * (gdy - jnp.mean(gdy, -1, keepdims=True) - xhat * jnp.mean(gdy * xhat, -1, keepdims=True))
    return dv, jnp.sum(dy * xhat, 0, keepdims=True), jnp.sum(dy, 0, keepdims=True)


def row_of(par_ref, i):
    return par_ref[i : i + 1, :].astype(F32)


def low_half(shape, dim):
    return lax.broadcasted_iota(jnp.int32, shape, dim) < HD


def stacked(t2):
    first = low_half(t2.shape, 1)
    zero = jnp.zeros_like(t2)
    return jnp.concatenate([jnp.where(first, t2, zero), jnp.where(first, zero, t2)], 0)


def unstacked(tT):
    R = tT.shape[1] // 2
    first = low_half((PAIR, R), 0)
    return jnp.where(first, tT[:, :R], tT[:, R:]).T


def causal_mask(R, length):
    key = lax.broadcasted_iota(jnp.int32, (R, 2 * R), 0)
    lane = lax.broadcasted_iota(jnp.int32, (R, 2 * R), 1)
    query = jnp.where(lane >= R, lane - R, lane)
    return (key <= query) & (key < length)


def local_weights(k2, qq, allowed):
    sT = nt(k2, qq)
    if allowed is not None:
        sT = jnp.where(allowed, sT, NEG_FILL)
    p = jnp.exp(sT - jnp.max(sT, 0, keepdims=True))
    return p * (1.0 / jnp.sum(p, 0, keepdims=True))


def gelu_parts(h):
    cdf = 0.5 * (1.0 + lax.erf(h * 0.7071067811865476))
    pdf = 0.3989422804014327 * jnp.exp(-0.5 * h * h)
    return h * cdf, cdf + h * pdf


def attend_fwd_body(causal, *refs):
    if causal:
        len_ref, refs = refs[0], refs[1:]
    x_ref, wq, wk, wv, wm, q_ref, k_ref, v_ref, o_ref, part_ref = refs
    x = x_ref[...]
    R = x.shape[0]
    q_ref[...] = (nn(x, wq[...]) * SCALE).astype(BF)
    k_ref[...] = nn(x, wk[...]).astype(BF)
    v_ref[...] = nn(x, wv[...]).astype(BF)
    flush(q_ref, k_ref, v_ref)
    allowed = causal_mask(R, len_ref[0]) if causal else None
    for c in range(0, q_ref.shape[1], PAIR):
        sl = slice(c, c + PAIR)
        w = local_weights(k_ref[:, sl], stacked(q_ref[:, sl]), allowed).astype(BF)
        o_ref[:, sl] = unstacked(tn(v_ref[:, sl], w)).astype(BF)
    flush(o_ref)
    part_ref[...] = nn(o_ref[...], wm[...]).astype(BF)


def attend_fwd(x, wq, wk, wv, wm, length=None, after=(), fetch=False):
    R, D = x.shape
    C = wq.shape[1]
    args = (x, wq, wk, wv, wm)
    if fetch:
        args = tuple(Far(a) for a in args)
    causal = length is not None
    if causal:
        args = (length,) + args
    return whole(
        functools.partial(attend_fwd_body, causal),
        "attend_fwd",
        [((R, C), BF, HBM)] * 4 + [((R, D), BF)],
        *args,
        smem=int(causal),
        after=after,
    )


def ffn_fwd_body(g, x_ref, own, oth, par, wu, wd, v_ref, u_ref, low_ref, act_ref, gp_ref, part_ref):
    R, D = x_ref.shape
    gain, shift = row_of(par, g), row_of(par, g + 1)
    for r in range(0, R, ROWS):
        s = slice(r, r + ROWS)
        v = x_ref[s, :].astype(F32) + (own[s, :].astype(F32) + oth[s, :].astype(F32))
        xhat, _ = norm_parts(v)
        u = xhat * gain + shift
        v_ref[s, :] = v
        u_ref[s, :] = u
        low_ref[s, :] = u.astype(BF)
    flush(v_ref, low_ref)
    low = low_ref[...]
    for c in range(0, wu.shape[1], 256):
        sl = slice(c, c + 256)
        a, gp = gelu_parts(nn(low, wu[:, sl]))
        act_ref[:, sl] = a.astype(BF)
        gp_ref[:, sl] = gp.astype(BF)
        flush(act_ref, gp_ref, upto=c + 256)
    part_ref[...] = nn(act_ref[...], wd[...]).astype(BF)


def ffn_fwd(g, x, own, oth, par, wu, wd, fetch, keep):
    R, D = x.shape
    FF = wu.shape[1]
    kept = (HBM,) if keep else ()
    return whole(
        functools.partial(ffn_fwd_body, g),
        "ffn_fwd",
        [((R, D), F32, HBM), ((R, D), F32), ((R, D), BF, HBM), ((R, FF), BF, *kept), ((R, FF), BF, HBM), ((R, D), BF)],
        x, own, oth, par, *((Far(wu), Far(wd)) if fetch else (wu, wd)),
    )


def order_matrix(R):
    t = lax.broadcasted_iota(jnp.int32, (R, R), 0)
    col = lax.broadcasted_iota(jnp.int32, (R, R), 1)
    src = jnp.where(t < R // 2, 2 * t, 2 * t - (R - 1))
    return (src == col).astype(F32).astype(BF)


def store_body(g, u_ref, own, oth, par, wk, wv, v_ref, enc_ref, low_ref, kv_ref):
    R = u_ref.shape[0]
    gain, shift = row_of(par, g), row_of(par, g + 1)
    for r in range(0, R, ROWS):
        s = slice(r, r + ROWS)
        v = u_ref[s, :] + (own[s, :].astype(F32) + oth[s, :].astype(F32))
        xhat, _ = norm_parts(v)
        v_ref[s, :] = v
        enc_ref[s, :] = xhat * gain + shift
    flush(v_ref, enc_ref)
    low_ref[...] = nn(order_matrix(R), enc_ref[...].astype(BF)).astype(BF)
    flush(low_ref)
    low = low_ref[...]
    kv_ref[0] = nn(low, wk[...]).astype(BF)
    kv_ref[1] = nn(low, wv[...]).astype(BF)


def store_fwd(g, u, own, oth, par, wk, wv):
    R, D = u.shape
    C = wk.shape[1]
    return whole(
        functools.partial(store_body, g),
        "store_fwd",
        [((R, D), F32, HBM), ((R, D), F32, HBM), ((R, D), BF, HBM), ((2, R, C), BF)],
        u, own, oth, par, wk, wv,
    )


def cross_q_body(g, x_ref, own, oth, par, wq, v_ref, u_ref, low_ref, q_ref):
    R = x_ref.shape[0]
    gain, shift = row_of(par, g), row_of(par, g + 1)
    for r in range(0, R, ROWS):
        s = slice(r, r + ROWS)
        v = x_ref[s, :].astype(F32) + (own[s, :].astype(F32) + oth[s, :].astype(F32))
        xhat, _ = norm_parts(v)
        u = xhat * gain + shift
        v_ref[s, :] = v
        u_ref[s, :] = u
        low_ref[s, :] = u.astype(BF)
    flush(v_ref, u_ref, low_ref)
    q_ref[...] = (nn(low_ref[...], wq[...]) * SCALE).astype(BF)


def cross_q(g, x, own, oth, par, wq):
    R, D = x.shape
    C = wq.shape[1]
    return whole(
        functools.partial(cross_q_body, g),
        "cross_q",
        [((R, D), F32, HBM), ((R, D), F32, HBM), ((R, D), BF, HBM), ((R, C), BF)],
        x, own, oth, par, wq,
    )


def pick_rows_body(from_ref, out_ref):
    for h in range(out_ref.shape[0]):
        out_ref[h] = (from_ref[h] & 1).astype(F32).T.astype(BF)


def pick_rows(retrieved, after):
    R, heads, picked = retrieved.shape
    return whole(pick_rows_body, "pick_rows", [((heads, picked, R), BF)], Far(retrieved.transpose(1, 0, 2)), after=after)[0]


def picks_body(core_ref, pick_ref, other_ref, band_ref, band_other, out_ref):
    g = 2 * pl.program_id(0) + core_ref[0]
    heads, picked, R = pick_ref.shape
    half = out_ref.shape[2]
    for h in range(heads):
        for i, (from_ref, start_ref) in enumerate(((pick_ref, band_ref), (other_ref, band_other))):
            rel = g - start_ref[h : h + 1, :]
            got = jnp.full((half, R), -1.0, F32)
            for b in range(picked // half):
                got = jnp.where(rel == b, from_ref[h, b * half : (b + 1) * half, :].astype(F32), got)
            at = (2 * (h % 2) + i) * R
            out_ref[0, h // 2, :, at : at + R] = got


def picks(core_index, pick, pick_other, band, band_other, groups, half):
    heads, picked, R = pick.shape
    return pl.pallas_call(
        picks_body,
        name="picks",
        grid=(groups,),
        out_shape=pltpu.HBM((groups, heads // 2, half, 4 * R), F32),
        in_specs=[pl.BlockSpec(memory_space=pltpu.SMEM)]
        + [pl.BlockSpec((heads, picked, R), lambda g: (0, 0, 0))] * 2
        + [pl.BlockSpec((heads, R), lambda g: (0, 0))] * 2,
        out_specs=pl.BlockSpec((1, heads // 2, half, 4 * R), lambda g: (g, 0, 0, 0)),
        compiler_params=pltpu.CompilerParams(vmem_limit_bytes=VMEM_LIMIT),
    )(core_index, pick, pick_other, band, band_other)


def chosen_scores(k2, qq, a):
    half = a.shape[0]
    sT = nt(k2, qq)
    s = jnp.where(a > 0.5, sT[half:], sT[:half])
    return jnp.where(a < -0.5, NEG_FILL, s)


def spread(p, a):
    zero = jnp.zeros_like(p)
    even = jnp.where(a == 0.0, p, zero).astype(BF)
    odd = jnp.where(a == 1.0, p, zero).astype(BF)
    return jnp.concatenate([even, odd], 0)


def of_both(own, other):
    return stacked(jnp.concatenate([own, other], 0))


def own_lanes(t):
    R = t.shape[1] // 4
    return jnp.concatenate([t[:, :R], t[:, 2 * R : 3 * R]], 1)


def other_lanes(t):
    R = t.shape[1] // 4
    return jnp.concatenate([t[:, R : 2 * R], t[:, 3 * R :]], 1)


def all_lanes(own, other):
    R = own.shape[1] // 2
    return jnp.concatenate([own[:, :R], other[:, :R], own[:, R:], other[:, R:]], 1)


def cross_fwd_body(first, last, gid_ref, q_ref, q_other, *refs):
    kv, a_refs, refs = refs[:2], refs[2:4], refs[4:]
    if not first:
        m_in, l_in, acc_in = refs[:3]
        refs = refs[3:]
    m_ref, l_ref, acc_ref = refs[:3]

    @pl.when(pl.program_id(0) == 0)
    def _():
        if first:
            m_ref[...] = jnp.full(m_ref.shape, NEG_FILL, F32)
            l_ref[...] = jnp.zeros(l_ref.shape, F32)
            acc_ref[...] = jnp.zeros(acc_ref.shape, F32)
        else:
            m_ref[...] = m_in[...]
            l_ref[...] = l_in[...]
            acc_ref[...] = acc_in[...]

    pairs = acc_ref.shape[0]
    for hp in range(pairs):
        sl = slice(hp * PAIR, (hp + 1) * PAIR)
        qq = of_both(q_ref[:, sl], q_other[:, sl])
        scores = [chosen_scores(kv[j][0, 0, :, sl], qq, a_refs[j][0, hp]) for j in range(2)]
        old = m_ref[hp : hp + 1, :]
        top = functools.reduce(jnp.maximum, [jnp.max(s, 0, keepdims=True) for s in scores], old)
        fade = jnp.exp(old - top)
        total = l_ref[hp : hp + 1, :] * fade
        acc = acc_ref[hp] * fade
        for j in range(2):
            a = a_refs[j][0, hp]
            p = jnp.where(a < -0.5, 0.0, jnp.exp(scores[j] - top))
            total = total + jnp.sum(p, 0, keepdims=True)
            acc = acc + tn(kv[j][0, 1, :, sl], spread(p, a))
        m_ref[hp : hp + 1, :] = top
        l_ref[hp : hp + 1, :] = total
        acc_ref[hp] = acc

    if last:
        own_ref, other_ref = refs[3:]

        @pl.when(pl.program_id(0) == pl.num_programs(0) - 1)
        def _():
            for out, lanes in ((own_ref, own_lanes), (other_ref, other_lanes)):
                out[pairs * PAIR :, :] = jnp.zeros((8, out.shape[1]), F32)
                for hp in range(pairs):
                    out[hp * PAIR : (hp + 1) * PAIR, :] = lanes(acc_ref[hp])
                    out[pairs * PAIR + hp : pairs * PAIR + hp + 1, :] = lanes(m_ref[hp : hp + 1, :])
                    out[pairs * PAIR + 4 + hp : pairs * PAIR + 5 + hp, :] = lanes(l_ref[hp : hp + 1, :])


def kv_specs(kv, a):
    rows, C = kv[0].shape[2:]
    specs = [pl.BlockSpec((1, 2, rows, C), lambda i, gid: (i, 0, 0, 0)) for _ in range(2)]
    for j in range(2):
        specs.append(
            pl.BlockSpec((1,) + a.shape[1:], functools.partial(lambda j, i, gid: (gid[2 * i + j], 0, 0, 0), j))
        )
    return specs


def fixed(shape):
    return pl.BlockSpec(shape, lambda i, gid: (0,) * len(shape))


def cross_fwd(gid, q, kv, a, state, last):
    R, C = q[0].shape
    pairs = C // PAIR
    hi, _, rows, _ = kv[0].shape
    shapes = [(8, 4 * R), (8, 4 * R), (pairs, PAIR, 4 * R)]
    first = state is None
    state = () if first else tuple(state)
    if last:
        shapes += [(C + 8, 2 * R)] * 2
    return pl.pallas_call(
        functools.partial(cross_fwd_body, first, last),
        name="cross_fwd",
        grid_spec=pltpu.PrefetchScalarGridSpec(
            num_scalar_prefetch=1,
            grid=(hi,),
            in_specs=[fixed(q[0].shape)] * 2 + kv_specs(kv, a) + [fixed(s.shape) for s in state],
            out_specs=[fixed(s) for s in shapes],
        ),
        out_shape=[jax.ShapeDtypeStruct(s, F32) for s in shapes],
        compiler_params=pltpu.CompilerParams(vmem_limit_bytes=VMEM_LIMIT),
        cost_estimate=pl.CostEstimate(flops=1, bytes_accessed=1, transcendentals=0),
    )(gid, *q, *kv, *([pltpu.with_memory_space_constraint(a, pltpu.HBM)] * 2), *state)


def merged(own_ref, got_ref, hp, C):
    sl = slice(hp * PAIR, (hp + 1) * PAIR)
    m, l = slice(C + hp, C + hp + 1), slice(C + 4 + hp, C + 5 + hp)
    m1, m2 = own_ref[m, :], got_ref[m, :]
    top = jnp.maximum(m1, m2)
    f1, f2 = jnp.exp(m1 - top), jnp.exp(m2 - top)
    total = own_ref[l, :] * f1 + got_ref[l, :] * f2
    return top + jnp.log(total), unstacked((own_ref[sl, :] * f1 + got_ref[sl, :] * f2) * (1.0 / total))


def cross_mix_body(own_ref, got_ref, wm, log_ref, of_ref, o_ref, part_ref):
    C = wm.shape[0]
    log_ref[...] = jnp.zeros(log_ref.shape, F32)
    for hp in range(C // PAIR):
        sl = slice(hp * PAIR, (hp + 1) * PAIR)
        log_ref[hp : hp + 1, :], o = merged(own_ref, got_ref, hp, C)
        of_ref[:, sl] = o
        o_ref[:, sl] = o.astype(BF)
    part_ref[...] = nn(o_ref[...], wm[...]).astype(BF)


def cross_mix_fwd(own, got, wm):
    R2 = own.shape[1]
    C, D = wm.shape
    R = R2 // 2
    return whole(
        cross_mix_body,
        "cross_mix",
        [((8, R2), F32), ((R, C), F32), ((R, C), BF), ((R, D), BF)],
        own, got, wm,
    )


def cross_merge_body(own_ref, got_ref, log_ref, of_ref):
    C = of_ref.shape[1]
    log_ref[...] = jnp.zeros(log_ref.shape, F32)
    for hp in range(C // PAIR):
        log_ref[hp : hp + 1, :], of_ref[:, hp * PAIR : (hp + 1) * PAIR] = merged(own_ref, got_ref, hp, C)


def cross_merge(own, got):
    rows, R2 = own.shape
    return whole(cross_merge_body, "cross_merge", [((8, R2), F32), ((R2 // 2, rows - 8), F32)], own, got)


def ffn_back_rest(dlow_ref, gp_ref, wu, wd, dh_ref, part_ref):
    low = dlow_ref[...]
    for c in range(0, wu.shape[1], 256):
        sl = slice(c, c + 256)
        dh_ref[:, sl] = (nt(low, wd[sl, :]) * gp_ref[:, sl].astype(F32)).astype(BF)
    part_ref[...] = nt(dh_ref[...], wu[...]).astype(BF)


def last_body(g, u_ref, own, oth, cot, par, gp_ref, wu, wd, out_ref, dv_ref, dlow_ref, dh_ref, gg_ref, part_ref):
    R, D = u_ref.shape
    gain, shift = row_of(par, g), row_of(par, g + 1)
    gg_ref[...] = jnp.zeros(gg_ref.shape, F32)
    for r in range(0, R, ROWS):
        s = slice(r, r + ROWS)
        v = u_ref[s, :] + (own[s, :].astype(F32) + oth[s, :].astype(F32))
        xhat, _ = norm_parts(v)
        out_ref[s, :] = xhat * gain + shift
        dv, dg, db = norm_back(v, gain, cot[s, :].astype(F32))
        dv_ref[s, :] = dv
        dlow_ref[s, :] = dv.astype(BF)
        gg_ref[0:1, :] += dg
        gg_ref[1:2, :] += db
    flush(gg_ref, out_ref)
    ffn_back_rest(dlow_ref, gp_ref, wu, wd, dh_ref, part_ref)


def last_fwd_back(g, u, own, oth, cot, par, gp, wu, wd):
    R, D = u.shape
    FF = wu.shape[1]
    return whole(
        functools.partial(last_body, g),
        "last_fwd_back",
        [((R, D), F32, HBM), ((R, D), F32), ((R, D), BF), ((R, FF), BF), ((8, D), F32, HBM), ((R, D), BF)],
        u, own, oth, cot, par, gp, wu, wd,
    )


def ffn_back_body(g, own, oth, v_ref, par, gp_ref, wu, wd, dv_ref, dlow_ref, dh_ref, gg_ref, part_ref):
    R, D = v_ref.shape
    gain = row_of(par, g)
    gg_ref[...] = jnp.zeros(gg_ref.shape, F32)
    for r in range(0, R, ROWS):
        s = slice(r, r + ROWS)
        dy = own[s, :].astype(F32) + oth[s, :].astype(F32)
        dv, dg, db = norm_back(v_ref[s, :], gain, dy)
        dv_ref[s, :] = dv
        dlow_ref[s, :] = dv.astype(BF)
        gg_ref[0:1, :] += dg
        gg_ref[1:2, :] += db
    flush(gg_ref)
    ffn_back_rest(dlow_ref, gp_ref, wu, wd, dh_ref, part_ref)


def ffn_back(g, own, oth, v, par, gp, wu, wd, after):
    R, D = v.shape
    FF = wu.shape[1]
    return whole(
        functools.partial(ffn_back_body, g),
        "ffn_back",
        [((R, D), F32), ((R, D), BF), ((R, FF), BF), ((8, D), F32, HBM), ((R, D), BF)],
        own, oth, v, par, gp, wu, wd,
        after=after,
    )


def branch_back(g, dres, own, oth, v_ref, par, dv_ref, dlow_ref, gg_ref):
    R, D = v_ref.shape
    gain = row_of(par, g)
    gg_ref[...] = jnp.zeros(gg_ref.shape, F32)
    for r in range(0, R, ROWS):
        s = slice(r, r + ROWS)
        dy = dres[s, :] + (own[s, :].astype(F32) + oth[s, :].astype(F32))
        dv, dg, db = norm_back(v_ref[s, :], gain, dy)
        dv_ref[s, :] = dv
        dlow_ref[s, :D] = dv.astype(BF)
        gg_ref[0:1, :] += dg
        gg_ref[1:2, :] += db


def cross_mix_back_body(g, dres, own, oth, v_ref, par, wm, dv_ref, pack_ref, gg_ref):
    branch_back(g, dres, own, oth, v_ref, par, dv_ref, pack_ref, gg_ref)
    flush(dv_ref, gg_ref)
    D = v_ref.shape[1]
    pack_ref[:, D:] = nt(pack_ref[:, :D], wm[...]).astype(BF)


def cross_mix_back(g, dres, own, oth, v, par, wm):
    R, D = v.shape
    C = wm.shape[0]
    return whole(
        functools.partial(cross_mix_back_body, g),
        "cross_mix_back",
        [((R, D), F32, HBM), ((R, D + C), BF), ((8, D), F32, HBM)],
        dres, own, oth, v, par, wm,
    )


def cross_back_body(first, last, gid_ref, q_ref, q_other, do_pack, do_pack_other, *refs):
    C = q_ref.shape[1]
    skip = do_pack.shape[1] - C
    do_ref, do_other = do_pack.at[:, skip:], do_pack_other.at[:, skip:]
    kv, a_refs, refs = refs[:2], refs[2:4], refs[4:]
    if first:
        of_ref, of_other, log_own, log_other = refs[:4]
        dq_ref, stat_ref, keep_ref, send_ref = refs[4:8]
    else:
        dq_in, stat_in = refs[:2]
        dq_ref, stat_ref, keep_ref, send_ref = refs[2:6]
    pairs = dq_ref.shape[0]

    @pl.when(pl.program_id(0) == 0)
    def _():
        if not first:
            dq_ref[...] = dq_in[...]
            stat_ref[...] = stat_in[...]
            return
        dq_ref[...] = jnp.zeros(dq_ref.shape, F32)
        stat_ref[...] = jnp.zeros(stat_ref.shape, F32)
        stat_ref[0:8, :] = all_lanes(log_own[...], log_other[...])
        for hp in range(pairs):
            sl = slice(hp * PAIR, (hp + 1) * PAIR)
            sums = []
            for d, o in ((do_ref, of_ref), (do_other, of_other)):
                prod = (d[:, sl].astype(F32) * o[:, sl]).T
                sums.append([jnp.sum(prod[:HD], 0, keepdims=True), jnp.sum(prod[HD:], 0, keepdims=True)])
            stat_ref[8 + hp : 9 + hp, :] = jnp.concatenate([sums[0][0], sums[1][0], sums[0][1], sums[1][1]], 1)

    for hp in range(pairs):
        sl = slice(hp * PAIR, (hp + 1) * PAIR)
        qq = of_both(q_ref[:, sl], q_other[:, sl])
        dd = of_both(do_ref[:, sl], do_other[:, sl])
        log_total = stat_ref[hp : hp + 1, :]
        delta = stat_ref[8 + hp : 9 + hp, :]
        dq = dq_ref[hp]
        for j, out_ref in enumerate((keep_ref, send_ref)):
            a = a_refs[j][0, hp]
            half = a.shape[0]
            k2 = kv[j][0, 0, :, sl]
            p = jnp.exp(chosen_scores(k2, qq, a) - log_total)
            daT = nt(kv[j][0, 1, :, sl], dd)
            ds = p * (jnp.where(a > 0.5, daT[half:], daT[:half]) - delta)
            dsT = spread(ds, a)
            out_ref[0, 0, :, sl] = nn(dsT, qq).astype(BF)
            out_ref[0, 1, :, sl] = nn(spread(p, a), dd).astype(BF)
            dq = dq + tn(k2, dsT)
        dq_ref[hp] = dq

    if last:
        own_ref, other_ref = refs[-2:]

        @pl.when(pl.program_id(0) == pl.num_programs(0) - 1)
        def _():
            for hp in range(pairs):
                own_ref[hp] = own_lanes(dq_ref[hp])
                other_ref[hp] = other_lanes(dq_ref[hp])


def cross_back(gid, q, do, kv, a, extra, first, last, after=()):
    R, C = q[0].shape
    pairs = C // PAIR
    hi, _, rows, _ = kv[0].shape
    grad_spec = pl.BlockSpec((1, 2, rows, C), lambda i, gid: (i, 0, 0, 0))
    shapes = [(pairs, PAIR, 4 * R), (16, 4 * R)]
    out_specs = [fixed(s) for s in shapes] + [grad_spec] * 2
    out_shape = [jax.ShapeDtypeStruct(s, F32) for s in shapes] + [jax.ShapeDtypeStruct(kv[0].shape, BF)] * 2
    if last:
        out_specs += [fixed((pairs, PAIR, 2 * R))] * 2
        out_shape += [jax.ShapeDtypeStruct((pairs, PAIR, 2 * R), F32)] * 2
    return pl.pallas_call(
        behind(functools.partial(cross_back_body, first, last), 9 + len(extra), len(after)),
        name="cross_back",
        grid_spec=pltpu.PrefetchScalarGridSpec(
            num_scalar_prefetch=1,
            grid=(hi,),
            in_specs=[fixed(q[0].shape)] * 2
            + [fixed(do[0].shape)] * 2
            + kv_specs(kv, a)
            + [fixed(e.shape) for e in extra]
            + [pl.BlockSpec(memory_space=pl.ANY)] * len(after),
            out_specs=out_specs,
        ),
        out_shape=out_shape,
        compiler_params=pltpu.CompilerParams(vmem_limit_bytes=VMEM_LIMIT),
        cost_estimate=pl.CostEstimate(flops=1, bytes_accessed=1, transcendentals=0),
    )(gid, *q, *do, *kv, *([pltpu.with_memory_space_constraint(a, pltpu.HBM)] * 2), *extra, *after)


def cross_q_back_body(dq_own, dq_got, wq, dq_ref, part_ref):
    for hp in range(dq_own.shape[0]):
        sl = slice(hp * PAIR, (hp + 1) * PAIR)
        dq_ref[:, sl] = (unstacked(dq_own[hp] + dq_got[hp]) * SCALE).astype(BF)
    flush(dq_ref)
    part_ref[...] = nt(dq_ref[...], wq[...]).astype(BF)


def cross_q_back(dq, got, wq, after):
    D, C = wq.shape
    R = dq.shape[2] // 2
    return whole(cross_q_back_body, "cross_q_back", [((R, C), BF), ((R, D), BF)], dq, got, wq, after=after)


def store_back_body(spread_at, *refs):
    n = len(refs) - 4
    wk, wv, dkv_ref, part_ref = refs[n:]
    R, C = dkv_ref.shape[0], dkv_ref.shape[1] // 2
    for i in range(2):
        parts = [t[0, i] for t in refs[:spread_at]]
        if spread_at < n:
            parts.append(refs[spread_at + i][0, 0])
        total = functools.reduce(lambda x, y: x + y, [t.astype(F32) for t in parts])
        dkv_ref[:, i * C : (i + 1) * C] = total.astype(BF)
    part = nt(dkv_ref[:, :C], wk[...]) + nt(dkv_ref[:, C:], wv[...])
    part_ref[...] = tn(order_matrix(R), part.astype(BF)).astype(BF)


def store_back(terms, wk, wv, after):
    D, C = wk.shape
    R = terms[0].shape[2]
    full = [t for t in terms if not isinstance(t, list)]
    halves = [h for t in terms if isinstance(t, list) for h in t]
    return whole(
        functools.partial(store_back_body, len(full)),
        "store_back",
        [((R, 2 * C), BF), ((R, D), BF)],
        *full, *halves, wk, wv,
        after=after,
    )


def attend_back_body(causal, g, n_more, *refs):
    if causal:
        len_ref, refs = refs[0], refs[1:]
    (dres, own, oth, v1_ref, par, q_ref, k_ref, v_ref, wq, wk, wv, wm) = refs[:12]
    R, D = v1_ref.shape
    dv_ref, pack_ref, gg_ref, part_ref = refs[12 + n_more : 16 + n_more]
    branch_back(g, dres, own, oth, v1_ref, par, dv_ref, pack_ref, gg_ref)
    flush(dv_ref, gg_ref)
    if n_more:
        gains_ref = refs[-1]
        rows = [gg_ref[0:2, :]] + [other[0:2, :] for other in refs[12 : 12 + n_more]]
        rows.append(jnp.zeros((gains_ref.shape[0] - 2 - 2 * n_more, D), F32))
        gains_ref[...] = jnp.concatenate(rows, 0).astype(BF)
        flush(gains_ref)
    C = wq.shape[1]
    do = nt(pack_ref[:, :D], wm[...]).astype(BF)
    allowed = causal_mask(R, len_ref[0]) if causal else None
    for c in range(0, C, PAIR):
        sl = slice(c, c + PAIR)
        k2 = k_ref[:, sl]
        qq = stacked(q_ref[:, sl])
        dd = stacked(do[:, sl])
        w = local_weights(k2, qq, allowed)
        daT = nt(v_ref[:, sl], dd)
        ds = (w * (daT - jnp.sum(w * daT, 0, keepdims=True))).astype(BF)
        at = D + c
        pack_ref[:, at : at + PAIR] = (unstacked(tn(k2, ds)) * SCALE).astype(BF)
        pack_ref[:, at + C : at + C + PAIR] = nn(ds, qq).astype(BF)
        pack_ref[:, at + 2 * C : at + 2 * C + PAIR] = nn(w.astype(BF), dd).astype(BF)
    flush(pack_ref)
    part = nt(pack_ref[:, D : D + C], wq[...]) + nt(pack_ref[:, D + C : D + 2 * C], wk[...])
    part_ref[...] = (part + nt(pack_ref[:, D + 2 * C :], wv[...])).astype(BF)


def attend_back(g, dres, own, oth, v1, par, kept, weights, length=None, more=(), after=()):
    R, D = v1.shape
    C = kept[0].shape[1]
    args = (dres, own, oth, v1, par, *kept, *weights, *more)
    causal = length is not None
    if causal:
        args = (length,) + args
    return whole(
        functools.partial(attend_back_body, causal, g, len(more)),
        "attend_back",
        [((R, D), F32, HBM), ((R, D + 3 * C), BF), ((8, D), F32, HBM), ((R, D), BF)]
        + [((16, D), BF)] * bool(more),
        *args,
        smem=int(causal),
        after=after,
    )


def weight_body(plan, chunks, sources, n_idx, *refs):
    idx_refs, ins, outs = refs[:n_idx], refs[n_idx : -2 * len(chunks)], refs[-2 * len(chunks) :]
    half = outs[0].shape[0]
    chunk, at, takes = 0, 0, {}
    for part, a_at, off, D, grads in plan:
        if part not in takes:
            spot = lax.broadcasted_iota(jnp.int32, (2 * half, D), 1) == idx_refs[part][...]
            takes[part] = spot.astype(F32).astype(BF)
        parts = [nt(takes[part], ins[a_at + i][:, off : off + D]) for i in range(sources)]
        aT = jnp.concatenate(parts, 1).astype(BF)
        for d_at, d_off, width in grads:
            step = 384 if width % 384 == 0 else 128
            for c in range(d_off, d_off + width, step):
                dy = jnp.concatenate([ins[d_at + i][:, c : c + step] for i in range(sources)], 0)
                got = nn(aT, dy)
                outs[2 * chunk][:, at : at + step] = got[:half].astype(BF)
                outs[2 * chunk + 1][:, at : at + step] = got[half:].astype(BF)
                at += step
                if at == chunks[chunk]:
                    chunk, at = chunk + 1, 0


def weight_grads(idxs, D, term_lists, chunks, after=()):
    ins, plan = [], []
    for part, terms in enumerate(term_lists):
        for a, off, grads in terms:
            at = len(ins)
            ins += list(a)
            ds = []
            for d, d_off, w in grads:
                ds.append((len(ins), d_off, w))
                ins += list(d)
            plan.append((part, at, off, D, ds))
    half = idxs[0].shape[0] // 2
    return whole(
        functools.partial(weight_body, plan, chunks, len(term_lists[0][0][0]), len(idxs)),
        "weight_grads",
        [((half, w), BF) for w in chunks for _ in range(2)],
        *idxs,
        *ins,
        after=after,
    )


def swap(x, bit, n):
    return lax.ppermute(x, "blk", [(i, i ^ bit) for i in range(n)])


def tied(x, *before):
    return lax.optimization_barrier((x, *before))[0]


def other_tp(x):
    return lax.ppermute(x, "tp", [(0, 1), (1, 0)])


class Halving:
    def __init__(self, keep, send, n, bits):
        self.keep, self.send, self.n, self.bits = keep, send, n, bits
        self.got = swap(send, bits[0], n)

    def hold(self, *before):
        self.send = tied(self.send, *before)
        self.got = swap(self.send, self.bits[0], self.n)

    def step(self, *before):
        got = tied(self.got, *before) if before else self.got
        total = self.keep.astype(F32) + got.astype(F32)
        self.bits = self.bits[1:]
        if not self.bits:
            return total
        half = total.shape[0] // 2
        self.keep, self.send = total[:half], total[half:].astype(BF)
        self.got = swap(self.send, self.bits[0], self.n)
        return self.send

    def end(self, *before):
        while len(self.bits) > 1:
            self.step(*before)
        return self.step(*before)


def on_device(
    n,
    encoder_in,
    decoder_in,
    lengths,
    retrieved,
    band_start,
    cotangent,
    enc_query,
    enc_key,
    enc_value,
    enc_mix,
    attn_gain,
    attn_shift,
    enc_up,
    enc_down,
    ffn_gain,
    ffn_shift,
    self_query,
    self_key,
    self_value,
    self_mix,
    self_gain,
    self_shift,
    cross_query,
    cross_key,
    cross_value,
    cross_mix,
    cross_gain,
    cross_shift,
    dec_up,
    dec_down,
    last_gain,
    last_shift,
):
    group_rows, D = encoder_in.shape
    C = cross_query.shape[1]
    FF = enc_up.shape[1]
    hi = n // 16
    me = lax.axis_index("blk")
    core = lambda x: swap(x, 1, n)
    par = jnp.stack(
        [attn_gain, attn_shift, ffn_gain, ffn_shift, self_gain, self_shift, cross_gain, cross_shift, last_gain, last_shift]
    )

    share = D // n
    bits = [1 << i for i in range(n.bit_length() - 1)]

    def rows_by(order):
        t = jnp.arange(share << len(order), dtype=jnp.int32)
        block = t // share
        rel = sum(((block >> (len(order) - 1 - i)) & 1) * bit for i, bit in enumerate(order))
        return ((me ^ rel) * share + t % share).reshape(-1, 1)

    def gradients(order, terms, after=()):
        width = sum(grad[2] for _, _, grads in terms for grad in grads)
        return Halving(*weight_grads([rows_by(order)], D, [terms], [width], after), n, order)

    def joint(parts, after=()):
        chunks = [w for _, _, widths in parts for w in widths]
        made = weight_grads([rows_by(order) for order, _, _ in parts], D, [terms for _, terms, _ in parts], chunks, after)
        gots = [swap(send, 1, n) for send in made[1::2]]

        def finish(*before):
            tied_gots = lax.optimization_barrier((*gots, *before))[: len(gots)]
            totals = [k.astype(F32) + g.astype(F32) for k, g in zip(made[0::2], tied_gots)]
            half, sums = totals[0].shape[0] // 2, []
            for order, _, widths in parts:
                mine, totals = totals[: len(widths)], totals[len(widths) :]
                keep = jnp.concatenate([t[:half] for t in mine], 1)
                send = jnp.concatenate([t[half:].astype(BF) for t in mine], 1)
                sums.append(Halving(keep, send, n, order[1:]))
            return sums

        return made[0], finish

    both = lambda x: (x, core(x))
    summed = lambda *arrays: functools.reduce(lambda x, y: x + y, [t.astype(F32) for t in arrays]).astype(BF)

    *enc_kept, enc_o, enc_part = attend_fwd(encoder_in, enc_query, enc_key, enc_value, enc_mix, fetch=True)
    enc_other = other_tp(enc_part)
    pick = pick_rows(retrieved, (enc_part,))
    band = tied(band_start.T, pick)
    pick_other, band_other = core(pick), core(band)
    *self_kept, self_o, self_part = attend_fwd(
        decoder_in, self_query, self_key, self_value, self_mix, lengths, (pick,)
    )
    enc_other = tied(enc_other, self_part)
    v1, u1, low1, act1, gp1, part1 = ffn_fwd(0, encoder_in, enc_part, enc_other, par, enc_up, enc_down, True, True)
    other1 = other_tp(part1)
    chosen = picks((me & 1).reshape(1), tied(pick, part1), pick_other, band, band_other, n // 2, group_rows // 2)
    other1 = tied(other1, chosen)
    v2, encoded, enc_low, store = store_fwd(2, u1, part1, other1, par, cross_key, cross_value)

    store = store[None]
    for b in range(4, n.bit_length() - 1):
        store = jnp.concatenate([store, swap(store, 1 << b, n)], 0)

    def gid_of(pair):
        return (me ^ jnp.array([16 * h + r for h in range(hi) for r in pair], jnp.int32)) >> 1

    near = swap(store, 4, n)
    y_own = swap(store, 2, n)
    far = swap(store, 8, n)
    self_part = tied(self_part, store)
    self_other = other_tp(self_part)
    vd, ud, lowd, qc = cross_q(4, decoder_in, self_part, self_other, par, cross_query)
    qcs = both(qc)
    far = tied(far, near, y_own, qcs[1])
    apart = swap(far, 4, n)
    y_far = swap(far, 2, n)
    state = cross_fwd(gid_of((0, 2)), qcs, (tied(store, far), y_own), chosen, None, False)
    state = cross_fwd(gid_of((4, 8)), qcs, (near, far), chosen, state, False)
    apart = tied(apart, *state)
    y_near = swap(tied(y_own, apart), 4, n)
    y_apart = swap(apart, 2, n)
    state = cross_fwd(gid_of((12, 10)), qcs, (apart, y_far), chosen, state, False)
    state_own, state_other = cross_fwd(gid_of((6, 14)), qcs, (y_near, y_apart), chosen, state, True)[3:]
    pieces = [(store, y_own), (near, y_near), (far, y_far), (apart, y_apart)]
    log_own, of_own, oc, partc = cross_mix_fwd(state_own, core(state_other), cross_mix)
    otherc = other_tp(partc)
    log_other, of_other = cross_merge(state_other, core(tied(state_own, partc)))
    otherc = tied(otherc, of_other)

    vc, uc, lowc, actc, gpc, part3 = ffn_fwd(6, ud, partc, otherc, par, dec_up, dec_down, False, False)
    other3 = other_tp(part3)
    actc_y = swap(actc, 2, n)
    decoded, dlast, dlowc, dhc, gg_last, part4 = last_fwd_back(8, uc, part3, other3, cotangent, par, gpc, dec_up, dec_down)
    dlowc_y = swap(dlowc, 2, n)
    other4 = tied(other_tp(part4), actc_y, dlowc_y)
    dcross, dpacko, gg_cross = cross_mix_back(6, dlast, part4, other4, vc, par, cross_mix)

    dpackos = both(dpacko)
    back = lambda k, extra, after: cross_back(
        gid_of((4 * k, 4 * k + 2)), qcs, dpackos, pieces[k], chosen, extra, k == 3, k == 0, after
    )
    *extra, keep3, send3 = back(3, (of_own, of_other, log_own, log_other), ())
    got3 = swap(send3, 2, n)
    no_y = bits[:1] + bits[2:]
    down = gradients(no_y, [((dlowc, dlowc_y), 0, [((actc, actc_y), 0, FF)])], (send3,))
    *extra, keep2, send2 = back(2, extra, (down.keep,))
    got2 = swap(send2, 2, n)
    one = lambda x: (x,)
    up = gradients(bits, [(one(lowc), 0, [(one(dhc), 0, FF)])], (send2,))
    sum3 = summed(keep3, tied(got3, up.keep))
    apart = swap(sum3, 4, n)
    down_z = down.step(sum3)
    *extra, keep1, send1 = back(1, extra, (sum3, down_z))
    got1 = swap(send1, 2, n)
    got2 = tied(got2, send1)
    sum2 = summed(keep2, got2, apart)
    far = swap(sum2, 8, n)
    _, _, keep0, send0, dq_own, dq_other = back(0, extra, (sum2,))
    got0 = swap(send0, 2, n)
    up_y = up.step(send0)
    sum1 = summed(keep1, tied(got1, send0, up_y))
    near = swap(sum1, 4, n)
    terms = [keep0, got0, near, far]
    bit = n // 2
    while terms[0].shape[0] > 1:
        half = terms[0].shape[0] // 2
        total = functools.reduce(lambda x, y: x + y, [t.astype(F32) for t in terms])
        terms = [total[:half].astype(BF), swap(total[half:].astype(BF), bit, n)]
        bit //= 2

    dqc, partq = cross_q_back(dq_own, core(tied(dq_other, sum1, far)), cross_query, ())
    otherq = other_tp(partq)
    up.hold(got0, near, far)
    up_y = up.send
    down.hold(up_y)
    dself, dpackd, gg_self, part6 = attend_back(
        4, dcross, partq, tied(otherq, up_y), vd, par, self_kept, (self_query, self_key, self_value, self_mix), lengths,
    )
    own_keep, own_sums = joint(
        [
            (
                bits,
                [
                    (one(lowd), 0, [(one(dqc), 0, C)]),
                    (one(dpacko), 0, [(one(oc), 0, C)]),
                    (one(decoder_in), 0, [(one(dpackd), D, 3 * C)]),
                    (one(dpackd), 0, [(one(self_o), 0, C)]),
                ],
                [C] * 6,
            )
        ]
    )
    down_z = down.step(up_y)
    up_z = up.step(down_z)
    (own,) = own_sums(up_z)

    dkv, part5 = store_back(terms, cross_key, cross_value, (own.send,))
    other5 = other_tp(part5)
    down_sum = down.end(part5)
    up_z = up.step(down_sum)
    dffn, dlow1, dh1, gg_ffn, part7 = ffn_back(
        2, part5, tied(other5, up_z), v2, par, gp1, enc_up, enc_down, ()
    )
    other7 = other_tp(part7)
    z_first = bits[:1] + bits[2:] + bits[1:2]
    ffn_keep, ffn_sums = joint(
        [
            (z_first, [(one(dlow1), 0, [(one(act1), 0, FF)])], [FF // 2] * 2),
            (
                bits,
                [(one(enc_low), 0, [(one(dkv), 0, 2 * C)]), (one(low1), 0, [(one(dh1), 0, FF)])],
                [2 * C] + [FF // 2] * 2,
            ),
        ],
    )
    own_z = own.step(ffn_keep)
    down1, up1 = ffn_sums(own_z)
    dattn, dpacke, _, part8, gains = attend_back(
        0, dffn, part7, tied(other7, up1.send, down1.send), v1, par, enc_kept, (enc_query, enc_key, enc_value, enc_mix), None,
        (gg_ffn, gg_self, gg_cross, gg_last),
    )
    up_sum = up.end(part8)
    own_z = own.step(up_sum)
    lanes = jnp.eye(16, 128, dtype=BF)
    last_keep, last_sums = joint(
        [
            (
                bits,
                [
                    (one(encoder_in), 0, [(one(dpacke), D, 3 * C)]),
                    (one(dpacke), 0, [(one(enc_o), 0, C)]),
                    (one(gains), 0, [(one(lanes), 0, 128)]),
                ],
                [2 * C, 2 * C + 128],
            )
        ],
        (own_z,),
    )
    up1_z = up1.step(last_keep)
    (last,) = last_sums(up1_z)
    other6, other8 = other_tp(tied(part6, last.send)), other_tp(tied(part8, last.send))
    down1_z = down1.step(last.send)
    own_sum = own.end(down1_z)
    up1_z = up1.step(own_sum)
    down1_z = down1.step(up1_z)
    last_z = last.step(down1_z)
    up1_sum = up1.end(last_z)
    down1_sum = down1.end(up1_sum)
    last_z = last.step(down1_sum, other6, other8)
    last_sum = last.end()
    grad_encoder_in = dattn + (part8.astype(F32) + other8.astype(F32))
    grad_decoder_in = dself + (part6.astype(F32) + other6.astype(F32))

    cut = lambda total, at, width: total[:, at : at + width]
    gain_of = [last_sum[:, 4 * C + i] for i in range(10)]
    return (
        encoded,
        decoded,
        grad_encoder_in,
        grad_decoder_in,
        cut(last_sum, 0, C),
        cut(last_sum, C, C),
        cut(last_sum, 2 * C, C),
        cut(last_sum, 3 * C, C).T,
        gain_of[0],
        gain_of[1],
        cut(up1_sum, 2 * C, FF),
        down1_sum.T,
        gain_of[2],
        gain_of[3],
        cut(own_sum, 2 * C, C),
        cut(own_sum, 3 * C, C),
        cut(own_sum, 4 * C, C),
        cut(own_sum, 5 * C, C).T,
        gain_of[4],
        gain_of[5],
        cut(own_sum, 0, C),
        cut(up1_sum, 0, C),
        cut(up1_sum, C, C),
        cut(own_sum, C, C).T,
        gain_of[6],
        gain_of[7],
        up_sum,
        down_sum.T,
        gain_of[8],
        gain_of[9],
    )


def solution(mesh):
    rows, both, cols, down = P("blk", None), P("blk", "tp"), P(None, "tp"), P("tp", None)
    attn = (cols, cols, cols, down, P(), P())
    ffn = (cols, down, P(), P())
    in_specs = (rows, rows, P("blk"), P("blk", "tp", None), both, rows) + attn + ffn + attn + attn + ffn
    mixed = P("tp", "blk")
    grad_attn = (both, both, both, mixed, P("blk"), P("blk"))
    grad_ffn = (both, mixed, P("blk"), P("blk"))
    out_specs = (rows,) * 4 + grad_attn + grad_ffn + grad_attn + grad_attn + grad_ffn
    return jax.shard_map(
        functools.partial(on_device, mesh.shape["blk"]),
        mesh=mesh,
        in_specs=in_specs,
        out_specs=out_specs,
        check_vma=False,
    )
```

```python
import functools

import jax
import jax.numpy as jnp
from jax import lax
from jax.experimental import pallas as pl
from jax.experimental.pallas import tpu as pltpu
from jax.sharding import PartitionSpec as P

HD = 64
PAIR = 2 * HD
NEG_FILL = -1e30
EPS_NORM = 1e-05
SCALE = 0.125
BF = jnp.bfloat16
F32 = jnp.float32
VMEM_LIMIT = 24 * 2**20
HBM = True
ROWS = 64


def nn(a, b):
    return lax.dot_general(a, b, (((1,), (0,)), ((), ())), preferred_element_type=F32)


def nt(a, b):
    return lax.dot_general(a, b, (((1,), (1,)), ((), ())), preferred_element_type=F32)


def tn(a, b):
    return lax.dot_general(a, b, (((0,), (0,)), ((), ())), preferred_element_type=F32)


def behind(body, n_in, n_after):
    if not n_after:
        return body
    return lambda *refs: body(*refs[:n_in], *refs[n_in + n_after :])


class Fetched:
    def __init__(self, far, near, sem):
        self.near, self.shape, self.pending = near, near.shape, pltpu.make_async_copy(far, near, sem)
        self.pending.start()

    def ready(self):
        if self.pending is not None:
            self.pending.wait()
            self.pending = None

    def __getitem__(self, at):
        self.ready()
        return self.near[at]


class Kept:
    def __init__(self, far, near, sem):
        self.far, self.near, self.shape, self.sem, self.copies, self.at = far, near, near.shape, sem, [], 0

    def flush(self, upto=None):
        if upto is None and self.at == 0:
            copy = pltpu.make_async_copy(self.near, self.far, self.sem.at[0])
        else:
            upto = self.shape[-1] if upto is None else upto
            if upto == self.at:
                return
            sl = (slice(None), slice(self.at, upto))
            copy = pltpu.make_async_copy(self.near.at[sl], self.far.at[sl], self.sem.at[len(self.copies)])
        self.at = self.shape[-1] if upto is None else upto
        copy.start()
        self.copies.append(copy)

    def wait(self):
        if self.at < self.shape[-1]:
            self.flush()
        for copy in self.copies:
            copy.wait()

    def __getitem__(self, at):
        return self.near[at]

    def __setitem__(self, at, value):
        self.near[at] = value


def flush(*refs, upto=None):
    for ref in refs:
        if isinstance(ref, Kept):
            ref.flush(upto)


class Far:
    def __init__(self, array):
        self.array = array


def whole(body, name, outs, *args, smem=0, after=()):
    far_in = [i for i, a in enumerate(args) if isinstance(a, Far)]
    far_out = [i for i, o in enumerate(outs) if len(o) > 2]
    args = [pltpu.with_memory_space_constraint(a.array, pltpu.HBM) if isinstance(a, Far) else a for a in args]
    n_in, n_out, n_after = len(args), len(outs), len(after)

    def run(*refs):
        ins = list(refs[:n_in])
        results = list(refs[n_in + n_after : n_in + n_after + n_out])
        scratch = refs[n_in + n_after + n_out :]
        for k, i in enumerate(far_in):
            ins[i] = Fetched(ins[i], scratch[k], scratch[-1].at[k, 0])
        for k, i in enumerate(far_out):
            results[i] = Kept(results[i], scratch[len(far_in) + k], scratch[-1].at[len(far_in) + k])
        body(*ins, *results)
        for i in far_in:
            ins[i].ready()
        for i in far_out:
            results[i].wait()

    moves = len(far_in) + len(far_out)
    scratch = [pltpu.VMEM(args[i].shape, args[i].dtype) for i in far_in]
    scratch += [pltpu.VMEM(outs[i][0], outs[i][1]) for i in far_out]
    if moves:
        scratch.append(pltpu.SemaphoreType.DMA((moves, 8)))
    in_specs = [pl.BlockSpec(memory_space=pltpu.SMEM if i < smem else pltpu.VMEM) for i in range(n_in)]
    out_specs = [pl.BlockSpec(memory_space=pltpu.VMEM) for _ in outs]
    for i in far_in:
        in_specs[i] = pl.BlockSpec(memory_space=pltpu.HBM)
    for i in far_out:
        out_specs[i] = pl.BlockSpec(memory_space=pltpu.HBM)
    return pl.pallas_call(
        run,
        name=name,
        out_shape=[pltpu.HBM(o[0], o[1]) if len(o) > 2 else jax.ShapeDtypeStruct(o[0], o[1]) for o in outs],
        in_specs=in_specs + [pl.BlockSpec(memory_space=pl.ANY)] * n_after,
        out_specs=out_specs,
        scratch_shapes=scratch,
        compiler_params=pltpu.CompilerParams(vmem_limit_bytes=VMEM_LIMIT),
        cost_estimate=pl.CostEstimate(flops=1, bytes_accessed=1, transcendentals=0),
    )(*args, *after)


def load_body(n, *refs):
    sems = refs[-1]
    copies = [pltpu.make_async_copy(refs[i], refs[n + i], sems.at[i]) for i in range(n)]
    for copy in copies:
        copy.start()
    for copy in copies:
        copy.wait()


def load(arrays, after):
    n, n_after = len(arrays), len(after)
    return pl.pallas_call(
        behind(functools.partial(load_body, n), n, n_after),
        name="load",
        out_shape=[pltpu.VMEM(a.shape, a.dtype) for a in arrays],
        in_specs=[pl.BlockSpec(memory_space=pltpu.HBM)] * n + [pl.BlockSpec(memory_space=pl.ANY)] * n_after,
        out_specs=[pl.BlockSpec(memory_space=pltpu.VMEM)] * n,
        scratch_shapes=[pltpu.SemaphoreType.DMA((n,))],
        compiler_params=pltpu.CompilerParams(vmem_limit_bytes=VMEM_LIMIT),
        cost_estimate=pl.CostEstimate(flops=1, bytes_accessed=1, transcendentals=0),
    )(*[pltpu.with_memory_space_constraint(a, pltpu.HBM) for a in arrays], *after)


def norm_parts(v):
    center = v - jnp.mean(v, -1, keepdims=True)
    r = lax.rsqrt(jnp.mean(center * center, -1, keepdims=True) + EPS_NORM)
    return center * r, r


def norm_back(v, gain, dy):
    xhat, r = norm_parts(v)
    gdy = gain * dy
    dv = r * (gdy - jnp.mean(gdy, -1, keepdims=True) - xhat * jnp.mean(gdy * xhat, -1, keepdims=True))
    return dv, jnp.sum(dy * xhat, 0, keepdims=True), jnp.sum(dy, 0, keepdims=True)


def row_of(par_ref, i):
    return par_ref[i : i + 1, :].astype(F32)


def low_half(shape, dim):
    return lax.broadcasted_iota(jnp.int32, shape, dim) < HD


def stacked(t2):
    first = low_half(t2.shape, 1)
    zero = jnp.zeros_like(t2)
    return jnp.concatenate([jnp.where(first, t2, zero), jnp.where(first, zero, t2)], 0)


def unstacked(tT):
    R = tT.shape[1] // 2
    first = low_half((PAIR, R), 0)
    return jnp.where(first, tT[:, :R], tT[:, R:]).T


def causal_mask(R, length):
    key = lax.broadcasted_iota(jnp.int32, (R, 2 * R), 0)
    lane = lax.broadcasted_iota(jnp.int32, (R, 2 * R), 1)
    query = jnp.where(lane >= R, lane - R, lane)
    return (key <= query) & (key < length)


def local_weights(k2, qq, allowed):
    sT = nt(k2, qq)
    if allowed is not None:
        sT = jnp.where(allowed, sT, NEG_FILL)
    p = jnp.exp(sT - jnp.max(sT, 0, keepdims=True))
    return p * (1.0 / jnp.sum(p, 0, keepdims=True))


def gelu_parts(h):
    cdf = 0.5 * (1.0 + lax.erf(h * 0.7071067811865476))
    pdf = 0.3989422804014327 * jnp.exp(-0.5 * h * h)
    return h * cdf, cdf + h * pdf


def attend_fwd_body(causal, *refs):
    if causal:
        len_ref, refs = refs[0], refs[1:]
    x_ref, wq, wk, wv, wm, q_ref, k_ref, v_ref, o_ref, part_ref = refs
    x = x_ref[...]
    R = x.shape[0]
    q_ref[...] = (nn(x, wq[...]) * SCALE).astype(BF)
    k_ref[...] = nn(x, wk[...]).astype(BF)
    v_ref[...] = nn(x, wv[...]).astype(BF)
    flush(q_ref, k_ref, v_ref)
    allowed = causal_mask(R, len_ref[0]) if causal else None
    for c in range(0, q_ref.shape[1], PAIR):
        sl = slice(c, c + PAIR)
        w = local_weights(k_ref[:, sl], stacked(q_ref[:, sl]), allowed).astype(BF)
        o_ref[:, sl] = unstacked(tn(v_ref[:, sl], w)).astype(BF)
    flush(o_ref)
    part_ref[...] = nn(o_ref[...], wm[...]).astype(BF)


def attend_fwd(x, wq, wk, wv, wm, length=None, after=(), fetch=False):
    R, D = x.shape
    C = wq.shape[1]
    args = (x, wq, wk, wv, wm)
    if fetch:
        args = tuple(Far(a) for a in args)
    causal = length is not None
    if causal:
        args = (length,) + args
    return whole(
        functools.partial(attend_fwd_body, causal),
        "attend_fwd",
        [((R, C), BF, HBM)] * 4 + [((R, D), BF)],
        *args,
        smem=int(causal),
        after=after,
    )


def ffn_fwd_body(g, x_ref, own, oth, par, wu, wd, v_ref, u_ref, low_ref, act_ref, gp_ref, part_ref):
    R, D = x_ref.shape
    gain, shift = row_of(par, g), row_of(par, g + 1)
    for r in range(0, R, ROWS):
        s = slice(r, r + ROWS)
        v = x_ref[s, :].astype(F32) + (own[s, :].astype(F32) + oth[s, :].astype(F32))
        xhat, _ = norm_parts(v)
        u = xhat * gain + shift
        v_ref[s, :] = v
        u_ref[s, :] = u
        low_ref[s, :] = u.astype(BF)
    flush(v_ref, low_ref)
    low = low_ref[...]
    for c in range(0, wu.shape[1], 256):
        sl = slice(c, c + 256)
        a, gp = gelu_parts(nn(low, wu[:, sl]))
        act_ref[:, sl] = a.astype(BF)
        gp_ref[:, sl] = gp.astype(BF)
        flush(act_ref, gp_ref, upto=c + 256)
    part_ref[...] = nn(act_ref[...], wd[...]).astype(BF)


def ffn_fwd(g, x, own, oth, par, wu, wd, fetch, keep):
    R, D = x.shape
    FF = wu.shape[1]
    kept = (HBM,) if keep else ()
    return whole(
        functools.partial(ffn_fwd_body, g),
        "ffn_fwd",
        [((R, D), F32, HBM), ((R, D), F32), ((R, D), BF, HBM), ((R, FF), BF, *kept), ((R, FF), BF, HBM), ((R, D), BF)],
        x, own, oth, par, *((Far(wu), Far(wd)) if fetch else (wu, wd)),
    )


def order_matrix(R):
    t = lax.broadcasted_iota(jnp.int32, (R, R), 0)
    col = lax.broadcasted_iota(jnp.int32, (R, R), 1)
    src = jnp.where(t < R // 2, 2 * t, 2 * t - (R - 1))
    return (src == col).astype(F32).astype(BF)


def store_body(g, u_ref, own, oth, par, wk, wv, v_ref, enc_ref, low_ref, kv_ref):
    R = u_ref.shape[0]
    gain, shift = row_of(par, g), row_of(par, g + 1)
    for r in range(0, R, ROWS):
        s = slice(r, r + ROWS)
        v = u_ref[s, :] + (own[s, :].astype(F32) + oth[s, :].astype(F32))
        xhat, _ = norm_parts(v)
        v_ref[s, :] = v
        enc_ref[s, :] = xhat * gain + shift
    flush(enc_ref)
    low_ref[...] = nn(order_matrix(R), enc_ref[...].astype(BF)).astype(BF)
    flush(low_ref)
    low = low_ref[...]
    kv_ref[0] = nn(low, wk[...]).astype(BF)
    kv_ref[1] = nn(low, wv[...]).astype(BF)


def store_fwd(g, u, own, oth, par, wk, wv):
    R, D = u.shape
    C = wk.shape[1]
    return whole(
        functools.partial(store_body, g),
        "store_fwd",
        [((R, D), F32), ((R, D), F32, HBM), ((R, D), BF), ((2, R, C), BF)],
        u, own, oth, par, wk, wv,
    )


def cross_q_body(g, x_ref, own, oth, par, wq, v_ref, u_ref, low_ref, q_ref):
    R = x_ref.shape[0]
    gain, shift = row_of(par, g), row_of(par, g + 1)
    for r in range(0, R, ROWS):
        s = slice(r, r + ROWS)
        v = x_ref[s, :].astype(F32) + (own[s, :].astype(F32) + oth[s, :].astype(F32))
        xhat, _ = norm_parts(v)
        u = xhat * gain + shift
        v_ref[s, :] = v
        u_ref[s, :] = u
        low_ref[s, :] = u.astype(BF)
    flush(v_ref, u_ref, low_ref)
    q_ref[...] = (nn(low_ref[...], wq[...]) * SCALE).astype(BF)


def cross_q(g, x, own, oth, par, wq):
    R, D = x.shape
    C = wq.shape[1]
    return whole(
        functools.partial(cross_q_body, g),
        "cross_q",
        [((R, D), F32, HBM), ((R, D), F32, HBM), ((R, D), BF, HBM), ((R, C), BF)],
        x, own, oth, par, wq,
    )


def pick_rows_body(from_ref, *out_refs):
    for pair, out_ref in enumerate(out_refs):
        for h in range(2):
            out_ref[h] = (from_ref[2 * pair + h] & 1).astype(F32).T.astype(BF)


def pick_rows(retrieved, after):
    R, heads, picked = retrieved.shape
    outs = [((2, picked, R), BF)] * (heads // 2)
    return whole(pick_rows_body, "pick_rows", outs, Far(retrieved.transpose(1, 0, 2)), after=after)


def picks_body(pairs, core_ref, *refs):
    own, other, (band_ref, band_other, out_ref) = refs[:pairs], refs[pairs : 2 * pairs], refs[2 * pairs :]
    g = 2 * pl.program_id(0) + core_ref[0]
    _, picked, R = own[0].shape
    half = out_ref.shape[2]
    for h in range(2 * pairs):
        for i, (from_ref, start_ref) in enumerate(((own[h // 2], band_ref), (other[h // 2], band_other))):
            rel = g - start_ref[h : h + 1, :]
            got = jnp.full((half, R), -1.0, F32)
            for b in range(picked // half):
                got = jnp.where(rel == b, from_ref[h % 2, b * half : (b + 1) * half, :].astype(F32), got)
            at = (2 * (h % 2) + i) * R
            out_ref[0, h // 2, :, at : at + R] = got


def picks(core_index, pick, pick_other, band, band_other, groups, half):
    pairs = len(pick)
    _, picked, R = pick[0].shape
    return pl.pallas_call(
        functools.partial(picks_body, pairs),
        name="picks",
        grid=(groups,),
        out_shape=pltpu.HBM((groups, pairs, half, 4 * R), F32),
        in_specs=[pl.BlockSpec(memory_space=pltpu.SMEM)]
        + [pl.BlockSpec((2, picked, R), lambda g: (0, 0, 0))] * (2 * pairs)
        + [pl.BlockSpec((2 * pairs, R), lambda g: (0, 0))] * 2,
        out_specs=pl.BlockSpec((1, pairs, half, 4 * R), lambda g: (g, 0, 0, 0)),
        compiler_params=pltpu.CompilerParams(vmem_limit_bytes=VMEM_LIMIT),
        cost_estimate=pl.CostEstimate(flops=1, bytes_accessed=1, transcendentals=0),
    )(core_index, *pick, *pick_other, band, band_other)


def chosen_scores(k2, qq, a):
    half = a.shape[0]
    sT = nt(k2, qq)
    s = jnp.where(a > 0.5, sT[half:], sT[:half])
    return jnp.where(a < -0.5, NEG_FILL, s)


def spread(p, a):
    zero = jnp.zeros_like(p)
    even = jnp.where(a == 0.0, p, zero).astype(BF)
    odd = jnp.where(a == 1.0, p, zero).astype(BF)
    return jnp.concatenate([even, odd], 0)


def of_both(own, other):
    return stacked(jnp.concatenate([own, other], 0))


def own_lanes(t):
    R = t.shape[1] // 4
    return jnp.concatenate([t[:, :R], t[:, 2 * R : 3 * R]], 1)


def other_lanes(t):
    R = t.shape[1] // 4
    return jnp.concatenate([t[:, R : 2 * R], t[:, 3 * R :]], 1)


def all_lanes(own, other):
    R = own.shape[1] // 2
    return jnp.concatenate([own[:, :R], other[:, :R], own[:, R:], other[:, R:]], 1)


def cross_fwd_body(first, last, gid_ref, q_ref, q_other, *refs):
    kv, a_refs, refs = refs[:2], refs[2:4], refs[4:]
    if not first:
        m_in, l_in, acc_in = refs[:3]
        refs = refs[3:]
    m_ref, l_ref, acc_ref = refs[:3]

    @pl.when(pl.program_id(0) == 0)
    def _():
        if first:
            m_ref[...] = jnp.full(m_ref.shape, NEG_FILL, F32)
            l_ref[...] = jnp.zeros(l_ref.shape, F32)
            acc_ref[...] = jnp.zeros(acc_ref.shape, F32)
        else:
            m_ref[...] = m_in[...]
            l_ref[...] = l_in[...]
            acc_ref[...] = acc_in[...]

    pairs = acc_ref.shape[0]
    for hp in range(pairs):
        sl = slice(hp * PAIR, (hp + 1) * PAIR)
        qq = of_both(q_ref[:, sl], q_other[:, sl])
        scores = [chosen_scores(kv[j][0, 0, :, sl], qq, a_refs[j][0, hp]) for j in range(2)]
        old = m_ref[hp : hp + 1, :]
        top = functools.reduce(jnp.maximum, [jnp.max(s, 0, keepdims=True) for s in scores], old)
        fade = jnp.exp(old - top)
        total = l_ref[hp : hp + 1, :] * fade
        acc = acc_ref[hp] * fade
        for j in range(2):
            a = a_refs[j][0, hp]
            p = jnp.where(a < -0.5, 0.0, jnp.exp(scores[j] - top))
            total = total + jnp.sum(p, 0, keepdims=True)
            acc = acc + tn(kv[j][0, 1, :, sl], spread(p, a))
        m_ref[hp : hp + 1, :] = top
        l_ref[hp : hp + 1, :] = total
        acc_ref[hp] = acc

    if last:
        own_ref, other_ref = refs[3:]

        @pl.when(pl.program_id(0) == pl.num_programs(0) - 1)
        def _():
            for out, lanes in ((own_ref, own_lanes), (other_ref, other_lanes)):
                out[pairs * PAIR :, :] = jnp.zeros((8, out.shape[1]), F32)
                for hp in range(pairs):
                    out[hp * PAIR : (hp + 1) * PAIR, :] = lanes(acc_ref[hp])
                    out[pairs * PAIR + hp : pairs * PAIR + hp + 1, :] = lanes(m_ref[hp : hp + 1, :])
                    out[pairs * PAIR + 4 + hp : pairs * PAIR + 5 + hp, :] = lanes(l_ref[hp : hp + 1, :])


def kv_specs(kv, a):
    rows, C = kv[0].shape[2:]
    specs = [pl.BlockSpec((1, 2, rows, C), lambda i, gid: (i, 0, 0, 0)) for _ in range(2)]
    for j in range(2):
        specs.append(
            pl.BlockSpec((1,) + a.shape[1:], functools.partial(lambda j, i, gid: (gid[2 * i + j], 0, 0, 0), j))
        )
    return specs


def fixed(shape):
    return pl.BlockSpec(shape, lambda i, gid: (0,) * len(shape))


def cross_fwd(gid, q, kv, a, state, last):
    R, C = q[0].shape
    pairs = C // PAIR
    hi, _, rows, _ = kv[0].shape
    shapes = [(8, 4 * R), (8, 4 * R), (pairs, PAIR, 4 * R)]
    first = state is None
    state = () if first else tuple(state)
    if last:
        shapes += [(C + 8, 2 * R)] * 2
    return pl.pallas_call(
        functools.partial(cross_fwd_body, first, last),
        name="cross_fwd",
        grid_spec=pltpu.PrefetchScalarGridSpec(
            num_scalar_prefetch=1,
            grid=(hi,),
            in_specs=[fixed(q[0].shape)] * 2 + kv_specs(kv, a) + [fixed(s.shape) for s in state],
            out_specs=[fixed(s) for s in shapes],
        ),
        out_shape=[jax.ShapeDtypeStruct(s, F32) for s in shapes],
        compiler_params=pltpu.CompilerParams(vmem_limit_bytes=VMEM_LIMIT),
        cost_estimate=pl.CostEstimate(flops=1, bytes_accessed=1, transcendentals=0),
    )(gid, *q, *kv, *([pltpu.with_memory_space_constraint(a, pltpu.HBM)] * 2), *state)


def merged(own_ref, got_ref, hp, C):
    sl = slice(hp * PAIR, (hp + 1) * PAIR)
    m, l = slice(C + hp, C + hp + 1), slice(C + 4 + hp, C + 5 + hp)
    m1, m2 = own_ref[m, :], got_ref[m, :]
    top = jnp.maximum(m1, m2)
    f1, f2 = jnp.exp(m1 - top), jnp.exp(m2 - top)
    total = own_ref[l, :] * f1 + got_ref[l, :] * f2
    return top + jnp.log(total), unstacked((own_ref[sl, :] * f1 + got_ref[sl, :] * f2) * (1.0 / total))


def cross_mix_body(own_ref, got_ref, wm, log_ref, of_ref, o_ref, part_ref):
    C = wm.shape[0]
    log_ref[...] = jnp.zeros(log_ref.shape, F32)
    for hp in range(C // PAIR):
        sl = slice(hp * PAIR, (hp + 1) * PAIR)
        log_ref[hp : hp + 1, :], o = merged(own_ref, got_ref, hp, C)
        of_ref[:, sl] = o
        o_ref[:, sl] = o.astype(BF)
    part_ref[...] = nn(o_ref[...], wm[...]).astype(BF)


def cross_mix_fwd(own, got, wm):
    R2 = own.shape[1]
    C, D = wm.shape
    R = R2 // 2
    return whole(
        cross_mix_body,
        "cross_mix",
        [((8, R2), F32), ((R, C), F32), ((R, C), BF), ((R, D), BF)],
        own, got, wm,
    )


def cross_merge_body(own_ref, got_ref, log_ref, of_ref):
    C = of_ref.shape[1]
    log_ref[...] = jnp.zeros(log_ref.shape, F32)
    for hp in range(C // PAIR):
        log_ref[hp : hp + 1, :], of_ref[:, hp * PAIR : (hp + 1) * PAIR] = merged(own_ref, got_ref, hp, C)


def cross_merge(own, got):
    rows, R2 = own.shape
    return whole(cross_merge_body, "cross_merge", [((8, R2), F32), ((R2 // 2, rows - 8), F32)], own, got)


def ffn_back_rest(dlow_ref, gp_ref, wu, wd, dh_ref, part_ref):
    low = dlow_ref[...]
    for c in range(0, wu.shape[1], 256):
        sl = slice(c, c + 256)
        dh_ref[:, sl] = (nt(low, wd[sl, :]) * gp_ref[:, sl].astype(F32)).astype(BF)
    part_ref[...] = nt(dh_ref[...], wu[...]).astype(BF)


def last_body(g, u_ref, own, oth, cot, par, gp_ref, wu, wd, out_ref, dv_ref, dlow_ref, dh_ref, gg_ref, part_ref):
    R, D = u_ref.shape
    gain, shift = row_of(par, g), row_of(par, g + 1)
    gg_ref[...] = jnp.zeros(gg_ref.shape, F32)
    for r in range(0, R, ROWS):
        s = slice(r, r + ROWS)
        v = u_ref[s, :] + (own[s, :].astype(F32) + oth[s, :].astype(F32))
        xhat, _ = norm_parts(v)
        out_ref[s, :] = xhat * gain + shift
        dv, dg, db = norm_back(v, gain, cot[s, :].astype(F32))
        dv_ref[s, :] = dv
        dlow_ref[s, :] = dv.astype(BF)
        gg_ref[0:1, :] += dg
        gg_ref[1:2, :] += db
    flush(gg_ref, out_ref)
    ffn_back_rest(dlow_ref, gp_ref, wu, wd, dh_ref, part_ref)


def last_fwd_back(g, u, own, oth, cot, par, gp, wu, wd):
    R, D = u.shape
    FF = wu.shape[1]
    return whole(
        functools.partial(last_body, g),
        "last_fwd_back",
        [((R, D), F32, HBM), ((R, D), F32), ((R, D), BF), ((R, FF), BF), ((8, D), F32, HBM), ((R, D), BF)],
        u, own, oth, cot, par, gp, wu, wd,
    )


def ffn_back_body(g, own, oth, v_ref, par, gp_ref, wu, wd, dv_ref, dlow_ref, dh_ref, gg_ref, part_ref):
    R, D = v_ref.shape
    gain = row_of(par, g)
    gg_ref[...] = jnp.zeros(gg_ref.shape, F32)
    for r in range(0, R, ROWS):
        s = slice(r, r + ROWS)
        dy = own[s, :].astype(F32) + oth[s, :].astype(F32)
        dv, dg, db = norm_back(v_ref[s, :], gain, dy)
        dv_ref[s, :] = dv
        dlow_ref[s, :] = dv.astype(BF)
        gg_ref[0:1, :] += dg
        gg_ref[1:2, :] += db
    flush(gg_ref)
    ffn_back_rest(dlow_ref, gp_ref, wu, wd, dh_ref, part_ref)


def ffn_back(g, own, oth, v, par, gp, wu, wd, after):
    R, D = v.shape
    FF = wu.shape[1]
    return whole(
        functools.partial(ffn_back_body, g),
        "ffn_back",
        [((R, D), F32), ((R, D), BF), ((R, FF), BF), ((8, D), F32, HBM), ((R, D), BF)],
        own, oth, v, par, gp, wu, wd,
        after=after,
    )


def branch_back(g, dres, own, oth, v_ref, par, dv_ref, dlow_ref, gg_ref):
    R, D = v_ref.shape
    gain = row_of(par, g)
    gg_ref[...] = jnp.zeros(gg_ref.shape, F32)
    for r in range(0, R, ROWS):
        s = slice(r, r + ROWS)
        dy = dres[s, :] + (own[s, :].astype(F32) + oth[s, :].astype(F32))
        dv, dg, db = norm_back(v_ref[s, :], gain, dy)
        dv_ref[s, :] = dv
        dlow_ref[s, :D] = dv.astype(BF)
        gg_ref[0:1, :] += dg
        gg_ref[1:2, :] += db


def cross_mix_back_body(g, dres, own, oth, v_ref, par, wm, dv_ref, pack_ref, gg_ref):
    branch_back(g, dres, own, oth, v_ref, par, dv_ref, pack_ref, gg_ref)
    flush(dv_ref, gg_ref)
    D = v_ref.shape[1]
    pack_ref[:, D:] = nt(pack_ref[:, :D], wm[...]).astype(BF)


def cross_mix_back(g, dres, own, oth, v, par, wm):
    R, D = v.shape
    C = wm.shape[0]
    return whole(
        functools.partial(cross_mix_back_body, g),
        "cross_mix_back",
        [((R, D), F32, HBM), ((R, D + C), BF), ((8, D), F32, HBM)],
        dres, own, oth, v, par, wm,
    )


def cross_back_body(first, last, gid_ref, q_ref, q_other, do_pack, do_pack_other, *refs):
    C = q_ref.shape[1]
    skip = do_pack.shape[1] - C
    do_ref, do_other = do_pack.at[:, skip:], do_pack_other.at[:, skip:]
    kv, a_refs, refs = refs[:2], refs[2:4], refs[4:]
    if first:
        of_ref, of_other, log_own, log_other = refs[:4]
        dq_ref, stat_ref, keep_ref, send_ref = refs[4:8]
    else:
        dq_in, stat_in = refs[:2]
        dq_ref, stat_ref, keep_ref, send_ref = refs[2:6]
    pairs = dq_ref.shape[0]

    @pl.when(pl.program_id(0) == 0)
    def _():
        if not first:
            dq_ref[...] = dq_in[...]
            stat_ref[...] = stat_in[...]
            return
        dq_ref[...] = jnp.zeros(dq_ref.shape, F32)
        stat_ref[...] = jnp.zeros(stat_ref.shape, F32)
        stat_ref[0:8, :] = all_lanes(log_own[...], log_other[...])
        for hp in range(pairs):
            sl = slice(hp * PAIR, (hp + 1) * PAIR)
            sums = []
            for d, o in ((do_ref, of_ref), (do_other, of_other)):
                prod = (d[:, sl].astype(F32) * o[:, sl]).T
                sums.append([jnp.sum(prod[:HD], 0, keepdims=True), jnp.sum(prod[HD:], 0, keepdims=True)])
            stat_ref[8 + hp : 9 + hp, :] = jnp.concatenate([sums[0][0], sums[1][0], sums[0][1], sums[1][1]], 1)

    for hp in range(pairs):
        sl = slice(hp * PAIR, (hp + 1) * PAIR)
        qq = of_both(q_ref[:, sl], q_other[:, sl])
        dd = of_both(do_ref[:, sl], do_other[:, sl])
        log_total = stat_ref[hp : hp + 1, :]
        delta = stat_ref[8 + hp : 9 + hp, :]
        dq = dq_ref[hp]
        for j, out_ref in enumerate((keep_ref, send_ref)):
            a = a_refs[j][0, hp]
            half = a.shape[0]
            k2 = kv[j][0, 0, :, sl]
            p = jnp.exp(chosen_scores(k2, qq, a) - log_total)
            daT = nt(kv[j][0, 1, :, sl], dd)
            ds = p * (jnp.where(a > 0.5, daT[half:], daT[:half]) - delta)
            dsT = spread(ds, a)
            out_ref[0, 0, :, sl] = nn(dsT, qq).astype(BF)
            out_ref[0, 1, :, sl] = nn(spread(p, a), dd).astype(BF)
            dq = dq + tn(k2, dsT)
        dq_ref[hp] = dq

    if last:
        own_ref, other_ref = refs[-2:]

        @pl.when(pl.program_id(0) == pl.num_programs(0) - 1)
        def _():
            for hp in range(pairs):
                own_ref[hp] = own_lanes(dq_ref[hp])
                other_ref[hp] = other_lanes(dq_ref[hp]).astype(BF)


def cross_back(gid, q, do, kv, a, extra, first, last, after=()):
    R, C = q[0].shape
    pairs = C // PAIR
    hi, _, rows, _ = kv[0].shape
    grad_spec = pl.BlockSpec((1, 2, rows, C), lambda i, gid: (i, 0, 0, 0))
    shapes = [(pairs, PAIR, 4 * R), (16, 4 * R)]
    out_specs = [fixed(s) for s in shapes] + [grad_spec] * 2
    out_shape = [jax.ShapeDtypeStruct(s, F32) for s in shapes] + [jax.ShapeDtypeStruct(kv[0].shape, BF)] * 2
    if last:
        out_specs += [fixed((pairs, PAIR, 2 * R))] * 2
        out_shape += [jax.ShapeDtypeStruct((pairs, PAIR, 2 * R), d) for d in (F32, BF)]
    return pl.pallas_call(
        behind(functools.partial(cross_back_body, first, last), 9 + len(extra), len(after)),
        name="cross_back",
        grid_spec=pltpu.PrefetchScalarGridSpec(
            num_scalar_prefetch=1,
            grid=(hi,),
            in_specs=[fixed(q[0].shape)] * 2
            + [fixed(do[0].shape)] * 2
            + kv_specs(kv, a)
            + [fixed(e.shape) for e in extra]
            + [pl.BlockSpec(memory_space=pl.ANY)] * len(after),
            out_specs=out_specs,
        ),
        out_shape=out_shape,
        compiler_params=pltpu.CompilerParams(vmem_limit_bytes=VMEM_LIMIT),
        cost_estimate=pl.CostEstimate(flops=1, bytes_accessed=1, transcendentals=0),
    )(gid, *q, *do, *kv, *([pltpu.with_memory_space_constraint(a, pltpu.HBM)] * 2), *extra, *after)


def cross_q_back_body(dq_own, dq_got, wq, dq_ref, part_ref):
    for hp in range(dq_own.shape[0]):
        sl = slice(hp * PAIR, (hp + 1) * PAIR)
        dq_ref[:, sl] = (unstacked(dq_own[hp] + dq_got[hp].astype(F32)) * SCALE).astype(BF)
    flush(dq_ref)
    part_ref[...] = nt(dq_ref[...], wq[...]).astype(BF)


def cross_q_back(dq, got, wq, after):
    D, C = wq.shape
    R = dq.shape[2] // 2
    return whole(cross_q_back_body, "cross_q_back", [((R, C), BF), ((R, D), BF)], dq, got, wq, after=after)


def store_back_body(spread_at, *refs):
    n = len(refs) - 4
    wk, wv, dkv_ref, part_ref = refs[n:]
    R, C = dkv_ref.shape[0], dkv_ref.shape[1] // 2
    for i in range(2):
        parts = [t[0, i] for t in refs[:spread_at]]
        if spread_at < n:
            parts.append(refs[spread_at + i][0, 0])
        total = functools.reduce(lambda x, y: x + y, [t.astype(F32) for t in parts])
        dkv_ref[:, i * C : (i + 1) * C] = total.astype(BF)
    part = nt(dkv_ref[:, :C], wk[...]) + nt(dkv_ref[:, C:], wv[...])
    part_ref[...] = tn(order_matrix(R), part.astype(BF)).astype(BF)


def store_back(terms, wk, wv, after):
    D, C = wk.shape
    R = terms[0].shape[2]
    full = [t for t in terms if not isinstance(t, list)]
    halves = [h for t in terms if isinstance(t, list) for h in t]
    return whole(
        functools.partial(store_back_body, len(full)),
        "store_back",
        [((R, 2 * C), BF), ((R, D), BF)],
        *full, *halves, wk, wv,
        after=after,
    )


def attend_back_body(causal, g, n_more, *refs):
    if causal:
        len_ref, refs = refs[0], refs[1:]
    (dres, own, oth, v1_ref, par, q_ref, k_ref, v_ref, wq, wk, wv, wm) = refs[:12]
    R, D = v1_ref.shape
    dv_ref, pack_ref, gg_ref, part_ref = refs[12 + n_more : 16 + n_more]
    branch_back(g, dres, own, oth, v1_ref, par, dv_ref, pack_ref, gg_ref)
    flush(dv_ref, gg_ref)
    if n_more:
        gains_ref = refs[-1]
        rows = [gg_ref[0:2, :]] + [other[0:2, :] for other in refs[12 : 12 + n_more]]
        rows.append(jnp.zeros((gains_ref.shape[0] - 2 - 2 * n_more, D), F32))
        gains_ref[...] = jnp.concatenate(rows, 0).astype(BF)
        flush(gains_ref)
    C = wq.shape[1]
    do = nt(pack_ref[:, :D], wm[...]).astype(BF)
    allowed = causal_mask(R, len_ref[0]) if causal else None
    for c in range(0, C, PAIR):
        sl = slice(c, c + PAIR)
        k2 = k_ref[:, sl]
        qq = stacked(q_ref[:, sl])
        dd = stacked(do[:, sl])
        w = local_weights(k2, qq, allowed)
        daT = nt(v_ref[:, sl], dd)
        ds = (w * (daT - jnp.sum(w * daT, 0, keepdims=True))).astype(BF)
        at = D + c
        pack_ref[:, at : at + PAIR] = (unstacked(tn(k2, ds)) * SCALE).astype(BF)
        pack_ref[:, at + C : at + C + PAIR] = nn(ds, qq).astype(BF)
        pack_ref[:, at + 2 * C : at + 2 * C + PAIR] = nn(w.astype(BF), dd).astype(BF)
    flush(pack_ref)
    part = nt(pack_ref[:, D : D + C], wq[...]) + nt(pack_ref[:, D + C : D + 2 * C], wk[...])
    part_ref[...] = (part + nt(pack_ref[:, D + 2 * C :], wv[...])).astype(BF)


def attend_back(g, dres, own, oth, v1, par, kept, weights, length=None, more=(), after=()):
    R, D = v1.shape
    C = kept[0].shape[1]
    args = (dres, own, oth, v1, par, *kept, *weights, *more)
    causal = length is not None
    if causal:
        args = (length,) + args
    return whole(
        functools.partial(attend_back_body, causal, g, len(more)),
        "attend_back",
        [((R, D), F32, HBM), ((R, D + 3 * C), BF), ((8, D), F32, HBM), ((R, D), BF)]
        + [((16, D), BF)] * bool(more),
        *args,
        smem=int(causal),
        after=after,
    )


def weight_body(plan, chunks, sources, n_idx, *refs):
    idx_refs, ins, outs = refs[:n_idx], refs[n_idx : -2 * len(chunks)], refs[-2 * len(chunks) :]
    half = outs[0].shape[0]
    chunk, at, takes = 0, 0, {}
    for part, a_at, off, D, grads in plan:
        if part not in takes:
            spot = lax.broadcasted_iota(jnp.int32, (2 * half, D), 1) == idx_refs[part][...]
            takes[part] = spot.astype(F32).astype(BF)
        parts = [nt(takes[part], ins[a_at + i][:, off : off + D]) for i in range(sources)]
        aT = jnp.concatenate(parts, 1).astype(BF)
        for d_at, d_off, width in grads:
            step = 384 if width % 384 == 0 else 128
            for c in range(d_off, d_off + width, step):
                dy = jnp.concatenate([ins[d_at + i][:, c : c + step] for i in range(sources)], 0)
                got = nn(aT, dy)
                outs[2 * chunk][:, at : at + step] = got[:half].astype(BF)
                outs[2 * chunk + 1][:, at : at + step] = got[half:].astype(BF)
                at += step
                if at == chunks[chunk]:
                    chunk, at = chunk + 1, 0


def weight_grads(idxs, D, term_lists, chunks, after=()):
    ins, plan = [], []
    for part, terms in enumerate(term_lists):
        for a, off, grads in terms:
            at = len(ins)
            ins += list(a)
            ds = []
            for d, d_off, w in grads:
                ds.append((len(ins), d_off, w))
                ins += list(d)
            plan.append((part, at, off, D, ds))
    half = idxs[0].shape[0] // 2
    return whole(
        functools.partial(weight_body, plan, chunks, len(term_lists[0][0][0]), len(idxs)),
        "weight_grads",
        [((half, w), BF) for w in chunks for _ in range(2)],
        *idxs,
        *ins,
        after=after,
    )


def swap(x, bit, n):
    return lax.ppermute(x, "blk", [(i, i ^ bit) for i in range(n)])


def tied(x, *before):
    return lax.optimization_barrier((x, *before))[0]


def other_tp(x):
    return lax.ppermute(x, "tp", [(0, 1), (1, 0)])


class Halving:
    def __init__(self, keep, send, n, bits):
        self.keep, self.send, self.n, self.bits = keep, send, n, bits
        self.got = swap(send, bits[0], n)

    def hold(self, *before):
        self.send = tied(self.send, *before)
        self.got = swap(self.send, self.bits[0], self.n)

    def step(self, *before):
        got = tied(self.got, *before) if before else self.got
        total = self.keep.astype(F32) + got.astype(F32)
        self.bits = self.bits[1:]
        if not self.bits:
            return total
        half = total.shape[0] // 2
        self.keep, self.send = total[:half], total[half:].astype(BF)
        self.got = swap(self.send, self.bits[0], self.n)
        return self.send

    def end(self, *before):
        while len(self.bits) > 1:
            self.step(*before)
        return self.step(*before)


def on_device(
    n,
    encoder_in,
    decoder_in,
    lengths,
    retrieved,
    band_start,
    cotangent,
    enc_query,
    enc_key,
    enc_value,
    enc_mix,
    attn_gain,
    attn_shift,
    enc_up,
    enc_down,
    ffn_gain,
    ffn_shift,
    self_query,
    self_key,
    self_value,
    self_mix,
    self_gain,
    self_shift,
    cross_query,
    cross_key,
    cross_value,
    cross_mix,
    cross_gain,
    cross_shift,
    dec_up,
    dec_down,
    last_gain,
    last_shift,
):
    group_rows, D = encoder_in.shape
    C = cross_query.shape[1]
    FF = enc_up.shape[1]
    hi = n // 16
    me = lax.axis_index("blk")
    core = lambda x: swap(x, 1, n)
    par = jnp.stack(
        [attn_gain, attn_shift, ffn_gain, ffn_shift, self_gain, self_shift, cross_gain, cross_shift, last_gain, last_shift]
    )

    share = D // n
    bits = [1 << i for i in range(n.bit_length() - 1)]

    def rows_by(order):
        t = jnp.arange(share << len(order), dtype=jnp.int32)
        block = t // share
        rel = sum(((block >> (len(order) - 1 - i)) & 1) * bit for i, bit in enumerate(order))
        return ((me ^ rel) * share + t % share).reshape(-1, 1)

    def gradients(order, terms, after=()):
        width = sum(grad[2] for _, _, grads in terms for grad in grads)
        return Halving(*weight_grads([rows_by(order)], D, [terms], [width], after), n, order)

    def joint(parts, after=()):
        chunks = [w for _, _, widths in parts for w in widths]
        made = weight_grads([rows_by(order) for order, _, _ in parts], D, [terms for _, terms, _ in parts], chunks, after)
        gots = [swap(send, 1, n) for send in made[1::2]]

        def finish(*before):
            tied_gots = lax.optimization_barrier((*gots, *before))[: len(gots)]
            totals = [k.astype(F32) + g.astype(F32) for k, g in zip(made[0::2], tied_gots)]
            half, sums = totals[0].shape[0] // 2, []
            for order, _, widths in parts:
                mine, totals = totals[: len(widths)], totals[len(widths) :]
                keep = jnp.concatenate([t[:half] for t in mine], 1)
                send = jnp.concatenate([t[half:].astype(BF) for t in mine], 1)
                sums.append(Halving(keep, send, n, order[1:]))
            return sums

        return made[0], finish

    both = lambda x: (x, core(x))
    summed = lambda *arrays: functools.reduce(lambda x, y: x + y, [t.astype(F32) for t in arrays]).astype(BF)

    *enc_kept, enc_o, enc_part = attend_fwd(encoder_in, enc_query, enc_key, enc_value, enc_mix, fetch=True)
    enc_other = other_tp(enc_part)
    pick = pick_rows(retrieved, (enc_part,))
    band = tied(band_start.T, *pick)
    pick_other, band_other = [core(p) for p in pick], core(band)
    *self_kept, self_o, self_part = attend_fwd(
        decoder_in, self_query, self_key, self_value, self_mix, lengths, pick
    )
    enc_other = tied(enc_other, self_part)
    v1, u1, low1, act1, gp1, part1 = ffn_fwd(0, encoder_in, enc_part, enc_other, par, enc_up, enc_down, True, True)
    other1 = other_tp(part1)
    chosen = picks(tied((me & 1).reshape(1), part1), pick, pick_other, band, band_other, n // 2, group_rows // 2)
    other1 = tied(other1, chosen)
    v2, encoded, enc_low, store = store_fwd(2, u1, part1, other1, par, cross_key, cross_value)

    store = store[None]
    for b in range(4, n.bit_length() - 1):
        store = jnp.concatenate([store, swap(store, 1 << b, n)], 0)

    def gid_of(pair):
        return (me ^ jnp.array([16 * h + r for h in range(hi) for r in pair], jnp.int32)) >> 1

    near = swap(store, 4, n)
    y_own = swap(store, 2, n)
    far = swap(store, 8, n)
    self_part = tied(self_part, store)
    self_other = other_tp(self_part)
    vd, ud, lowd, qc = cross_q(4, decoder_in, self_part, self_other, par, cross_query)
    qcs = both(qc)
    far = tied(far, near, y_own, qcs[1])
    apart = swap(far, 4, n)
    y_far = swap(far, 2, n)
    state = cross_fwd(gid_of((0, 2)), qcs, (tied(store, far), y_own), chosen, None, False)
    state = cross_fwd(gid_of((4, 8)), qcs, (near, far), chosen, state, False)
    apart = tied(apart, *state)
    y_near = swap(tied(y_own, apart), 4, n)
    y_apart = swap(apart, 2, n)
    state = cross_fwd(gid_of((12, 10)), qcs, (apart, y_far), chosen, state, False)
    state_own, state_other = cross_fwd(gid_of((6, 14)), qcs, (y_near, y_apart), chosen, state, True)[3:]
    pieces = [(store, y_own), (near, y_near), (far, y_far), (apart, y_apart)]
    log_own, of_own, oc, partc = cross_mix_fwd(state_own, core(state_other), cross_mix)
    otherc = other_tp(partc)
    log_other, of_other = cross_merge(state_other, core(tied(state_own, partc)))
    otherc = tied(otherc, of_other)

    vc, uc, lowc, actc, gpc, part3 = ffn_fwd(6, ud, partc, otherc, par, dec_up, dec_down, False, False)
    other3 = other_tp(part3)
    actc_y = swap(actc, 2, n)
    decoded, dlast, dlowc, dhc, gg_last, part4 = last_fwd_back(8, uc, part3, other3, cotangent, par, gpc, dec_up, dec_down)
    dlowc_y = swap(dlowc, 2, n)
    other4 = tied(other_tp(part4), actc_y, dlowc_y)
    dcross, dpacko, gg_cross = cross_mix_back(6, dlast, part4, other4, vc, par, cross_mix)

    dpackos = both(dpacko)
    back = lambda k, extra, after: cross_back(
        gid_of((4 * k, 4 * k + 2)), qcs, dpackos, pieces[k], chosen, extra, k == 3, k == 0, after
    )
    no_y = bits[:1] + bits[2:]
    down = gradients(no_y, [((dlowc, dlowc_y), 0, [((actc, actc_y), 0, FF)])], (dpacko,))
    *extra, keep3, send3 = back(3, (of_own, of_other, log_own, log_other), (down.keep,))
    got3 = swap(send3, 2, n)
    down_z = down.step(send3)
    *extra, keep1, send1 = back(1, extra, (down_z,))
    got1 = swap(send1, 2, n)
    one = lambda x: (x,)
    up = gradients(bits, [(one(lowc), 0, [(one(dhc), 0, FF)])], (send1,))
    sum3 = summed(keep3, tied(got3, up.keep))
    apart = swap(sum3, 4, n)
    down_z = down.step(sum3)
    *extra, keep2, send2 = back(2, extra, (sum3, down_z))
    got2 = swap(send2, 2, n)
    sum1 = summed(keep1, tied(got1, send2))
    near = swap(sum1, 4, n)
    down_sum = down.end(sum1)
    _, _, keep0, send0, dq_own, dq_other = back(0, extra, (sum1, down_sum))
    got0 = swap(send0, 2, n)
    up_y = up.step(send0)
    sum2 = summed(keep2, tied(got2, send0, up_y), apart)
    far = swap(sum2, 8, n)
    terms = [keep0, got0, near, far]
    bit = n // 2
    while terms[0].shape[0] > 1:
        half = terms[0].shape[0] // 2
        total = functools.reduce(lambda x, y: x + y, [t.astype(F32) for t in terms])
        terms = [total[:half].astype(BF), swap(total[half:].astype(BF), bit, n)]
        bit //= 2

    dqc, partq = cross_q_back(dq_own, core(tied(dq_other, sum2)), cross_query, ())
    otherq = other_tp(partq)
    v2_near, gp1_near, *loaded = load((v2, gp1, enc_up, enc_down), (partq,))
    dkv, part5 = store_back(terms, cross_key, cross_value, (gp1_near,))
    other5 = other_tp(part5)
    up.hold(got0)
    dself, dpackd, gg_self, part6 = attend_back(
        4, dcross, partq, tied(otherq, got0, near, far), vd, par, self_kept, (self_query, self_key, self_value, self_mix), lengths,
    )
    own_keep, own_sums = joint(
        [
            (
                bits,
                [
                    (one(lowd), 0, [(one(dqc), 0, C)]),
                    (one(dpacko), 0, [(one(oc), 0, C)]),
                    (one(dpackd), 0, [(one(self_o), 0, C)]),
                ],
                [C] * 3,
            ),
            (bits, [(one(decoder_in), 0, [(one(dpackd), D, 3 * C)])], [C] * 3),
        ]
    )
    up_z = up.step(other5)
    mixes, own = own_sums(up_z)
    dffn, dlow1, dh1, gg_ffn, part7 = ffn_back(
        2, part5, tied(other5, mixes.send, own.send), v2_near, par, gp1_near, *loaded, ()
    )
    other7 = other_tp(part7)
    z_first = bits[:1] + bits[2:] + bits[1:2]
    ffn_keep, ffn_sums = joint(
        [
            (z_first, [(one(dlow1), 0, [(one(act1), 0, FF)])], [FF // 2] * 2),
            (
                bits,
                [
                    (one(enc_low), 0, [(one(dkv), 0, 2 * C)]),
                    (one(low1), 0, [(one(dh1), 0, FF)]),
                ],
                [2 * C] + [FF // 2] * 2,
            ),
        ],
    )
    up_z = up.step(ffn_keep)
    mixes_z = mixes.step(up_z)
    down1, up1 = ffn_sums(mixes_z)
    own_z = own.step(up1.send)
    dattn, dpacke, _, part8, gains = attend_back(
        0, dffn, part7, tied(other7, own_z, down1.send), v1, par, enc_kept, (enc_query, enc_key, enc_value, enc_mix), None,
        (gg_ffn, gg_self, gg_cross, gg_last),
    )
    up_sum = up.end(part8)
    mixes_z = mixes.step(up_sum)
    own_z = own.step(mixes_z)
    lanes = jnp.eye(16, 128, dtype=BF)
    last_keep, last_sums = joint(
        [
            (
                bits,
                [
                    (one(encoder_in), 0, [(one(dpacke), D, 3 * C)]),
                    (one(dpacke), 0, [(one(enc_o), 0, C)]),
                    (one(gains), 0, [(one(lanes), 0, 128)]),
                ],
                [2 * C, 2 * C + 128],
            )
        ],
        (own_z,),
    )
    up1_z = up1.step(last_keep)
    (last,) = last_sums(up1_z)
    other6, other8 = other_tp(tied(part6, last.send)), other_tp(tied(part8, last.send))
    down1_z = down1.step(last.send)
    mixes_sum = mixes.end(down1_z)
    own_sum = own.end(mixes_sum)
    up1_z = up1.step(own_sum)
    down1_z = down1.step(up1_z)
    last_z = last.step(down1_z)
    up1_sum = up1.end(last_z)
    down1_sum = down1.end(up1_sum)
    last_z = last.step(down1_sum, other6, other8)
    last_sum = last.end()
    grad_encoder_in = dattn + (part8.astype(F32) + other8.astype(F32))
    grad_decoder_in = dself + (part6.astype(F32) + other6.astype(F32))

    cut = lambda total, at, width: total[:, at : at + width]
    gain_of = [last_sum[:, 4 * C + i] for i in range(10)]
    return (
        encoded,
        decoded,
        grad_encoder_in,
        grad_decoder_in,
        cut(last_sum, 0, C),
        cut(last_sum, C, C),
        cut(last_sum, 2 * C, C),
        cut(last_sum, 3 * C, C).T,
        gain_of[0],
        gain_of[1],
        cut(up1_sum, 2 * C, FF),
        down1_sum.T,
        gain_of[2],
        gain_of[3],
        cut(own_sum, 0, C),
        cut(own_sum, C, C),
        cut(own_sum, 2 * C, C),
        cut(mixes_sum, 2 * C, C).T,
        gain_of[4],
        gain_of[5],
        cut(mixes_sum, 0, C),
        cut(up1_sum, 0, C),
        cut(up1_sum, C, C),
        cut(mixes_sum, C, C).T,
        gain_of[6],
        gain_of[7],
        up_sum,
        down_sum.T,
        gain_of[8],
        gain_of[9],
    )


def solution(mesh):
    rows, both, cols, down = P("blk", None), P("blk", "tp"), P(None, "tp"), P("tp", None)
    attn = (cols, cols, cols, down, P(), P())
    ffn = (cols, down, P(), P())
    in_specs = (rows, rows, P("blk"), P("blk", "tp", None), both, rows) + attn + ffn + attn + attn + ffn
    mixed = P("tp", "blk")
    grad_attn = (both, both, both, mixed, P("blk"), P("blk"))
    grad_ffn = (both, mixed, P("blk"), P("blk"))
    out_specs = (rows,) * 4 + grad_attn + grad_ffn + grad_attn + grad_attn + grad_ffn
    return jax.shard_map(
        functools.partial(on_device, mesh.shape["blk"]),
        mesh=mesh,
        in_specs=in_specs,
        out_specs=out_specs,
        check_vma=False,
    )
```

```python
import functools

import jax
import jax.numpy as jnp
from jax import lax
from jax.experimental import pallas as pl
from jax.experimental.pallas import tpu as pltpu
from jax.sharding import PartitionSpec as P

HD = 64
PAIR = 2 * HD
NEG_FILL = -1e30
EPS_NORM = 1e-05
SCALE = 0.125
BF = jnp.bfloat16
F32 = jnp.float32
VMEM_LIMIT = 24 * 2**20
HBM = True
ROWS = 64


def nn(a, b):
    return lax.dot_general(a, b, (((1,), (0,)), ((), ())), preferred_element_type=F32)


def nt(a, b):
    return lax.dot_general(a, b, (((1,), (1,)), ((), ())), preferred_element_type=F32)


def tn(a, b):
    return lax.dot_general(a, b, (((0,), (0,)), ((), ())), preferred_element_type=F32)


def behind(body, n_in, n_after):
    if not n_after:
        return body
    return lambda *refs: body(*refs[:n_in], *refs[n_in + n_after :])


class Fetched:
    def __init__(self, far, near, sem):
        self.near, self.shape, self.pending = near, near.shape, pltpu.make_async_copy(far, near, sem)
        self.pending.start()

    def ready(self):
        if self.pending is not None:
            self.pending.wait()
            self.pending = None

    def __getitem__(self, at):
        self.ready()
        return self.near[at]


class Kept:
    def __init__(self, far, near, sem):
        self.far, self.near, self.shape, self.sem, self.copies, self.at = far, near, near.shape, sem, [], 0

    def flush(self, upto=None):
        if upto is None and self.at == 0:
            copy = pltpu.make_async_copy(self.near, self.far, self.sem.at[0])
        else:
            upto = self.shape[-1] if upto is None else upto
            if upto == self.at:
                return
            sl = (slice(None), slice(self.at, upto))
            copy = pltpu.make_async_copy(self.near.at[sl], self.far.at[sl], self.sem.at[len(self.copies)])
        self.at = self.shape[-1] if upto is None else upto
        copy.start()
        self.copies.append(copy)

    def wait(self):
        if self.at < self.shape[-1]:
            self.flush()
        for copy in self.copies:
            copy.wait()

    def __getitem__(self, at):
        return self.near[at]

    def __setitem__(self, at, value):
        self.near[at] = value


def flush(*refs, upto=None):
    for ref in refs:
        if isinstance(ref, Kept):
            ref.flush(upto)


class Far:
    def __init__(self, array):
        self.array = array


def whole(body, name, outs, *args, smem=0, after=()):
    far_in = [i for i, a in enumerate(args) if isinstance(a, Far)]
    far_out = [i for i, o in enumerate(outs) if len(o) > 2]
    args = [pltpu.with_memory_space_constraint(a.array, pltpu.HBM) if isinstance(a, Far) else a for a in args]
    n_in, n_out, n_after = len(args), len(outs), len(after)

    def run(*refs):
        ins = list(refs[:n_in])
        results = list(refs[n_in + n_after : n_in + n_after + n_out])
        scratch = refs[n_in + n_after + n_out :]
        for k, i in enumerate(far_in):
            ins[i] = Fetched(ins[i], scratch[k], scratch[-1].at[k, 0])
        for k, i in enumerate(far_out):
            results[i] = Kept(results[i], scratch[len(far_in) + k], scratch[-1].at[len(far_in) + k])
        body(*ins, *results)
        for i in far_in:
            ins[i].ready()
        for i in far_out:
            results[i].wait()

    moves = len(far_in) + len(far_out)
    scratch = [pltpu.VMEM(args[i].shape, args[i].dtype) for i in far_in]
    scratch += [pltpu.VMEM(outs[i][0], outs[i][1]) for i in far_out]
    if moves:
        scratch.append(pltpu.SemaphoreType.DMA((moves, 8)))
    in_specs = [pl.BlockSpec(memory_space=pltpu.SMEM if i < smem else pltpu.VMEM) for i in range(n_in)]
    out_specs = [pl.BlockSpec(memory_space=pltpu.VMEM) for _ in outs]
    for i in far_in:
        in_specs[i] = pl.BlockSpec(memory_space=pltpu.HBM)
    for i in far_out:
        out_specs[i] = pl.BlockSpec(memory_space=pltpu.HBM)
    return pl.pallas_call(
        run,
        name=name,
        out_shape=[pltpu.HBM(o[0], o[1]) if len(o) > 2 else jax.ShapeDtypeStruct(o[0], o[1]) for o in outs],
        in_specs=in_specs + [pl.BlockSpec(memory_space=pl.ANY)] * n_after,
        out_specs=out_specs,
        scratch_shapes=scratch,
        compiler_params=pltpu.CompilerParams(vmem_limit_bytes=VMEM_LIMIT),
        cost_estimate=pl.CostEstimate(flops=1, bytes_accessed=1, transcendentals=0),
    )(*args, *after)


def load_body(n, *refs):
    sems = refs[-1]
    copies = [pltpu.make_async_copy(refs[i], refs[n + i], sems.at[i]) for i in range(n)]
    for copy in copies:
        copy.start()
    for copy in copies:
        copy.wait()


def load(arrays, after):
    n, n_after = len(arrays), len(after)
    return pl.pallas_call(
        behind(functools.partial(load_body, n), n, n_after),
        name="load",
        out_shape=[pltpu.VMEM(a.shape, a.dtype) for a in arrays],
        in_specs=[pl.BlockSpec(memory_space=pltpu.HBM)] * n + [pl.BlockSpec(memory_space=pl.ANY)] * n_after,
        out_specs=[pl.BlockSpec(memory_space=pltpu.VMEM)] * n,
        scratch_shapes=[pltpu.SemaphoreType.DMA((n,))],
        compiler_params=pltpu.CompilerParams(vmem_limit_bytes=VMEM_LIMIT),
        cost_estimate=pl.CostEstimate(flops=1, bytes_accessed=1, transcendentals=0),
    )(*[pltpu.with_memory_space_constraint(a, pltpu.HBM) for a in arrays], *after)


def norm_parts(v):
    center = v - jnp.mean(v, -1, keepdims=True)
    r = lax.rsqrt(jnp.mean(center * center, -1, keepdims=True) + EPS_NORM)
    return center * r, r


def norm_back(v, gain, dy):
    xhat, r = norm_parts(v)
    gdy = gain * dy
    dv = r * (gdy - jnp.mean(gdy, -1, keepdims=True) - xhat * jnp.mean(gdy * xhat, -1, keepdims=True))
    return dv, jnp.sum(dy * xhat, 0, keepdims=True), jnp.sum(dy, 0, keepdims=True)


def row_of(par_ref, i):
    return par_ref[i : i + 1, :].astype(F32)


def low_half(shape, dim):
    return lax.broadcasted_iota(jnp.int32, shape, dim) < HD


def stacked(t2):
    first = low_half(t2.shape, 1)
    zero = jnp.zeros_like(t2)
    return jnp.concatenate([jnp.where(first, t2, zero), jnp.where(first, zero, t2)], 0)


def unstacked(tT):
    R = tT.shape[1] // 2
    first = low_half((PAIR, R), 0)
    return jnp.where(first, tT[:, :R], tT[:, R:]).T


def causal_mask(R, length):
    key = lax.broadcasted_iota(jnp.int32, (R, 2 * R), 0)
    lane = lax.broadcasted_iota(jnp.int32, (R, 2 * R), 1)
    query = jnp.where(lane >= R, lane - R, lane)
    return (key <= query) & (key < length)


def local_weights(k2, qq, allowed):
    sT = nt(k2, qq)
    if allowed is not None:
        sT = jnp.where(allowed, sT, NEG_FILL)
    p = jnp.exp(sT - jnp.max(sT, 0, keepdims=True))
    return p * (1.0 / jnp.sum(p, 0, keepdims=True))


def gelu_parts(h):
    cdf = 0.5 * (1.0 + lax.erf(h * 0.7071067811865476))
    pdf = 0.3989422804014327 * jnp.exp(-0.5 * h * h)
    return h * cdf, cdf + h * pdf


def attend_fwd_body(causal, *refs):
    if causal:
        len_ref, refs = refs[0], refs[1:]
    x_ref, wq, wk, wv, wm, q_ref, k_ref, v_ref, o_ref, part_ref = refs
    x = x_ref[...]
    R = x.shape[0]
    q_ref[...] = (nn(x, wq[...]) * SCALE).astype(BF)
    k_ref[...] = nn(x, wk[...]).astype(BF)
    v_ref[...] = nn(x, wv[...]).astype(BF)
    flush(q_ref, k_ref, v_ref)
    allowed = causal_mask(R, len_ref[0]) if causal else None
    for c in range(0, q_ref.shape[1], PAIR):
        sl = slice(c, c + PAIR)
        w = local_weights(k_ref[:, sl], stacked(q_ref[:, sl]), allowed).astype(BF)
        o_ref[:, sl] = unstacked(tn(v_ref[:, sl], w)).astype(BF)
    flush(o_ref)
    part_ref[...] = nn(o_ref[...], wm[...]).astype(BF)


def attend_fwd(x, wq, wk, wv, wm, length=None, after=(), fetch=False):
    R, D = x.shape
    C = wq.shape[1]
    args = (x, wq, wk, wv, wm)
    if fetch:
        args = tuple(Far(a) for a in args)
    causal = length is not None
    if causal:
        args = (length,) + args
    return whole(
        functools.partial(attend_fwd_body, causal),
        "attend_fwd",
        [((R, C), BF, HBM)] * 4 + [((R, D), BF)],
        *args,
        smem=int(causal),
        after=after,
    )


def ffn_fwd_body(g, x_ref, own, oth, par, wu, wd, v_ref, u_ref, low_ref, act_ref, gp_ref, part_ref):
    R, D = x_ref.shape
    gain, shift = row_of(par, g), row_of(par, g + 1)
    for r in range(0, R, ROWS):
        s = slice(r, r + ROWS)
        v = x_ref[s, :].astype(F32) + (own[s, :].astype(F32) + oth[s, :].astype(F32))
        xhat, _ = norm_parts(v)
        u = xhat * gain + shift
        v_ref[s, :] = v
        u_ref[s, :] = u
        low_ref[s, :] = u.astype(BF)
    flush(v_ref, low_ref)
    low = low_ref[...]
    for c in range(0, wu.shape[1], 256):
        sl = slice(c, c + 256)
        a, gp = gelu_parts(nn(low, wu[:, sl]))
        act_ref[:, sl] = a.astype(BF)
        gp_ref[:, sl] = gp.astype(BF)
        flush(act_ref, gp_ref, upto=c + 256)
    part_ref[...] = nn(act_ref[...], wd[...]).astype(BF)


def ffn_fwd(g, x, own, oth, par, wu, wd, fetch, keep):
    R, D = x.shape
    FF = wu.shape[1]
    kept = (HBM,) if keep else ()
    return whole(
        functools.partial(ffn_fwd_body, g),
        "ffn_fwd",
        [((R, D), F32, HBM), ((R, D), F32), ((R, D), BF, HBM), ((R, FF), BF, *kept), ((R, FF), BF, HBM), ((R, D), BF)],
        x, own, oth, par, *((Far(wu), Far(wd)) if fetch else (wu, wd)),
    )


def order_matrix(R):
    t = lax.broadcasted_iota(jnp.int32, (R, R), 0)
    col = lax.broadcasted_iota(jnp.int32, (R, R), 1)
    src = jnp.where(t < R // 2, 2 * t, 2 * t - (R - 1))
    return (src == col).astype(F32).astype(BF)


def store_body(g, u_ref, own, oth, par, wk, wv, v_ref, low_ref, kv_ref):
    R = u_ref.shape[0]
    gain, shift = row_of(par, g), row_of(par, g + 1)
    low = []
    for r in range(0, R, ROWS):
        s = slice(r, r + ROWS)
        v = u_ref[s, :] + (own[s, :].astype(F32) + oth[s, :].astype(F32))
        xhat, _ = norm_parts(v)
        v_ref[s, :] = v
        low.append((xhat * gain + shift).astype(BF))
    low_ref[...] = nn(order_matrix(R), jnp.concatenate(low, 0)).astype(BF)
    low = low_ref[...]
    kv_ref[0] = nn(low, wk[...]).astype(BF)
    kv_ref[1] = nn(low, wv[...]).astype(BF)


def store_fwd(g, u, own, oth, par, wk, wv):
    R, D = u.shape
    C = wk.shape[1]
    return whole(
        functools.partial(store_body, g),
        "store_fwd",
        [((R, D), F32), ((R, D), BF), ((2, R, C), BF)],
        u, own, oth, par, wk, wv,
    )


def norm_body(g, v_ref, par, out_ref):
    for r in range(0, v_ref.shape[0], ROWS):
        s = slice(r, r + ROWS)
        xhat, _ = norm_parts(v_ref[s, :])
        out_ref[s, :] = xhat * row_of(par, g) + row_of(par, g + 1)


def norm_of(g, v, par, after):
    return whole(functools.partial(norm_body, g), "norm_of", [(v.shape, F32, HBM)], v, par, after=after)[0]


def cross_q_body(g, x_ref, own, oth, par, wq, v_ref, u_ref, low_ref, q_ref):
    R = x_ref.shape[0]
    gain, shift = row_of(par, g), row_of(par, g + 1)
    for r in range(0, R, ROWS):
        s = slice(r, r + ROWS)
        v = x_ref[s, :].astype(F32) + (own[s, :].astype(F32) + oth[s, :].astype(F32))
        xhat, _ = norm_parts(v)
        u = xhat * gain + shift
        v_ref[s, :] = v
        u_ref[s, :] = u
        low_ref[s, :] = u.astype(BF)
    flush(v_ref, u_ref, low_ref)
    q_ref[...] = (nn(low_ref[...], wq[...]) * SCALE).astype(BF)


def cross_q(g, x, own, oth, par, wq):
    R, D = x.shape
    C = wq.shape[1]
    return whole(
        functools.partial(cross_q_body, g),
        "cross_q",
        [((R, D), F32, HBM), ((R, D), F32, HBM), ((R, D), BF, HBM), ((R, C), BF)],
        x, own, oth, par, wq,
    )


def pick_rows_body(from_ref, *out_refs):
    for pair, out_ref in enumerate(out_refs):
        for h in range(2):
            out_ref[h] = (from_ref[2 * pair + h] & 1).astype(F32).T.astype(BF)


def pick_rows(retrieved, after):
    R, heads, picked = retrieved.shape
    outs = [((2, picked, R), BF)] * (heads // 2)
    return whole(pick_rows_body, "pick_rows", outs, Far(retrieved.transpose(1, 0, 2)), after=after)


def picks_body(pairs, core_ref, *refs):
    own, other, (band_ref, band_other, out_ref) = refs[:pairs], refs[pairs : 2 * pairs], refs[2 * pairs :]
    g = 2 * pl.program_id(0) + core_ref[0]
    _, picked, R = own[0].shape
    half = out_ref.shape[2]
    for h in range(2 * pairs):
        for i, (from_ref, start_ref) in enumerate(((own[h // 2], band_ref), (other[h // 2], band_other))):
            rel = g - start_ref[h : h + 1, :]
            got = jnp.full((half, R), -1.0, F32)
            for b in range(picked // half):
                got = jnp.where(rel == b, from_ref[h % 2, b * half : (b + 1) * half, :].astype(F32), got)
            at = (2 * (h % 2) + i) * R
            out_ref[0, h // 2, :, at : at + R] = got


def picks(core_index, pick, pick_other, band, band_other, groups, half):
    pairs = len(pick)
    _, picked, R = pick[0].shape
    return pl.pallas_call(
        functools.partial(picks_body, pairs),
        name="picks",
        grid=(groups,),
        out_shape=pltpu.HBM((groups, pairs, half, 4 * R), F32),
        in_specs=[pl.BlockSpec(memory_space=pltpu.SMEM)]
        + [pl.BlockSpec((2, picked, R), lambda g: (0, 0, 0))] * (2 * pairs)
        + [pl.BlockSpec((2 * pairs, R), lambda g: (0, 0))] * 2,
        out_specs=pl.BlockSpec((1, pairs, half, 4 * R), lambda g: (g, 0, 0, 0)),
        compiler_params=pltpu.CompilerParams(vmem_limit_bytes=VMEM_LIMIT),
        cost_estimate=pl.CostEstimate(flops=1, bytes_accessed=1, transcendentals=0),
    )(core_index, *pick, *pick_other, band, band_other)


def chosen_scores(k2, qq, a):
    half = a.shape[0]
    sT = nt(k2, qq)
    s = jnp.where(a > 0.5, sT[half:], sT[:half])
    return jnp.where(a < -0.5, NEG_FILL, s)


def spread(p, a):
    zero = jnp.zeros_like(p)
    even = jnp.where(a == 0.0, p, zero).astype(BF)
    odd = jnp.where(a == 1.0, p, zero).astype(BF)
    return jnp.concatenate([even, odd], 0)


def of_both(own, other):
    return stacked(jnp.concatenate([own, other], 0))


def own_lanes(t):
    R = t.shape[1] // 4
    return jnp.concatenate([t[:, :R], t[:, 2 * R : 3 * R]], 1)


def other_lanes(t):
    R = t.shape[1] // 4
    return jnp.concatenate([t[:, R : 2 * R], t[:, 3 * R :]], 1)


def all_lanes(own, other):
    R = own.shape[1] // 2
    return jnp.concatenate([own[:, :R], other[:, :R], own[:, R:], other[:, R:]], 1)


def cross_fwd_body(first, last, gid_ref, q_ref, q_other, *refs):
    kv, a_refs, refs = refs[:2], refs[2:4], refs[4:]
    if not first:
        m_in, l_in, acc_in = refs[:3]
        refs = refs[3:]
    m_ref, l_ref, acc_ref = refs[:3]

    @pl.when(pl.program_id(0) == 0)
    def _():
        if first:
            m_ref[...] = jnp.full(m_ref.shape, NEG_FILL, F32)
            l_ref[...] = jnp.zeros(l_ref.shape, F32)
            acc_ref[...] = jnp.zeros(acc_ref.shape, F32)
        else:
            m_ref[...] = m_in[...]
            l_ref[...] = l_in[...]
            acc_ref[...] = acc_in[...]

    pairs = acc_ref.shape[0]
    for hp in range(pairs):
        sl = slice(hp * PAIR, (hp + 1) * PAIR)
        qq = of_both(q_ref[:, sl], q_other[:, sl])
        scores = [chosen_scores(kv[j][0, 0, :, sl], qq, a_refs[j][0, hp]) for j in range(2)]
        old = m_ref[hp : hp + 1, :]
        top = functools.reduce(jnp.maximum, [jnp.max(s, 0, keepdims=True) for s in scores], old)
        fade = jnp.exp(old - top)
        total = l_ref[hp : hp + 1, :] * fade
        acc = acc_ref[hp] * fade
        for j in range(2):
            a = a_refs[j][0, hp]
            p = jnp.where(a < -0.5, 0.0, jnp.exp(scores[j] - top))
            total = total + jnp.sum(p, 0, keepdims=True)
            acc = acc + tn(kv[j][0, 1, :, sl], spread(p, a))
        m_ref[hp : hp + 1, :] = top
        l_ref[hp : hp + 1, :] = total
        acc_ref[hp] = acc

    if last:
        own_ref, other_ref = refs[3:]

        @pl.when(pl.program_id(0) == pl.num_programs(0) - 1)
        def _():
            for out, lanes in ((own_ref, own_lanes), (other_ref, other_lanes)):
                out[pairs * PAIR :, :] = jnp.zeros((8, out.shape[1]), F32)
                for hp in range(pairs):
                    out[hp * PAIR : (hp + 1) * PAIR, :] = lanes(acc_ref[hp])
                    out[pairs * PAIR + hp : pairs * PAIR + hp + 1, :] = lanes(m_ref[hp : hp + 1, :])
                    out[pairs * PAIR + 4 + hp : pairs * PAIR + 5 + hp, :] = lanes(l_ref[hp : hp + 1, :])


def kv_specs(kv, a):
    rows, C = kv[0].shape[2:]
    specs = [pl.BlockSpec((1, 2, rows, C), lambda i, gid: (i, 0, 0, 0)) for _ in range(2)]
    for j in range(2):
        specs.append(
            pl.BlockSpec((1,) + a.shape[1:], functools.partial(lambda j, i, gid: (gid[2 * i + j], 0, 0, 0), j))
        )
    return specs


def fixed(shape):
    return pl.BlockSpec(shape, lambda i, gid: (0,) * len(shape))


def cross_fwd(gid, q, kv, a, state, last):
    R, C = q[0].shape
    pairs = C // PAIR
    hi, _, rows, _ = kv[0].shape
    shapes = [(8, 4 * R), (8, 4 * R), (pairs, PAIR, 4 * R)]
    first = state is None
    state = () if first else tuple(state)
    if last:
        shapes += [(C + 8, 2 * R)] * 2
    return pl.pallas_call(
        functools.partial(cross_fwd_body, first, last),
        name="cross_fwd",
        grid_spec=pltpu.PrefetchScalarGridSpec(
            num_scalar_prefetch=1,
            grid=(hi,),
            in_specs=[fixed(q[0].shape)] * 2 + kv_specs(kv, a) + [fixed(s.shape) for s in state],
            out_specs=[fixed(s) for s in shapes],
        ),
        out_shape=[jax.ShapeDtypeStruct(s, F32) for s in shapes],
        compiler_params=pltpu.CompilerParams(vmem_limit_bytes=VMEM_LIMIT),
        cost_estimate=pl.CostEstimate(flops=1, bytes_accessed=1, transcendentals=0),
    )(gid, *q, *kv, *([pltpu.with_memory_space_constraint(a, pltpu.HBM)] * 2), *state)


def merged(own_ref, got_ref, hp, C):
    sl = slice(hp * PAIR, (hp + 1) * PAIR)
    m, l = slice(C + hp, C + hp + 1), slice(C + 4 + hp, C + 5 + hp)
    m1, m2 = own_ref[m, :], got_ref[m, :]
    top = jnp.maximum(m1, m2)
    f1, f2 = jnp.exp(m1 - top), jnp.exp(m2 - top)
    total = own_ref[l, :] * f1 + got_ref[l, :] * f2
    return top + jnp.log(total), unstacked((own_ref[sl, :] * f1 + got_ref[sl, :] * f2) * (1.0 / total))


def cross_mix_body(own_ref, got_ref, wm, log_ref, of_ref, o_ref, part_ref):
    C = wm.shape[0]
    log_ref[...] = jnp.zeros(log_ref.shape, F32)
    for hp in range(C // PAIR):
        sl = slice(hp * PAIR, (hp + 1) * PAIR)
        log_ref[hp : hp + 1, :], o = merged(own_ref, got_ref, hp, C)
        of_ref[:, sl] = o
        o_ref[:, sl] = o.astype(BF)
    part_ref[...] = nn(o_ref[...], wm[...]).astype(BF)


def cross_mix_fwd(own, got, wm):
    R2 = own.shape[1]
    C, D = wm.shape
    R = R2 // 2
    return whole(
        cross_mix_body,
        "cross_mix",
        [((8, R2), F32), ((R, C), F32), ((R, C), BF), ((R, D), BF)],
        own, got, wm,
    )


def cross_merge_body(own_ref, got_ref, log_ref, of_ref):
    C = of_ref.shape[1]
    log_ref[...] = jnp.zeros(log_ref.shape, F32)
    for hp in range(C // PAIR):
        log_ref[hp : hp + 1, :], of_ref[:, hp * PAIR : (hp + 1) * PAIR] = merged(own_ref, got_ref, hp, C)


def cross_merge(own, got):
    rows, R2 = own.shape
    return whole(cross_merge_body, "cross_merge", [((8, R2), F32), ((R2 // 2, rows - 8), F32)], own, got)


def ffn_back_rest(dlow_ref, gp_ref, wu, wd, dh_ref, part_ref):
    low = dlow_ref[...]
    for c in range(0, wu.shape[1], 256):
        sl = slice(c, c + 256)
        dh_ref[:, sl] = (nt(low, wd[sl, :]) * gp_ref[:, sl].astype(F32)).astype(BF)
    part_ref[...] = nt(dh_ref[...], wu[...]).astype(BF)


def last_body(g, u_ref, own, oth, cot, par, gp_ref, wu, wd, out_ref, dv_ref, dlow_ref, dh_ref, gg_ref, part_ref):
    R, D = u_ref.shape
    gain, shift = row_of(par, g), row_of(par, g + 1)
    gg_ref[...] = jnp.zeros(gg_ref.shape, F32)
    for r in range(0, R, ROWS):
        s = slice(r, r + ROWS)
        v = u_ref[s, :] + (own[s, :].astype(F32) + oth[s, :].astype(F32))
        xhat, _ = norm_parts(v)
        out_ref[s, :] = xhat * gain + shift
        dv, dg, db = norm_back(v, gain, cot[s, :].astype(F32))
        dv_ref[s, :] = dv
        dlow_ref[s, :] = dv.astype(BF)
        gg_ref[0:1, :] += dg
        gg_ref[1:2, :] += db
    flush(gg_ref, out_ref)
    ffn_back_rest(dlow_ref, gp_ref, wu, wd, dh_ref, part_ref)


def last_fwd_back(g, u, own, oth, cot, par, gp, wu, wd):
    R, D = u.shape
    FF = wu.shape[1]
    return whole(
        functools.partial(last_body, g),
        "last_fwd_back",
        [((R, D), F32, HBM), ((R, D), F32), ((R, D), BF), ((R, FF), BF), ((8, D), F32, HBM), ((R, D), BF)],
        u, own, oth, cot, par, gp, wu, wd,
    )


def ffn_back_body(g, own, oth, v_ref, par, gp_ref, wu, wd, dv_ref, dlow_ref, dh_ref, gg_ref, part_ref):
    R, D = v_ref.shape
    gain = row_of(par, g)
    gg_ref[...] = jnp.zeros(gg_ref.shape, F32)
    for r in range(0, R, ROWS):
        s = slice(r, r + ROWS)
        dy = own[s, :].astype(F32) + oth[s, :].astype(F32)
        dv, dg, db = norm_back(v_ref[s, :], gain, dy)
        dv_ref[s, :] = dv
        dlow_ref[s, :] = dv.astype(BF)
        gg_ref[0:1, :] += dg
        gg_ref[1:2, :] += db
    flush(gg_ref)
    ffn_back_rest(dlow_ref, gp_ref, wu, wd, dh_ref, part_ref)


def ffn_back(g, own, oth, v, par, gp, wu, wd, after):
    R, D = v.shape
    FF = wu.shape[1]
    return whole(
        functools.partial(ffn_back_body, g),
        "ffn_back",
        [((R, D), F32), ((R, D), BF), ((R, FF), BF), ((8, D), F32, HBM), ((R, D), BF)],
        own, oth, v, par, gp, wu, wd,
        after=after,
    )


def branch_back(g, dres, own, oth, v_ref, par, dv_ref, dlow_ref, gg_ref):
    R, D = v_ref.shape
    gain = row_of(par, g)
    gg_ref[...] = jnp.zeros(gg_ref.shape, F32)
    for r in range(0, R, ROWS):
        s = slice(r, r + ROWS)
        dy = dres[s, :] + (own[s, :].astype(F32) + oth[s, :].astype(F32))
        dv, dg, db = norm_back(v_ref[s, :], gain, dy)
        dv_ref[s, :] = dv
        dlow_ref[s, :D] = dv.astype(BF)
        gg_ref[0:1, :] += dg
        gg_ref[1:2, :] += db


def cross_mix_back_body(g, dres, own, oth, v_ref, par, wm, dv_ref, pack_ref, gg_ref):
    branch_back(g, dres, own, oth, v_ref, par, dv_ref, pack_ref, gg_ref)
    flush(dv_ref, gg_ref)
    D = v_ref.shape[1]
    pack_ref[:, D:] = nt(pack_ref[:, :D], wm[...]).astype(BF)


def cross_mix_back(g, dres, own, oth, v, par, wm):
    R, D = v.shape
    C = wm.shape[0]
    return whole(
        functools.partial(cross_mix_back_body, g),
        "cross_mix_back",
        [((R, D), F32, HBM), ((R, D + C), BF), ((8, D), F32, HBM)],
        dres, own, oth, v, par, wm,
    )


def cross_back_body(first, last, gid_ref, q_ref, q_other, do_pack, do_pack_other, *refs):
    C = q_ref.shape[1]
    skip = do_pack.shape[1] - C
    do_ref, do_other = do_pack.at[:, skip:], do_pack_other.at[:, skip:]
    kv, a_refs, refs = refs[:2], refs[2:4], refs[4:]
    if first:
        of_ref, of_other, log_own, log_other = refs[:4]
        dq_ref, stat_ref, keep_ref, send_ref = refs[4:8]
    else:
        dq_in, stat_in = refs[:2]
        dq_ref, stat_ref, keep_ref, send_ref = refs[2:6]
    pairs = dq_ref.shape[0]

    @pl.when(pl.program_id(0) == 0)
    def _():
        if not first:
            dq_ref[...] = dq_in[...]
            stat_ref[...] = stat_in[...]
            return
        dq_ref[...] = jnp.zeros(dq_ref.shape, F32)
        stat_ref[...] = jnp.zeros(stat_ref.shape, F32)
        stat_ref[0:8, :] = all_lanes(log_own[...], log_other[...])
        for hp in range(pairs):
            sl = slice(hp * PAIR, (hp + 1) * PAIR)
            sums = []
            for d, o in ((do_ref, of_ref), (do_other, of_other)):
                prod = (d[:, sl].astype(F32) * o[:, sl]).T
                sums.append([jnp.sum(prod[:HD], 0, keepdims=True), jnp.sum(prod[HD:], 0, keepdims=True)])
            stat_ref[8 + hp : 9 + hp, :] = jnp.concatenate([sums[0][0], sums[1][0], sums[0][1], sums[1][1]], 1)

    for hp in range(pairs):
        sl = slice(hp * PAIR, (hp + 1) * PAIR)
        qq = of_both(q_ref[:, sl], q_other[:, sl])
        dd = of_both(do_ref[:, sl], do_other[:, sl])
        log_total = stat_ref[hp : hp + 1, :]
        delta = stat_ref[8 + hp : 9 + hp, :]
        dq = dq_ref[hp]
        for j, out_ref in enumerate((keep_ref, send_ref)):
            a = a_refs[j][0, hp]
            half = a.shape[0]
            k2 = kv[j][0, 0, :, sl]
            p = jnp.exp(chosen_scores(k2, qq, a) - log_total)
            daT = nt(kv[j][0, 1, :, sl], dd)
            ds = p * (jnp.where(a > 0.5, daT[half:], daT[:half]) - delta)
            dsT = spread(ds, a)
            out_ref[0, 0, :, sl] = nn(dsT, qq).astype(BF)
            out_ref[0, 1, :, sl] = nn(spread(p, a), dd).astype(BF)
            dq = dq + tn(k2, dsT)
        dq_ref[hp] = dq

    if last:
        own_ref, other_ref = refs[-2:]

        @pl.when(pl.program_id(0) == pl.num_programs(0) - 1)
        def _():
            for hp in range(pairs):
                own_ref[hp] = own_lanes(dq_ref[hp])
                other_ref[hp] = other_lanes(dq_ref[hp]).astype(BF)


def cross_back(gid, q, do, kv, a, extra, first, last, after=()):
    R, C = q[0].shape
    pairs = C // PAIR
    hi, _, rows, _ = kv[0].shape
    grad_spec = pl.BlockSpec((1, 2, rows, C), lambda i, gid: (i, 0, 0, 0))
    shapes = [(pairs, PAIR, 4 * R), (16, 4 * R)]
    out_specs = [fixed(s) for s in shapes] + [grad_spec] * 2
    out_shape = [jax.ShapeDtypeStruct(s, F32) for s in shapes] + [jax.ShapeDtypeStruct(kv[0].shape, BF)] * 2
    if last:
        out_specs += [fixed((pairs, PAIR, 2 * R))] * 2
        out_shape += [jax.ShapeDtypeStruct((pairs, PAIR, 2 * R), d) for d in (F32, BF)]
    return pl.pallas_call(
        behind(functools.partial(cross_back_body, first, last), 9 + len(extra), len(after)),
        name="cross_back",
        grid_spec=pltpu.PrefetchScalarGridSpec(
            num_scalar_prefetch=1,
            grid=(hi,),
            in_specs=[fixed(q[0].shape)] * 2
            + [fixed(do[0].shape)] * 2
            + kv_specs(kv, a)
            + [fixed(e.shape) for e in extra]
            + [pl.BlockSpec(memory_space=pl.ANY)] * len(after),
            out_specs=out_specs,
        ),
        out_shape=out_shape,
        compiler_params=pltpu.CompilerParams(vmem_limit_bytes=VMEM_LIMIT),
        cost_estimate=pl.CostEstimate(flops=1, bytes_accessed=1, transcendentals=0),
    )(gid, *q, *do, *kv, *([pltpu.with_memory_space_constraint(a, pltpu.HBM)] * 2), *extra, *after)


def cross_q_back_body(dq_own, dq_got, wq, dq_ref, part_ref):
    for hp in range(dq_own.shape[0]):
        sl = slice(hp * PAIR, (hp + 1) * PAIR)
        dq_ref[:, sl] = (unstacked(dq_own[hp] + dq_got[hp].astype(F32)) * SCALE).astype(BF)
    flush(dq_ref)
    part_ref[...] = nt(dq_ref[...], wq[...]).astype(BF)


def cross_q_back(dq, got, wq, after):
    D, C = wq.shape
    R = dq.shape[2] // 2
    return whole(cross_q_back_body, "cross_q_back", [((R, C), BF), ((R, D), BF)], dq, got, wq, after=after)


def store_back_body(spread_at, *refs):
    n = len(refs) - 4
    wk, wv, dkv_ref, part_ref = refs[n:]
    R, C = dkv_ref.shape[0], dkv_ref.shape[1] // 2
    for i in range(2):
        parts = [t[0, i] for t in refs[:spread_at]]
        if spread_at < n:
            parts.append(refs[spread_at + i][0, 0])
        total = functools.reduce(lambda x, y: x + y, [t.astype(F32) for t in parts])
        dkv_ref[:, i * C : (i + 1) * C] = total.astype(BF)
    part = nt(dkv_ref[:, :C], wk[...]) + nt(dkv_ref[:, C:], wv[...])
    part_ref[...] = tn(order_matrix(R), part.astype(BF)).astype(BF)


def store_back(terms, wk, wv, after):
    D, C = wk.shape
    R = terms[0].shape[2]
    full = [t for t in terms if not isinstance(t, list)]
    halves = [h for t in terms if isinstance(t, list) for h in t]
    return whole(
        functools.partial(store_back_body, len(full)),
        "store_back",
        [((R, 2 * C), BF), ((R, D), BF)],
        *full, *halves, wk, wv,
        after=after,
    )


def attend_back_body(causal, g, n_more, *refs):
    if causal:
        len_ref, refs = refs[0], refs[1:]
    (dres, own, oth, v1_ref, par, q_ref, k_ref, v_ref, wq, wk, wv, wm) = refs[:12]
    R, D = v1_ref.shape
    dv_ref, pack_ref, gg_ref, part_ref = refs[12 + n_more : 16 + n_more]
    branch_back(g, dres, own, oth, v1_ref, par, dv_ref, pack_ref, gg_ref)
    flush(dv_ref, gg_ref)
    if n_more:
        gains_ref = refs[-1]
        rows = [gg_ref[0:2, :]] + [other[0:2, :] for other in refs[12 : 12 + n_more]]
        rows.append(jnp.zeros((gains_ref.shape[0] - 2 - 2 * n_more, D), F32))
        gains_ref[...] = jnp.concatenate(rows, 0).astype(BF)
        flush(gains_ref)
    C = wq.shape[1]
    do = nt(pack_ref[:, :D], wm[...]).astype(BF)
    allowed = causal_mask(R, len_ref[0]) if causal else None
    for c in range(0, C, PAIR):
        sl = slice(c, c + PAIR)
        k2 = k_ref[:, sl]
        qq = stacked(q_ref[:, sl])
        dd = stacked(do[:, sl])
        w = local_weights(k2, qq, allowed)
        daT = nt(v_ref[:, sl], dd)
        ds = (w * (daT - jnp.sum(w * daT, 0, keepdims=True))).astype(BF)
        at = D + c
        pack_ref[:, at : at + PAIR] = (unstacked(tn(k2, ds)) * SCALE).astype(BF)
        pack_ref[:, at + C : at + C + PAIR] = nn(ds, qq).astype(BF)
        pack_ref[:, at + 2 * C : at + 2 * C + PAIR] = nn(w.astype(BF), dd).astype(BF)
    flush(pack_ref)
    part = nt(pack_ref[:, D : D + C], wq[...]) + nt(pack_ref[:, D + C : D + 2 * C], wk[...])
    part_ref[...] = (part + nt(pack_ref[:, D + 2 * C :], wv[...])).astype(BF)


def attend_back(g, dres, own, oth, v1, par, kept, weights, length=None, more=(), after=()):
    R, D = v1.shape
    C = kept[0].shape[1]
    args = (dres, own, oth, v1, par, *kept, *weights, *more)
    causal = length is not None
    if causal:
        args = (length,) + args
    return whole(
        functools.partial(attend_back_body, causal, g, len(more)),
        "attend_back",
        [((R, D), F32, HBM), ((R, D + 3 * C), BF), ((8, D), F32, HBM), ((R, D), BF)]
        + [((16, D), BF)] * bool(more),
        *args,
        smem=int(causal),
        after=after,
    )


def weight_body(plan, chunks, sources, n_idx, *refs):
    idx_refs, ins, outs = refs[:n_idx], refs[n_idx : -2 * len(chunks)], refs[-2 * len(chunks) :]
    half = outs[0].shape[0]
    chunk, at, takes = 0, 0, {}
    for part, a_at, off, D, grads in plan:
        if part not in takes:
            spot = lax.broadcasted_iota(jnp.int32, (2 * half, D), 1) == idx_refs[part][...]
            takes[part] = spot.astype(F32).astype(BF)
        parts = [nt(takes[part], ins[a_at + i][:, off : off + D]) for i in range(sources)]
        aT = jnp.concatenate(parts, 1).astype(BF)
        for d_at, d_off, width in grads:
            step = 384 if width % 384 == 0 else 128
            for c in range(d_off, d_off + width, step):
                dy = jnp.concatenate([ins[d_at + i][:, c : c + step] for i in range(sources)], 0)
                got = nn(aT, dy)
                outs[2 * chunk][:, at : at + step] = got[:half].astype(BF)
                outs[2 * chunk + 1][:, at : at + step] = got[half:].astype(BF)
                at += step
                if at == chunks[chunk]:
                    chunk, at = chunk + 1, 0


def weight_grads(idxs, D, term_lists, chunks, after=()):
    ins, plan = [], []
    for part, terms in enumerate(term_lists):
        for a, off, grads in terms:
            at = len(ins)
            ins += list(a)
            ds = []
            for d, d_off, w in grads:
                ds.append((len(ins), d_off, w))
                ins += list(d)
            plan.append((part, at, off, D, ds))
    half = idxs[0].shape[0] // 2
    return whole(
        functools.partial(weight_body, plan, chunks, len(term_lists[0][0][0]), len(idxs)),
        "weight_grads",
        [((half, w), BF) for w in chunks for _ in range(2)],
        *idxs,
        *ins,
        after=after,
    )


def swap(x, bit, n):
    return lax.ppermute(x, "blk", [(i, i ^ bit) for i in range(n)])


def tied(x, *before):
    return lax.optimization_barrier((x, *before))[0]


def other_tp(x):
    return lax.ppermute(x, "tp", [(0, 1), (1, 0)])


class Halving:
    def __init__(self, keep, send, n, bits):
        self.keep, self.send, self.n, self.bits = keep, send, n, bits
        self.got = swap(send, bits[0], n)

    def hold(self, *before):
        self.send = tied(self.send, *before)
        self.got = swap(self.send, self.bits[0], self.n)

    def step(self, *before):
        got = tied(self.got, *before) if before else self.got
        total = self.keep.astype(F32) + got.astype(F32)
        self.bits = self.bits[1:]
        if not self.bits:
            return total
        half = total.shape[0] // 2
        self.keep, self.send = total[:half], total[half:].astype(BF)
        self.got = swap(self.send, self.bits[0], self.n)
        return self.send

    def end(self, *before):
        while len(self.bits) > 1:
            self.step(*before)
        return self.step(*before)


def on_device(
    n,
    encoder_in,
    decoder_in,
    lengths,
    retrieved,
    band_start,
    cotangent,
    enc_query,
    enc_key,
    enc_value,
    enc_mix,
    attn_gain,
    attn_shift,
    enc_up,
    enc_down,
    ffn_gain,
    ffn_shift,
    self_query,
    self_key,
    self_value,
    self_mix,
    self_gain,
    self_shift,
    cross_query,
    cross_key,
    cross_value,
    cross_mix,
    cross_gain,
    cross_shift,
    dec_up,
    dec_down,
    last_gain,
    last_shift,
):
    group_rows, D = encoder_in.shape
    C = cross_query.shape[1]
    FF = enc_up.shape[1]
    hi = n // 16
    me = lax.axis_index("blk")
    core = lambda x: swap(x, 1, n)
    par = jnp.stack(
        [attn_gain, attn_shift, ffn_gain, ffn_shift, self_gain, self_shift, cross_gain, cross_shift, last_gain, last_shift]
    )

    share = D // n
    bits = [1 << i for i in range(n.bit_length() - 1)]

    def rows_by(order):
        t = jnp.arange(share << len(order), dtype=jnp.int32)
        block = t // share
        rel = sum(((block >> (len(order) - 1 - i)) & 1) * bit for i, bit in enumerate(order))
        return ((me ^ rel) * share + t % share).reshape(-1, 1)

    def gradients(order, terms, after=()):
        width = sum(grad[2] for _, _, grads in terms for grad in grads)
        return Halving(*weight_grads([rows_by(order)], D, [terms], [width], after), n, order)

    def joint(parts, after=()):
        chunks = [w for _, _, widths in parts for w in widths]
        made = weight_grads([rows_by(order) for order, _, _ in parts], D, [terms for _, terms, _ in parts], chunks, after)
        gots = [swap(send, 1, n) for send in made[1::2]]

        def finish(*before):
            tied_gots = lax.optimization_barrier((*gots, *before))[: len(gots)]
            totals = [k.astype(F32) + g.astype(F32) for k, g in zip(made[0::2], tied_gots)]
            half, sums = totals[0].shape[0] // 2, []
            for order, _, widths in parts:
                mine, totals = totals[: len(widths)], totals[len(widths) :]
                keep = jnp.concatenate([t[:half] for t in mine], 1)
                send = jnp.concatenate([t[half:].astype(BF) for t in mine], 1)
                sums.append(Halving(keep, send, n, order[1:]))
            return sums

        return made[0], finish

    both = lambda x: (x, core(x))
    summed = lambda *arrays: functools.reduce(lambda x, y: x + y, [t.astype(F32) for t in arrays]).astype(BF)

    *enc_kept, enc_o, enc_part = attend_fwd(encoder_in, enc_query, enc_key, enc_value, enc_mix, fetch=True)
    enc_other = other_tp(enc_part)
    pick = pick_rows(retrieved, (enc_part,))
    band = tied(band_start.T, *pick)
    pick_other, band_other = [core(p) for p in pick], core(band)
    *self_kept, self_o, self_part = attend_fwd(
        decoder_in, self_query, self_key, self_value, self_mix, lengths, pick
    )
    enc_other = tied(enc_other, self_part)
    v1, u1, low1, act1, gp1, part1 = ffn_fwd(0, encoder_in, enc_part, enc_other, par, enc_up, enc_down, True, True)
    other1 = other_tp(part1)
    chosen = picks(tied((me & 1).reshape(1), part1), pick, pick_other, band, band_other, n // 2, group_rows // 2)
    other1 = tied(other1, chosen)
    v2, enc_low, store = store_fwd(2, u1, part1, other1, par, cross_key, cross_value)

    store = store[None]
    for b in range(4, n.bit_length() - 1):
        store = jnp.concatenate([store, swap(store, 1 << b, n)], 0)

    def gid_of(pair):
        return (me ^ jnp.array([16 * h + r for h in range(hi) for r in pair], jnp.int32)) >> 1

    near = swap(store, 4, n)
    y_own = swap(store, 2, n)
    far = swap(store, 8, n)
    self_part = tied(self_part, store)
    self_other = other_tp(self_part)
    vd, ud, lowd, qc = cross_q(4, decoder_in, self_part, self_other, par, cross_query)
    qcs = both(qc)
    encoded = norm_of(2, v2, par, (qc,))
    far = tied(far, near, y_own, qcs[1], encoded)
    apart = swap(far, 4, n)
    y_far = swap(far, 2, n)
    state = cross_fwd(gid_of((0, 2)), qcs, (tied(store, far), y_own), chosen, None, False)
    state = cross_fwd(gid_of((4, 8)), qcs, (near, far), chosen, state, False)
    apart = tied(apart, *state)
    y_near = swap(tied(y_own, apart), 4, n)
    y_apart = swap(apart, 2, n)
    state = cross_fwd(gid_of((12, 10)), qcs, (apart, y_far), chosen, state, False)
    state_own, state_other = cross_fwd(gid_of((6, 14)), qcs, (y_near, y_apart), chosen, state, True)[3:]
    pieces = [(store, y_own), (near, y_near), (far, y_far), (apart, y_apart)]
    log_own, of_own, oc, partc = cross_mix_fwd(state_own, core(state_other), cross_mix)
    otherc = other_tp(partc)
    log_other, of_other = cross_merge(state_other, core(tied(state_own, partc)))
    otherc = tied(otherc, of_other)

    vc, uc, lowc, actc, gpc, part3 = ffn_fwd(6, ud, partc, otherc, par, dec_up, dec_down, False, False)
    other3 = other_tp(part3)
    actc_y = swap(actc, 2, n)
    decoded, dlast, dlowc, dhc, gg_last, part4 = last_fwd_back(8, uc, part3, other3, cotangent, par, gpc, dec_up, dec_down)
    dlowc_y = swap(dlowc, 2, n)
    other4 = tied(other_tp(part4), actc_y, dlowc_y)
    dcross, dpacko, gg_cross = cross_mix_back(6, dlast, part4, other4, vc, par, cross_mix)

    dpackos = both(dpacko)
    back = lambda k, extra, after: cross_back(
        gid_of((4 * k, 4 * k + 2)), qcs, dpackos, pieces[k], chosen, extra, k == 3, k == 0, after
    )
    *extra, keep3, send3 = back(3, (of_own, of_other, log_own, log_other), ())
    got3 = swap(send3, 2, n)
    no_y = bits[:1] + bits[2:]
    down_keep, down_sums = joint([(no_y, [((dlowc, dlowc_y), 0, [((actc, actc_y), 0, FF)])], [FF // 2] * 2)], (send3,))
    *extra, keep1, send1 = back(1, extra, (down_keep,))
    got1 = swap(send1, 2, n)
    one = lambda x: (x,)
    (down,) = down_sums(send1)
    up = gradients(bits, [(one(lowc), 0, [(one(dhc), 0, FF)])], (down.send,))
    sum3 = summed(keep3, tied(got3, up.keep))
    apart = swap(sum3, 4, n)
    *extra, keep2, send2 = back(2, extra, (sum3,))
    got2 = swap(send2, 2, n)
    sum1 = summed(keep1, tied(got1, send2))
    near = swap(sum1, 4, n)
    down_z = down.step(sum1)
    _, _, keep0, send0, dq_own, dq_other = back(0, extra, (sum1, down_z))
    got0 = swap(send0, 2, n)
    up_y = up.step(send0)
    sum2 = summed(keep2, tied(got2, send0, up_y), apart)
    far = swap(sum2, 8, n)
    down.hold(far)
    terms = [keep0, got0, near, far]
    bit = n // 2
    while terms[0].shape[0] > 1:
        half = terms[0].shape[0] // 2
        total = functools.reduce(lambda x, y: x + y, [t.astype(F32) for t in terms])
        terms = [total[:half].astype(BF), swap(total[half:].astype(BF), bit, n)]
        bit //= 2

    dqc, partq = cross_q_back(dq_own, core(tied(dq_other, sum2)), cross_query, ())
    otherq = other_tp(partq)
    v2_near, gp1_near, *loaded = load((v2, gp1, enc_up, enc_down), (partq,))
    dkv, part5 = store_back(terms, cross_key, cross_value, (gp1_near,))
    other5 = other_tp(part5)
    up.hold(got0)
    dself, dpackd, gg_self, part6 = attend_back(
        4, dcross, partq, tied(otherq, got0, near, far), vd, par, self_kept, (self_query, self_key, self_value, self_mix), lengths,
    )
    own_keep, own_sums = joint(
        [
            (
                bits,
                [
                    (one(lowd), 0, [(one(dqc), 0, C)]),
                    (one(dpacko), 0, [(one(oc), 0, C)]),
                    (one(dpackd), 0, [(one(self_o), 0, C)]),
                ],
                [C] * 3,
            ),
            (bits, [(one(decoder_in), 0, [(one(dpackd), D, 3 * C)])], [C] * 3),
        ]
    )
    up_z = up.step(other5)
    mixes, own = own_sums(up_z)
    dffn, dlow1, dh1, gg_ffn, part7 = ffn_back(
        2, part5, tied(other5, mixes.send, own.send), v2_near, par, gp1_near, *loaded, ()
    )
    other7 = other_tp(part7)
    z_first = bits[:1] + bits[2:] + bits[1:2]
    ffn_keep, ffn_sums = joint(
        [
            (z_first, [(one(dlow1), 0, [(one(act1), 0, FF)])], [FF // 2] * 2),
            (
                bits,
                [
                    (one(enc_low), 0, [(one(dkv), 0, 2 * C)]),
                    (one(low1), 0, [(one(dh1), 0, FF)]),
                ],
                [2 * C] + [FF // 2] * 2,
            ),
        ],
    )
    down_sum = down.end(ffn_keep)
    up_z = up.step(down_sum)
    mixes_z = mixes.step(up_z)
    down1, up1 = ffn_sums(mixes_z)
    own_z = own.step(up1.send)
    dattn, dpacke, _, part8, gains = attend_back(
        0, dffn, part7, tied(other7, own_z, down1.send), v1, par, enc_kept, (enc_query, enc_key, enc_value, enc_mix), None,
        (gg_ffn, gg_self, gg_cross, gg_last),
    )
    up_sum = up.end(part8)
    mixes_z = mixes.step(up_sum)
    own_z = own.step(mixes_z)
    lanes = jnp.eye(16, 128, dtype=BF)
    last_keep, last_sums = joint(
        [
            (
                bits,
                [
                    (one(encoder_in), 0, [(one(dpacke), D, 3 * C)]),
                    (one(dpacke), 0, [(one(enc_o), 0, C)]),
                    (one(gains), 0, [(one(lanes), 0, 128)]),
                ],
                [2 * C, 2 * C + 128],
            )
        ],
        (own_z,),
    )
    up1_z = up1.step(last_keep)
    (last,) = last_sums(up1_z)
    other6, other8 = other_tp(tied(part6, last.send)), other_tp(tied(part8, last.send))
    down1_z = down1.step(last.send)
    mixes_sum = mixes.end(down1_z)
    own_sum = own.end(mixes_sum)
    up1_z = up1.step(own_sum)
    down1_z = down1.step(up1_z)
    last_z = last.step(down1_z)
    up1_sum = up1.end(last_z)
    down1_sum = down1.end(up1_sum)
    last_z = last.step(down1_sum)
    last_sum = last.end()
    grad_encoder_in = tied(dattn, last_z) + (part8.astype(F32) + other8.astype(F32))
    grad_decoder_in = tied(dself, last_z) + (part6.astype(F32) + other6.astype(F32))

    cut = lambda total, at, width: total[:, at : at + width]
    gain_of = [last_sum[:, 4 * C + i] for i in range(10)]
    return (
        encoded,
        decoded,
        grad_encoder_in,
        grad_decoder_in,
        cut(last_sum, 0, C),
        cut(last_sum, C, C),
        cut(last_sum, 2 * C, C),
        cut(last_sum, 3 * C, C).T,
        gain_of[0],
        gain_of[1],
        cut(up1_sum, 2 * C, FF),
        down1_sum.T,
        gain_of[2],
        gain_of[3],
        cut(own_sum, 0, C),
        cut(own_sum, C, C),
        cut(own_sum, 2 * C, C),
        cut(mixes_sum, 2 * C, C).T,
        gain_of[4],
        gain_of[5],
        cut(mixes_sum, 0, C),
        cut(up1_sum, 0, C),
        cut(up1_sum, C, C),
        cut(mixes_sum, C, C).T,
        gain_of[6],
        gain_of[7],
        up_sum,
        down_sum.T,
        gain_of[8],
        gain_of[9],
    )


def solution(mesh):
    rows, both, cols, down = P("blk", None), P("blk", "tp"), P(None, "tp"), P("tp", None)
    attn = (cols, cols, cols, down, P(), P())
    ffn = (cols, down, P(), P())
    in_specs = (rows, rows, P("blk"), P("blk", "tp", None), both, rows) + attn + ffn + attn + attn + ffn
    mixed = P("tp", "blk")
    grad_attn = (both, both, both, mixed, P("blk"), P("blk"))
    grad_ffn = (both, mixed, P("blk"), P("blk"))
    out_specs = (rows,) * 4 + grad_attn + grad_ffn + grad_attn + grad_attn + grad_ffn
    return jax.shard_map(
        functools.partial(on_device, mesh.shape["blk"]),
        mesh=mesh,
        in_specs=in_specs,
        out_specs=out_specs,
        check_vma=False,
    )
```

```python
import functools

import jax
import jax.numpy as jnp
from jax import lax
from jax.experimental import pallas as pl
from jax.experimental.pallas import tpu as pltpu
from jax.sharding import PartitionSpec as P

HD = 64
PAIR = 2 * HD
NEG_FILL = -1e30
EPS_NORM = 1e-05
SCALE = 0.125
BF = jnp.bfloat16
F32 = jnp.float32
VMEM_LIMIT = 24 * 2**20
HBM = True
ROWS = 64
BAND_ROWS = 16


def nn(a, b):
    return lax.dot_general(a, b, (((1,), (0,)), ((), ())), preferred_element_type=F32)


def nt(a, b):
    return lax.dot_general(a, b, (((1,), (1,)), ((), ())), preferred_element_type=F32)


def tn(a, b):
    return lax.dot_general(a, b, (((0,), (0,)), ((), ())), preferred_element_type=F32)


def behind(body, n_in, n_after):
    if not n_after:
        return body
    return lambda *refs: body(*refs[:n_in], *refs[n_in + n_after :])


class Fetched:
    def __init__(self, far, near, sem):
        self.near, self.shape, self.pending, self.begun = near, near.shape, pltpu.make_async_copy(far, near, sem), False

    def begin(self):
        if not self.begun:
            self.pending.start()
            self.begun = True

    def ready(self):
        if self.pending is not None:
            self.begin()
            self.pending.wait()
            self.pending = None

    def __getitem__(self, at):
        self.ready()
        return self.near[at]


class Kept:
    def __init__(self, far, near, sem):
        self.far, self.near, self.shape, self.sem, self.copies, self.at = far, near, near.shape, sem, [], 0

    def flush(self, upto=None):
        if upto is None and self.at == 0:
            copy = pltpu.make_async_copy(self.near, self.far, self.sem.at[0])
        else:
            upto = self.shape[-1] if upto is None else upto
            if upto == self.at:
                return
            sl = (slice(None), slice(self.at, upto))
            copy = pltpu.make_async_copy(self.near.at[sl], self.far.at[sl], self.sem.at[len(self.copies)])
        self.at = self.shape[-1] if upto is None else upto
        copy.start()
        self.copies.append(copy)

    def wait(self):
        if self.at < self.shape[-1]:
            self.flush()
        for copy in self.copies:
            copy.wait()

    def __getitem__(self, at):
        return self.near[at]

    def __setitem__(self, at, value):
        self.near[at] = value


def flush(*refs, upto=None):
    for ref in refs:
        if isinstance(ref, Kept):
            ref.flush(upto)


class Far:
    def __init__(self, array, late=False):
        self.array, self.late = array, late


def begin(*refs):
    for ref in refs:
        if isinstance(ref, Fetched):
            ref.begin()


def whole(body, name, outs, *args, smem=0, after=()):
    far_in = [i for i, a in enumerate(args) if isinstance(a, Far)]
    late = [i for i in far_in if args[i].late]
    far_out = [i for i, o in enumerate(outs) if len(o) > 2]
    args = [pltpu.with_memory_space_constraint(a.array, pltpu.HBM) if isinstance(a, Far) else a for a in args]
    n_in, n_out, n_after = len(args), len(outs), len(after)

    def run(*refs):
        ins = list(refs[:n_in])
        results = list(refs[n_in + n_after : n_in + n_after + n_out])
        scratch = refs[n_in + n_after + n_out :]
        for k, i in enumerate(far_in):
            ins[i] = Fetched(ins[i], scratch[k], scratch[-1].at[k, 0])
            if i not in late:
                ins[i].begin()
        for k, i in enumerate(far_out):
            results[i] = Kept(results[i], scratch[len(far_in) + k], scratch[-1].at[len(far_in) + k])
        body(*ins, *results)
        for i in far_in:
            ins[i].ready()
        for i in far_out:
            results[i].wait()

    moves = len(far_in) + len(far_out)
    scratch = [pltpu.VMEM(args[i].shape, args[i].dtype) for i in far_in]
    scratch += [pltpu.VMEM(outs[i][0], outs[i][1]) for i in far_out]
    if moves:
        scratch.append(pltpu.SemaphoreType.DMA((moves, 8)))
    in_specs = [pl.BlockSpec(memory_space=pltpu.SMEM if i < smem else pltpu.VMEM) for i in range(n_in)]
    out_specs = [pl.BlockSpec(memory_space=pltpu.VMEM) for _ in outs]
    for i in far_in:
        in_specs[i] = pl.BlockSpec(memory_space=pltpu.HBM)
    for i in far_out:
        out_specs[i] = pl.BlockSpec(memory_space=pltpu.HBM)
    return pl.pallas_call(
        run,
        name=name,
        out_shape=[pltpu.HBM(o[0], o[1]) if len(o) > 2 else jax.ShapeDtypeStruct(o[0], o[1]) for o in outs],
        in_specs=in_specs + [pl.BlockSpec(memory_space=pl.ANY)] * n_after,
        out_specs=out_specs,
        scratch_shapes=scratch,
        compiler_params=pltpu.CompilerParams(vmem_limit_bytes=VMEM_LIMIT),
        cost_estimate=pl.CostEstimate(flops=1, bytes_accessed=1, transcendentals=0),
    )(*args, *after)


def load_body(n, *refs):
    sems = refs[-1]
    copies = [pltpu.make_async_copy(refs[i], refs[n + i], sems.at[i]) for i in range(n)]
    for copy in copies:
        copy.start()
    for copy in copies:
        copy.wait()


def load(arrays, after):
    n, n_after = len(arrays), len(after)
    return pl.pallas_call(
        behind(functools.partial(load_body, n), n, n_after),
        name="load",
        out_shape=[pltpu.VMEM(a.shape, a.dtype) for a in arrays],
        in_specs=[pl.BlockSpec(memory_space=pltpu.HBM)] * n + [pl.BlockSpec(memory_space=pl.ANY)] * n_after,
        out_specs=[pl.BlockSpec(memory_space=pltpu.VMEM)] * n,
        scratch_shapes=[pltpu.SemaphoreType.DMA((n,))],
        compiler_params=pltpu.CompilerParams(vmem_limit_bytes=VMEM_LIMIT),
        cost_estimate=pl.CostEstimate(flops=1, bytes_accessed=1, transcendentals=0),
    )(*[pltpu.with_memory_space_constraint(a, pltpu.HBM) for a in arrays], *after)


def norm_parts(v):
    center = v - jnp.mean(v, -1, keepdims=True)
    r = lax.rsqrt(jnp.mean(center * center, -1, keepdims=True) + EPS_NORM)
    return center * r, r


def norm_back(v, gain, dy):
    xhat, r = norm_parts(v)
    gdy = gain * dy
    dv = r * (gdy - jnp.mean(gdy, -1, keepdims=True) - xhat * jnp.mean(gdy * xhat, -1, keepdims=True))
    return dv, jnp.sum(dy * xhat, 0, keepdims=True), jnp.sum(dy, 0, keepdims=True)


def row_of(par_ref, i):
    return par_ref[i : i + 1, :].astype(F32)


def low_half(shape, dim):
    return lax.broadcasted_iota(jnp.int32, shape, dim) < HD


def stacked(t2):
    first = low_half(t2.shape, 1)
    zero = jnp.zeros_like(t2)
    return jnp.concatenate([jnp.where(first, t2, zero), jnp.where(first, zero, t2)], 0)


def unstacked(tT):
    R = tT.shape[1] // 2
    first = low_half((PAIR, R), 0)
    return jnp.where(first, tT[:, :R], tT[:, R:]).T


def causal_mask(R, length):
    key = lax.broadcasted_iota(jnp.int32, (R, 2 * R), 0)
    lane = lax.broadcasted_iota(jnp.int32, (R, 2 * R), 1)
    query = jnp.where(lane >= R, lane - R, lane)
    return (key <= query) & (key < length)


def local_weights(k2, qq, allowed):
    sT = nt(k2, qq)
    if allowed is not None:
        sT = jnp.where(allowed, sT, NEG_FILL)
    p = jnp.exp(sT - jnp.max(sT, 0, keepdims=True))
    return p * (1.0 / jnp.sum(p, 0, keepdims=True))


def gelu_parts(h):
    cdf = 0.5 * (1.0 + lax.erf(h * 0.7071067811865476))
    pdf = 0.3989422804014327 * jnp.exp(-0.5 * h * h)
    return h * cdf, cdf + h * pdf


def attend_fwd_body(causal, *refs):
    if causal:
        len_ref, refs = refs[0], refs[1:]
    x_ref, wq, wk, wv, wm, q_ref, k_ref, v_ref, o_ref, part_ref = refs
    x = x_ref[...]
    R = x.shape[0]
    q_ref[...] = (nn(x, wq[...]) * SCALE).astype(BF)
    k_ref[...] = nn(x, wk[...]).astype(BF)
    v_ref[...] = nn(x, wv[...]).astype(BF)
    flush(q_ref, k_ref, v_ref)
    allowed = causal_mask(R, len_ref[0]) if causal else None
    for c in range(0, q_ref.shape[1], PAIR):
        sl = slice(c, c + PAIR)
        w = local_weights(k_ref[:, sl], stacked(q_ref[:, sl]), allowed).astype(BF)
        o_ref[:, sl] = unstacked(tn(v_ref[:, sl], w)).astype(BF)
    flush(o_ref)
    part_ref[...] = nn(o_ref[...], wm[...]).astype(BF)


def attend_fwd(x, wq, wk, wv, wm, length=None, after=(), fetch=False):
    R, D = x.shape
    C = wq.shape[1]
    args = (x, wq, wk, wv, wm)
    if fetch:
        args = tuple(Far(a) for a in args)
    causal = length is not None
    if causal:
        args = (length,) + args
    return whole(
        functools.partial(attend_fwd_body, causal),
        "attend_fwd",
        [((R, C), BF, HBM)] * 4 + [((R, D), BF)],
        *args,
        smem=int(causal),
        after=after,
    )


def ffn_fwd_body(g, x_ref, own, oth, par, wu, wd, v_ref, u_ref, low_ref, act_ref, gp_ref, part_ref):
    R, D = x_ref.shape
    gain, shift = row_of(par, g), row_of(par, g + 1)
    for r in range(0, R, ROWS):
        s = slice(r, r + ROWS)
        v = x_ref[s, :].astype(F32) + (own[s, :].astype(F32) + oth[s, :].astype(F32))
        xhat, _ = norm_parts(v)
        u = xhat * gain + shift
        v_ref[s, :] = v
        u_ref[s, :] = u
        low_ref[s, :] = u.astype(BF)
    flush(v_ref, low_ref)
    begin(wd)
    low = low_ref[...]
    for c in range(0, wu.shape[1], 256):
        sl = slice(c, c + 256)
        a, gp = gelu_parts(nn(low, wu[:, sl]))
        act_ref[:, sl] = a.astype(BF)
        gp_ref[:, sl] = gp.astype(BF)
        flush(act_ref, gp_ref, upto=c + 256)
    part_ref[...] = nn(act_ref[...], wd[...]).astype(BF)


def ffn_fwd(g, x, own, oth, par, wu, wd, fetch, keep):
    R, D = x.shape
    FF = wu.shape[1]
    kept = (HBM,) if keep else ()
    return whole(
        functools.partial(ffn_fwd_body, g),
        "ffn_fwd",
        [((R, D), F32, HBM), ((R, D), F32), ((R, D), BF, HBM), ((R, FF), BF, *kept), ((R, FF), BF, HBM), ((R, D), BF)],
        x, own, oth, par, *((Far(wu), Far(wd, True)) if fetch else (wu, wd)),
    )


def order_matrix(R):
    t = lax.broadcasted_iota(jnp.int32, (R, R), 0)
    col = lax.broadcasted_iota(jnp.int32, (R, R), 1)
    src = jnp.where(t < R // 2, 2 * t, 2 * t - (R - 1))
    return (src == col).astype(F32).astype(BF)


def store_body(g, u_ref, own, oth, par, wk, wv, v_ref, low_ref, kv_ref):
    R = u_ref.shape[0]
    gain, shift = row_of(par, g), row_of(par, g + 1)
    low = []
    for r in range(0, R, ROWS):
        s = slice(r, r + ROWS)
        v = u_ref[s, :] + (own[s, :].astype(F32) + oth[s, :].astype(F32))
        xhat, _ = norm_parts(v)
        v_ref[s, :] = v
        low.append((xhat * gain + shift).astype(BF))
    low_ref[...] = nn(order_matrix(R), jnp.concatenate(low, 0)).astype(BF)
    low = low_ref[...]
    kv_ref[0] = nn(low, wk[...]).astype(BF)
    kv_ref[1] = nn(low, wv[...]).astype(BF)


def store_fwd(g, u, own, oth, par, wk, wv):
    R, D = u.shape
    C = wk.shape[1]
    return whole(
        functools.partial(store_body, g),
        "store_fwd",
        [((R, D), F32), ((R, D), BF), ((2, R, C), BF)],
        u, own, oth, par, wk, wv,
    )


def norm_body(g, v_ref, par, out_ref):
    for r in range(0, v_ref.shape[0], ROWS):
        s = slice(r, r + ROWS)
        xhat, _ = norm_parts(v_ref[s, :])
        out_ref[s, :] = xhat * row_of(par, g) + row_of(par, g + 1)


def norm_of(g, v, par, after):
    return whole(functools.partial(norm_body, g), "norm_of", [(v.shape, F32, HBM)], v, par, after=after)[0]


def cross_q_body(g, x_ref, own, oth, par, wq, v_ref, u_ref, low_ref, q_ref):
    R = x_ref.shape[0]
    gain, shift = row_of(par, g), row_of(par, g + 1)
    for r in range(0, R, ROWS):
        s = slice(r, r + ROWS)
        v = x_ref[s, :].astype(F32) + (own[s, :].astype(F32) + oth[s, :].astype(F32))
        xhat, _ = norm_parts(v)
        u = xhat * gain + shift
        v_ref[s, :] = v
        u_ref[s, :] = u
        low_ref[s, :] = u.astype(BF)
    flush(v_ref, u_ref, low_ref)
    q_ref[...] = (nn(low_ref[...], wq[...]) * SCALE).astype(BF)


def cross_q(g, x, own, oth, par, wq):
    R, D = x.shape
    C = wq.shape[1]
    return whole(
        functools.partial(cross_q_body, g),
        "cross_q",
        [((R, D), F32, HBM), ((R, D), F32, HBM), ((R, D), BF, HBM), ((R, C), BF)],
        x, own, oth, par, wq,
    )


def pick_rows_body(from_ref, band_ref, *out_refs):
    picked = from_ref.shape[2]
    for pair, out_ref in enumerate(out_refs):
        for h in range(2):
            out_ref[h, :picked] = ((from_ref[2 * pair + h] & 1) + 1).astype(F32).T.astype(BF)
        band = band_ref[2 * pair : 2 * pair + 2, :].astype(F32)
        for h in range(2):
            out_ref[h, picked:] = jnp.broadcast_to(band[h : h + 1], (BAND_ROWS, band.shape[1])).astype(BF)


def pick_rows(retrieved, band_start, after):
    R, heads, picked = retrieved.shape
    outs = [((2, picked + BAND_ROWS, R), BF)] * (heads // 2)
    args = (Far(retrieved.transpose(1, 0, 2)), band_start.T)
    return whole(pick_rows_body, "pick_rows", outs, *args, after=after)


def picks_body(pairs, core_ref, *refs):
    own, other, out_ref = refs[:pairs], refs[pairs : 2 * pairs], refs[2 * pairs]
    g = (2 * pl.program_id(0) + core_ref[0]).astype(F32)
    _, rows, R = own[0].shape
    picked = rows - BAND_ROWS
    half = out_ref.shape[2]
    for h in range(2 * pairs):
        for i, from_ref in enumerate((own[h // 2], other[h // 2])):
            rel = g - from_ref[h % 2, picked : picked + BAND_ROWS, :].astype(F32)[:1]
            got = None
            for b in range(picked // half):
                here = (rel == b).astype(F32).astype(BF) * from_ref[h % 2, b * half : (b + 1) * half, :]
                got = here if got is None else got + here
            at = (2 * (h % 2) + i) * R
            out_ref[0, h // 2, :, at : at + R] = got


def picks(core_index, pick, pick_other, groups, half):
    pairs = len(pick)
    _, rows, R = pick[0].shape
    return pl.pallas_call(
        functools.partial(picks_body, pairs),
        name="picks",
        grid=(groups,),
        out_shape=pltpu.HBM((groups, pairs, half, 4 * R), BF),
        in_specs=[pl.BlockSpec(memory_space=pltpu.SMEM)]
        + [pl.BlockSpec((2, rows, R), lambda g: (0, 0, 0))] * (2 * pairs),
        out_specs=pl.BlockSpec((1, pairs, half, 4 * R), lambda g: (g, 0, 0, 0)),
        compiler_params=pltpu.CompilerParams(vmem_limit_bytes=VMEM_LIMIT),
        cost_estimate=pl.CostEstimate(flops=1, bytes_accessed=1, transcendentals=0),
    )(core_index, *pick, *pick_other)


def chosen_scores(k2, qq, a):
    half = a.shape[0]
    sT = nt(k2, qq)
    s = jnp.where(a > 1.5, sT[half:], sT[:half])
    return jnp.where(a < 0.5, NEG_FILL, s)


def spread(p, a):
    zero = jnp.zeros_like(p)
    even = jnp.where(a == 1.0, p, zero).astype(BF)
    odd = jnp.where(a == 2.0, p, zero).astype(BF)
    return jnp.concatenate([even, odd], 0)


def of_both(own, other):
    return stacked(jnp.concatenate([own, other], 0))


def own_lanes(t):
    R = t.shape[1] // 4
    return jnp.concatenate([t[:, :R], t[:, 2 * R : 3 * R]], 1)


def other_lanes(t):
    R = t.shape[1] // 4
    return jnp.concatenate([t[:, R : 2 * R], t[:, 3 * R :]], 1)


def all_lanes(own, other):
    R = own.shape[1] // 2
    return jnp.concatenate([own[:, :R], other[:, :R], own[:, R:], other[:, R:]], 1)


def cross_fwd_body(first, last, gid_ref, q_ref, q_other, *refs):
    kv, a_refs, refs = refs[:2], refs[2:4], refs[4:]
    if not first:
        m_in, l_in, acc_in = refs[:3]
        refs = refs[3:]
    m_ref, l_ref, acc_ref = refs[:3]

    @pl.when(pl.program_id(0) == 0)
    def _():
        if first:
            m_ref[...] = jnp.full(m_ref.shape, NEG_FILL, F32)
            l_ref[...] = jnp.zeros(l_ref.shape, F32)
            acc_ref[...] = jnp.zeros(acc_ref.shape, F32)
        else:
            m_ref[...] = m_in[...]
            l_ref[...] = l_in[...]
            acc_ref[...] = acc_in[...]

    pairs = acc_ref.shape[0]
    for hp in range(pairs):
        sl = slice(hp * PAIR, (hp + 1) * PAIR)
        qq = of_both(q_ref[:, sl], q_other[:, sl])
        codes = [a_refs[j][0, hp].astype(F32) for j in range(2)]
        scores = [chosen_scores(kv[j][0, 0, :, sl], qq, codes[j]) for j in range(2)]
        old = m_ref[hp : hp + 1, :]
        top = functools.reduce(jnp.maximum, [jnp.max(s, 0, keepdims=True) for s in scores], old)
        fade = jnp.exp(old - top)
        total = l_ref[hp : hp + 1, :] * fade
        acc = acc_ref[hp] * fade
        for j in range(2):
            a = codes[j]
            p = jnp.where(a < 0.5, 0.0, jnp.exp(scores[j] - top))
            total = total + jnp.sum(p, 0, keepdims=True)
            acc = acc + tn(kv[j][0, 1, :, sl], spread(p, a))
        m_ref[hp : hp + 1, :] = top
        l_ref[hp : hp + 1, :] = total
        acc_ref[hp] = acc

    if last:
        own_ref, other_ref = refs[3:]

        @pl.when(pl.program_id(0) == pl.num_programs(0) - 1)
        def _():
            for out, lanes in ((own_ref, own_lanes), (other_ref, other_lanes)):
                out[pairs * PAIR :, :] = jnp.zeros((8, out.shape[1]), F32)
                for hp in range(pairs):
                    out[hp * PAIR : (hp + 1) * PAIR, :] = lanes(acc_ref[hp])
                    out[pairs * PAIR + hp : pairs * PAIR + hp + 1, :] = lanes(m_ref[hp : hp + 1, :])
                    out[pairs * PAIR + 4 + hp : pairs * PAIR + 5 + hp, :] = lanes(l_ref[hp : hp + 1, :])


def kv_specs(kv, a):
    rows, C = kv[0].shape[2:]
    specs = [pl.BlockSpec((1, 2, rows, C), lambda i, gid: (i, 0, 0, 0)) for _ in range(2)]
    for j in range(2):
        specs.append(
            pl.BlockSpec((1,) + a.shape[1:], functools.partial(lambda j, i, gid: (gid[2 * i + j], 0, 0, 0), j))
        )
    return specs


def fixed(shape):
    return pl.BlockSpec(shape, lambda i, gid: (0,) * len(shape))


def cross_fwd(gid, q, kv, a, state, last):
    R, C = q[0].shape
    pairs = C // PAIR
    hi, _, rows, _ = kv[0].shape
    shapes = [(8, 4 * R), (8, 4 * R), (pairs, PAIR, 4 * R)]
    first = state is None
    state = () if first else tuple(state)
    if last:
        shapes += [(C + 8, 2 * R)] * 2
    return pl.pallas_call(
        functools.partial(cross_fwd_body, first, last),
        name="cross_fwd",
        grid_spec=pltpu.PrefetchScalarGridSpec(
            num_scalar_prefetch=1,
            grid=(hi,),
            in_specs=[fixed(q[0].shape)] * 2 + kv_specs(kv, a) + [fixed(s.shape) for s in state],
            out_specs=[fixed(s) for s in shapes],
        ),
        out_shape=[jax.ShapeDtypeStruct(s, F32) for s in shapes],
        compiler_params=pltpu.CompilerParams(vmem_limit_bytes=VMEM_LIMIT),
        cost_estimate=pl.CostEstimate(flops=1, bytes_accessed=1, transcendentals=0),
    )(gid, *q, *kv, *([pltpu.with_memory_space_constraint(a, pltpu.HBM)] * 2), *state)


def merged(own_ref, got_ref, hp, C):
    sl = slice(hp * PAIR, (hp + 1) * PAIR)
    m, l = slice(C + hp, C + hp + 1), slice(C + 4 + hp, C + 5 + hp)
    m1, m2 = own_ref[m, :], got_ref[m, :]
    top = jnp.maximum(m1, m2)
    f1, f2 = jnp.exp(m1 - top), jnp.exp(m2 - top)
    total = own_ref[l, :] * f1 + got_ref[l, :] * f2
    return top + jnp.log(total), unstacked((own_ref[sl, :] * f1 + got_ref[sl, :] * f2) * (1.0 / total))


def cross_mix_body(own_ref, got_ref, wm, log_ref, of_ref, o_ref, part_ref):
    C = wm.shape[0]
    log_ref[...] = jnp.zeros(log_ref.shape, F32)
    for hp in range(C // PAIR):
        sl = slice(hp * PAIR, (hp + 1) * PAIR)
        log_ref[hp : hp + 1, :], o = merged(own_ref, got_ref, hp, C)
        of_ref[:, sl] = o
        o_ref[:, sl] = o.astype(BF)
    part_ref[...] = nn(o_ref[...], wm[...]).astype(BF)


def cross_mix_fwd(own, got, wm):
    R2 = own.shape[1]
    C, D = wm.shape
    R = R2 // 2
    return whole(
        cross_mix_body,
        "cross_mix",
        [((8, R2), F32), ((R, C), F32), ((R, C), BF), ((R, D), BF)],
        own, got, wm,
    )


def cross_merge_body(own_ref, got_ref, log_ref, of_ref):
    C = of_ref.shape[1]
    log_ref[...] = jnp.zeros(log_ref.shape, F32)
    for hp in range(C // PAIR):
        log_ref[hp : hp + 1, :], of_ref[:, hp * PAIR : (hp + 1) * PAIR] = merged(own_ref, got_ref, hp, C)


def cross_merge(own, got):
    rows, R2 = own.shape
    return whole(cross_merge_body, "cross_merge", [((8, R2), F32), ((R2 // 2, rows - 8), F32)], own, got)


def ffn_back_rest(dlow_ref, gp_ref, wu, wd, dh_ref, part_ref):
    low = dlow_ref[...]
    for c in range(0, wu.shape[1], 256):
        sl = slice(c, c + 256)
        dh_ref[:, sl] = (nt(low, wd[sl, :]) * gp_ref[:, sl].astype(F32)).astype(BF)
    part_ref[...] = nt(dh_ref[...], wu[...]).astype(BF)


def last_body(g, u_ref, own, oth, cot, par, gp_ref, wu, wd, out_ref, dv_ref, dlow_ref, dh_ref, gg_ref, part_ref):
    R, D = u_ref.shape
    gain, shift = row_of(par, g), row_of(par, g + 1)
    gg_ref[...] = jnp.zeros(gg_ref.shape, F32)
    for r in range(0, R, ROWS):
        s = slice(r, r + ROWS)
        v = u_ref[s, :] + (own[s, :].astype(F32) + oth[s, :].astype(F32))
        xhat, _ = norm_parts(v)
        out_ref[s, :] = xhat * gain + shift
        dv, dg, db = norm_back(v, gain, cot[s, :].astype(F32))
        dv_ref[s, :] = dv
        dlow_ref[s, :] = dv.astype(BF)
        gg_ref[0:1, :] += dg
        gg_ref[1:2, :] += db
    flush(gg_ref, out_ref)
    ffn_back_rest(dlow_ref, gp_ref, wu, wd, dh_ref, part_ref)


def last_fwd_back(g, u, own, oth, cot, par, gp, wu, wd):
    R, D = u.shape
    FF = wu.shape[1]
    return whole(
        functools.partial(last_body, g),
        "last_fwd_back",
        [((R, D), F32, HBM), ((R, D), F32), ((R, D), BF), ((R, FF), BF), ((8, D), F32, HBM), ((R, D), BF)],
        u, own, oth, cot, par, gp, wu, wd,
    )


def ffn_back_body(g, own, oth, v_ref, par, gp_ref, wu, wd, dv_ref, dlow_ref, dh_ref, gg_ref, part_ref):
    R, D = v_ref.shape
    gain = row_of(par, g)
    gg_ref[...] = jnp.zeros(gg_ref.shape, F32)
    for r in range(0, R, ROWS):
        s = slice(r, r + ROWS)
        dy = own[s, :].astype(F32) + oth[s, :].astype(F32)
        dv, dg, db = norm_back(v_ref[s, :], gain, dy)
        dv_ref[s, :] = dv
        dlow_ref[s, :] = dv.astype(BF)
        gg_ref[0:1, :] += dg
        gg_ref[1:2, :] += db
    flush(gg_ref)
    ffn_back_rest(dlow_ref, gp_ref, wu, wd, dh_ref, part_ref)


def ffn_back(g, own, oth, v, par, gp, wu, wd, after):
    R, D = v.shape
    FF = wu.shape[1]
    return whole(
        functools.partial(ffn_back_body, g),
        "ffn_back",
        [((R, D), F32), ((R, D), BF), ((R, FF), BF), ((8, D), F32, HBM), ((R, D), BF)],
        own, oth, v, par, gp, wu, wd,
        after=after,
    )


def branch_back(g, dres, own, oth, v_ref, par, dv_ref, dlow_ref, gg_ref):
    R, D = v_ref.shape
    gain = row_of(par, g)
    gg_ref[...] = jnp.zeros(gg_ref.shape, F32)
    for r in range(0, R, ROWS):
        s = slice(r, r + ROWS)
        dy = dres[s, :] + (own[s, :].astype(F32) + oth[s, :].astype(F32))
        dv, dg, db = norm_back(v_ref[s, :], gain, dy)
        dv_ref[s, :] = dv
        dlow_ref[s, :D] = dv.astype(BF)
        gg_ref[0:1, :] += dg
        gg_ref[1:2, :] += db


def cross_mix_back_body(g, dres, own, oth, v_ref, par, wm, dv_ref, pack_ref, gg_ref):
    branch_back(g, dres, own, oth, v_ref, par, dv_ref, pack_ref, gg_ref)
    flush(dv_ref, gg_ref)
    D = v_ref.shape[1]
    pack_ref[:, D:] = nt(pack_ref[:, :D], wm[...]).astype(BF)


def cross_mix_back(g, dres, own, oth, v, par, wm):
    R, D = v.shape
    C = wm.shape[0]
    return whole(
        functools.partial(cross_mix_back_body, g),
        "cross_mix_back",
        [((R, D), F32, HBM), ((R, D + C), BF), ((8, D), F32, HBM)],
        dres, own, oth, v, par, wm,
    )


def cross_back_body(first, last, gid_ref, q_ref, q_other, do_pack, do_pack_other, *refs):
    C = q_ref.shape[1]
    skip = do_pack.shape[1] - C
    do_ref, do_other = do_pack.at[:, skip:], do_pack_other.at[:, skip:]
    kv, a_refs, refs = refs[:2], refs[2:4], refs[4:]
    if first:
        of_ref, of_other, log_own, log_other = refs[:4]
        dq_ref, stat_ref, keep_ref, send_ref = refs[4:8]
    else:
        dq_in, stat_in = refs[:2]
        dq_ref, stat_ref, keep_ref, send_ref = refs[2:6]
    pairs = dq_ref.shape[0]

    @pl.when(pl.program_id(0) == 0)
    def _():
        if not first:
            dq_ref[...] = dq_in[...]
            stat_ref[...] = stat_in[...]
            return
        dq_ref[...] = jnp.zeros(dq_ref.shape, F32)
        stat_ref[...] = jnp.zeros(stat_ref.shape, F32)
        stat_ref[0:8, :] = all_lanes(log_own[...], log_other[...])
        for hp in range(pairs):
            sl = slice(hp * PAIR, (hp + 1) * PAIR)
            sums = []
            for d, o in ((do_ref, of_ref), (do_other, of_other)):
                prod = (d[:, sl].astype(F32) * o[:, sl]).T
                sums.append([jnp.sum(prod[:HD], 0, keepdims=True), jnp.sum(prod[HD:], 0, keepdims=True)])
            stat_ref[8 + hp : 9 + hp, :] = jnp.concatenate([sums[0][0], sums[1][0], sums[0][1], sums[1][1]], 1)

    for hp in range(pairs):
        sl = slice(hp * PAIR, (hp + 1) * PAIR)
        qq = of_both(q_ref[:, sl], q_other[:, sl])
        dd = of_both(do_ref[:, sl], do_other[:, sl])
        log_total = stat_ref[hp : hp + 1, :]
        delta = stat_ref[8 + hp : 9 + hp, :]
        dq = dq_ref[hp]
        for j, out_ref in enumerate((keep_ref, send_ref)):
            a = a_refs[j][0, hp].astype(F32)
            half = a.shape[0]
            k2 = kv[j][0, 0, :, sl]
            p = jnp.exp(chosen_scores(k2, qq, a) - log_total)
            daT = nt(kv[j][0, 1, :, sl], dd)
            ds = p * (jnp.where(a > 1.5, daT[half:], daT[:half]) - delta)
            dsT = spread(ds, a)
            out_ref[0, 0, :, sl] = nn(dsT, qq).astype(BF)
            out_ref[0, 1, :, sl] = nn(spread(p, a), dd).astype(BF)
            dq = dq + tn(k2, dsT)
        dq_ref[hp] = dq

    if last:
        own_ref, other_ref = refs[-2:]

        @pl.when(pl.program_id(0) == pl.num_programs(0) - 1)
        def _():
            for hp in range(pairs):
                own_ref[hp] = own_lanes(dq_ref[hp])
                other_ref[hp] = other_lanes(dq_ref[hp]).astype(BF)


def cross_back(gid, q, do, kv, a, extra, first, last, after=()):
    R, C = q[0].shape
    pairs = C // PAIR
    hi, _, rows, _ = kv[0].shape
    grad_spec = pl.BlockSpec((1, 2, rows, C), lambda i, gid: (i, 0, 0, 0))
    shapes = [(pairs, PAIR, 4 * R), (16, 4 * R)]
    out_specs = [fixed(s) for s in shapes] + [grad_spec] * 2
    out_shape = [jax.ShapeDtypeStruct(s, F32) for s in shapes] + [jax.ShapeDtypeStruct(kv[0].shape, BF)] * 2
    if last:
        out_specs += [fixed((pairs, PAIR, 2 * R))] * 2
        out_shape += [jax.ShapeDtypeStruct((pairs, PAIR, 2 * R), d) for d in (F32, BF)]
    return pl.pallas_call(
        behind(functools.partial(cross_back_body, first, last), 9 + len(extra), len(after)),
        name="cross_back",
        grid_spec=pltpu.PrefetchScalarGridSpec(
            num_scalar_prefetch=1,
            grid=(hi,),
            in_specs=[fixed(q[0].shape)] * 2
            + [fixed(do[0].shape)] * 2
            + kv_specs(kv, a)
            + [fixed(e.shape) for e in extra]
            + [pl.BlockSpec(memory_space=pl.ANY)] * len(after),
            out_specs=out_specs,
        ),
        out_shape=out_shape,
        compiler_params=pltpu.CompilerParams(vmem_limit_bytes=VMEM_LIMIT),
        cost_estimate=pl.CostEstimate(flops=1, bytes_accessed=1, transcendentals=0),
    )(gid, *q, *do, *kv, *([pltpu.with_memory_space_constraint(a, pltpu.HBM)] * 2), *extra, *after)


def cross_q_back_body(dq_own, dq_got, wq, dq_ref, part_ref):
    for hp in range(dq_own.shape[0]):
        sl = slice(hp * PAIR, (hp + 1) * PAIR)
        dq_ref[:, sl] = (unstacked(dq_own[hp] + dq_got[hp].astype(F32)) * SCALE).astype(BF)
    flush(dq_ref)
    part_ref[...] = nt(dq_ref[...], wq[...]).astype(BF)


def cross_q_back(dq, got, wq, after):
    D, C = wq.shape
    R = dq.shape[2] // 2
    return whole(cross_q_back_body, "cross_q_back", [((R, C), BF), ((R, D), BF)], dq, got, wq, after=after)


def store_back_body(spread_at, *refs):
    n = len(refs) - 4
    wk, wv, dkv_ref, part_ref = refs[n:]
    R, C = dkv_ref.shape[0], dkv_ref.shape[1] // 2
    for i in range(2):
        parts = [t[0, i] for t in refs[:spread_at]]
        if spread_at < n:
            parts.append(refs[spread_at + i][0, 0])
        total = functools.reduce(lambda x, y: x + y, [t.astype(F32) for t in parts])
        dkv_ref[:, i * C : (i + 1) * C] = total.astype(BF)
    part = nt(dkv_ref[:, :C], wk[...]) + nt(dkv_ref[:, C:], wv[...])
    part_ref[...] = tn(order_matrix(R), part.astype(BF)).astype(BF)


def store_back(terms, wk, wv, after):
    D, C = wk.shape
    R = terms[0].shape[2]
    full = [t for t in terms if not isinstance(t, list)]
    halves = [h for t in terms if isinstance(t, list) for h in t]
    return whole(
        functools.partial(store_back_body, len(full)),
        "store_back",
        [((R, 2 * C), BF), ((R, D), BF)],
        *full, *halves, wk, wv,
        after=after,
    )


def attend_back_body(causal, g, n_more, *refs):
    if causal:
        len_ref, refs = refs[0], refs[1:]
    (dres, own, oth, v1_ref, par, q_ref, k_ref, v_ref, wq, wk, wv, wm) = refs[:12]
    R, D = v1_ref.shape
    dv_ref, pack_ref, gg_ref, part_ref = refs[12 + n_more : 16 + n_more]
    branch_back(g, dres, own, oth, v1_ref, par, dv_ref, pack_ref, gg_ref)
    flush(dv_ref, gg_ref)
    if n_more:
        gains_ref = refs[-1]
        rows = [gg_ref[0:2, :]] + [other[0:2, :] for other in refs[12 : 12 + n_more]]
        rows.append(jnp.zeros((gains_ref.shape[0] - 2 - 2 * n_more, D), F32))
        gains_ref[...] = jnp.concatenate(rows, 0).astype(BF)
        flush(gains_ref)
    C = wq.shape[1]
    do = nt(pack_ref[:, :D], wm[...]).astype(BF)
    allowed = causal_mask(R, len_ref[0]) if causal else None
    for c in range(0, C, PAIR):
        sl = slice(c, c + PAIR)
        k2 = k_ref[:, sl]
        qq = stacked(q_ref[:, sl])
        dd = stacked(do[:, sl])
        w = local_weights(k2, qq, allowed)
        daT = nt(v_ref[:, sl], dd)
        ds = (w * (daT - jnp.sum(w * daT, 0, keepdims=True))).astype(BF)
        at = D + c
        pack_ref[:, at : at + PAIR] = (unstacked(tn(k2, ds)) * SCALE).astype(BF)
        pack_ref[:, at + C : at + C + PAIR] = nn(ds, qq).astype(BF)
        pack_ref[:, at + 2 * C : at + 2 * C + PAIR] = nn(w.astype(BF), dd).astype(BF)
    flush(pack_ref)
    part = nt(pack_ref[:, D : D + C], wq[...]) + nt(pack_ref[:, D + C : D + 2 * C], wk[...])
    part_ref[...] = (part + nt(pack_ref[:, D + 2 * C :], wv[...])).astype(BF)


def attend_back(g, dres, own, oth, v1, par, kept, weights, length=None, more=(), after=()):
    R, D = v1.shape
    C = kept[0].shape[1]
    args = (dres, own, oth, v1, par, *kept, *weights, *more)
    causal = length is not None
    if causal:
        args = (length,) + args
    return whole(
        functools.partial(attend_back_body, causal, g, len(more)),
        "attend_back",
        [((R, D), F32, HBM), ((R, D + 3 * C), BF), ((8, D), F32, HBM), ((R, D), BF)]
        + [((16, D), BF)] * bool(more),
        *args,
        smem=int(causal),
        after=after,
    )


def weight_body(plan, chunks, sources, n_idx, *refs):
    idx_refs, ins, outs = refs[:n_idx], refs[n_idx : -2 * len(chunks)], refs[-2 * len(chunks) :]
    half = outs[0].shape[0]
    chunk, at, takes = 0, 0, {}
    for part, a_at, off, D, grads in plan:
        if part not in takes:
            spot = lax.broadcasted_iota(jnp.int32, (2 * half, D), 1) == idx_refs[part][...]
            takes[part] = spot.astype(F32).astype(BF)
        parts = [nt(takes[part], ins[a_at + i][:, off : off + D]) for i in range(sources)]
        aT = jnp.concatenate(parts, 1).astype(BF)
        for d_at, d_off, width in grads:
            step = 384 if width % 384 == 0 else 128
            for c in range(d_off, d_off + width, step):
                dy = jnp.concatenate([ins[d_at + i][:, c : c + step] for i in range(sources)], 0)
                got = nn(aT, dy)
                outs[2 * chunk][:, at : at + step] = got[:half].astype(BF)
                outs[2 * chunk + 1][:, at : at + step] = got[half:].astype(BF)
                at += step
                if at == chunks[chunk]:
                    chunk, at = chunk + 1, 0


def weight_grads(idxs, D, term_lists, chunks, after=()):
    ins, plan = [], []
    for part, terms in enumerate(term_lists):
        for a, off, grads in terms:
            at = len(ins)
            ins += list(a)
            ds = []
            for d, d_off, w in grads:
                ds.append((len(ins), d_off, w))
                ins += list(d)
            plan.append((part, at, off, D, ds))
    half = idxs[0].shape[0] // 2
    return whole(
        functools.partial(weight_body, plan, chunks, len(term_lists[0][0][0]), len(idxs)),
        "weight_grads",
        [((half, w), BF) for w in chunks for _ in range(2)],
        *idxs,
        *ins,
        after=after,
    )


def swap(x, bit, n):
    return lax.ppermute(x, "blk", [(i, i ^ bit) for i in range(n)])


def tied(x, *before):
    return lax.optimization_barrier((x, *before))[0]


def other_tp(x):
    return lax.ppermute(x, "tp", [(0, 1), (1, 0)])


class Halving:
    def __init__(self, keep, send, n, bits):
        self.keep, self.send, self.n, self.bits = keep, send, n, bits
        self.got = swap(send, bits[0], n)

    def hold(self, *before):
        self.send = tied(self.send, *before)
        self.got = swap(self.send, self.bits[0], self.n)

    def step(self, *before):
        got = tied(self.got, *before) if before else self.got
        total = self.keep.astype(F32) + got.astype(F32)
        self.bits = self.bits[1:]
        if not self.bits:
            return total
        half = total.shape[0] // 2
        self.keep, self.send = total[:half], total[half:].astype(BF)
        self.got = swap(self.send, self.bits[0], self.n)
        return self.send

    def end(self, *before):
        while len(self.bits) > 1:
            self.step(*before)
        return self.step(*before)


def on_device(
    n,
    encoder_in,
    decoder_in,
    lengths,
    retrieved,
    band_start,
    cotangent,
    enc_query,
    enc_key,
    enc_value,
    enc_mix,
    attn_gain,
    attn_shift,
    enc_up,
    enc_down,
    ffn_gain,
    ffn_shift,
    self_query,
    self_key,
    self_value,
    self_mix,
    self_gain,
    self_shift,
    cross_query,
    cross_key,
    cross_value,
    cross_mix,
    cross_gain,
    cross_shift,
    dec_up,
    dec_down,
    last_gain,
    last_shift,
):
    group_rows, D = encoder_in.shape
    C = cross_query.shape[1]
    FF = enc_up.shape[1]
    hi = n // 16
    me = lax.axis_index("blk")
    core = lambda x: swap(x, 1, n)
    par = jnp.stack(
        [attn_gain, attn_shift, ffn_gain, ffn_shift, self_gain, self_shift, cross_gain, cross_shift, last_gain, last_shift]
    )

    share = D // n
    bits = [1 << i for i in range(n.bit_length() - 1)]

    def rows_by(order):
        t = jnp.arange(share << len(order), dtype=jnp.int32)
        block = t // share
        rel = sum(((block >> (len(order) - 1 - i)) & 1) * bit for i, bit in enumerate(order))
        return ((me ^ rel) * share + t % share).reshape(-1, 1)

    def gradients(order, terms, after=()):
        width = sum(grad[2] for _, _, grads in terms for grad in grads)
        return Halving(*weight_grads([rows_by(order)], D, [terms], [width], after), n, order)

    def joint(parts, after=()):
        chunks = [w for _, _, widths in parts for w in widths]
        made = weight_grads([rows_by(order) for order, _, _ in parts], D, [terms for _, terms, _ in parts], chunks, after)
        gots = [swap(send, 1, n) for send in made[1::2]]

        def finish(*before):
            tied_gots = lax.optimization_barrier((*gots, *before))[: len(gots)]
            totals = [k.astype(F32) + g.astype(F32) for k, g in zip(made[0::2], tied_gots)]
            half, sums = totals[0].shape[0] // 2, []
            for order, _, widths in parts:
                mine, totals = totals[: len(widths)], totals[len(widths) :]
                keep = jnp.concatenate([t[:half] for t in mine], 1)
                send = jnp.concatenate([t[half:].astype(BF) for t in mine], 1)
                sums.append(Halving(keep, send, n, order[1:]))
            return sums

        return made[0], finish

    both = lambda x: (x, core(x))
    summed = lambda *arrays: functools.reduce(lambda x, y: x + y, [t.astype(F32) for t in arrays]).astype(BF)

    *enc_kept, enc_o, enc_part = attend_fwd(encoder_in, enc_query, enc_key, enc_value, enc_mix, fetch=True)
    enc_other = other_tp(enc_part)
    pick = pick_rows(retrieved, band_start, (enc_part,))
    pick_other = [core(p) for p in pick]
    *self_kept, self_o, self_part = attend_fwd(
        decoder_in, self_query, self_key, self_value, self_mix, lengths, pick
    )
    enc_other = tied(enc_other, self_part)
    v1, u1, low1, act1, gp1, part1 = ffn_fwd(0, encoder_in, enc_part, enc_other, par, enc_up, enc_down, True, True)
    other1 = other_tp(part1)
    chosen = picks(tied((me & 1).reshape(1), part1), pick, pick_other, n // 2, group_rows // 2)
    other1 = tied(other1, chosen)
    v2, enc_low, store = store_fwd(2, u1, part1, other1, par, cross_key, cross_value)

    store = store[None]
    for b in range(4, n.bit_length() - 1):
        store = jnp.concatenate([store, swap(store, 1 << b, n)], 0)

    def gid_of(pair):
        return (me ^ jnp.array([16 * h + r for h in range(hi) for r in pair], jnp.int32)) >> 1

    near = swap(store, 4, n)
    y_own = swap(store, 2, n)
    far = swap(store, 8, n)
    self_part = tied(self_part, store)
    self_other = other_tp(self_part)
    vd, ud, lowd, qc = cross_q(4, decoder_in, self_part, self_other, par, cross_query)
    qcs = both(qc)
    encoded = norm_of(2, v2, par, (qc,))
    far = tied(far, near, y_own, qcs[1], encoded)
    apart = swap(far, 4, n)
    y_far = swap(far, 2, n)
    state = cross_fwd(gid_of((0, 2)), qcs, (tied(store, far), y_own), chosen, None, False)
    state = cross_fwd(gid_of((4, 8)), qcs, (near, far), chosen, state, False)
    apart = tied(apart, *state)
    y_near = swap(tied(y_own, apart), 4, n)
    y_apart = swap(apart, 2, n)
    state = cross_fwd(gid_of((12, 10)), qcs, (apart, y_far), chosen, state, False)
    state_own, state_other = cross_fwd(gid_of((6, 14)), qcs, (y_near, y_apart), chosen, state, True)[3:]
    pieces = [(store, y_own), (near, y_near), (far, y_far), (apart, y_apart)]
    log_own, of_own, oc, partc = cross_mix_fwd(state_own, core(state_other), cross_mix)
    otherc = other_tp(partc)
    log_other, of_other = cross_merge(state_other, core(tied(state_own, partc)))
    otherc = tied(otherc, of_other)

    vc, uc, lowc, actc, gpc, part3 = ffn_fwd(6, ud, partc, otherc, par, dec_up, dec_down, False, False)
    other3 = other_tp(part3)
    actc_y = swap(actc, 2, n)
    decoded, dlast, dlowc, dhc, gg_last, part4 = last_fwd_back(8, uc, part3, other3, cotangent, par, gpc, dec_up, dec_down)
    dlowc_y = swap(dlowc, 2, n)
    other4 = tied(other_tp(part4), actc_y, dlowc_y)
    dcross, dpacko, gg_cross = cross_mix_back(6, dlast, part4, other4, vc, par, cross_mix)

    dpackos = both(dpacko)
    back = lambda k, extra, after: cross_back(
        gid_of((4 * k, 4 * k + 2)), qcs, dpackos, pieces[k], chosen, extra, k == 3, k == 0, after
    )
    *extra, keep3, send3 = back(3, (of_own, of_other, log_own, log_other), ())
    got3 = swap(send3, 2, n)
    no_y = bits[:1] + bits[2:]
    down_keep, down_sums = joint([(no_y, [((dlowc, dlowc_y), 0, [((actc, actc_y), 0, FF)])], [FF // 2] * 2)], (send3,))
    *extra, keep1, send1 = back(1, extra, (down_keep,))
    got1 = swap(send1, 2, n)
    one = lambda x: (x,)
    (down,) = down_sums(send1)
    up = gradients(bits, [(one(lowc), 0, [(one(dhc), 0, FF)])], (down.send,))
    sum3 = summed(keep3, tied(got3, up.keep))
    apart = swap(sum3, 4, n)
    *extra, keep2, send2 = back(2, extra, (sum3,))
    got2 = swap(send2, 2, n)
    sum1 = summed(keep1, tied(got1, send2))
    near = swap(sum1, 4, n)
    down_z = down.step(sum1)
    _, _, keep0, send0, dq_own, dq_other = back(0, extra, (sum1, down_z))
    got0 = swap(send0, 2, n)
    up_y = up.step(send0)
    sum2 = summed(keep2, tied(got2, send0, up_y), apart)
    far = swap(sum2, 8, n)
    down.hold(far)
    terms = [keep0, got0, near, far]
    bit = n // 2
    while terms[0].shape[0] > 1:
        half = terms[0].shape[0] // 2
        total = functools.reduce(lambda x, y: x + y, [t.astype(F32) for t in terms])
        terms = [total[:half].astype(BF), swap(total[half:].astype(BF), bit, n)]
        bit //= 2

    dqc, partq = cross_q_back(dq_own, core(tied(dq_other, sum2)), cross_query, ())
    otherq = other_tp(partq)
    v2_near, gp1_near, *loaded = load((v2, gp1, enc_up, enc_down), (partq,))
    dkv, part5 = store_back(terms, cross_key, cross_value, (gp1_near,))
    other5 = other_tp(part5)
    up.hold(got0)
    dself, dpackd, gg_self, part6 = attend_back(
        4, dcross, partq, tied(otherq, got0, near, far), vd, par, self_kept, (self_query, self_key, self_value, self_mix), lengths,
    )
    own_keep, own_sums = joint(
        [
            (
                bits,
                [
                    (one(lowd), 0, [(one(dqc), 0, C)]),
                    (one(dpacko), 0, [(one(oc), 0, C)]),
                    (one(dpackd), 0, [(one(self_o), 0, C)]),
                ],
                [C] * 3,
            ),
            (bits, [(one(decoder_in), 0, [(one(dpackd), D, 3 * C)])], [C] * 3),
        ]
    )
    up_z = up.step(other5)
    mixes, own = own_sums(up_z)
    dffn, dlow1, dh1, gg_ffn, part7 = ffn_back(
        2, part5, tied(other5, mixes.send, own.send), v2_near, par, gp1_near, *loaded, ()
    )
    other7 = other_tp(part7)
    z_first = bits[:1] + bits[2:] + bits[1:2]
    ffn_keep, ffn_sums = joint(
        [
            (z_first, [(one(dlow1), 0, [(one(act1), 0, FF)])], [FF // 2] * 2),
            (
                bits,
                [
                    (one(enc_low), 0, [(one(dkv), 0, 2 * C)]),
                    (one(low1), 0, [(one(dh1), 0, FF)]),
                ],
                [2 * C] + [FF // 2] * 2,
            ),
        ],
    )
    down_sum = down.end(ffn_keep)
    up_z = up.step(down_sum)
    mixes_z = mixes.step(up_z)
    down1, up1 = ffn_sums(mixes_z)
    own_z = own.step(up1.send)
    dattn, dpacke, _, part8, gains = attend_back(
        0, dffn, part7, tied(other7, own_z, down1.send), v1, par, enc_kept, (enc_query, enc_key, enc_value, enc_mix), None,
        (gg_ffn, gg_self, gg_cross, gg_last),
    )
    up_sum = up.end(part8)
    mixes_z = mixes.step(up_sum)
    own_z = own.step(mixes_z)
    lanes = jnp.eye(16, 128, dtype=BF)
    last_keep, last_sums = joint(
        [
            (
                bits,
                [
                    (one(encoder_in), 0, [(one(dpacke), D, 3 * C)]),
                    (one(dpacke), 0, [(one(enc_o), 0, C)]),
                    (one(gains), 0, [(one(lanes), 0, 128)]),
                ],
                [2 * C, 2 * C + 128],
            )
        ],
        (own_z,),
    )
    up1_z = up1.step(last_keep)
    (last,) = last_sums(up1_z)
    other6, other8 = other_tp(tied(part6, last.send)), other_tp(tied(part8, last.send))
    down1_z = down1.step(last.send)
    mixes_sum = mixes.end(down1_z)
    own_sum = own.end(mixes_sum)
    up1_z = up1.step(own_sum)
    down1_z = down1.step(up1_z)
    last_z = last.step(down1_z)
    up1_sum = up1.end(last_z)
    down1_sum = down1.end(up1_sum)
    last_z = last.step(down1_sum)
    last_sum = last.end()
    grad_encoder_in = tied(dattn, last_z) + (part8.astype(F32) + other8.astype(F32))
    grad_decoder_in = tied(dself, last_z) + (part6.astype(F32) + other6.astype(F32))

    cut = lambda total, at, width: total[:, at : at + width]
    gain_of = [last_sum[:, 4 * C + i] for i in range(10)]
    return (
        encoded,
        decoded,
        grad_encoder_in,
        grad_decoder_in,
        cut(last_sum, 0, C),
        cut(last_sum, C, C),
        cut(last_sum, 2 * C, C),
        cut(last_sum, 3 * C, C).T,
        gain_of[0],
        gain_of[1],
        cut(up1_sum, 2 * C, FF),
        down1_sum.T,
        gain_of[2],
        gain_of[3],
        cut(own_sum, 0, C),
        cut(own_sum, C, C),
        cut(own_sum, 2 * C, C),
        cut(mixes_sum, 2 * C, C).T,
        gain_of[4],
        gain_of[5],
        cut(mixes_sum, 0, C),
        cut(up1_sum, 0, C),
        cut(up1_sum, C, C),
        cut(mixes_sum, C, C).T,
        gain_of[6],
        gain_of[7],
        up_sum,
        down_sum.T,
        gain_of[8],
        gain_of[9],
    )


def solution(mesh):
    rows, both, cols, down = P("blk", None), P("blk", "tp"), P(None, "tp"), P("tp", None)
    attn = (cols, cols, cols, down, P(), P())
    ffn = (cols, down, P(), P())
    in_specs = (rows, rows, P("blk"), P("blk", "tp", None), both, rows) + attn + ffn + attn + attn + ffn
    mixed = P("tp", "blk")
    grad_attn = (both, both, both, mixed, P("blk"), P("blk"))
    grad_ffn = (both, mixed, P("blk"), P("blk"))
    out_specs = (rows,) * 4 + grad_attn + grad_ffn + grad_attn + grad_attn + grad_ffn
    return jax.shard_map(
        functools.partial(on_device, mesh.shape["blk"]),
        mesh=mesh,
        in_specs=in_specs,
        out_specs=out_specs,
        check_vma=False,
    )
```

```python
import functools

import jax
import jax.numpy as jnp
from jax import lax
from jax.experimental import pallas as pl
from jax.experimental.pallas import tpu as pltpu
from jax.sharding import PartitionSpec as P

HD = 64
PAIR = 2 * HD
NEG_FILL = -1e30
EPS_NORM = 1e-05
SCALE = 0.125
BF = jnp.bfloat16
F32 = jnp.float32
VMEM_LIMIT = 24 * 2**20
HBM = True
ROWS = 64
BAND_ROWS = 16


def nn(a, b):
    return lax.dot_general(a, b, (((1,), (0,)), ((), ())), preferred_element_type=F32)


def nt(a, b):
    return lax.dot_general(a, b, (((1,), (1,)), ((), ())), preferred_element_type=F32)


def tn(a, b):
    return lax.dot_general(a, b, (((0,), (0,)), ((), ())), preferred_element_type=F32)


def behind(body, n_in, n_after):
    if not n_after:
        return body
    return lambda *refs: body(*refs[:n_in], *refs[n_in + n_after :])


class Fetched:
    def __init__(self, far, near, sem):
        self.near, self.shape, self.pending, self.begun = near, near.shape, pltpu.make_async_copy(far, near, sem), False

    def begin(self):
        if not self.begun:
            self.pending.start()
            self.begun = True

    def ready(self):
        if self.pending is not None:
            self.begin()
            self.pending.wait()
            self.pending = None

    def __getitem__(self, at):
        self.ready()
        return self.near[at]


class Kept:
    def __init__(self, far, near, sem):
        self.far, self.near, self.shape, self.sem, self.copies, self.at = far, near, near.shape, sem, [], 0

    def flush(self, upto=None):
        if upto is None and self.at == 0:
            copy = pltpu.make_async_copy(self.near, self.far, self.sem.at[0])
        else:
            upto = self.shape[-1] if upto is None else upto
            if upto == self.at:
                return
            sl = (slice(None), slice(self.at, upto))
            copy = pltpu.make_async_copy(self.near.at[sl], self.far.at[sl], self.sem.at[len(self.copies)])
        self.at = self.shape[-1] if upto is None else upto
        copy.start()
        self.copies.append(copy)

    def wait(self):
        if self.at < self.shape[-1]:
            self.flush()
        for copy in self.copies:
            copy.wait()

    def __getitem__(self, at):
        return self.near[at]

    def __setitem__(self, at, value):
        self.near[at] = value


def flush(*refs, upto=None):
    for ref in refs:
        if isinstance(ref, Kept):
            ref.flush(upto)


class Far:
    def __init__(self, array, late=False):
        self.array, self.late = array, late


def begin(*refs):
    for ref in refs:
        if isinstance(ref, Fetched):
            ref.begin()


def whole(body, name, outs, *args, smem=0, after=()):
    far_in = [i for i, a in enumerate(args) if isinstance(a, Far)]
    late = [i for i in far_in if args[i].late]
    far_out = [i for i, o in enumerate(outs) if len(o) > 2]
    args = [pltpu.with_memory_space_constraint(a.array, pltpu.HBM) if isinstance(a, Far) else a for a in args]
    n_in, n_out, n_after = len(args), len(outs), len(after)

    def run(*refs):
        ins = list(refs[:n_in])
        results = list(refs[n_in + n_after : n_in + n_after + n_out])
        scratch = refs[n_in + n_after + n_out :]
        for k, i in enumerate(far_in):
            ins[i] = Fetched(ins[i], scratch[k], scratch[-1].at[k, 0])
            if i not in late:
                ins[i].begin()
        for k, i in enumerate(far_out):
            results[i] = Kept(results[i], scratch[len(far_in) + k], scratch[-1].at[len(far_in) + k])
        body(*ins, *results)
        for i in far_in:
            ins[i].ready()
        for i in far_out:
            results[i].wait()

    moves = len(far_in) + len(far_out)
    scratch = [pltpu.VMEM(args[i].shape, args[i].dtype) for i in far_in]
    scratch += [pltpu.VMEM(outs[i][0], outs[i][1]) for i in far_out]
    if moves:
        scratch.append(pltpu.SemaphoreType.DMA((moves, 8)))
    in_specs = [pl.BlockSpec(memory_space=pltpu.SMEM if i < smem else pltpu.VMEM) for i in range(n_in)]
    out_specs = [pl.BlockSpec(memory_space=pltpu.VMEM) for _ in outs]
    for i in far_in:
        in_specs[i] = pl.BlockSpec(memory_space=pltpu.HBM)
    for i in far_out:
        out_specs[i] = pl.BlockSpec(memory_space=pltpu.HBM)
    return pl.pallas_call(
        run,
        name=name,
        out_shape=[pltpu.HBM(o[0], o[1]) if len(o) > 2 else jax.ShapeDtypeStruct(o[0], o[1]) for o in outs],
        in_specs=in_specs + [pl.BlockSpec(memory_space=pl.ANY)] * n_after,
        out_specs=out_specs,
        scratch_shapes=scratch,
        compiler_params=pltpu.CompilerParams(vmem_limit_bytes=VMEM_LIMIT),
        cost_estimate=pl.CostEstimate(flops=1, bytes_accessed=1, transcendentals=0),
    )(*args, *after)


def load_body(n, *refs):
    sems = refs[-1]
    copies = [pltpu.make_async_copy(refs[i], refs[n + i], sems.at[i]) for i in range(n)]
    for copy in copies:
        copy.start()
    for copy in copies:
        copy.wait()


def load(arrays, after):
    n, n_after = len(arrays), len(after)
    return pl.pallas_call(
        behind(functools.partial(load_body, n), n, n_after),
        name="load",
        out_shape=[pltpu.VMEM(a.shape, a.dtype) for a in arrays],
        in_specs=[pl.BlockSpec(memory_space=pltpu.HBM)] * n + [pl.BlockSpec(memory_space=pl.ANY)] * n_after,
        out_specs=[pl.BlockSpec(memory_space=pltpu.VMEM)] * n,
        scratch_shapes=[pltpu.SemaphoreType.DMA((n,))],
        compiler_params=pltpu.CompilerParams(vmem_limit_bytes=VMEM_LIMIT),
        cost_estimate=pl.CostEstimate(flops=1, bytes_accessed=1, transcendentals=0),
    )(*[pltpu.with_memory_space_constraint(a, pltpu.HBM) for a in arrays], *after)


def norm_parts(v):
    center = v - jnp.mean(v, -1, keepdims=True)
    r = lax.rsqrt(jnp.mean(center * center, -1, keepdims=True) + EPS_NORM)
    return center * r, r


def norm_back(v, gain, dy):
    xhat, r = norm_parts(v)
    gdy = gain * dy
    dv = r * (gdy - jnp.mean(gdy, -1, keepdims=True) - xhat * jnp.mean(gdy * xhat, -1, keepdims=True))
    return dv, jnp.sum(dy * xhat, 0, keepdims=True), jnp.sum(dy, 0, keepdims=True)


def row_of(par_ref, i):
    return par_ref[i : i + 1, :].astype(F32)


def low_half(shape, dim):
    return lax.broadcasted_iota(jnp.int32, shape, dim) < HD


def stacked(t2):
    first = low_half(t2.shape, 1)
    zero = jnp.zeros_like(t2)
    return jnp.concatenate([jnp.where(first, t2, zero), jnp.where(first, zero, t2)], 0)


def unstacked(tT):
    R = tT.shape[1] // 2
    first = low_half((PAIR, R), 0)
    return jnp.where(first, tT[:, :R], tT[:, R:]).T


def causal_mask(R, length):
    key = lax.broadcasted_iota(jnp.int32, (R, 2 * R), 0)
    lane = lax.broadcasted_iota(jnp.int32, (R, 2 * R), 1)
    query = jnp.where(lane >= R, lane - R, lane)
    return (key <= query) & (key < length)


def local_weights(k2, qq, allowed):
    sT = nt(k2, qq)
    if allowed is not None:
        sT = jnp.where(allowed, sT, NEG_FILL)
    p = jnp.exp(sT - jnp.max(sT, 0, keepdims=True))
    return p * (1.0 / jnp.sum(p, 0, keepdims=True))


def gelu_parts(h):
    cdf = 0.5 * (1.0 + lax.erf(h * 0.7071067811865476))
    pdf = 0.3989422804014327 * jnp.exp(-0.5 * h * h)
    return h * cdf, cdf + h * pdf


def attend_fwd_body(causal, *refs):
    if causal:
        len_ref, refs = refs[0], refs[1:]
    x_ref, wq, wk, wv, wm, q_ref, k_ref, v_ref, o_ref, part_ref = refs
    x = x_ref[...]
    R = x.shape[0]
    q_ref[...] = (nn(x, wq[...]) * SCALE).astype(BF)
    k_ref[...] = nn(x, wk[...]).astype(BF)
    v_ref[...] = nn(x, wv[...]).astype(BF)
    flush(q_ref, k_ref, v_ref)
    allowed = causal_mask(R, len_ref[0]) if causal else None
    for c in range(0, q_ref.shape[1], PAIR):
        sl = slice(c, c + PAIR)
        w = local_weights(k_ref[:, sl], stacked(q_ref[:, sl]), allowed).astype(BF)
        o_ref[:, sl] = unstacked(tn(v_ref[:, sl], w)).astype(BF)
    flush(o_ref)
    part_ref[...] = nn(o_ref[...], wm[...]).astype(BF)


def attend_fwd(x, wq, wk, wv, wm, length=None, after=(), fetch=False):
    R, D = x.shape
    C = wq.shape[1]
    args = (x, wq, wk, wv, wm)
    if fetch:
        args = tuple(Far(a) for a in args)
    causal = length is not None
    if causal:
        args = (length,) + args
    return whole(
        functools.partial(attend_fwd_body, causal),
        "attend_fwd",
        [((R, C), BF, HBM)] * 4 + [((R, D), BF)],
        *args,
        smem=int(causal),
        after=after,
    )


def ffn_fwd_body(g, x_ref, own, oth, par, wu, wd, v_ref, u_ref, low_ref, act_ref, gp_ref, part_ref):
    R, D = x_ref.shape
    gain, shift = row_of(par, g), row_of(par, g + 1)
    for r in range(0, R, ROWS):
        s = slice(r, r + ROWS)
        v = x_ref[s, :].astype(F32) + (own[s, :].astype(F32) + oth[s, :].astype(F32))
        xhat, _ = norm_parts(v)
        u = xhat * gain + shift
        v_ref[s, :] = v
        u_ref[s, :] = u
        low_ref[s, :] = u.astype(BF)
    flush(u_ref, v_ref, low_ref)
    low = low_ref[...]
    for c in range(0, wu.shape[1], 256):
        sl = slice(c, c + 256)
        a, gp = gelu_parts(nn(low, wu[:, sl]))
        act_ref[:, sl] = a.astype(BF)
        gp_ref[:, sl] = gp.astype(BF)
        flush(act_ref, gp_ref, upto=c + 256)
    part_ref[...] = nn(act_ref[...], wd[...]).astype(BF)


def ffn_fwd(g, x, own, oth, par, wu, wd, fetch, keep):
    R, D = x.shape
    FF = wu.shape[1]
    kept = (HBM,) if keep else ()
    return whole(
        functools.partial(ffn_fwd_body, g),
        "ffn_fwd",
        [((R, D), F32, HBM), ((R, D), F32, *kept), ((R, D), BF, HBM), ((R, FF), BF, *kept), ((R, FF), BF, *kept), ((R, D), BF)],
        x, own, oth, par, *((Far(wu), Far(wd)) if fetch else (wu, wd)),
    )


def order_matrix(R):
    t = lax.broadcasted_iota(jnp.int32, (R, R), 0)
    col = lax.broadcasted_iota(jnp.int32, (R, R), 1)
    src = jnp.where(t < R // 2, 2 * t, 2 * t - (R - 1))
    return (src == col).astype(F32).astype(BF)


def store_body(g, u_ref, own, oth, par, wk, wv, v_ref, low_ref, kv_ref):
    R = u_ref.shape[0]
    gain, shift = row_of(par, g), row_of(par, g + 1)
    low = []
    for r in range(0, R, ROWS):
        s = slice(r, r + ROWS)
        v = u_ref[s, :] + (own[s, :].astype(F32) + oth[s, :].astype(F32))
        xhat, _ = norm_parts(v)
        v_ref[s, :] = v
        low.append((xhat * gain + shift).astype(BF))
    low_ref[...] = nn(order_matrix(R), jnp.concatenate(low, 0)).astype(BF)
    low = low_ref[...]
    kv_ref[0] = nn(low, wk[...]).astype(BF)
    kv_ref[1] = nn(low, wv[...]).astype(BF)


def store_fwd(g, u, own, oth, par, wk, wv):
    R, D = u.shape
    C = wk.shape[1]
    return whole(
        functools.partial(store_body, g),
        "store_fwd",
        [((R, D), F32), ((R, D), BF), ((2, R, C), BF)],
        u, own, oth, par, wk, wv,
    )


def norm_body(g, v_ref, par, out_ref):
    for r in range(0, v_ref.shape[0], ROWS):
        s = slice(r, r + ROWS)
        xhat, _ = norm_parts(v_ref[s, :])
        out_ref[s, :] = xhat * row_of(par, g) + row_of(par, g + 1)


def norm_of(g, v, par, after):
    return whole(functools.partial(norm_body, g), "norm_of", [(v.shape, F32, HBM)], v, par, after=after)[0]


def cross_q_body(g, x_ref, own, oth, par, wq, v_ref, u_ref, low_ref, q_ref):
    R = x_ref.shape[0]
    gain, shift = row_of(par, g), row_of(par, g + 1)
    for r in range(0, R, ROWS):
        s = slice(r, r + ROWS)
        v = x_ref[s, :].astype(F32) + (own[s, :].astype(F32) + oth[s, :].astype(F32))
        xhat, _ = norm_parts(v)
        u = xhat * gain + shift
        v_ref[s, :] = v
        u_ref[s, :] = u
        low_ref[s, :] = u.astype(BF)
    flush(v_ref, u_ref, low_ref)
    q_ref[...] = (nn(low_ref[...], wq[...]) * SCALE).astype(BF)


def cross_q(g, x, own, oth, par, wq):
    R, D = x.shape
    C = wq.shape[1]
    return whole(
        functools.partial(cross_q_body, g),
        "cross_q",
        [((R, D), F32, HBM), ((R, D), F32, HBM), ((R, D), BF, HBM), ((R, C), BF)],
        x, own, oth, par, wq,
    )


def pick_rows_body(from_ref, band_ref, *out_refs):
    picked = from_ref.shape[2]
    for pair, out_ref in enumerate(out_refs):
        for h in range(2):
            out_ref[h, :picked] = ((from_ref[2 * pair + h] & 1) + 1).astype(F32).T.astype(BF)
        band = band_ref[2 * pair : 2 * pair + 2, :].astype(F32)
        for h in range(2):
            out_ref[h, picked:] = jnp.broadcast_to(band[h : h + 1], (BAND_ROWS, band.shape[1])).astype(BF)


def pick_rows(retrieved, band_start, after):
    R, heads, picked = retrieved.shape
    outs = [((2, picked + BAND_ROWS, R), BF)] * (heads // 2)
    args = (Far(retrieved.transpose(1, 0, 2)), band_start.T)
    return whole(pick_rows_body, "pick_rows", outs, *args, after=after)


def picks_body(pairs, core_ref, *refs):
    own, other, out_ref = refs[:pairs], refs[pairs : 2 * pairs], refs[2 * pairs]
    g = (2 * pl.program_id(0) + core_ref[0]).astype(F32)
    _, rows, R = own[0].shape
    picked = rows - BAND_ROWS
    half = out_ref.shape[2]
    for h in range(2 * pairs):
        for i, from_ref in enumerate((own[h // 2], other[h // 2])):
            rel = g - from_ref[h % 2, picked : picked + BAND_ROWS, :].astype(F32)[:1]
            got = None
            for b in range(picked // half):
                here = (rel == b).astype(F32).astype(BF) * from_ref[h % 2, b * half : (b + 1) * half, :]
                got = here if got is None else got + here
            at = (2 * (h % 2) + i) * R
            out_ref[0, h // 2, :, at : at + R] = got


def picks(core_index, pick, pick_other, groups, half):
    pairs = len(pick)
    _, rows, R = pick[0].shape
    return pl.pallas_call(
        functools.partial(picks_body, pairs),
        name="picks",
        grid=(groups,),
        out_shape=pltpu.HBM((groups, pairs, half, 4 * R), BF),
        in_specs=[pl.BlockSpec(memory_space=pltpu.SMEM)]
        + [pl.BlockSpec((2, rows, R), lambda g: (0, 0, 0))] * (2 * pairs),
        out_specs=pl.BlockSpec((1, pairs, half, 4 * R), lambda g: (g, 0, 0, 0)),
        compiler_params=pltpu.CompilerParams(vmem_limit_bytes=VMEM_LIMIT),
        cost_estimate=pl.CostEstimate(flops=1, bytes_accessed=1, transcendentals=0),
    )(core_index, *pick, *pick_other)


def chosen_scores(k2, qq, a):
    half = a.shape[0]
    sT = nt(k2, qq)
    s = jnp.where(a > 1.5, sT[half:], sT[:half])
    return jnp.where(a < 0.5, NEG_FILL, s)


def spread(p, a):
    zero = jnp.zeros_like(p)
    even = jnp.where(a == 1.0, p, zero).astype(BF)
    odd = jnp.where(a == 2.0, p, zero).astype(BF)
    return jnp.concatenate([even, odd], 0)


def of_both(own, other):
    return stacked(jnp.concatenate([own, other], 0))


def own_lanes(t):
    R = t.shape[1] // 4
    return jnp.concatenate([t[:, :R], t[:, 2 * R : 3 * R]], 1)


def other_lanes(t):
    R = t.shape[1] // 4
    return jnp.concatenate([t[:, R : 2 * R], t[:, 3 * R :]], 1)


def all_lanes(own, other):
    R = own.shape[1] // 2
    return jnp.concatenate([own[:, :R], other[:, :R], own[:, R:], other[:, R:]], 1)


def cross_fwd_body(first, last, gid_ref, q_ref, q_other, *refs):
    kv, a_refs, refs = refs[:2], refs[2:4], refs[4:]
    if not first:
        m_in, l_in, acc_in = refs[:3]
        refs = refs[3:]
    m_ref, l_ref, acc_ref = refs[:3]

    @pl.when(pl.program_id(0) == 0)
    def _():
        if first:
            m_ref[...] = jnp.full(m_ref.shape, NEG_FILL, F32)
            l_ref[...] = jnp.zeros(l_ref.shape, F32)
            acc_ref[...] = jnp.zeros(acc_ref.shape, F32)
        else:
            m_ref[...] = m_in[...]
            l_ref[...] = l_in[...]
            acc_ref[...] = acc_in[...]

    pairs = acc_ref.shape[0]
    for hp in range(pairs):
        sl = slice(hp * PAIR, (hp + 1) * PAIR)
        qq = of_both(q_ref[:, sl], q_other[:, sl])
        codes = [a_refs[j][0, hp].astype(F32) for j in range(2)]
        scores = [chosen_scores(kv[j][0, 0, :, sl], qq, codes[j]) for j in range(2)]
        old = m_ref[hp : hp + 1, :]
        top = functools.reduce(jnp.maximum, [jnp.max(s, 0, keepdims=True) for s in scores], old)
        fade = jnp.exp(old - top)
        total = l_ref[hp : hp + 1, :] * fade
        acc = acc_ref[hp] * fade
        for j in range(2):
            a = codes[j]
            p = jnp.where(a < 0.5, 0.0, jnp.exp(scores[j] - top))
            total = total + jnp.sum(p, 0, keepdims=True)
            acc = acc + tn(kv[j][0, 1, :, sl], spread(p, a))
        m_ref[hp : hp + 1, :] = top
        l_ref[hp : hp + 1, :] = total
        acc_ref[hp] = acc

    if last:
        own_ref, other_ref = refs[3:]

        @pl.when(pl.program_id(0) == pl.num_programs(0) - 1)
        def _():
            for out, lanes in ((own_ref, own_lanes), (other_ref, other_lanes)):
                out[pairs * PAIR :, :] = jnp.zeros((8, out.shape[1]), F32)
                for hp in range(pairs):
                    out[hp * PAIR : (hp + 1) * PAIR, :] = lanes(acc_ref[hp])
                    out[pairs * PAIR + hp : pairs * PAIR + hp + 1, :] = lanes(m_ref[hp : hp + 1, :])
                    out[pairs * PAIR + 4 + hp : pairs * PAIR + 5 + hp, :] = lanes(l_ref[hp : hp + 1, :])


def kv_specs(kv, a):
    rows, C = kv[0].shape[2:]
    specs = [pl.BlockSpec((1, 2, rows, C), lambda i, gid: (i, 0, 0, 0)) for _ in range(2)]
    for j in range(2):
        specs.append(
            pl.BlockSpec((1,) + a.shape[1:], functools.partial(lambda j, i, gid: (gid[2 * i + j], 0, 0, 0), j))
        )
    return specs


def fixed(shape):
    return pl.BlockSpec(shape, lambda i, gid: (0,) * len(shape))


def cross_fwd(gid, q, kv, a, state, last):
    R, C = q[0].shape
    pairs = C // PAIR
    hi, _, rows, _ = kv[0].shape
    shapes = [(8, 4 * R), (8, 4 * R), (pairs, PAIR, 4 * R)]
    first = state is None
    state = () if first else tuple(state)
    if last:
        shapes += [(C + 8, 2 * R)] * 2
    return pl.pallas_call(
        functools.partial(cross_fwd_body, first, last),
        name="cross_fwd",
        grid_spec=pltpu.PrefetchScalarGridSpec(
            num_scalar_prefetch=1,
            grid=(hi,),
            in_specs=[fixed(q[0].shape)] * 2 + kv_specs(kv, a) + [fixed(s.shape) for s in state],
            out_specs=[fixed(s) for s in shapes],
        ),
        out_shape=[jax.ShapeDtypeStruct(s, F32) for s in shapes],
        compiler_params=pltpu.CompilerParams(vmem_limit_bytes=VMEM_LIMIT),
        cost_estimate=pl.CostEstimate(flops=1, bytes_accessed=1, transcendentals=0),
    )(gid, *q, *kv, *([pltpu.with_memory_space_constraint(a, pltpu.HBM)] * 2), *state)


def merged(own_ref, got_ref, hp, C):
    sl = slice(hp * PAIR, (hp + 1) * PAIR)
    m, l = slice(C + hp, C + hp + 1), slice(C + 4 + hp, C + 5 + hp)
    m1, m2 = own_ref[m, :], got_ref[m, :]
    top = jnp.maximum(m1, m2)
    f1, f2 = jnp.exp(m1 - top), jnp.exp(m2 - top)
    total = own_ref[l, :] * f1 + got_ref[l, :] * f2
    return top + jnp.log(total), unstacked((own_ref[sl, :] * f1 + got_ref[sl, :] * f2) * (1.0 / total))


def cross_mix_body(own_ref, got_ref, wm, log_ref, of_ref, o_ref, part_ref):
    C = wm.shape[0]
    log_ref[...] = jnp.zeros(log_ref.shape, F32)
    for hp in range(C // PAIR):
        sl = slice(hp * PAIR, (hp + 1) * PAIR)
        log_ref[hp : hp + 1, :], o = merged(own_ref, got_ref, hp, C)
        of_ref[:, sl] = o
        o_ref[:, sl] = o.astype(BF)
    part_ref[...] = nn(o_ref[...], wm[...]).astype(BF)


def cross_mix_fwd(own, got, wm):
    R2 = own.shape[1]
    C, D = wm.shape
    R = R2 // 2
    return whole(
        cross_mix_body,
        "cross_mix",
        [((8, R2), F32), ((R, C), F32), ((R, C), BF), ((R, D), BF)],
        own, got, wm,
    )


def cross_merge_body(own_ref, got_ref, log_ref, of_ref):
    C = of_ref.shape[1]
    log_ref[...] = jnp.zeros(log_ref.shape, F32)
    for hp in range(C // PAIR):
        log_ref[hp : hp + 1, :], of_ref[:, hp * PAIR : (hp + 1) * PAIR] = merged(own_ref, got_ref, hp, C)


def cross_merge(own, got):
    rows, R2 = own.shape
    return whole(cross_merge_body, "cross_merge", [((8, R2), F32), ((R2 // 2, rows - 8), F32)], own, got)


def ffn_back_rest(dlow_ref, gp_ref, wu, wd, dh_ref, part_ref):
    low = dlow_ref[...]
    for c in range(0, wu.shape[1], 256):
        sl = slice(c, c + 256)
        dh_ref[:, sl] = (nt(low, wd[sl, :]) * gp_ref[:, sl].astype(F32)).astype(BF)
    part_ref[...] = nt(dh_ref[...], wu[...]).astype(BF)


def last_body(g, u_ref, own, oth, cot, par, gp_ref, wu, wd, out_ref, dv_ref, dlow_ref, dh_ref, gg_ref, part_ref):
    R, D = u_ref.shape
    gain, shift = row_of(par, g), row_of(par, g + 1)
    gg_ref[...] = jnp.zeros(gg_ref.shape, F32)
    for r in range(0, R, ROWS):
        s = slice(r, r + ROWS)
        v = u_ref[s, :] + (own[s, :].astype(F32) + oth[s, :].astype(F32))
        xhat, _ = norm_parts(v)
        out_ref[s, :] = xhat * gain + shift
        dv, dg, db = norm_back(v, gain, cot[s, :].astype(F32))
        dv_ref[s, :] = dv
        dlow_ref[s, :] = dv.astype(BF)
        gg_ref[0:1, :] += dg
        gg_ref[1:2, :] += db
    flush(gg_ref, out_ref)
    ffn_back_rest(dlow_ref, gp_ref, wu, wd, dh_ref, part_ref)


def last_fwd_back(g, u, own, oth, cot, par, gp, wu, wd):
    R, D = u.shape
    FF = wu.shape[1]
    return whole(
        functools.partial(last_body, g),
        "last_fwd_back",
        [((R, D), F32, HBM), ((R, D), F32), ((R, D), BF), ((R, FF), BF), ((8, D), F32, HBM), ((R, D), BF)],
        u, own, oth, cot, par, gp, wu, wd,
    )


def ffn_back_body(g, own, oth, v_ref, par, gp_ref, wu, wd, dv_ref, dlow_ref, dh_ref, gg_ref, part_ref):
    R, D = v_ref.shape
    gain = row_of(par, g)
    gg_ref[...] = jnp.zeros(gg_ref.shape, F32)
    for r in range(0, R, ROWS):
        s = slice(r, r + ROWS)
        dy = own[s, :].astype(F32) + oth[s, :].astype(F32)
        dv, dg, db = norm_back(v_ref[s, :], gain, dy)
        dv_ref[s, :] = dv
        dlow_ref[s, :] = dv.astype(BF)
        gg_ref[0:1, :] += dg
        gg_ref[1:2, :] += db
    flush(gg_ref)
    ffn_back_rest(dlow_ref, gp_ref, wu, wd, dh_ref, part_ref)


def ffn_back(g, own, oth, v, par, gp, wu, wd, after):
    R, D = v.shape
    FF = wu.shape[1]
    return whole(
        functools.partial(ffn_back_body, g),
        "ffn_back",
        [((R, D), F32), ((R, D), BF), ((R, FF), BF), ((8, D), F32, HBM), ((R, D), BF)],
        own, oth, v, par, gp, wu, wd,
        after=after,
    )


def branch_back(g, dres, own, oth, v_ref, par, dv_ref, dlow_ref, gg_ref):
    R, D = v_ref.shape
    gain = row_of(par, g)
    gg_ref[...] = jnp.zeros(gg_ref.shape, F32)
    for r in range(0, R, ROWS):
        s = slice(r, r + ROWS)
        dy = dres[s, :] + (own[s, :].astype(F32) + oth[s, :].astype(F32))
        dv, dg, db = norm_back(v_ref[s, :], gain, dy)
        dv_ref[s, :] = dv
        dlow_ref[s, :D] = dv.astype(BF)
        gg_ref[0:1, :] += dg
        gg_ref[1:2, :] += db


def cross_mix_back_body(g, dres, own, oth, v_ref, par, wm, dv_ref, pack_ref, gg_ref):
    branch_back(g, dres, own, oth, v_ref, par, dv_ref, pack_ref, gg_ref)
    flush(dv_ref, gg_ref)
    D = v_ref.shape[1]
    pack_ref[:, D:] = nt(pack_ref[:, :D], wm[...]).astype(BF)


def cross_mix_back(g, dres, own, oth, v, par, wm):
    R, D = v.shape
    C = wm.shape[0]
    return whole(
        functools.partial(cross_mix_back_body, g),
        "cross_mix_back",
        [((R, D), F32, HBM), ((R, D + C), BF), ((8, D), F32, HBM)],
        dres, own, oth, v, par, wm,
    )


def cross_back_body(first, last, gid_ref, q_ref, q_other, do_pack, do_pack_other, *refs):
    C = q_ref.shape[1]
    skip = do_pack.shape[1] - C
    do_ref, do_other = do_pack.at[:, skip:], do_pack_other.at[:, skip:]
    kv, a_refs, refs = refs[:2], refs[2:4], refs[4:]
    if first:
        of_ref, of_other, log_own, log_other = refs[:4]
        dq_ref, stat_ref, keep_ref, send_ref = refs[4:8]
    else:
        dq_in, stat_in = refs[:2]
        dq_ref, stat_ref, keep_ref, send_ref = refs[2:6]
    pairs = dq_ref.shape[0]

    @pl.when(pl.program_id(0) == 0)
    def _():
        if not first:
            dq_ref[...] = dq_in[...]
            stat_ref[...] = stat_in[...]
            return
        dq_ref[...] = jnp.zeros(dq_ref.shape, F32)
        stat_ref[...] = jnp.zeros(stat_ref.shape, F32)
        stat_ref[0:8, :] = all_lanes(log_own[...], log_other[...])
        for hp in range(pairs):
            sl = slice(hp * PAIR, (hp + 1) * PAIR)
            sums = []
            for d, o in ((do_ref, of_ref), (do_other, of_other)):
                prod = (d[:, sl].astype(F32) * o[:, sl]).T
                sums.append([jnp.sum(prod[:HD], 0, keepdims=True), jnp.sum(prod[HD:], 0, keepdims=True)])
            stat_ref[8 + hp : 9 + hp, :] = jnp.concatenate([sums[0][0], sums[1][0], sums[0][1], sums[1][1]], 1)

    for hp in range(pairs):
        sl = slice(hp * PAIR, (hp + 1) * PAIR)
        qq = of_both(q_ref[:, sl], q_other[:, sl])
        dd = of_both(do_ref[:, sl], do_other[:, sl])
        log_total = stat_ref[hp : hp + 1, :]
        delta = stat_ref[8 + hp : 9 + hp, :]
        dq = dq_ref[hp]
        for j, out_ref in enumerate((keep_ref, send_ref)):
            a = a_refs[j][0, hp].astype(F32)
            half = a.shape[0]
            k2 = kv[j][0, 0, :, sl]
            p = jnp.exp(chosen_scores(k2, qq, a) - log_total)
            daT = nt(kv[j][0, 1, :, sl], dd)
            ds = p * (jnp.where(a > 1.5, daT[half:], daT[:half]) - delta)
            dsT = spread(ds, a)
            out_ref[0, 0, :, sl] = nn(dsT, qq).astype(BF)
            out_ref[0, 1, :, sl] = nn(spread(p, a), dd).astype(BF)
            dq = dq + tn(k2, dsT)
        dq_ref[hp] = dq

    if last:
        own_ref, other_ref = refs[-2:]

        @pl.when(pl.program_id(0) == pl.num_programs(0) - 1)
        def _():
            for hp in range(pairs):
                own_ref[hp] = own_lanes(dq_ref[hp])
                other_ref[hp] = other_lanes(dq_ref[hp]).astype(BF)


def cross_back(gid, q, do, kv, a, extra, first, last, after=()):
    R, C = q[0].shape
    pairs = C // PAIR
    hi, _, rows, _ = kv[0].shape
    grad_spec = pl.BlockSpec((1, 2, rows, C), lambda i, gid: (i, 0, 0, 0))
    shapes = [(pairs, PAIR, 4 * R), (16, 4 * R)]
    out_specs = [fixed(s) for s in shapes] + [grad_spec] * 2
    out_shape = [jax.ShapeDtypeStruct(s, F32) for s in shapes] + [jax.ShapeDtypeStruct(kv[0].shape, BF)] * 2
    if last:
        out_specs += [fixed((pairs, PAIR, 2 * R))] * 2
        out_shape += [jax.ShapeDtypeStruct((pairs, PAIR, 2 * R), d) for d in (F32, BF)]
    return pl.pallas_call(
        behind(functools.partial(cross_back_body, first, last), 9 + len(extra), len(after)),
        name="cross_back",
        grid_spec=pltpu.PrefetchScalarGridSpec(
            num_scalar_prefetch=1,
            grid=(hi,),
            in_specs=[fixed(q[0].shape)] * 2
            + [fixed(do[0].shape)] * 2
            + kv_specs(kv, a)
            + [fixed(e.shape) for e in extra]
            + [pl.BlockSpec(memory_space=pl.ANY)] * len(after),
            out_specs=out_specs,
        ),
        out_shape=out_shape,
        compiler_params=pltpu.CompilerParams(vmem_limit_bytes=VMEM_LIMIT),
        cost_estimate=pl.CostEstimate(flops=1, bytes_accessed=1, transcendentals=0),
    )(gid, *q, *do, *kv, *([pltpu.with_memory_space_constraint(a, pltpu.HBM)] * 2), *extra, *after)


def cross_q_back_body(dq_own, dq_got, wq, dq_ref, part_ref):
    for hp in range(dq_own.shape[0]):
        sl = slice(hp * PAIR, (hp + 1) * PAIR)
        dq_ref[:, sl] = (unstacked(dq_own[hp] + dq_got[hp].astype(F32)) * SCALE).astype(BF)
    flush(dq_ref)
    part_ref[...] = nt(dq_ref[...], wq[...]).astype(BF)


def cross_q_back(dq, got, wq, after):
    D, C = wq.shape
    R = dq.shape[2] // 2
    return whole(cross_q_back_body, "cross_q_back", [((R, C), BF), ((R, D), BF)], dq, got, wq, after=after)


def store_back_body(spread_at, *refs):
    n = len(refs) - 4
    wk, wv, dkv_ref, part_ref = refs[n:]
    R, C = dkv_ref.shape[0], dkv_ref.shape[1] // 2
    for i in range(2):
        parts = [t[0, i] for t in refs[:spread_at]]
        if spread_at < n:
            parts.append(refs[spread_at + i][0, 0])
        total = functools.reduce(lambda x, y: x + y, [t.astype(F32) for t in parts])
        dkv_ref[:, i * C : (i + 1) * C] = total.astype(BF)
    part = nt(dkv_ref[:, :C], wk[...]) + nt(dkv_ref[:, C:], wv[...])
    part_ref[...] = tn(order_matrix(R), part.astype(BF)).astype(BF)


def store_back(terms, wk, wv, after):
    D, C = wk.shape
    R = terms[0].shape[2]
    full = [t for t in terms if not isinstance(t, list)]
    halves = [h for t in terms if isinstance(t, list) for h in t]
    return whole(
        functools.partial(store_back_body, len(full)),
        "store_back",
        [((R, 2 * C), BF), ((R, D), BF)],
        *full, *halves, wk, wv,
        after=after,
    )


def attend_back_body(causal, g, n_more, *refs):
    if causal:
        len_ref, refs = refs[0], refs[1:]
    (dres, own, oth, v1_ref, par, q_ref, k_ref, v_ref, wq, wk, wv, wm) = refs[:12]
    R, D = v1_ref.shape
    dv_ref, pack_ref, gg_ref, part_ref = refs[12 + n_more : 16 + n_more]
    branch_back(g, dres, own, oth, v1_ref, par, dv_ref, pack_ref, gg_ref)
    flush(dv_ref, gg_ref)
    if n_more:
        gains_ref = refs[-1]
        rows = [gg_ref[0:2, :]] + [other[0:2, :] for other in refs[12 : 12 + n_more]]
        rows.append(jnp.zeros((gains_ref.shape[0] - 2 - 2 * n_more, D), F32))
        gains_ref[...] = jnp.concatenate(rows, 0).astype(BF)
        flush(gains_ref)
    C = wq.shape[1]
    do = nt(pack_ref[:, :D], wm[...]).astype(BF)
    allowed = causal_mask(R, len_ref[0]) if causal else None
    for c in range(0, C, PAIR):
        sl = slice(c, c + PAIR)
        k2 = k_ref[:, sl]
        qq = stacked(q_ref[:, sl])
        dd = stacked(do[:, sl])
        w = local_weights(k2, qq, allowed)
        daT = nt(v_ref[:, sl], dd)
        ds = (w * (daT - jnp.sum(w * daT, 0, keepdims=True))).astype(BF)
        at = D + c
        pack_ref[:, at : at + PAIR] = (unstacked(tn(k2, ds)) * SCALE).astype(BF)
        pack_ref[:, at + C : at + C + PAIR] = nn(ds, qq).astype(BF)
        pack_ref[:, at + 2 * C : at + 2 * C + PAIR] = nn(w.astype(BF), dd).astype(BF)
    flush(pack_ref)
    part = nt(pack_ref[:, D : D + C], wq[...]) + nt(pack_ref[:, D + C : D + 2 * C], wk[...])
    part_ref[...] = (part + nt(pack_ref[:, D + 2 * C :], wv[...])).astype(BF)


def attend_back(g, dres, own, oth, v1, par, kept, weights, length=None, more=(), after=()):
    R, D = v1.shape
    C = kept[0].shape[1]
    args = (dres, own, oth, v1, par, *kept, *weights, *more)
    causal = length is not None
    if causal:
        args = (length,) + args
    return whole(
        functools.partial(attend_back_body, causal, g, len(more)),
        "attend_back",
        [((R, D), F32, HBM), ((R, D + 3 * C), BF), ((8, D), F32, HBM), ((R, D), BF)]
        + [((16, D), BF)] * bool(more),
        *args,
        smem=int(causal),
        after=after,
    )


def weight_body(plan, chunks, sources, n_idx, *refs):
    idx_refs, ins, outs = refs[:n_idx], refs[n_idx : -2 * len(chunks)], refs[-2 * len(chunks) :]
    half = outs[0].shape[0]
    chunk, at, takes = 0, 0, {}
    for part, a_at, off, D, grads in plan:
        if part not in takes:
            spot = lax.broadcasted_iota(jnp.int32, (2 * half, D), 1) == idx_refs[part][...]
            takes[part] = spot.astype(F32).astype(BF)
        parts = [nt(takes[part], ins[a_at + i][:, off : off + D]) for i in range(sources)]
        aT = jnp.concatenate(parts, 1).astype(BF)
        for d_at, d_off, width in grads:
            step = 384 if width % 384 == 0 else 128
            for c in range(d_off, d_off + width, step):
                dy = jnp.concatenate([ins[d_at + i][:, c : c + step] for i in range(sources)], 0)
                got = nn(aT, dy)
                outs[2 * chunk][:, at : at + step] = got[:half].astype(BF)
                outs[2 * chunk + 1][:, at : at + step] = got[half:].astype(BF)
                at += step
                if at == chunks[chunk]:
                    chunk, at = chunk + 1, 0


def weight_grads(idxs, D, term_lists, chunks, after=()):
    ins, plan = [], []
    for part, terms in term_lists:
        for a, off, grads in terms:
            at = len(ins)
            ins += list(a)
            ds = []
            for d, d_off, w in grads:
                ds.append((len(ins), d_off, w))
                ins += list(d)
            plan.append((part, at, off, D, ds))
    half = idxs[0].shape[0] // 2
    return whole(
        functools.partial(weight_body, plan, chunks, len(term_lists[0][1][0][0]), len(idxs)),
        "weight_grads",
        [((half, w), BF) for w in chunks for _ in range(2)],
        *idxs,
        *ins,
        after=after,
    )


def swap(x, bit, n):
    return lax.ppermute(x, "blk", [(i, i ^ bit) for i in range(n)])


def tied(x, *before):
    return lax.optimization_barrier((x, *before))[0]


def other_tp(x):
    return lax.ppermute(x, "tp", [(0, 1), (1, 0)])


class Halving:
    def __init__(self, keep, send, n, bits):
        self.keep, self.send, self.n, self.bits = keep, send, n, bits
        self.got = swap(send, bits[0], n)

    def hold(self, *before):
        self.send = tied(self.send, *before)
        self.got = swap(self.send, self.bits[0], self.n)

    def step(self, *before):
        got = tied(self.got, *before) if before else self.got
        total = self.keep.astype(F32) + got.astype(F32)
        self.bits = self.bits[1:]
        if not self.bits:
            return total
        half = total.shape[0] // 2
        self.keep, self.send = total[:half], total[half:].astype(BF)
        self.got = swap(self.send, self.bits[0], self.n)
        return self.send

    def end(self, *before):
        while len(self.bits) > 1:
            self.step(*before)
        return self.step(*before)


def on_device(
    n,
    encoder_in,
    decoder_in,
    lengths,
    retrieved,
    band_start,
    cotangent,
    enc_query,
    enc_key,
    enc_value,
    enc_mix,
    attn_gain,
    attn_shift,
    enc_up,
    enc_down,
    ffn_gain,
    ffn_shift,
    self_query,
    self_key,
    self_value,
    self_mix,
    self_gain,
    self_shift,
    cross_query,
    cross_key,
    cross_value,
    cross_mix,
    cross_gain,
    cross_shift,
    dec_up,
    dec_down,
    last_gain,
    last_shift,
):
    group_rows, D = encoder_in.shape
    C = cross_query.shape[1]
    FF = enc_up.shape[1]
    hi = n // 16
    me = lax.axis_index("blk")
    core = lambda x: swap(x, 1, n)
    par = jnp.stack(
        [attn_gain, attn_shift, ffn_gain, ffn_shift, self_gain, self_shift, cross_gain, cross_shift, last_gain, last_shift]
    )

    share = D // n
    bits = [1 << i for i in range(n.bit_length() - 1)]

    def rows_by(order):
        t = jnp.arange(share << len(order), dtype=jnp.int32)
        block = t // share
        rel = sum(((block >> (len(order) - 1 - i)) & 1) * bit for i, bit in enumerate(order))
        return ((me ^ rel) * share + t % share).reshape(-1, 1)

    def gradients(order, terms, after=()):
        width = sum(grad[2] for _, _, grads in terms for grad in grads)
        return Halving(*weight_grads([rows_by(order)], D, [(0, terms)], [width], after), n, order)

    def joint(parts, after=()):
        chunks = [w for _, _, widths in parts for w in widths]
        orders = [order for order, _, _ in parts]
        kinds = [order for i, order in enumerate(orders) if order not in orders[:i]]
        term_lists = [(kinds.index(order), terms) for order, terms, _ in parts]
        made = weight_grads([rows_by(order) for order in kinds], D, term_lists, chunks, after)
        gots = [swap(send, 1, n) for send in made[1::2]]

        def finish(*before):
            tied_gots = lax.optimization_barrier((*gots, *before))[: len(gots)]
            totals = [k.astype(F32) + g.astype(F32) for k, g in zip(made[0::2], tied_gots)]
            half, sums = totals[0].shape[0] // 2, []
            for order, _, widths in parts:
                mine, totals = totals[: len(widths)], totals[len(widths) :]
                keep = jnp.concatenate([t[:half] for t in mine], 1)
                send = jnp.concatenate([t[half:].astype(BF) for t in mine], 1)
                sums.append(Halving(keep, send, n, order[1:]))
            return sums

        return made[0], finish

    both = lambda x: (x, core(x))
    summed = lambda *arrays: functools.reduce(lambda x, y: x + y, [t.astype(F32) for t in arrays]).astype(BF)

    *enc_kept, enc_o, enc_part = attend_fwd(encoder_in, enc_query, enc_key, enc_value, enc_mix, fetch=True)
    enc_other = other_tp(enc_part)
    pick = pick_rows(retrieved, band_start, (enc_part,))
    pick_other = [core(p) for p in pick]
    *self_kept, self_o, self_part = attend_fwd(
        decoder_in, self_query, self_key, self_value, self_mix, lengths, pick
    )
    enc_other = tied(enc_other, self_part)
    v1, u1, low1, act1, gp1, part1 = ffn_fwd(0, encoder_in, enc_part, enc_other, par, enc_up, enc_down, True, True)
    other1 = other_tp(part1)
    chosen = picks(tied((me & 1).reshape(1), part1), pick, pick_other, n // 2, group_rows // 2)
    other1 = tied(other1, chosen)
    v2, enc_low, store = store_fwd(2, u1, part1, other1, par, cross_key, cross_value)

    store = store[None]
    for b in range(4, n.bit_length() - 1):
        store = jnp.concatenate([store, swap(store, 1 << b, n)], 0)

    def gid_of(pair):
        return (me ^ jnp.array([16 * h + r for h in range(hi) for r in pair], jnp.int32)) >> 1

    near = swap(store, 4, n)
    y_own = swap(store, 2, n)
    far = swap(store, 8, n)
    self_part = tied(self_part, store)
    self_other = other_tp(self_part)
    vd, ud, lowd, qc = cross_q(4, decoder_in, self_part, self_other, par, cross_query)
    qcs = both(qc)
    encoded = norm_of(2, v2, par, (qc,))
    far = tied(far, near, y_own, qcs[1], encoded)
    apart = swap(far, 4, n)
    y_far = swap(far, 2, n)
    state = cross_fwd(gid_of((0, 2)), qcs, (tied(store, far), y_own), chosen, None, False)
    state = cross_fwd(gid_of((4, 8)), qcs, (near, far), chosen, state, False)
    apart = tied(apart, *state)
    y_near = swap(tied(y_own, apart), 4, n)
    y_apart = swap(apart, 2, n)
    state = cross_fwd(gid_of((12, 10)), qcs, (apart, y_far), chosen, state, False)
    state_own, state_other = cross_fwd(gid_of((6, 14)), qcs, (y_near, y_apart), chosen, state, True)[3:]
    pieces = [(store, y_own), (near, y_near), (far, y_far), (apart, y_apart)]
    log_own, of_own, oc, partc = cross_mix_fwd(state_own, core(state_other), cross_mix)
    otherc = other_tp(partc)
    log_other, of_other = cross_merge(state_other, core(tied(state_own, partc)))
    otherc = tied(otherc, of_other)

    vc, uc, lowc, actc, gpc, part3 = ffn_fwd(6, ud, partc, otherc, par, dec_up, dec_down, False, False)
    other3 = other_tp(part3)
    actc_y = swap(actc, 2, n)
    decoded, dlast, dlowc, dhc, gg_last, part4 = last_fwd_back(8, uc, part3, other3, cotangent, par, gpc, dec_up, dec_down)
    dlowc_y = swap(dlowc, 2, n)
    other4 = tied(other_tp(part4), actc_y, dlowc_y)
    dcross, dpacko, gg_cross = cross_mix_back(6, dlast, part4, other4, vc, par, cross_mix)

    dpackos = both(dpacko)
    back = lambda k, extra, after: cross_back(
        gid_of((4 * k, 4 * k + 2)), qcs, dpackos, pieces[k], chosen, extra, k == 3, k == 0, after
    )
    *extra, keep3, send3 = back(3, (of_own, of_other, log_own, log_other), ())
    got3 = swap(send3, 2, n)
    no_y = bits[:1] + bits[2:]
    down_keep, down_sums = joint([(no_y, [((dlowc, dlowc_y), 0, [((actc, actc_y), 0, FF)])], [FF // 2] * 2)], (send3,))
    *extra, keep1, send1 = back(1, extra, (down_keep,))
    got1 = swap(send1, 2, n)
    one = lambda x: (x,)
    (down,) = down_sums(send1)
    up = gradients(bits, [(one(lowc), 0, [(one(dhc), 0, FF)])], (down.send,))
    sum3 = summed(keep3, tied(got3, up.keep))
    apart = swap(sum3, 4, n)
    *extra, keep2, send2 = back(2, extra, (sum3,))
    got2 = swap(send2, 2, n)
    sum1 = summed(keep1, tied(got1, send2))
    near = swap(sum1, 4, n)
    down_z = down.step(sum1)
    _, _, keep0, send0, dq_own, dq_other = back(0, extra, (sum1, down_z))
    got0 = swap(send0, 2, n)
    up_y = up.step(send0)
    sum2 = summed(keep2, tied(got2, send0, up_y), apart)
    far = swap(sum2, 8, n)
    down.hold(far)
    terms = [keep0, got0, near, far]
    bit = n // 2
    while terms[0].shape[0] > 1:
        half = terms[0].shape[0] // 2
        total = functools.reduce(lambda x, y: x + y, [t.astype(F32) for t in terms])
        terms = [total[:half].astype(BF), swap(total[half:].astype(BF), bit, n)]
        bit //= 2

    dqc, partq = cross_q_back(dq_own, core(tied(dq_other, sum2)), cross_query, ())
    otherq = other_tp(partq)
    v2_near, gp1_near, *loaded = load((v2, gp1, enc_up, enc_down), (partq,))
    dkv, part5 = store_back(terms, cross_key, cross_value, (gp1_near,))
    other5 = other_tp(part5)
    up.hold(got0)
    dself, dpackd, gg_self, part6 = attend_back(
        4, dcross, partq, tied(otherq, got0, near, far), vd, par, self_kept, (self_query, self_key, self_value, self_mix), lengths,
    )
    own_keep, own_sums = joint(
        [
            (
                bits,
                [
                    (one(lowd), 0, [(one(dqc), 0, C)]),
                    (one(dpacko), 0, [(one(oc), 0, C)]),
                    (one(dpackd), 0, [(one(self_o), 0, C)]),
                ],
                [C] * 3,
            ),
            (bits, [(one(decoder_in), 0, [(one(dpackd), D, 3 * C)])], [C] * 3),
        ]
    )
    up_z = up.step(other5)
    mixes, own = own_sums(up_z)
    dffn, dlow1, dh1, gg_ffn, part7 = ffn_back(
        2, part5, tied(other5, mixes.send, own.send), v2_near, par, gp1_near, *loaded, ()
    )
    other7 = other_tp(part7)
    z_first = bits[:1] + bits[2:] + bits[1:2]
    ffn_keep, ffn_sums = joint(
        [
            (z_first, [(one(dlow1), 0, [(one(act1), 0, FF)])], [FF // 2] * 2),
            (
                bits,
                [
                    (one(enc_low), 0, [(one(dkv), 0, 2 * C)]),
                    (one(low1), 0, [(one(dh1), 0, FF)]),
                ],
                [2 * C] + [FF // 2] * 2,
            ),
        ],
    )
    down_sum = down.end(ffn_keep)
    up_z = up.step(down_sum)
    mixes_z = mixes.step(up_z)
    down1, up1 = ffn_sums(mixes_z)
    own_z = own.step(up1.send)
    dattn, dpacke, _, part8, gains = attend_back(
        0, dffn, part7, tied(other7, own_z, down1.send), v1, par, enc_kept, (enc_query, enc_key, enc_value, enc_mix), None,
        (gg_ffn, gg_self, gg_cross, gg_last),
    )
    up_sum = up.end(part8)
    mixes_z = mixes.step(up_sum)
    own_z = own.step(mixes_z)
    lanes = jnp.eye(16, 128, dtype=BF)
    last_keep, last_sums = joint(
        [
            (
                bits,
                [
                    (one(encoder_in), 0, [(one(dpacke), D, 3 * C)]),
                    (one(dpacke), 0, [(one(enc_o), 0, C)]),
                    (one(gains), 0, [(one(lanes), 0, 128)]),
                ],
                [2 * C, 2 * C + 128],
            )
        ],
        (own_z,),
    )
    up1_z = up1.step(last_keep)
    (last,) = last_sums(up1_z)
    other6, other8 = other_tp(tied(part6, last.send)), other_tp(tied(part8, last.send))
    down1_z = down1.step(last.send)
    mixes_sum = mixes.end(down1_z)
    own_sum = own.end(mixes_sum)
    up1_z = up1.step(own_sum)
    down1_z = down1.step(up1_z)
    last_z = last.step(down1_z)
    up1_sum = up1.end(last_z)
    down1_sum = down1.end(up1_sum)
    last_z = last.step(down1_sum)
    last_sum = last.end()
    grad_encoder_in = tied(dattn, last_z) + (part8.astype(F32) + other8.astype(F32))
    grad_decoder_in = tied(dself, last_z) + (part6.astype(F32) + other6.astype(F32))

    cut = lambda total, at, width: total[:, at : at + width]
    gain_of = [last_sum[:, 4 * C + i] for i in range(10)]
    return (
        encoded,
        decoded,
        grad_encoder_in,
        grad_decoder_in,
        cut(last_sum, 0, C),
        cut(last_sum, C, C),
        cut(last_sum, 2 * C, C),
        cut(last_sum, 3 * C, C).T,
        gain_of[0],
        gain_of[1],
        cut(up1_sum, 2 * C, FF),
        down1_sum.T,
        gain_of[2],
        gain_of[3],
        cut(own_sum, 0, C),
        cut(own_sum, C, C),
        cut(own_sum, 2 * C, C),
        cut(mixes_sum, 2 * C, C).T,
        gain_of[4],
        gain_of[5],
        cut(mixes_sum, 0, C),
        cut(up1_sum, 0, C),
        cut(up1_sum, C, C),
        cut(mixes_sum, C, C).T,
        gain_of[6],
        gain_of[7],
        up_sum,
        down_sum.T,
        gain_of[8],
        gain_of[9],
    )


def solution(mesh):
    rows, both, cols, down = P("blk", None), P("blk", "tp"), P(None, "tp"), P("tp", None)
    attn = (cols, cols, cols, down, P(), P())
    ffn = (cols, down, P(), P())
    in_specs = (rows, rows, P("blk"), P("blk", "tp", None), both, rows) + attn + ffn + attn + attn + ffn
    mixed = P("tp", "blk")
    grad_attn = (both, both, both, mixed, P("blk"), P("blk"))
    grad_ffn = (both, mixed, P("blk"), P("blk"))
    out_specs = (rows,) * 4 + grad_attn + grad_ffn + grad_attn + grad_attn + grad_ffn
    return jax.shard_map(
        functools.partial(on_device, mesh.shape["blk"]),
        mesh=mesh,
        in_specs=in_specs,
        out_specs=out_specs,
        check_vma=False,
    )
```
